32 devices in a mesh: ctx: 8 (over z, x), rep: 4 (over y, core).
Axes of the slice: x: 2, y: 2, z: 4, core: 2. Of those that a mesh axis runs over, the one named last changes fastest.
Arguments:
- tokens: bfloat16 [4, 1024, 2880], P('rep', 'ctx'), may hold values from -6 to 6
- router_w: bfloat16 [2880, 32], replicated, may hold values from -0.109375 to 0.109375
- router_b: float32 [32], replicated, may hold values from -4 to 4
- hidden: bfloat16 [4, 1024, 4, 1536], P('rep', 'ctx'), may hold values from -6 to 6
- teacher_idx: int32 [4, 1024, 4], P('rep', 'ctx'), may hold values from 0 to 31, all different within a row
- merge_map: int32 [32], replicated, may hold values from 0 to 15, as said below
- merge_coef: float32 [32], replicated, may hold values from 0.3 to 1.5
- source_w: bfloat16 [32, 1536, 1536], P(None, 'ctx'), may hold values from -0.15625 to 0.15625
- out_grad: bfloat16 [4, 1024, 1536], P('rep', 'ctx'), may hold values from -6 to 6
Outputs:
- mixed: bfloat16 [4, 1024, 1536], P('rep', 'ctx')
- hidden_grad: bfloat16 [4, 1024, 4, 1536], P('rep', 'ctx')
- token_grad: bfloat16 [4, 1024, 2880], P('rep', 'ctx')
- router_w_grad: float32 [2880, 32], replicated
- router_b_grad: float32 [32], replicated
- coef_grad: float32 [32], replicated
- source_w_grad: float32 [32, 1536, 1536], P(None, 'ctx', 'rep')
The draws below stay inside these ranges and needn't reach their ends.
Inputs may be any that keep to these rules, and one draw needn't show every extreme that they name: `teacher_idx`: each token names 4 different experts. `merge_map`: each of the 16 combinations takes exactly two of the 32 experts.
All inputs are finite; a program needn't handle non-finite values.
Results may differ from the reference program's by a relative error of at most 0.0064.
Values may be sent and summed in bfloat16 or wider, within the bound.
No kernel may reach another device: no remote copies, remote signals or barrier semaphores. Data moves between devices by JAX's collectives and lax.ppermute only.
A program may use at most 128 MiB of HBM per device.

```python
import math
import jax
import jax.numpy as jnp
from jax import lax

D = 2880
SOURCES = 32
TOP = 4
MERGED = 16
DW = 1536
FFW = 1536
TOK_DEV = 128
SEQS = 4
LENGTH = 1024
LOCAL_M = 2
COPIES = 1
CAP = 80
ALL_TOK = 4096
N_CTX = 8


def draw_merge_map(key, part):
    order = jax.random.permutation(jax.random.fold_in(key, 11), SOURCES)
    return (order // 2).astype(jnp.int32)


def block_scale(stream_key, dims, split, smallest, largest):
    loudness, own = 1.0, jax.random.fold_in(stream_key, 6)
    for dim, shards_of in split:
        steps = jnp.exp(jax.random.uniform(jax.random.fold_in(own, dim), (shards_of,), jnp.float32, smallest / len(split), largest / len(split)))
        loudness = loudness * jnp.repeat(steps, dims[dim] // shards_of).reshape([-1 if axis == dim else 1 for axis in range(len(dims))])
    return loudness


def distinct(stream_key, rows, number_of, top, lift):
    sequence = jax.random.permutation(jax.random.fold_in(stream_key, 1), number_of)
    boost = sequence
    for power in range(3):
        boost = boost * boost // number_of
    boost = boost * lift // number_of
    lots = jax.random.randint(jax.random.fold_in(stream_key, 2), (rows, number_of), 0, 4096) + boost
    holders = jax.random.permutation(jax.random.fold_in(stream_key, 3), rows)[jnp.arange(number_of) % rows]
    lots = jnp.where(jnp.arange(rows)[:, None] == holders[None, :], 1 << 14, lots)
    merit = lots * number_of + jnp.arange(number_of)
    return lax.top_k(merit.astype(jnp.int32), top)[1].astype(jnp.int32)


def normal_values(stream_key, dims, spread, bound, cuts=(), held_as=jnp.bfloat16):
    loudness = block_scale(stream_key, dims, cuts, -0.22, 0.18) if cuts else 1.0
    drawn = jax.random.normal(stream_key, dims, jnp.float32) * spread * loudness
    return jnp.minimum(jnp.maximum(drawn, -bound), bound).astype(held_as)


def setup_inputs(seed: int = 0) -> dict:
    splits = jax.random.split(jax.random.key(seed), 10)
    tokens = normal_values(splits[0], (SEQS, LENGTH, D), 1.0, 6.0, ((0, 4), (1, 8)))
    router_w = normal_values(splits[1], (D, SOURCES), D ** -0.5, 0.109375)
    router_b = normal_values(splits[2], (SOURCES,), 1.0, 4.0, (), jnp.float32)
    hidden = normal_values(splits[3], (SEQS, LENGTH, TOP, FFW), 1.0, 6.0, ((0, 4), (1, 8)))
    teacher_idx = distinct(splits[4], SEQS * LENGTH, SOURCES, TOP, 0).reshape((SEQS, LENGTH, TOP))
    merge_map = draw_merge_map(jax.random.fold_in(splits[9], 71), 0)
    merge_coef = jnp.clip(jnp.exp(jax.random.uniform(splits[6], (SOURCES,), jnp.float32, math.log(0.3), math.log(1.5))), 0.3, 1.5)
    source_w = normal_values(splits[7], (SOURCES, DW, FFW), FFW ** -0.5, 0.15625, ((1, 8),))
    out_grad = normal_values(splits[8], (SEQS, LENGTH, DW), 1.0, 6.0, ((0, 4), (1, 8)))
    return dict(tokens=tokens, router_w=router_w, router_b=router_b, hidden=hidden, teacher_idx=teacher_idx, merge_map=merge_map, merge_coef=merge_coef, source_w=source_w, out_grad=out_grad)


def reference(tokens, router_w, router_b, hidden, teacher_idx, merge_map, merge_coef, source_w, out_grad):
    seq_count = tokens.shape[0]
    seq_len = tokens.shape[1]
    blocks = seq_count * N_CTX
    per_block = TOK_DEV * TOP
    grad_scale = 1.0 / math.sqrt(ALL_TOK)
    flat_x = tokens.reshape(-1, D)
    logits = jnp.dot(flat_x, router_w, preferred_element_type=jnp.float32) + router_b
    choice_ids = teacher_idx.reshape(-1, TOP)
    chosen = jnp.take_along_axis(logits, choice_ids, axis=1)
    raised = jnp.exp(chosen)
    gate_probs = raised / lax.optimization_barrier(jnp.sum(raised, axis=1, keepdims=True))
    merged_id = merge_map[choice_ids]
    position = jnp.tile(jnp.arange(seq_len, dtype=jnp.int32), seq_count)
    lane_id = merged_id // LOCAL_M * COPIES + (position % COPIES)[:, None]
    member_id = merged_id % LOCAL_M
    lane_blocks = lane_id.reshape(blocks, per_block)
    onehot = (lane_blocks[:, :, None] == jnp.arange(N_CTX, dtype=jnp.int32)[None, None, :]).astype(jnp.int32)
    before = jnp.cumsum(onehot, axis=1) - onehot
    slot_rank = lax.optimization_barrier(jnp.sum(before * onehot, axis=2))
    is_kept = slot_rank < CAP
    slot_index = jnp.where(is_kept, lane_blocks * CAP + slot_rank, N_CTX * CAP)
    block_ids = jnp.broadcast_to(jnp.arange(blocks, dtype=jnp.int32)[:, None], (blocks, per_block))
    slot_numbers = jnp.broadcast_to(jnp.arange(per_block, dtype=jnp.int32)[None, :], (blocks, per_block))
    slot_source = jnp.full((blocks, N_CTX * CAP + 1), per_block, jnp.int32)
    slot_source = slot_source.at[block_ids, slot_index].set(slot_numbers)
    slot_source = slot_source[:, :N_CTX * CAP].reshape(blocks, N_CTX, CAP)
    slot_grad = (gate_probs[:, :, None] * out_grad.reshape(-1, 1, DW).astype(jnp.float32)).astype(jnp.bfloat16)
    pad_hidden = jnp.concatenate([hidden.reshape(blocks, per_block, FFW), jnp.zeros((blocks, 1, FFW), jnp.bfloat16)], axis=1)
    pad_grad = jnp.concatenate([slot_grad.reshape(blocks, per_block, DW), jnp.zeros((blocks, 1, DW), jnp.bfloat16)], axis=1)
    pad_member = jnp.concatenate([member_id.reshape(blocks, per_block), jnp.zeros((blocks, 1), jnp.int32)], axis=1)
    mixing = (merge_map[:, None] == jnp.arange(MERGED, dtype=jnp.int32)[None, :]).astype(jnp.float32) * merge_coef[:, None]
    merged = jnp.einsum('eg,edf->gdf', mixing, source_w.astype(jnp.float32), precision=lax.Precision.HIGHEST).astype(jnp.bfloat16)

    def lane_work(lane_now):
        source_now = lax.dynamic_index_in_dim(slot_source, lane_now, 1, keepdims=False)
        rows_hidden = jnp.take_along_axis(pad_hidden, source_now[:, :, None], axis=1).reshape(-1, FFW)
        rows_grad = jnp.take_along_axis(pad_grad, source_now[:, :, None], axis=1).reshape(-1, DW)
        rows_member = jnp.take_along_axis(pad_member, source_now, axis=1).reshape(-1)
        out_rows = jnp.zeros((rows_hidden.shape[0], DW), jnp.float32)
        back_rows = jnp.zeros((rows_hidden.shape[0], FFW), jnp.float32)
        grad_list = []
        for member_now in range(LOCAL_M):
            weight = lax.dynamic_index_in_dim(merged, lane_now // COPIES * LOCAL_M + member_now, 0, keepdims=False)
            selected = (rows_member == member_now)[:, None]
            forward = lax.dot_general(rows_hidden, weight, (((1,), (1,)), ((), ())), preferred_element_type=jnp.float32)
            out_rows = jnp.where(selected, forward, out_rows)
            backward = jnp.dot(rows_grad, weight, preferred_element_type=jnp.float32)
            back_rows = jnp.where(selected, backward, back_rows)
            masked = jnp.where(selected, rows_grad, jnp.zeros_like(rows_grad))
            grad_list.append(lax.dot_general(masked, rows_hidden, (((0,), (0,)), ((), ())), preferred_element_type=jnp.float32))
        return (out_rows.astype(jnp.bfloat16).reshape(blocks, CAP, DW), back_rows.astype(jnp.bfloat16).reshape(blocks, CAP, FFW), jnp.stack(grad_list))
    lane_out, lane_back, lane_grads = lax.map(lane_work, jnp.arange(N_CTX, dtype=jnp.int32))
    merged_grad = lane_grads.reshape(MERGED // LOCAL_M, COPIES, LOCAL_M, DW, FFW).sum(axis=1).reshape(MERGED, DW, FFW)
    lane_safe = jnp.where(is_kept, lane_blocks, 0)
    rank_safe = jnp.where(is_kept, slot_rank, 0)
    slot_out = jnp.where(is_kept[:, :, None], lane_out[lane_safe, block_ids, rank_safe], jnp.zeros((), jnp.bfloat16)).reshape(-1, TOP, DW)
    hidden_grad = jnp.where(is_kept[:, :, None], lane_back[lane_safe, block_ids, rank_safe], jnp.zeros((), jnp.bfloat16)).reshape(seq_count, seq_len, TOP, FFW)
    mixed = lax.optimization_barrier(jnp.sum(gate_probs[:, :, None] * slot_out.astype(jnp.float32), axis=1)).astype(jnp.bfloat16).reshape(seq_count, seq_len, DW)
    score_grad = lax.optimization_barrier(jnp.sum(out_grad.reshape(-1, 1, DW).astype(jnp.float32) * slot_out.astype(jnp.float32), axis=2))
    chosen_grad = gate_probs * (score_grad - lax.optimization_barrier(jnp.sum(gate_probs * score_grad, axis=1, keepdims=True)))
    pick_table = (choice_ids[:, :, None] == jnp.arange(SOURCES, dtype=jnp.int32)[None, None, :]).astype(jnp.float32)
    logit_grad = lax.optimization_barrier(jnp.sum(pick_table * chosen_grad[:, :, None], axis=1))
    logit_half = logit_grad.astype(jnp.bfloat16)
    token_grad = lax.dot_general(logit_half, router_w, (((1,), (1,)), ((), ())), preferred_element_type=jnp.float32).astype(jnp.bfloat16).reshape(seq_count, seq_len, D)
    router_w_grad = lax.dot_general(flat_x, logit_half, (((0,), (0,)), ((), ())), preferred_element_type=jnp.float32) * grad_scale
    router_b_grad = lax.optimization_barrier(jnp.sum(logit_grad, axis=0)) * grad_scale
    source_grad = merged_grad[merge_map]
    coef_grad = jnp.einsum('edf,edf->e', source_grad, source_w.astype(jnp.float32), precision=lax.Precision.HIGHEST) * grad_scale
    source_w_grad = source_grad * merge_coef[:, None, None] * grad_scale
    return (mixed, hidden_grad, token_grad, router_w_grad, router_b_grad, coef_grad, source_w_grad)
```

```python
import functools
import math

import jax
import jax.numpy as jnp
from jax import lax
from jax.experimental import pallas as pl
from jax.experimental.pallas import tpu as pltpu
from jax.sharding import PartitionSpec as P

MERGED = 16


def expert_rows(rows_hidden, rows_grad, rows_member, lane_weights):
    row_count = rows_hidden.shape[0]
    out_rows = jnp.zeros((row_count, lane_weights.shape[1]), jnp.float32)
    back_rows = jnp.zeros((row_count, lane_weights.shape[2]), jnp.float32)
    grad_list = []
    for member_now in range(lane_weights.shape[0]):
        weight = lane_weights[member_now]
        selected = (rows_member == member_now)[:, None]
        forward = lax.dot_general(
            rows_hidden, weight, (((1,), (1,)), ((), ())), preferred_element_type=jnp.float32
        )
        out_rows = jnp.where(selected, forward, out_rows)
        backward = jnp.dot(rows_grad, weight, preferred_element_type=jnp.float32)
        back_rows = jnp.where(selected, backward, back_rows)
        masked = jnp.where(selected, rows_grad, jnp.zeros_like(rows_grad))
        grad_list.append(
            lax.dot_general(
                masked, rows_hidden, (((0,), (0,)), ((), ())), preferred_element_type=jnp.float32
            )
        )
    return (out_rows, back_rows, jnp.stack(grad_list))


def on_device(
    tokens, router_w, router_b, hidden, teacher_idx, merge_map, merge_coef, source_w, out_grad
):
    ctx_count = lax.axis_size("ctx")
    rep_count = lax.axis_size("rep")
    tok_count = tokens.shape[1]
    feature_count = tokens.shape[2]
    top_count = teacher_idx.shape[2]
    hidden_width = hidden.shape[3]
    out_width = out_grad.shape[2]
    source_count = router_w.shape[1]
    row_share = source_w.shape[1]
    per_lane = max(1, MERGED // ctx_count)
    copies = max(1, ctx_count // MERGED)
    capacity = 5 * tok_count * top_count // (4 * ctx_count)
    slot_count = tok_count * top_count
    grad_scale = 1.0 / math.sqrt(tok_count * ctx_count * rep_count)
    flat_x = tokens.reshape(tok_count, feature_count)
    logits = jnp.dot(flat_x, router_w, preferred_element_type=jnp.float32) + router_b
    choice_ids = teacher_idx.reshape(tok_count, top_count)
    pick_table = choice_ids[:, :, None] == jnp.arange(source_count, dtype=jnp.int32)[None, None, :]
    pick_float = pick_table.astype(jnp.float32)
    chosen = jnp.sum(pick_float * logits[:, None, :], axis=2)
    raised = jnp.exp(chosen)
    gate_probs = raised / jnp.sum(raised, axis=1, keepdims=True)
    merged_id = jnp.sum(jnp.where(pick_table, merge_map[None, None, :], 0), axis=2)
    position = lax.axis_index("ctx") * tok_count + jnp.arange(tok_count, dtype=jnp.int32)
    lane_id = merged_id // per_lane * copies + (position % copies)[:, None]
    member_id = (merged_id % per_lane).reshape(-1)
    lane_flat = lane_id.reshape(-1)
    onehot = (lane_flat[:, None] == jnp.arange(ctx_count, dtype=jnp.int32)[None, :]).astype(
        jnp.int32
    )
    before = jnp.cumsum(onehot, axis=0) - onehot
    slot_rank = jnp.sum(before * onehot, axis=1)
    is_kept = slot_rank < capacity
    slot_index = jnp.where(is_kept, lane_flat * capacity + slot_rank, ctx_count * capacity)
    slot_source = (
        jnp.full((ctx_count * capacity + 1,), slot_count, jnp.int32)
        .at[slot_index]
        .set(jnp.arange(slot_count, dtype=jnp.int32))[: ctx_count * capacity]
    )
    slot_grad = (gate_probs[:, :, None] * out_grad.reshape(tok_count, 1, out_width)).astype(
        jnp.bfloat16
    )
    pad_hidden = jnp.concatenate(
        [hidden.reshape(slot_count, hidden_width), jnp.zeros((1, hidden_width), jnp.bfloat16)],
        axis=0,
    )
    pad_grad = jnp.concatenate(
        [slot_grad.reshape(slot_count, out_width), jnp.zeros((1, out_width), jnp.bfloat16)], axis=0
    )
    pad_member = jnp.concatenate([member_id, jnp.zeros((1,), jnp.int32)], axis=0)
    send_hidden = pad_hidden[slot_source].reshape(ctx_count, capacity, hidden_width)
    send_grad = pad_grad[slot_source].reshape(ctx_count, capacity, out_width)
    send_member = pad_member[slot_source].reshape(ctx_count, capacity)
    lane_group = lax.axis_index("ctx") // copies
    same_group = merge_map[:, None] == merge_map[None, :]
    earlier = jnp.arange(source_count)[:, None] > jnp.arange(source_count)[None, :]
    member_rank = jnp.sum((same_group & earlier).astype(jnp.int32), axis=1)
    source_order = (
        jnp.zeros((source_count,), jnp.int32)
        .at[2 * merge_map + member_rank]
        .set(jnp.arange(source_count, dtype=jnp.int32))
    )
    picked = source_w[source_order].reshape(
        MERGED // per_lane, 2 * per_lane, row_share, hidden_width
    )
    outgoing = jnp.repeat(picked, copies, axis=0)
    arrived = lax.all_to_all(outgoing, "ctx", split_axis=0, concat_axis=2, tiled=True)
    pair_rows = arrived.reshape(per_lane, 2, row_share * ctx_count, hidden_width)
    coef_table = merge_coef[source_order].reshape(MERGED // per_lane, per_lane, 2)
    pair_coef = lax.dynamic_index_in_dim(coef_table, lane_group, 0, keepdims=False)
    lane_weights = (
        pair_coef[:, 0, None, None] * pair_rows[:, 0].astype(jnp.float32)
        + pair_coef[:, 1, None, None] * pair_rows[:, 1].astype(jnp.float32)
    ).astype(jnp.bfloat16)
    recv_hidden, recv_grad, recv_member = (
        lax.all_to_all(send_hidden, "ctx", split_axis=0, concat_axis=0, tiled=True),
        lax.all_to_all(send_grad, "ctx", split_axis=0, concat_axis=0, tiled=True),
        lax.all_to_all(send_member, "ctx", split_axis=0, concat_axis=0, tiled=True),
    )
    out_rows, back_rows, lane_grads = expert_rows(
        recv_hidden.reshape(-1, hidden_width),
        recv_grad.reshape(-1, out_width),
        recv_member.reshape(-1),
        lane_weights,
    )
    home_out, home_back = (
        lax.all_to_all(
            out_rows.astype(jnp.bfloat16).reshape(ctx_count, capacity, out_width),
            "ctx",
            split_axis=0,
            concat_axis=0,
            tiled=True,
        ),
        lax.all_to_all(
            back_rows.astype(jnp.bfloat16).reshape(ctx_count, capacity, hidden_width),
            "ctx",
            split_axis=0,
            concat_axis=0,
            tiled=True,
        ),
    )
    slot_out = jnp.concatenate(
        [home_out.reshape(-1, out_width), jnp.zeros((1, out_width), jnp.bfloat16)], axis=0
    )[slot_index].reshape(tok_count, top_count, out_width)
    hidden_grad = jnp.concatenate(
        [home_back.reshape(-1, hidden_width), jnp.zeros((1, hidden_width), jnp.bfloat16)], axis=0
    )[slot_index].reshape(1, tok_count, top_count, hidden_width)
    mixed = (
        jnp.sum(gate_probs[:, :, None] * slot_out.astype(jnp.float32), axis=1)
        .astype(jnp.bfloat16)
        .reshape(1, tok_count, out_width)
    )
    score_grad = jnp.einsum(
        "td,tkd->tk",
        out_grad.reshape(tok_count, out_width),
        slot_out,
        preferred_element_type=jnp.float32,
    )
    chosen_grad = gate_probs * (
        score_grad - jnp.sum(gate_probs * score_grad, axis=1, keepdims=True)
    )
    logit_grad = jnp.sum(pick_float * chosen_grad[:, :, None], axis=1)
    logit_half = logit_grad.astype(jnp.bfloat16)
    token_grad = (
        lax.dot_general(
            logit_half, router_w, (((1,), (1,)), ((), ())), preferred_element_type=jnp.float32
        )
        .astype(jnp.bfloat16)
        .reshape(1, tok_count, feature_count)
    )
    part_router_w = lax.dot_general(
        flat_x, logit_half, (((0,), (0,)), ((), ())), preferred_element_type=jnp.float32
    )
    part_router_b = jnp.sum(logit_grad, axis=0)
    arrived_grads = lax.all_to_all(
        lane_grads.reshape(per_lane, ctx_count, row_share, hidden_width),
        "ctx",
        split_axis=1,
        concat_axis=0,
        tiled=True,
    )
    merged_grad = (
        arrived_grads.reshape(MERGED // per_lane, copies, per_lane, row_share, hidden_width)
        .sum(axis=1)
        .reshape(MERGED, row_share, hidden_width)
    )
    source_grad = merged_grad[merge_map]
    coef_part = jnp.einsum(
        "edf,edf->e", source_grad, source_w.astype(jnp.float32), precision=lax.Precision.HIGHEST
    )
    summed = lax.psum_scatter(
        source_grad * merge_coef[:, None, None], "rep", scatter_dimension=2, tiled=True
    )
    source_w_grad = summed * grad_scale
    router_sum, bias_sum, coef_sum = lax.psum(
        (part_router_w, part_router_b, coef_part), ("ctx", "rep")
    )
    return (
        mixed,
        hidden_grad,
        token_grad,
        router_sum * grad_scale,
        bias_sum * grad_scale,
        coef_sum * grad_scale,
        source_w_grad,
    )


BF = jnp.bfloat16
F32 = jnp.float32
I32 = jnp.int32
TILE = 256


def any_spec():
    return pl.BlockSpec(memory_space=pl.ANY)


def smem_spec():
    return pl.BlockSpec(memory_space=pltpu.SMEM)


def vmem_spec():
    return pl.BlockSpec(memory_space=pltpu.VMEM)


def params(mib):
    return pltpu.CompilerParams(vmem_limit_bytes=mib * 1024 * 1024)


def dot(a, b, dims):
    return lax.dot_general(a, b, (dims, ((), ())), preferred_element_type=F32)


def merge_kernel(order_ref, place_ref, coef_ref, one_ref, two_ref, out_ref):
    first = 2 * combo_of(pl.program_id(0), pl.program_id(1), place_ref)
    one = coef_ref[order_ref[first]]
    two = coef_ref[order_ref[first + 1]]
    out_ref[0, 0] = (one * one_ref[0].astype(F32) + two * two_ref[0].astype(F32)).astype(BF)


def combo_of(step, member, place_ref):
    return 4 * jnp.bitwise_xor(place_ref[0], step) + 2 * place_ref[1] + member


def merge_experts(order, where_am_i, merge_coef, source_w, places):
    _, rows, width = source_w.shape
    half = width // 2

    def pick(which):
        def index(j, m, order_ref, place_ref):
            return (order_ref[2 * combo_of(j, m, place_ref) + which], 0, place_ref[2])

        return index

    return pl.pallas_call(
        merge_kernel,
        grid_spec=pltpu.PrefetchScalarGridSpec(
            num_scalar_prefetch=2,
            grid=(places, 2),
            in_specs=[
                smem_spec(),
                pl.BlockSpec((1, rows, half), pick(0)),
                pl.BlockSpec((1, rows, half), pick(1)),
            ],
            out_specs=pl.BlockSpec((1, 1, rows, half), lambda j, m, *_: (j, m, 0, 0)),
        ),
        out_shape=jax.ShapeDtypeStruct((places, 2, rows, half), BF),
        compiler_params=params(56),
        name="merge_experts",
    )(order, where_am_i, merge_coef, source_w, source_w)


def column(row):
    size = row.shape[1]
    same = lax.broadcasted_iota(I32, (size, size), 0) == lax.broadcasted_iota(I32, (size, size), 1)
    return jnp.sum(jnp.where(same, row, jnp.zeros_like(row)), axis=1, keepdims=True)


def to_row(col):
    size = col.shape[0]
    same = lax.broadcasted_iota(I32, (size, size), 0) == lax.broadcasted_iota(I32, (size, size), 1)
    return jnp.sum(jnp.where(same, col, jnp.zeros_like(col)), axis=0, keepdims=True)


def picks_of(idx_ref, k, sources):
    tok = idx_ref.shape[1]
    return lax.broadcasted_iota(I32, (sources, tok), 0) == idx_ref[k : k + 1, :]


def route_kernel(
    capacity, lanes,
    xt_ref, rwt_ref, rb_ref, idx_ref, map_ref, hid_ref, og_ref,
    sh_ref, sg_ref, gate_ref, pos_ref, slot_ref,
):
    top, tok = idx_ref.shape
    sources = rwt_ref.shape[0]
    slots, width = hid_ref.shape
    places = lanes * capacity
    logits = jnp.dot(rwt_ref[...], xt_ref[...], preferred_element_type=F32) + rb_ref[...]
    raised, merged = [], []
    for k in range(top):
        pick = picks_of(idx_ref, k, sources)
        chosen = jnp.sum(jnp.where(pick, logits, 0.0), axis=0, keepdims=True)
        raised.append(jnp.exp(chosen))
        merged.append(jnp.sum(jnp.where(pick, map_ref[...], 0), axis=0, keepdims=True))
    total = raised[0]
    for k in range(1, top):
        total = total + raised[k]
    gates = [r / total for r in raised]
    lane = [jnp.right_shift(g, 1) for g in merged]
    member = [jnp.bitwise_and(g, 1) for g in merged]
    onehot = [(lax.broadcasted_iota(I32, (lanes, tok), 0) == l).astype(F32) for l in lane]
    all_hot = onehot[0]
    for k in range(1, top):
        all_hot = all_hot + onehot[k]
    earlier = (
        lax.broadcasted_iota(I32, (tok, tok), 0) < lax.broadcasted_iota(I32, (tok, tok), 1)
    ).astype(BF)
    before = jnp.dot(all_hot.astype(BF), earlier, preferred_element_type=F32)
    position = []
    for k in range(top):
        rank = jnp.sum(before * onehot[k], axis=0, keepdims=True).astype(I32)
        before = before + onehot[k]
        position.append(jnp.where(rank < capacity, lane[k] * capacity + rank, -1))
    gate_ref[...] = jnp.zeros_like(gate_ref)
    pos_ref[...] = jnp.full_like(pos_ref, -1)
    for k in range(top):
        gate_ref[k : k + 1, :] = gates[k]
        pos_ref[k : k + 1, :] = position[k]
    spot = jnp.zeros((8, slots), F32)
    for k in range(top):
        spread = (
            lax.broadcasted_iota(I32, (tok, slots), 1)
            == lax.broadcasted_iota(I32, (tok, slots), 0) * top + k
        ).astype(BF)
        kept = position[k] >= 0
        parts = [
            jnp.where(kept, jnp.right_shift(position[k], 5), 0),
            jnp.where(kept, jnp.bitwise_and(position[k], 31), 0),
            jnp.where(kept, 1, 0),
            member[k],
        ]
        stacked = jnp.concatenate(
            [p.astype(F32) for p in parts] + [jnp.zeros((4, tok), F32)], axis=0
        ).astype(BF)
        spot = spot + jnp.dot(stacked, spread, preferred_element_type=F32)
    spot = spot.astype(I32)
    slot_pos = jnp.where(spot[2:3] > 0, spot[0:1] * 32 + spot[1:2], -1)
    slot_ref[...] = jnp.broadcast_to(slot_pos, slot_ref.shape)
    take = lax.broadcasted_iota(I32, (places, slots), 0) == slot_pos
    placed = jnp.sum(jnp.where(take, spot[3:4].astype(F32), 0.0), axis=1, keepdims=True)
    sh_ref[:, width:] = jnp.broadcast_to(placed, (places, sh_ref.shape[1] - width)).astype(BF)
    take = take.astype(BF)
    for n in range(0, width, TILE):
        sh_ref[:, n : n + TILE] = jnp.dot(
            take, hid_ref[:, n : n + TILE], preferred_element_type=F32
        ).astype(BF)
    takes = [
        (lax.broadcasted_iota(I32, (places, tok), 0) == position[k]).astype(BF) for k in range(top)
    ]
    columns = [column(g) for g in gates]
    for n in range(0, og_ref.shape[1], TILE):
        og = og_ref[:, n : n + TILE].astype(F32)
        rows = jnp.zeros((places, TILE), F32)
        for k in range(top):
            rows = rows + jnp.dot(takes[k], (columns[k] * og).astype(BF), preferred_element_type=F32)
        sg_ref[:, n : n + TILE] = rows.astype(BF)


def route(xt, rwt, router_b, idx_t, merge_map, hid, og, capacity, lanes):
    places = lanes * capacity
    slots, width = hid.shape
    tok = idx_t.shape[1]
    return pl.pallas_call(
        functools.partial(route_kernel, capacity, lanes),
        in_specs=[vmem_spec()] * 7,
        out_specs=[vmem_spec()] * 5,
        out_shape=[
            jax.ShapeDtypeStruct((places, width + 128), BF),
            jax.ShapeDtypeStruct((places, og.shape[1]), BF),
            jax.ShapeDtypeStruct((8, tok), F32),
            jax.ShapeDtypeStruct((8, tok), I32),
            jax.ShapeDtypeStruct((8, slots), I32),
        ],
        compiler_params=params(56),
        name="route",
    )(xt, rwt, router_b[:, None], idx_t, merge_map[:, None], hid, og)


def load_weights(spot_ref, mine, other, w_ref, sems):
    rows = mine[0].shape[1]
    core = spot_ref[8]
    copies = []
    for d in range(len(mine)):
        at = pl.ds(pl.multiple_of(spot_ref[d], rows), rows)
        for n, part in enumerate((mine[d], other[d])):
            copies.append(
                pltpu.make_async_copy(
                    part, w_ref.at[core if n == 0 else 1 - core, :, at, :], sems.at[2 * d + n]
                )
            )
    for copy in copies:
        copy.start()
    for copy in copies:
        copy.wait()


def forward_kernel(spot_ref, rows_ref, *refs):
    parts, (out_ref, w_ref, sems) = refs[:-3], refs[-3:]
    load_weights(spot_ref, parts[0::2], parts[1::2], w_ref, sems)
    half = w_ref.shape[3]
    member = rows_ref[:, 2 * half : 2 * half + 1].astype(F32)

    @pl.loop(0, out_ref.shape[1] // TILE)
    def _(n):
        at = pl.ds(pl.multiple_of(n * TILE, TILE), TILE)
        both = [
            dot(rows_ref[:, :half], w_ref[0, m, at, :], ((1,), (1,)))
            + dot(rows_ref[:, half : 2 * half], w_ref[1, m, at, :], ((1,), (1,)))
            for m in range(2)
        ]
        out_ref[:, at] = jnp.where(member == 0.0, both[0], both[1]).astype(BF)


def backward_kernel(spot_ref, rows_ref, flag_ref, *refs):
    parts, (out_ref, w_ref, sems) = refs[:-3], refs[-3:]
    load_weights(spot_ref, parts[0::2], parts[1::2], w_ref, sems)
    half = w_ref.shape[3]
    member = flag_ref[:, :1].astype(F32)
    for h in range(2):

        @pl.loop(0, half // TILE)
        def _(n, h=h):
            at = pl.ds(pl.multiple_of(n * TILE, TILE), TILE)
            both = [dot(rows_ref[...], w_ref[h, m, :, at], ((1,), (0,))) for m in range(2)]
            to = pl.ds(pl.multiple_of(h * half + n * TILE, TILE), TILE)
            out_ref[:, to] = jnp.where(member == 0.0, both[0], both[1]).astype(BF)


def run_lane(kernel, spots, row_args, row_specs, mine, other, out_width, name):
    parts = [p for pair in zip(mine, other) for p in pair]
    members, rows, half = mine[0].shape
    depth = rows * len(mine)
    count = row_args[0].shape[0]
    return pl.pallas_call(
        kernel,
        grid=(1,),
        in_specs=[smem_spec()] + row_specs + [any_spec()] * len(parts),
        out_specs=pl.BlockSpec((count, out_width), lambda i: (0, 0)),
        out_shape=jax.ShapeDtypeStruct((count, out_width), BF),
        scratch_shapes=[
            pltpu.VMEM((2, members, depth, half), BF),
            pltpu.SemaphoreType.DMA((len(parts),)),
        ],
        compiler_params=params(56),
        cost_estimate=pl.CostEstimate(
            flops=4 * count * depth * 2 * half,
            bytes_accessed=4 * members * depth * half + 8 * count * half,
            transcendentals=0,
        ),
        name=name,
    )(spots, *row_args, *parts)


def lane_grad_kernel(has_other, _, hid_ref, flag_ref, grd_ref, *refs):
    out_ref = refs[-1]
    chosen = flag_ref[:, :1].astype(F32) == pl.program_id(1).astype(F32)
    hid = jnp.where(chosen, hid_ref[...], jnp.zeros_like(hid_ref))
    blocks, _, _, rows, cols = out_ref.shape
    each = 2

    @pl.loop(0, blocks // each)
    def _(n):
        at = pl.ds(pl.multiple_of(n * each * rows, each * rows), each * rows)
        part = dot(grd_ref[:, at], hid, ((0,), (0,))).reshape(each, rows, cols)
        to = pl.ds(n * each, each)
        if has_other:
            part = part + refs[0][to, 0, 0].astype(F32)
        out_ref[to, 0, 0] = part.astype(BF)


def lane_grads(select, hid, grd, other, blocks, reps):
    count, depth = grd.shape
    width = hid.shape[1] - 128
    cols = width // reps
    shape = (blocks, 2, 2, depth // blocks, cols)
    block = pl.BlockSpec((blocks, 1, 1, depth // blocks, cols), lambda y, m, s: (0, y, m, 0, 0))
    extra = [] if other is None else [other]
    return pl.pallas_call(
        functools.partial(lane_grad_kernel, other is not None),
        grid_spec=pltpu.PrefetchScalarGridSpec(
            num_scalar_prefetch=1,
            grid=(2, 2),
            in_specs=[
                pl.BlockSpec((count, cols), lambda y, m, s: (0, 2 * y + s[0])),
                pl.BlockSpec((count, 128), lambda y, m, s: (0, width // 128)),
                pl.BlockSpec((count, depth), lambda y, m, s: (0, 0)),
            ]
            + [block] * len(extra),
            out_specs=block,
        ),
        out_shape=jax.ShapeDtypeStruct(shape, BF),
        compiler_params=params(56),
        cost_estimate=pl.CostEstimate(
            flops=4 * count * depth * cols * 2,
            bytes_accessed=4 * depth * cols * 4 + 4 * count * depth,
            transcendentals=0,
        ),
        name="lane_grads_add" if extra else "lane_grads_first",
    )(select, hid, hid, grd, *extra)


def combine_kernel(
    out_ref, og_ref, gate_ref, pos_ref, idx_ref, rwt_ref, xt_ref, mixed_ref, tg_ref, part_ref
):
    places, width = out_ref.shape
    top, tok = idx_ref.shape
    sources, features = rwt_ref.shape
    takes = [
        (lax.broadcasted_iota(I32, (places, tok), 0) == pos_ref[k : k + 1, :]).astype(BF)
        for k in range(top)
    ]
    gates = [gate_ref[k : k + 1, :] for k in range(top)]
    columns = [column(g) for g in gates]
    scores = [jnp.zeros((tok, 1), F32) for _ in range(top)]
    for n in range(0, width, TILE):
        og = og_ref[:, n : n + TILE].astype(F32)
        rows = out_ref[:, n : n + TILE]
        mixed = jnp.zeros((tok, TILE), F32)
        for k in range(top):
            slot_out = dot(takes[k], rows, ((0,), (0,)))
            mixed = mixed + columns[k] * slot_out
            scores[k] = scores[k] + jnp.sum(og * slot_out, axis=1, keepdims=True)
        mixed_ref[:, n : n + TILE] = mixed.astype(BF)
    scores = [to_row(s) for s in scores]
    middle = gates[0] * scores[0]
    for k in range(1, top):
        middle = middle + gates[k] * scores[k]
    logit_grad = jnp.zeros((sources, tok), F32)
    for k in range(top):
        chosen_grad = gates[k] * (scores[k] - middle)
        logit_grad = logit_grad + jnp.where(picks_of(idx_ref, k, sources), chosen_grad, 0.0)
    logit_half = logit_grad.astype(BF)
    tg_ref[...] = dot(rwt_ref[...], logit_half, ((0,), (0,))).astype(BF)
    part_ref[:sources, :] = dot(logit_half, xt_ref[...], ((1,), (1,)))
    part_ref[sources:, :] = jnp.zeros_like(part_ref[sources:, :])
    bias = to_row(jnp.sum(logit_grad, axis=1, keepdims=True))
    part_ref[sources : sources + 1, :sources] = bias


def combine(home_out, og, gates, pos, idx_t, rwt, xt):
    sources, features = rwt.shape
    tok = idx_t.shape[1]
    return pl.pallas_call(
        combine_kernel,
        in_specs=[vmem_spec()] * 7,
        out_specs=[vmem_spec()] * 3,
        out_shape=[
            jax.ShapeDtypeStruct(og.shape, BF),
            jax.ShapeDtypeStruct((features, tok), BF),
            jax.ShapeDtypeStruct((sources + 8, features), F32),
        ],
        compiler_params=params(56),
        name="combine",
    )(home_out, og, gates, pos, idx_t, rwt, xt)


def unplace_kernel(back_ref, slot_ref, out_ref):
    places, width = back_ref.shape
    slots = slot_ref.shape[1]
    take = (lax.broadcasted_iota(I32, (places, slots), 0) == slot_ref[0:1, :]).astype(BF)
    for n in range(0, width, TILE):
        out_ref[:, n : n + TILE] = dot(take, back_ref[:, n : n + TILE], ((0,), (0,))).astype(BF)


def unplace(home_back, slot_pos):
    return pl.pallas_call(
        unplace_kernel,
        in_specs=[vmem_spec()] * 2,
        out_specs=vmem_spec(),
        out_shape=jax.ShapeDtypeStruct((slot_pos.shape[1], home_back.shape[1]), BF),
        compiler_params=params(56),
        name="unplace",
    )(home_back, slot_pos)


def finish_kernel(scale, order_ref, rep_ref, coef_ref, got_ref, src_ref, out_ref, dot_ref):
    merged = got_ref[0, 0].astype(F32) + got_ref[1, 0].astype(F32)
    expert = order_ref[pl.program_id(0)]
    out_ref[0] = merged * (coef_ref[expert] * scale)
    product = merged * src_ref[0].astype(F32)
    rows, cols = product.shape
    folded = jnp.sum(product.reshape(rows // 8, 8, cols), axis=0)
    total = folded[:, :128]
    for n in range(128, cols, 128):
        total = total + folded[:, n : n + 128]
    dot_ref[0] = total


def finish(order, rep_index, merge_coef, arrived, source_w, scale):
    halves, _, rows, cols = arrived.shape
    count = source_w.shape[0]
    return pl.pallas_call(
        functools.partial(finish_kernel, scale),
        grid_spec=pltpu.PrefetchScalarGridSpec(
            num_scalar_prefetch=2,
            grid=(count,),
            in_specs=[
                smem_spec(),
                pl.BlockSpec((halves, 1, rows, cols), lambda i, o, r: (0, i // 2, 0, 0)),
                pl.BlockSpec((1, rows, cols), lambda i, o, r: (o[i], 0, r[0])),
            ],
            out_specs=[
                pl.BlockSpec((1, rows, cols), lambda i, o, r: (o[i], 0, 0)),
                pl.BlockSpec((1, 8, 128), lambda i, o, r: (o[i], 0, 0)),
            ],
        ),
        out_shape=[
            jax.ShapeDtypeStruct((count, rows, cols), F32),
            jax.ShapeDtypeStruct((count, 8, 128), F32),
        ],
        compiler_params=params(56),
        name="finish",
    )(order, rep_index, merge_coef, arrived, source_w)


def swap(x):
    return lax.ppermute(x, "core", [(0, 1), (1, 0)])


def on_pairs(
    tokens, router_w, router_b, hidden, teacher_idx, merge_map, merge_coef, source_w, out_grad
):
    places = lax.axis_size("place")
    blocks = 2 * places
    reps = 4
    tok = tokens.shape[1]
    features = tokens.shape[2]
    top = teacher_idx.shape[2]
    width = hidden.shape[3]
    depth = out_grad.shape[2]
    sources = router_w.shape[1]
    row_share = source_w.shape[1]
    lanes = 2 * places
    capacity = 5 * tok * top // (4 * blocks)
    scale = 1.0 / math.sqrt(tok * blocks * reps)
    half_i, place_i = lax.axis_index("half"), lax.axis_index("place")
    row_i, core_i = lax.axis_index("row"), lax.axis_index("core")
    ctx_i = half_i * places + place_i
    numbers = jnp.arange(sources, dtype=I32)
    same = merge_map[:, None] == merge_map[None, :]
    rank = jnp.sum((same & (numbers[:, None] > numbers[None, :])).astype(I32), axis=1)
    target = 2 * merge_map + rank
    order = jnp.sum(jnp.where(target[None, :] == numbers[:, None], numbers[None, :], 0), axis=1)
    order = order.astype(I32)
    me = jnp.stack([place_i, row_i, core_i]).astype(I32)
    rep_index = (2 * row_i + core_i).astype(I32)[None]

    combos = merge_experts(order, me, merge_coef, source_w, places)
    mine = [combos[0]]
    for d in range(1, blocks):
        mine.append(
            lax.ppermute(
                combos[d % places], ("half", "place"), [(i, i ^ d) for i in range(blocks)]
            )
        )
    other = [swap(part) for part in mine]
    spots = jnp.stack(
        [jnp.bitwise_xor(ctx_i, d) * row_share for d in range(blocks)] + [core_i]
    ).astype(I32)

    xt = tokens.reshape(tok, features).T
    rwt = router_w.T
    idx_t = teacher_idx.reshape(tok, top).T
    og = out_grad.reshape(tok, depth)
    send_hidden, send_grad, gates, pos, slot_pos = route(
        xt, rwt, router_b, idx_t, merge_map, hidden.reshape(tok * top, width), og, capacity, lanes
    )

    def trade(rows):
        rows = rows.reshape(lanes, capacity, rows.shape[1])
        rows = lax.all_to_all(rows, ("place", "row"), split_axis=0, concat_axis=0, tiled=True)
        return rows.reshape(lanes * capacity, rows.shape[2])

    hid = trade(send_hidden)
    grd = trade(send_grad)
    first = lane_grads((1 - core_i).astype(I32)[None], hid, grd, None, blocks, reps)
    summed = lane_grads(core_i.astype(I32)[None], hid, grd, swap(first), blocks, reps)
    whole = lambda rows: pl.BlockSpec(rows.shape, lambda i: (0, 0))
    out_rows = run_lane(
        forward_kernel, spots, [hid], [whole(hid)], mine, other, depth, "lane_forward"
    )
    back_rows = run_lane(
        backward_kernel, spots, [grd, hid],
        [whole(grd), pl.BlockSpec((hid.shape[0], 128), lambda i: (0, width // 128))],
        mine, other, width, "lane_backward",
    )
    home_out = trade(out_rows)
    mixed, token_grad, part = combine(home_out, og, gates, pos, idx_t, rwt, xt)
    part = lax.psum(part, ("half", "place", "row", "core"))
    home_back = trade(back_rows)
    hidden_grad = unplace(home_back, slot_pos)
    arrived = lax.all_to_all(
        summed.reshape(2 * blocks, 2, row_share, width // reps),
        ("half", "place", "row"), split_axis=0, concat_axis=0, tiled=True,
    )
    source_w_grad, coef_part = finish(
        order, rep_index, merge_coef,
        arrived.reshape(2, 2 * lanes, row_share, width // reps), source_w, scale,
    )
    coef_sum = lax.psum(jnp.sum(coef_part, axis=(1, 2)), ("half", "place", "row", "core"))
    return (
        mixed.reshape(1, tok, depth),
        hidden_grad.reshape(1, tok, top, width),
        token_grad.T.reshape(1, tok, features),
        part[:sources].T * scale,
        part[sources, :sources] * scale,
        coef_sum * scale,
        source_w_grad,
    )


def solution(mesh):
    if mesh.shape["ctx"] == 8 and mesh.shape["rep"] == 4:
        mesh = jax.sharding.Mesh(
            mesh.devices.reshape(2, 4, 2, 2), ("half", "place", "row", "core")
        )
        ctx, rep, body = ("half", "place"), ("row", "core"), on_pairs
    else:
        ctx, rep, body = "ctx", "rep", on_device
    in_specs = (
        P(rep, ctx, None),
        P(),
        P(),
        P(rep, ctx, None, None),
        P(rep, ctx, None),
        P(),
        P(),
        P(None, ctx, None),
        P(rep, ctx, None),
    )
    out_specs = (
        P(rep, ctx, None),
        P(rep, ctx, None, None),
        P(rep, ctx, None),
        P(),
        P(),
        P(),
        P(None, ctx, rep),
    )
    return jax.shard_map(
        body, mesh=mesh, in_specs=in_specs, out_specs=out_specs, check_vma=False
    )
```

```python
import functools
import math

import jax
import jax.numpy as jnp
from jax import lax
from jax.experimental import pallas as pl
from jax.experimental.pallas import tpu as pltpu
from jax.sharding import PartitionSpec as P

MERGED = 16


def expert_rows(rows_hidden, rows_grad, rows_member, lane_weights):
    row_count = rows_hidden.shape[0]
    out_rows = jnp.zeros((row_count, lane_weights.shape[1]), jnp.float32)
    back_rows = jnp.zeros((row_count, lane_weights.shape[2]), jnp.float32)
    grad_list = []
    for member_now in range(lane_weights.shape[0]):
        weight = lane_weights[member_now]
        selected = (rows_member == member_now)[:, None]
        forward = lax.dot_general(
            rows_hidden, weight, (((1,), (1,)), ((), ())), preferred_element_type=jnp.float32
        )
        out_rows = jnp.where(selected, forward, out_rows)
        backward = jnp.dot(rows_grad, weight, preferred_element_type=jnp.float32)
        back_rows = jnp.where(selected, backward, back_rows)
        masked = jnp.where(selected, rows_grad, jnp.zeros_like(rows_grad))
        grad_list.append(
            lax.dot_general(
                masked, rows_hidden, (((0,), (0,)), ((), ())), preferred_element_type=jnp.float32
            )
        )
    return (out_rows, back_rows, jnp.stack(grad_list))


def on_device(
    tokens, router_w, router_b, hidden, teacher_idx, merge_map, merge_coef, source_w, out_grad
):
    ctx_count = lax.axis_size("ctx")
    rep_count = lax.axis_size("rep")
    tok_count = tokens.shape[1]
    feature_count = tokens.shape[2]
    top_count = teacher_idx.shape[2]
    hidden_width = hidden.shape[3]
    out_width = out_grad.shape[2]
    source_count = router_w.shape[1]
    row_share = source_w.shape[1]
    per_lane = max(1, MERGED // ctx_count)
    copies = max(1, ctx_count // MERGED)
    capacity = 5 * tok_count * top_count // (4 * ctx_count)
    slot_count = tok_count * top_count
    grad_scale = 1.0 / math.sqrt(tok_count * ctx_count * rep_count)
    flat_x = tokens.reshape(tok_count, feature_count)
    logits = jnp.dot(flat_x, router_w, preferred_element_type=jnp.float32) + router_b
    choice_ids = teacher_idx.reshape(tok_count, top_count)
    pick_table = choice_ids[:, :, None] == jnp.arange(source_count, dtype=jnp.int32)[None, None, :]
    pick_float = pick_table.astype(jnp.float32)
    chosen = jnp.sum(pick_float * logits[:, None, :], axis=2)
    raised = jnp.exp(chosen)
    gate_probs = raised / jnp.sum(raised, axis=1, keepdims=True)
    merged_id = jnp.sum(jnp.where(pick_table, merge_map[None, None, :], 0), axis=2)
    position = lax.axis_index("ctx") * tok_count + jnp.arange(tok_count, dtype=jnp.int32)
    lane_id = merged_id // per_lane * copies + (position % copies)[:, None]
    member_id = (merged_id % per_lane).reshape(-1)
    lane_flat = lane_id.reshape(-1)
    onehot = (lane_flat[:, None] == jnp.arange(ctx_count, dtype=jnp.int32)[None, :]).astype(
        jnp.int32
    )
    before = jnp.cumsum(onehot, axis=0) - onehot
    slot_rank = jnp.sum(before * onehot, axis=1)
    is_kept = slot_rank < capacity
    slot_index = jnp.where(is_kept, lane_flat * capacity + slot_rank, ctx_count * capacity)
    slot_source = (
        jnp.full((ctx_count * capacity + 1,), slot_count, jnp.int32)
        .at[slot_index]
        .set(jnp.arange(slot_count, dtype=jnp.int32))[: ctx_count * capacity]
    )
    slot_grad = (gate_probs[:, :, None] * out_grad.reshape(tok_count, 1, out_width)).astype(
        jnp.bfloat16
    )
    pad_hidden = jnp.concatenate(
        [hidden.reshape(slot_count, hidden_width), jnp.zeros((1, hidden_width), jnp.bfloat16)],
        axis=0,
    )
    pad_grad = jnp.concatenate(
        [slot_grad.reshape(slot_count, out_width), jnp.zeros((1, out_width), jnp.bfloat16)], axis=0
    )
    pad_member = jnp.concatenate([member_id, jnp.zeros((1,), jnp.int32)], axis=0)
    send_hidden = pad_hidden[slot_source].reshape(ctx_count, capacity, hidden_width)
    send_grad = pad_grad[slot_source].reshape(ctx_count, capacity, out_width)
    send_member = pad_member[slot_source].reshape(ctx_count, capacity)
    lane_group = lax.axis_index("ctx") // copies
    same_group = merge_map[:, None] == merge_map[None, :]
    earlier = jnp.arange(source_count)[:, None] > jnp.arange(source_count)[None, :]
    member_rank = jnp.sum((same_group & earlier).astype(jnp.int32), axis=1)
    source_order = (
        jnp.zeros((source_count,), jnp.int32)
        .at[2 * merge_map + member_rank]
        .set(jnp.arange(source_count, dtype=jnp.int32))
    )
    picked = source_w[source_order].reshape(
        MERGED // per_lane, 2 * per_lane, row_share, hidden_width
    )
    outgoing = jnp.repeat(picked, copies, axis=0)
    arrived = lax.all_to_all(outgoing, "ctx", split_axis=0, concat_axis=2, tiled=True)
    pair_rows = arrived.reshape(per_lane, 2, row_share * ctx_count, hidden_width)
    coef_table = merge_coef[source_order].reshape(MERGED // per_lane, per_lane, 2)
    pair_coef = lax.dynamic_index_in_dim(coef_table, lane_group, 0, keepdims=False)
    lane_weights = (
        pair_coef[:, 0, None, None] * pair_rows[:, 0].astype(jnp.float32)
        + pair_coef[:, 1, None, None] * pair_rows[:, 1].astype(jnp.float32)
    ).astype(jnp.bfloat16)
    recv_hidden, recv_grad, recv_member = (
        lax.all_to_all(send_hidden, "ctx", split_axis=0, concat_axis=0, tiled=True),
        lax.all_to_all(send_grad, "ctx", split_axis=0, concat_axis=0, tiled=True),
        lax.all_to_all(send_member, "ctx", split_axis=0, concat_axis=0, tiled=True),
    )
    out_rows, back_rows, lane_grads = expert_rows(
        recv_hidden.reshape(-1, hidden_width),
        recv_grad.reshape(-1, out_width),
        recv_member.reshape(-1),
        lane_weights,
    )
    home_out, home_back = (
        lax.all_to_all(
            out_rows.astype(jnp.bfloat16).reshape(ctx_count, capacity, out_width),
            "ctx",
            split_axis=0,
            concat_axis=0,
            tiled=True,
        ),
        lax.all_to_all(
            back_rows.astype(jnp.bfloat16).reshape(ctx_count, capacity, hidden_width),
            "ctx",
            split_axis=0,
            concat_axis=0,
            tiled=True,
        ),
    )
    slot_out = jnp.concatenate(
        [home_out.reshape(-1, out_width), jnp.zeros((1, out_width), jnp.bfloat16)], axis=0
    )[slot_index].reshape(tok_count, top_count, out_width)
    hidden_grad = jnp.concatenate(
        [home_back.reshape(-1, hidden_width), jnp.zeros((1, hidden_width), jnp.bfloat16)], axis=0
    )[slot_index].reshape(1, tok_count, top_count, hidden_width)
    mixed = (
        jnp.sum(gate_probs[:, :, None] * slot_out.astype(jnp.float32), axis=1)
        .astype(jnp.bfloat16)
        .reshape(1, tok_count, out_width)
    )
    score_grad = jnp.einsum(
        "td,tkd->tk",
        out_grad.reshape(tok_count, out_width),
        slot_out,
        preferred_element_type=jnp.float32,
    )
    chosen_grad = gate_probs * (
        score_grad - jnp.sum(gate_probs * score_grad, axis=1, keepdims=True)
    )
    logit_grad = jnp.sum(pick_float * chosen_grad[:, :, None], axis=1)
    logit_half = logit_grad.astype(jnp.bfloat16)
    token_grad = (
        lax.dot_general(
            logit_half, router_w, (((1,), (1,)), ((), ())), preferred_element_type=jnp.float32
        )
        .astype(jnp.bfloat16)
        .reshape(1, tok_count, feature_count)
    )
    part_router_w = lax.dot_general(
        flat_x, logit_half, (((0,), (0,)), ((), ())), preferred_element_type=jnp.float32
    )
    part_router_b = jnp.sum(logit_grad, axis=0)
    arrived_grads = lax.all_to_all(
        lane_grads.reshape(per_lane, ctx_count, row_share, hidden_width),
        "ctx",
        split_axis=1,
        concat_axis=0,
        tiled=True,
    )
    merged_grad = (
        arrived_grads.reshape(MERGED // per_lane, copies, per_lane, row_share, hidden_width)
        .sum(axis=1)
        .reshape(MERGED, row_share, hidden_width)
    )
    source_grad = merged_grad[merge_map]
    coef_part = jnp.einsum(
        "edf,edf->e", source_grad, source_w.astype(jnp.float32), precision=lax.Precision.HIGHEST
    )
    summed = lax.psum_scatter(
        source_grad * merge_coef[:, None, None], "rep", scatter_dimension=2, tiled=True
    )
    source_w_grad = summed * grad_scale
    router_sum, bias_sum, coef_sum = lax.psum(
        (part_router_w, part_router_b, coef_part), ("ctx", "rep")
    )
    return (
        mixed,
        hidden_grad,
        token_grad,
        router_sum * grad_scale,
        bias_sum * grad_scale,
        coef_sum * grad_scale,
        source_w_grad,
    )


BF = jnp.bfloat16
F32 = jnp.float32
I32 = jnp.int32
TILE = 256


def any_spec():
    return pl.BlockSpec(memory_space=pl.ANY)


def smem_spec():
    return pl.BlockSpec(memory_space=pltpu.SMEM)


def vmem_spec():
    return pl.BlockSpec(memory_space=pltpu.VMEM)


def params(mib):
    return pltpu.CompilerParams(vmem_limit_bytes=mib * 1024 * 1024)


def dot(a, b, dims):
    return lax.dot_general(a, b, (dims, ((), ())), preferred_element_type=F32)


def merge_kernel(map_ref, coef_ref, place_ref, src_ref, out_ref, order_ref, count_ref, held, sems):
    halves, places = out_ref.shape[:2]
    half = held.shape[2]
    expert_order(map_ref, order_ref, count_ref)
    at = pl.ds(pl.multiple_of(place_ref[1] * half, half), half)
    copies, experts = [], []
    for j in range(places):
        for m in range(2):
            combo = 4 * j + 2 * place_ref[0] + m
            for n in range(2):
                expert = order_ref[2 * combo + n]
                experts.append(expert)
                i = len(copies)
                copies.append(
                    pltpu.make_async_copy(src_ref.at[expert, :, at], held.at[i], sems.at[i])
                )
                copies[-1].start()
    for j in range(places):
        for m in range(2):
            i = 4 * j + 2 * m
            copies[i].wait()
            copies[i + 1].wait()
            one, two = coef_ref[experts[i]], coef_ref[experts[i + 1]]
            merged = (one * held[i].astype(F32) + two * held[i + 1].astype(F32)).astype(BF)
            for h in range(halves):
                out_ref[h, j, m] = merged


def expert_order(map_ref, order_ref, count_ref):
    @pl.loop(0, count_ref.shape[0])
    def _(g):
        count_ref[g] = 0

    @pl.loop(0, order_ref.shape[0])
    def _(e):
        g = map_ref[e]
        n = count_ref[g]
        order_ref[2 * g + n] = e
        count_ref[g] = n + 1


def merge_experts(where_am_i, merge_map, merge_coef, source_w, places):
    count, rows, width = source_w.shape
    half = width // 2
    return pl.pallas_call(
        merge_kernel,
        in_specs=[smem_spec(), smem_spec(), smem_spec(), any_spec()],
        out_specs=vmem_spec(),
        out_shape=jax.ShapeDtypeStruct((2, places, 2, rows, half), BF),
        scratch_shapes=[
            pltpu.SMEM((count,), I32),
            pltpu.SMEM((count // 2,), I32),
            pltpu.VMEM((4 * places, rows, half), BF),
            pltpu.SemaphoreType.DMA((4 * places,)),
        ],
        compiler_params=params(56),
        name="merge_experts",
    )(merge_map, merge_coef, where_am_i, source_w)


def hbm_spec():
    return pl.BlockSpec(memory_space=pltpu.HBM)


def hold(arrays, *after):
    count = len(arrays)
    return pl.pallas_call(
        lambda *refs: None,
        in_specs=[hbm_spec()] * count + [any_spec()] * len(after),
        out_specs=[hbm_spec()] * count,
        out_shape=[jax.ShapeDtypeStruct(a.shape, a.dtype) for a in arrays],
        input_output_aliases={i: i for i in range(count)},
        name="hold",
    )(*arrays, *after)


def column(row):
    size = row.shape[1]
    same = lax.broadcasted_iota(I32, (size, size), 0) == lax.broadcasted_iota(I32, (size, size), 1)
    return jnp.sum(jnp.where(same, row, jnp.zeros_like(row)), axis=1, keepdims=True)


def to_row(col):
    size = col.shape[0]
    same = lax.broadcasted_iota(I32, (size, size), 0) == lax.broadcasted_iota(I32, (size, size), 1)
    return jnp.sum(jnp.where(same, col, jnp.zeros_like(col)), axis=0, keepdims=True)


def picks_of(idx_ref, k, sources):
    tok = idx_ref.shape[1]
    return lax.broadcasted_iota(I32, (sources, tok), 0) == idx_ref[k : k + 1, :]


def place_rows(refs, at, rows):
    each = refs[0].shape[0]
    rows = rows.astype(BF)
    for d, ref in enumerate(refs):
        ref[:, at : at + rows.shape[1]] = rows[d * each : (d + 1) * each]


def route_kernel(
    capacity, lanes,
    me_ref, xt_ref, rwt_ref, rb_ref, idx_ref, map_ref, hid_ref, og_ref, _, *refs
):
    sends, (gate_ref, pos_ref, slot_ref) = refs[:-3], refs[-3:]
    top, tok = idx_ref.shape
    sources = rwt_ref.shape[0]
    slots, width = hid_ref.shape
    places = lanes * capacity
    logits = jnp.dot(rwt_ref[...], xt_ref[...], preferred_element_type=F32) + column(rb_ref[...])
    raised, merged = [], []
    combos = column(map_ref[...])
    for k in range(top):
        pick = picks_of(idx_ref, k, sources)
        chosen = jnp.sum(jnp.where(pick, logits, 0.0), axis=0, keepdims=True)
        raised.append(jnp.exp(chosen))
        merged.append(jnp.sum(jnp.where(pick, combos, 0), axis=0, keepdims=True))
    total = raised[0]
    for k in range(1, top):
        total = total + raised[k]
    gates = [r / total for r in raised]
    lane = [jnp.right_shift(g, 1) for g in merged]
    member = [jnp.bitwise_and(g, 1) for g in merged]
    partner = [jnp.bitwise_xor(l, me_ref[0]) for l in lane]
    onehot = [(lax.broadcasted_iota(I32, (lanes, tok), 0) == l).astype(F32) for l in lane]
    all_hot = onehot[0]
    for k in range(1, top):
        all_hot = all_hot + onehot[k]
    earlier = (
        lax.broadcasted_iota(I32, (tok, tok), 0) < lax.broadcasted_iota(I32, (tok, tok), 1)
    ).astype(BF)
    before = jnp.dot(all_hot.astype(BF), earlier, preferred_element_type=F32)
    position = []
    for k in range(top):
        rank = jnp.sum(before * onehot[k], axis=0, keepdims=True).astype(I32)
        before = before + onehot[k]
        position.append(jnp.where(rank < capacity, partner[k] * capacity + rank, -1))
    gate_ref[...] = jnp.zeros_like(gate_ref)
    pos_ref[...] = jnp.full_like(pos_ref, -1)
    for k in range(top):
        gate_ref[k : k + 1, :] = gates[k]
        pos_ref[k : k + 1, :] = position[k]
    spot = jnp.zeros((8, slots), F32)
    for k in range(top):
        spread = (
            lax.broadcasted_iota(I32, (tok, slots), 1)
            == lax.broadcasted_iota(I32, (tok, slots), 0) * top + k
        ).astype(BF)
        kept = position[k] >= 0
        parts = [
            jnp.where(kept, jnp.right_shift(position[k], 5), 0),
            jnp.where(kept, jnp.bitwise_and(position[k], 31), 0),
            jnp.where(kept, 1, 0),
            member[k],
        ]
        stacked = jnp.concatenate(
            [p.astype(F32) for p in parts] + [jnp.zeros((4, tok), F32)], axis=0
        ).astype(BF)
        spot = spot + jnp.dot(stacked, spread, preferred_element_type=F32)
    spot = spot.astype(I32)
    slot_pos = jnp.where(spot[2:3] > 0, spot[0:1] * 32 + spot[1:2], -1)
    slot_ref[...] = jnp.broadcast_to(slot_pos, slot_ref.shape)
    take = lax.broadcasted_iota(I32, (places, slots), 0) == slot_pos
    placed = jnp.sum(jnp.where(take, spot[3:4].astype(F32), 0.0), axis=1, keepdims=True)
    depth = og_ref.shape[1]
    place_rows(sends, depth + width, jnp.broadcast_to(placed, (places, 128)))
    take = take.astype(BF)
    for n in range(0, width, TILE):
        rows = jnp.dot(take, hid_ref[:, n : n + TILE], preferred_element_type=F32)
        place_rows(sends, depth + n, rows)
    takes = [
        (lax.broadcasted_iota(I32, (places, tok), 0) == position[k]).astype(BF) for k in range(top)
    ]
    columns = [column(g) for g in gates]
    for n in range(0, depth, TILE):
        og = og_ref[:, n : n + TILE].astype(F32)
        rows = jnp.zeros((places, TILE), F32)
        for k in range(top):
            rows = rows + jnp.dot(takes[k], (columns[k] * og).astype(BF), preferred_element_type=F32)
        place_rows(sends, n, rows)


def route(me, xt, rwt, router_b, idx_t, merge_map, hid, og, after, capacity, lanes):
    slots, width = hid.shape
    tok = idx_t.shape[1]
    return pl.pallas_call(
        functools.partial(route_kernel, capacity, lanes),
        in_specs=[smem_spec()] + [vmem_spec()] * 7 + [any_spec()],
        out_specs=[vmem_spec()] * (lanes + 3),
        out_shape=[jax.ShapeDtypeStruct((capacity, og.shape[1] + width + 128), BF)] * lanes
        + [
            jax.ShapeDtypeStruct((8, tok), F32),
            jax.ShapeDtypeStruct((8, tok), I32),
            jax.ShapeDtypeStruct((8, slots), I32),
        ],
        compiler_params=params(56),
        name="route",
    )(me, xt, rwt, router_b[None, :], idx_t, merge_map[None, :], hid, og, after)


def load_weights(core_ref, mine, other, w_ref, sems):
    core = core_ref[0]
    blocks, _, rows, _ = mine.shape
    copies = []
    for c in range(blocks):
        at = pl.ds(c * rows, rows)
        for n, part in enumerate((mine, other)):
            to = core if n == 0 else 1 - core
            i = 2 * c + n
            copies.append(
                pltpu.make_async_copy(part.at[c], w_ref.at[to, :, at, :], sems.at[i])
            )
    for copy in copies:
        copy.start()
    for copy in copies:
        copy.wait()


def forward_kernel(core_ref, rows_ref, flag_ref, mine, other, *refs):
    outs, (w_ref, sems) = refs[:-2], refs[-2:]
    load_weights(core_ref, mine, other, w_ref, sems)
    half = w_ref.shape[3]
    member = flag_ref[:, :1].astype(F32)

    for n in range(0, w_ref.shape[2], TILE):
        at = slice(n, n + TILE)
        both = [
            dot(rows_ref[:, :half], w_ref[0, m, at, :], ((1,), (1,)))
            + dot(rows_ref[:, half : 2 * half], w_ref[1, m, at, :], ((1,), (1,)))
            for m in range(2)
        ]
        place_rows(outs, n, jnp.where(member == 0.0, both[0], both[1]))


def backward_kernel(core_ref, rows_ref, flag_ref, mine, other, *refs):
    outs, (w_ref, sems) = refs[:-2], refs[-2:]
    load_weights(core_ref, mine, other, w_ref, sems)
    half = w_ref.shape[3]
    member = flag_ref[:, :1].astype(F32)
    for h in range(2):
        for n in range(0, half, TILE):
            at = slice(n, n + TILE)
            both = [dot(rows_ref[...], w_ref[h, m, :, at], ((1,), (0,))) for m in range(2)]
            place_rows(outs, h * half + n, jnp.where(member == 0.0, both[0], both[1]))


def run_lane(kernel, core, rows, which, mine, other, lanes, name):
    blocks, members, share, half = mine.shape
    depth = share * blocks
    count = rows.shape[0]
    wide = (rows.shape[1] - 128) // 2
    return pl.pallas_call(
        kernel,
        grid=(1,),
        in_specs=[
            smem_spec(),
            pl.BlockSpec((count, wide), lambda i: (0, which)),
            pl.BlockSpec((count, 128), lambda i: (0, 2 * wide // 128)),
            hbm_spec(),
            hbm_spec(),
        ],
        out_specs=[pl.BlockSpec((count // lanes, wide), lambda i: (0, 0))] * lanes,
        out_shape=[jax.ShapeDtypeStruct((count // lanes, wide), BF)] * lanes,
        scratch_shapes=[
            pltpu.VMEM((2, members, depth, half), BF),
            pltpu.SemaphoreType.DMA((2 * blocks,)),
        ],
        compiler_params=params(56),
        cost_estimate=pl.CostEstimate(
            flops=4 * count * depth * 2 * half,
            bytes_accessed=4 * members * depth * half + 8 * count * half,
            transcendentals=0,
        ),
        name=name,
    )(core, rows, rows, mine, other)


def lane_grad_kernel(has_other, _, grd_ref, hid_ref, flag_ref, *refs):
    out_ref = refs[-1]
    chosen = flag_ref[:, :1].astype(F32) == pl.program_id(1).astype(F32)
    hid = jnp.where(chosen, hid_ref[...], jnp.zeros_like(hid_ref))
    blocks, _, _, rows, cols = out_ref.shape
    each = 2 if blocks % 2 == 0 and 2 * rows % 128 == 0 else blocks
    for n in range(0, blocks, each):
        part = dot(grd_ref[:, n * rows : (n + each) * rows], hid, ((0,), (0,)))
        part = part.reshape(each, rows, cols)
        if has_other:
            part = part + refs[0][n : n + each, 0, 0].astype(F32)
        out_ref[n : n + each, 0, 0] = part.astype(BF)


def lane_grads(core, rows, other, blocks, reps):
    count = rows.shape[0]
    width = (rows.shape[1] - 128) // 2
    cols = width // reps
    shape = (blocks, 2, 2, width // blocks, cols)
    block = pl.BlockSpec((blocks, 1, 1, width // blocks, cols), lambda y, m, s: (0, y, m, 0, 0))
    extra = [] if other is None else [other]
    return pl.pallas_call(
        functools.partial(lane_grad_kernel, other is not None),
        grid_spec=pltpu.PrefetchScalarGridSpec(
            num_scalar_prefetch=1,
            grid=(2, 2),
            in_specs=[
                pl.BlockSpec((count, width), lambda y, m, s: (0, 0)),
                pl.BlockSpec((count, cols), lambda y, m, s: (0, reps + 2 * y + s[0])),
                pl.BlockSpec((count, 128), lambda y, m, s: (0, 2 * width // 128)),
            ]
            + [block] * len(extra),
            out_specs=block,
        ),
        out_shape=jax.ShapeDtypeStruct(shape, BF),
        compiler_params=params(56),
        cost_estimate=pl.CostEstimate(
            flops=8 * count * width * cols,
            bytes_accessed=8 * width * cols + 4 * count * width,
            transcendentals=0,
        ),
        name="lane_grads_add" if extra else "lane_grads_first",
    )(core, rows, rows, rows, *extra)


def gather_rows(refs, keep):
    each = refs[0].shape[0]
    for d, ref in enumerate(refs):
        keep[d * each : (d + 1) * each, :] = ref[...]


def combine_kernel(og_ref, gate_ref, pos_ref, idx_ref, rwt_ref, xt_ref, *refs):
    homes, (mixed_ref, tg_ref, part_ref, out_ref) = refs[:-4], refs[-4:]
    gather_rows(homes, out_ref)
    places, width = out_ref.shape
    top, tok = idx_ref.shape
    sources, features = rwt_ref.shape
    takes = [
        (lax.broadcasted_iota(I32, (places, tok), 0) == pos_ref[k : k + 1, :]).astype(BF)
        for k in range(top)
    ]
    gates = [gate_ref[k : k + 1, :] for k in range(top)]
    columns = [column(g) for g in gates]
    scores = [jnp.zeros((tok, 1), F32) for _ in range(top)]
    for n in range(0, width, TILE):
        og = og_ref[:, n : n + TILE].astype(F32)
        rows = out_ref[:, n : n + TILE]
        mixed = jnp.zeros((tok, TILE), F32)
        for k in range(top):
            slot_out = dot(takes[k], rows, ((0,), (0,)))
            mixed = mixed + columns[k] * slot_out
            scores[k] = scores[k] + jnp.sum(og * slot_out, axis=1, keepdims=True)
        mixed_ref[:, n : n + TILE] = mixed.astype(BF)
    scores = [to_row(s) for s in scores]
    middle = gates[0] * scores[0]
    for k in range(1, top):
        middle = middle + gates[k] * scores[k]
    logit_grad = jnp.zeros((sources, tok), F32)
    for k in range(top):
        chosen_grad = gates[k] * (scores[k] - middle)
        logit_grad = logit_grad + jnp.where(picks_of(idx_ref, k, sources), chosen_grad, 0.0)
    logit_half = logit_grad.astype(BF)
    tg_ref[...] = dot(rwt_ref[...], logit_half, ((0,), (0,))).astype(BF)
    part_ref[...] = jnp.zeros_like(part_ref)
    part_ref[:, :features] = dot(logit_half, xt_ref[...], ((1,), (1,)))
    bias = jnp.sum(logit_grad, axis=1, keepdims=True)
    last = part_ref.shape[1] - 128
    part_ref[:, last:] = jnp.broadcast_to(bias, (sources, 128))


def combine(homes, og, gates, pos, idx_t, rwt, xt):
    sources, features = rwt.shape
    tok = idx_t.shape[1]
    return pl.pallas_call(
        combine_kernel,
        in_specs=[vmem_spec()] * (6 + len(homes)),
        out_specs=[vmem_spec()] * 3,
        out_shape=[
            jax.ShapeDtypeStruct(og.shape, BF),
            jax.ShapeDtypeStruct((features, tok), BF),
            jax.ShapeDtypeStruct((sources, (features + 127) // 128 * 128 + 128), F32),
        ],
        scratch_shapes=[pltpu.VMEM((len(homes) * homes[0].shape[0], homes[0].shape[1]), BF)],
        compiler_params=params(56),
        name="combine",
    )(og, gates, pos, idx_t, rwt, xt, *homes)


def unplace_kernel(slot_ref, *refs):
    homes, (out_ref, back_ref) = refs[:-2], refs[-2:]
    gather_rows(homes, back_ref)
    places, width = back_ref.shape
    slots = slot_ref.shape[1]
    take = (lax.broadcasted_iota(I32, (places, slots), 0) == slot_ref[0:1, :]).astype(BF)
    for n in range(0, width, TILE):
        out_ref[:, n : n + TILE] = dot(take, back_ref[:, n : n + TILE], ((0,), (0,))).astype(BF)


def unplace(homes, slot_pos):
    rows, width = homes[0].shape
    return pl.pallas_call(
        unplace_kernel,
        in_specs=[vmem_spec()] * (1 + len(homes)),
        out_specs=vmem_spec(),
        out_shape=jax.ShapeDtypeStruct((slot_pos.shape[1], width), BF),
        scratch_shapes=[pltpu.VMEM((len(homes) * rows, width), BF)],
        compiler_params=params(56),
        name="unplace",
    )(slot_pos, *homes)


def coef_kernel(rep_ref, map_ref, src_ref, got_ref, out_ref, order_ref, count_ref, held, weights, sems):
    count, rows, cols = weights.shape
    at = pl.ds(pl.multiple_of(rep_ref[0] * cols, cols), cols)
    copies = [
        pltpu.make_async_copy(src_ref.at[:, :, at], weights, sems.at[0]),
        pltpu.make_async_copy(got_ref, held, sems.at[1]),
    ]
    for copy in copies:
        copy.start()
    expert_order(map_ref, order_ref, count_ref)
    for copy in copies:
        copy.wait()
    lane = lax.broadcasted_iota(I32, (8, 128), 1)

    def one(g, total):
        merged = held[0, g].astype(F32) + held[1, g].astype(F32)
        for n in range(2):
            expert = order_ref[2 * g + n]
            product = merged * weights[expert].astype(F32)
            folded = jnp.sum(product.reshape(rows // 8, 8, cols), axis=0)
            small = folded[:, :128]
            for c in range(128, cols, 128):
                small = small + folded[:, c : c + 128]
            small = jnp.sum(jnp.sum(small, axis=0, keepdims=True), axis=1, keepdims=True)
            total = total + jnp.where(lane == expert, small, 0.0)
        return total

    out_ref[...] = lax.fori_loop(0, count // 2, one, jnp.zeros((8, 128), F32))


def finish_kernel(scale, map_ref, coef_ref, got_ref, out_ref, order_ref, count_ref, held, ready, sems, more):
    count = ready.shape[0]

    def load(g):
        return pltpu.make_async_copy(got_ref.at[:, g], held.at[:, g], sems.at[g])

    def send(i):
        return pltpu.make_async_copy(ready.at[i], out_ref.at[order_ref[i]], more.at[i])

    @pl.loop(0, count // 2)
    def _(g):
        load(g).start()

    expert_order(map_ref, order_ref, count_ref)

    @pl.loop(0, count // 2)
    def _(g):
        load(g).wait()
        merged = held[0, g].astype(F32) + held[1, g].astype(F32)
        for n in range(2):
            i = 2 * g + n
            ready[i] = merged * (coef_ref[order_ref[i]] * scale)
            send(i).start()

    @pl.loop(0, count)
    def _(i):
        send(i).wait()


def coef_dots(rep_index, merge_map, source_w, arrived):
    count = source_w.shape[0]
    _, _, rows, cols = arrived.shape
    return pl.pallas_call(
        coef_kernel,
        in_specs=[smem_spec(), smem_spec(), hbm_spec(), hbm_spec()],
        out_specs=vmem_spec(),
        out_shape=jax.ShapeDtypeStruct((8, 128), F32),
        scratch_shapes=[
            pltpu.SMEM((count,), I32),
            pltpu.SMEM((count // 2,), I32),
            pltpu.VMEM(arrived.shape, BF),
            pltpu.VMEM((count, rows, cols), BF),
            pltpu.SemaphoreType.DMA((2,)),
        ],
        compiler_params=params(56),
        name="coef_dots",
    )(rep_index, merge_map, source_w, arrived)


def finish(merge_map, merge_coef, arrived, after, scale):
    count = merge_map.shape[0]
    _, _, rows, cols = arrived.shape
    return pl.pallas_call(
        lambda a, b, c, _, *refs: finish_kernel(scale, a, b, c, *refs),
        in_specs=[smem_spec(), smem_spec(), hbm_spec(), any_spec()],
        out_specs=hbm_spec(),
        out_shape=jax.ShapeDtypeStruct((count, rows, cols), F32),
        scratch_shapes=[
            pltpu.SMEM((count,), I32),
            pltpu.SMEM((count // 2,), I32),
            pltpu.VMEM(arrived.shape, BF),
            pltpu.VMEM((count, rows, cols), F32),
            pltpu.SemaphoreType.DMA((count // 2,)),
            pltpu.SemaphoreType.DMA((count,)),
        ],
        compiler_params=params(56),
        cost_estimate=pl.CostEstimate(
            flops=4 * count * rows * cols,
            bytes_accessed=8 * count * rows * cols,
            transcendentals=0,
        ),
        name="finish",
    )(merge_map, merge_coef, arrived, after)


def add_up(x, bits):
    for axis, distance, bit in bits:
        x = x.reshape((2, x.shape[0] // 2) + x.shape[1:])
        keep = lax.dynamic_index_in_dim(x, bit, 0, keepdims=False)
        give = lax.dynamic_index_in_dim(x, 1 - bit, 0, keepdims=False)
        size = lax.axis_size(axis)
        x = keep + lax.ppermute(give, axis, [(i, i ^ distance) for i in range(size)])
    return x


def swap(x):
    return lax.ppermute(x, "core", [(0, 1), (1, 0)])


def on_pairs(
    tokens, router_w, router_b, hidden, teacher_idx, merge_map, merge_coef, source_w, out_grad
):
    places = lax.axis_size("place")
    blocks = 2 * places
    reps = 4
    tok = tokens.shape[1]
    features = tokens.shape[2]
    top = teacher_idx.shape[2]
    width = hidden.shape[3]
    depth = out_grad.shape[2]
    sources = router_w.shape[1]
    row_share = source_w.shape[1]
    lanes = 2 * places
    capacity = 5 * tok * top // (4 * blocks)
    scale = 1.0 / math.sqrt(tok * blocks * reps)
    half_i, place_i = lax.axis_index("half"), lax.axis_index("place")
    row_i, core_i = lax.axis_index("row"), lax.axis_index("core")
    ctx_i = half_i * places + place_i
    everyone = ("half", "place", "row", "core")
    devices = blocks * reps

    def stack(numbers):
        return jnp.stack([jnp.asarray(n, I32) for n in numbers])

    combos = merge_experts(stack([row_i, core_i]), merge_map, merge_coef, source_w, places)
    mine = lax.all_to_all(
        combos.reshape((blocks,) + combos.shape[2:]), ("half", "place"),
        split_axis=0, concat_axis=0, tiled=True,
    )

    xt = tokens.reshape(tok, features).T
    rwt = router_w.T
    idx_t = teacher_idx.reshape(tok, top).T
    og = out_grad.reshape(tok, depth)
    *parts, gates, pos, slot_pos = route(
        stack([2 * place_i + row_i]), xt, rwt, router_b, idx_t, merge_map,
        hidden.reshape(tok * top, width), og, combos, capacity, lanes,
    )

    def trade(parts):
        return [parts[0]] + [
            lax.ppermute(parts[d], ("place", "row"), [(i, i ^ d) for i in range(lanes)])
            for d in range(1, lanes)
        ]

    rows = jnp.concatenate(trade(parts), axis=0)
    here = stack([core_i])
    first = lane_grads(stack([1 - core_i]), rows, None, blocks, reps)
    summed = lane_grads(here, rows, swap(first), blocks, reps)
    arrived = lax.all_to_all(
        summed.reshape(2 * blocks, 2, row_share, width // reps),
        ("half", "place", "row"), split_axis=0, concat_axis=0, tiled=True,
    )

    (mine,) = hold([mine], summed)
    other = swap(mine)
    out_parts = run_lane(forward_kernel, here, rows, 1, mine, other, lanes, "lane_forward")
    home_out = trade(out_parts)
    back_parts = run_lane(backward_kernel, here, rows, 0, mine, other, lanes, "lane_backward")
    mixed, token_grad, part = combine(home_out, og, gates, pos, idx_t, rwt, xt)
    hidden_grad = unplace(trade(back_parts), slot_pos)

    part = add_up(
        part,
        [
            ("half", 1, half_i),
            ("place", 2, place_i // 2),
            ("place", 1, place_i % 2),
            ("row", 1, row_i),
            ("core", 1, core_i),
        ],
    )
    (arrived,) = hold([arrived], hidden_grad, part)
    arrived = arrived.reshape(2, 2 * lanes, row_share, width // reps)
    dots = coef_dots(stack([2 * row_i + core_i]), merge_map, source_w, arrived)
    news = jnp.concatenate([part, dots[:1]], axis=1)
    news = lax.all_to_all(
        jnp.broadcast_to(news[None], (devices,) + news.shape), everyone,
        split_axis=0, concat_axis=0, tiled=True,
    )
    source_w_grad = finish(merge_map, merge_coef, arrived, dots, scale)
    end = part.shape[1]
    return (
        mixed.reshape(1, tok, depth),
        hidden_grad.reshape(1, tok, top, width),
        token_grad.T.reshape(1, tok, features),
        news[:, 0, :features].T * scale,
        news[:, 0, end - 1] * scale,
        jnp.sum(news[:, 0, end : end + sources], axis=0) * scale,
        source_w_grad,
    )


def solution(mesh):
    if mesh.shape["ctx"] == 8 and mesh.shape["rep"] == 4:
        mesh = jax.sharding.Mesh(
            mesh.devices.reshape(2, 4, 2, 2), ("half", "place", "row", "core")
        )
        ctx, rep, body = ("half", "place"), ("row", "core"), on_pairs
    else:
        ctx, rep, body = "ctx", "rep", on_device
    in_specs = (
        P(rep, ctx, None),
        P(),
        P(),
        P(rep, ctx, None, None),
        P(rep, ctx, None),
        P(),
        P(),
        P(None, ctx, None),
        P(rep, ctx, None),
    )
    out_specs = (
        P(rep, ctx, None),
        P(rep, ctx, None, None),
        P(rep, ctx, None),
        P(),
        P(),
        P(),
        P(None, ctx, rep),
    )
    return jax.shard_map(
        body, mesh=mesh, in_specs=in_specs, out_specs=out_specs, check_vma=False
    )
```

```python
import functools
import math

import jax
import jax.numpy as jnp
from jax import lax
from jax.experimental import pallas as pl
from jax.experimental.pallas import tpu as pltpu
from jax.sharding import PartitionSpec as P

MERGED = 16


def expert_rows(rows_hidden, rows_grad, rows_member, lane_weights):
    row_count = rows_hidden.shape[0]
    out_rows = jnp.zeros((row_count, lane_weights.shape[1]), jnp.float32)
    back_rows = jnp.zeros((row_count, lane_weights.shape[2]), jnp.float32)
    grad_list = []
    for member_now in range(lane_weights.shape[0]):
        weight = lane_weights[member_now]
        selected = (rows_member == member_now)[:, None]
        forward = lax.dot_general(
            rows_hidden, weight, (((1,), (1,)), ((), ())), preferred_element_type=jnp.float32
        )
        out_rows = jnp.where(selected, forward, out_rows)
        backward = jnp.dot(rows_grad, weight, preferred_element_type=jnp.float32)
        back_rows = jnp.where(selected, backward, back_rows)
        masked = jnp.where(selected, rows_grad, jnp.zeros_like(rows_grad))
        grad_list.append(
            lax.dot_general(
                masked, rows_hidden, (((0,), (0,)), ((), ())), preferred_element_type=jnp.float32
            )
        )
    return (out_rows, back_rows, jnp.stack(grad_list))


def on_device(
    tokens, router_w, router_b, hidden, teacher_idx, merge_map, merge_coef, source_w, out_grad
):
    ctx_count = lax.axis_size("ctx")
    rep_count = lax.axis_size("rep")
    tok_count = tokens.shape[1]
    feature_count = tokens.shape[2]
    top_count = teacher_idx.shape[2]
    hidden_width = hidden.shape[3]
    out_width = out_grad.shape[2]
    source_count = router_w.shape[1]
    row_share = source_w.shape[1]
    per_lane = max(1, MERGED // ctx_count)
    copies = max(1, ctx_count // MERGED)
    capacity = 5 * tok_count * top_count // (4 * ctx_count)
    slot_count = tok_count * top_count
    grad_scale = 1.0 / math.sqrt(tok_count * ctx_count * rep_count)
    flat_x = tokens.reshape(tok_count, feature_count)
    logits = jnp.dot(flat_x, router_w, preferred_element_type=jnp.float32) + router_b
    choice_ids = teacher_idx.reshape(tok_count, top_count)
    pick_table = choice_ids[:, :, None] == jnp.arange(source_count, dtype=jnp.int32)[None, None, :]
    pick_float = pick_table.astype(jnp.float32)
    chosen = jnp.sum(pick_float * logits[:, None, :], axis=2)
    raised = jnp.exp(chosen)
    gate_probs = raised / jnp.sum(raised, axis=1, keepdims=True)
    merged_id = jnp.sum(jnp.where(pick_table, merge_map[None, None, :], 0), axis=2)
    position = lax.axis_index("ctx") * tok_count + jnp.arange(tok_count, dtype=jnp.int32)
    lane_id = merged_id // per_lane * copies + (position % copies)[:, None]
    member_id = (merged_id % per_lane).reshape(-1)
    lane_flat = lane_id.reshape(-1)
    onehot = (lane_flat[:, None] == jnp.arange(ctx_count, dtype=jnp.int32)[None, :]).astype(
        jnp.int32
    )
    before = jnp.cumsum(onehot, axis=0) - onehot
    slot_rank = jnp.sum(before * onehot, axis=1)
    is_kept = slot_rank < capacity
    slot_index = jnp.where(is_kept, lane_flat * capacity + slot_rank, ctx_count * capacity)
    slot_source = (
        jnp.full((ctx_count * capacity + 1,), slot_count, jnp.int32)
        .at[slot_index]
        .set(jnp.arange(slot_count, dtype=jnp.int32))[: ctx_count * capacity]
    )
    slot_grad = (gate_probs[:, :, None] * out_grad.reshape(tok_count, 1, out_width)).astype(
        jnp.bfloat16
    )
    pad_hidden = jnp.concatenate(
        [hidden.reshape(slot_count, hidden_width), jnp.zeros((1, hidden_width), jnp.bfloat16)],
        axis=0,
    )
    pad_grad = jnp.concatenate(
        [slot_grad.reshape(slot_count, out_width), jnp.zeros((1, out_width), jnp.bfloat16)], axis=0
    )
    pad_member = jnp.concatenate([member_id, jnp.zeros((1,), jnp.int32)], axis=0)
    send_hidden = pad_hidden[slot_source].reshape(ctx_count, capacity, hidden_width)
    send_grad = pad_grad[slot_source].reshape(ctx_count, capacity, out_width)
    send_member = pad_member[slot_source].reshape(ctx_count, capacity)
    lane_group = lax.axis_index("ctx") // copies
    same_group = merge_map[:, None] == merge_map[None, :]
    earlier = jnp.arange(source_count)[:, None] > jnp.arange(source_count)[None, :]
    member_rank = jnp.sum((same_group & earlier).astype(jnp.int32), axis=1)
    source_order = (
        jnp.zeros((source_count,), jnp.int32)
        .at[2 * merge_map + member_rank]
        .set(jnp.arange(source_count, dtype=jnp.int32))
    )
    picked = source_w[source_order].reshape(
        MERGED // per_lane, 2 * per_lane, row_share, hidden_width
    )
    outgoing = jnp.repeat(picked, copies, axis=0)
    arrived = lax.all_to_all(outgoing, "ctx", split_axis=0, concat_axis=2, tiled=True)
    pair_rows = arrived.reshape(per_lane, 2, row_share * ctx_count, hidden_width)
    coef_table = merge_coef[source_order].reshape(MERGED // per_lane, per_lane, 2)
    pair_coef = lax.dynamic_index_in_dim(coef_table, lane_group, 0, keepdims=False)
    lane_weights = (
        pair_coef[:, 0, None, None] * pair_rows[:, 0].astype(jnp.float32)
        + pair_coef[:, 1, None, None] * pair_rows[:, 1].astype(jnp.float32)
    ).astype(jnp.bfloat16)
    recv_hidden, recv_grad, recv_member = (
        lax.all_to_all(send_hidden, "ctx", split_axis=0, concat_axis=0, tiled=True),
        lax.all_to_all(send_grad, "ctx", split_axis=0, concat_axis=0, tiled=True),
        lax.all_to_all(send_member, "ctx", split_axis=0, concat_axis=0, tiled=True),
    )
    out_rows, back_rows, lane_grads = expert_rows(
        recv_hidden.reshape(-1, hidden_width),
        recv_grad.reshape(-1, out_width),
        recv_member.reshape(-1),
        lane_weights,
    )
    home_out, home_back = (
        lax.all_to_all(
            out_rows.astype(jnp.bfloat16).reshape(ctx_count, capacity, out_width),
            "ctx",
            split_axis=0,
            concat_axis=0,
            tiled=True,
        ),
        lax.all_to_all(
            back_rows.astype(jnp.bfloat16).reshape(ctx_count, capacity, hidden_width),
            "ctx",
            split_axis=0,
            concat_axis=0,
            tiled=True,
        ),
    )
    slot_out = jnp.concatenate(
        [home_out.reshape(-1, out_width), jnp.zeros((1, out_width), jnp.bfloat16)], axis=0
    )[slot_index].reshape(tok_count, top_count, out_width)
    hidden_grad = jnp.concatenate(
        [home_back.reshape(-1, hidden_width), jnp.zeros((1, hidden_width), jnp.bfloat16)], axis=0
    )[slot_index].reshape(1, tok_count, top_count, hidden_width)
    mixed = (
        jnp.sum(gate_probs[:, :, None] * slot_out.astype(jnp.float32), axis=1)
        .astype(jnp.bfloat16)
        .reshape(1, tok_count, out_width)
    )
    score_grad = jnp.einsum(
        "td,tkd->tk",
        out_grad.reshape(tok_count, out_width),
        slot_out,
        preferred_element_type=jnp.float32,
    )
    chosen_grad = gate_probs * (
        score_grad - jnp.sum(gate_probs * score_grad, axis=1, keepdims=True)
    )
    logit_grad = jnp.sum(pick_float * chosen_grad[:, :, None], axis=1)
    logit_half = logit_grad.astype(jnp.bfloat16)
    token_grad = (
        lax.dot_general(
            logit_half, router_w, (((1,), (1,)), ((), ())), preferred_element_type=jnp.float32
        )
        .astype(jnp.bfloat16)
        .reshape(1, tok_count, feature_count)
    )
    part_router_w = lax.dot_general(
        flat_x, logit_half, (((0,), (0,)), ((), ())), preferred_element_type=jnp.float32
    )
    part_router_b = jnp.sum(logit_grad, axis=0)
    arrived_grads = lax.all_to_all(
        lane_grads.reshape(per_lane, ctx_count, row_share, hidden_width),
        "ctx",
        split_axis=1,
        concat_axis=0,
        tiled=True,
    )
    merged_grad = (
        arrived_grads.reshape(MERGED // per_lane, copies, per_lane, row_share, hidden_width)
        .sum(axis=1)
        .reshape(MERGED, row_share, hidden_width)
    )
    source_grad = merged_grad[merge_map]
    coef_part = jnp.einsum(
        "edf,edf->e", source_grad, source_w.astype(jnp.float32), precision=lax.Precision.HIGHEST
    )
    summed = lax.psum_scatter(
        source_grad * merge_coef[:, None, None], "rep", scatter_dimension=2, tiled=True
    )
    source_w_grad = summed * grad_scale
    router_sum, bias_sum, coef_sum = lax.psum(
        (part_router_w, part_router_b, coef_part), ("ctx", "rep")
    )
    return (
        mixed,
        hidden_grad,
        token_grad,
        router_sum * grad_scale,
        bias_sum * grad_scale,
        coef_sum * grad_scale,
        source_w_grad,
    )


BF = jnp.bfloat16
F32 = jnp.float32
I32 = jnp.int32
TILE = 256
BRIEF = pl.CostEstimate(flops=1, bytes_accessed=1, transcendentals=0)


def any_spec():
    return pl.BlockSpec(memory_space=pl.ANY)


def smem_spec():
    return pl.BlockSpec(memory_space=pltpu.SMEM)


def vmem_spec():
    return pl.BlockSpec(memory_space=pltpu.VMEM)


def params(mib):
    return pltpu.CompilerParams(vmem_limit_bytes=mib * 1024 * 1024)


def dot(a, b, dims):
    return lax.dot_general(a, b, (dims, ((), ())), preferred_element_type=F32)


def merge_kernel(map_ref, coef_ref, place_ref, src_ref, *refs):
    outs, (order_ref, count_ref, held, sems) = refs[:-4], refs[-4:]
    half = held.shape[2]
    expert_order(map_ref, order_ref, count_ref)
    at = pl.ds(pl.multiple_of(place_ref[1] * half, half), half)
    copies, experts = [], []
    for m in range(2):
        for j in range(outs[0].shape[0]):
            combo = 4 * j + 2 * place_ref[0] + m
            for n in range(2):
                expert = order_ref[2 * combo + n]
                experts.append(expert)
                i = len(copies)
                copies.append(
                    pltpu.make_async_copy(src_ref.at[expert, :, at], held.at[i], sems.at[i])
                )
                copies[-1].start()
    for m, out_ref in enumerate(outs):
        for j in range(out_ref.shape[0]):
            i = 2 * (m * out_ref.shape[0] + j)
            copies[i].wait()
            copies[i + 1].wait()
            one, two = coef_ref[experts[i]], coef_ref[experts[i + 1]]
            out_ref[j] = (one * held[i].astype(F32) + two * held[i + 1].astype(F32)).astype(BF)


def expert_order(map_ref, order_ref, count_ref):
    @pl.loop(0, count_ref.shape[0])
    def _(g):
        count_ref[g] = 0

    @pl.loop(0, order_ref.shape[0])
    def _(e):
        g = map_ref[e]
        n = count_ref[g]
        order_ref[2 * g + n] = e
        count_ref[g] = n + 1


def merge_experts(where_am_i, merge_map, merge_coef, source_w, places):
    count, rows, width = source_w.shape
    half = width // 2
    return pl.pallas_call(
        merge_kernel,
        in_specs=[smem_spec(), smem_spec(), smem_spec(), any_spec()],
        out_specs=[vmem_spec()] * 2,
        out_shape=[jax.ShapeDtypeStruct((places, rows, half), BF)] * 2,
        scratch_shapes=[
            pltpu.SMEM((count,), I32),
            pltpu.SMEM((count // 2,), I32),
            pltpu.VMEM((4 * places, rows, half), BF),
            pltpu.SemaphoreType.DMA((4 * places,)),
        ],
        compiler_params=params(56),
        cost_estimate=BRIEF,
        name="merge_experts",
    )(merge_map, merge_coef, where_am_i, source_w)


def hbm_spec():
    return pl.BlockSpec(memory_space=pltpu.HBM)


def hold(arrays, *after):
    count = len(arrays)
    return pl.pallas_call(
        lambda *refs: None,
        in_specs=[hbm_spec()] * count + [any_spec()] * len(after),
        out_specs=[hbm_spec()] * count,
        out_shape=[jax.ShapeDtypeStruct(a.shape, a.dtype) for a in arrays],
        input_output_aliases={i: i for i in range(count)},
        cost_estimate=BRIEF,
        name="hold",
    )(*arrays, *after)


def column(row):
    size = row.shape[1]
    same = lax.broadcasted_iota(I32, (size, size), 0) == lax.broadcasted_iota(I32, (size, size), 1)
    return jnp.sum(jnp.where(same, row, jnp.zeros_like(row)), axis=1, keepdims=True)


def to_row(col):
    size = col.shape[0]
    same = lax.broadcasted_iota(I32, (size, size), 0) == lax.broadcasted_iota(I32, (size, size), 1)
    return jnp.sum(jnp.where(same, col, jnp.zeros_like(col)), axis=0, keepdims=True)


def picks_of(idx_ref, k, sources):
    tok = idx_ref.shape[1]
    return lax.broadcasted_iota(I32, (sources, tok), 0) == idx_ref[k : k + 1, :]


def route_kernel(
    capacity, lanes,
    xt_ref, rwt_ref, rb_ref, idx_ref, map_ref, hid_ref, og_ref, _,
    send_ref, gate_ref, pos_ref, slot_ref,
):
    top, tok = idx_ref.shape
    sources = rwt_ref.shape[0]
    slots, width = hid_ref.shape
    places = lanes * capacity
    logits = jnp.dot(rwt_ref[...], xt_ref[...], preferred_element_type=F32) + column(rb_ref[...])
    raised, merged = [], []
    combos = column(map_ref[...])
    for k in range(top):
        pick = picks_of(idx_ref, k, sources)
        chosen = jnp.sum(jnp.where(pick, logits, 0.0), axis=0, keepdims=True)
        raised.append(jnp.exp(chosen))
        merged.append(jnp.sum(jnp.where(pick, combos, 0), axis=0, keepdims=True))
    total = raised[0]
    for k in range(1, top):
        total = total + raised[k]
    gates = [r / total for r in raised]
    lane = [jnp.right_shift(g, 1) for g in merged]
    member = [jnp.bitwise_and(g, 1) for g in merged]
    onehot = [(lax.broadcasted_iota(I32, (lanes, tok), 0) == l).astype(F32) for l in lane]
    all_hot = onehot[0]
    for k in range(1, top):
        all_hot = all_hot + onehot[k]
    earlier = (
        lax.broadcasted_iota(I32, (tok, tok), 0) < lax.broadcasted_iota(I32, (tok, tok), 1)
    ).astype(BF)
    before = jnp.dot(all_hot.astype(BF), earlier, preferred_element_type=F32)
    position = []
    for k in range(top):
        rank = jnp.sum(before * onehot[k], axis=0, keepdims=True).astype(I32)
        before = before + onehot[k]
        position.append(jnp.where(rank < capacity, lane[k] * capacity + rank, -1))
    gate_ref[...] = jnp.zeros_like(gate_ref)
    pos_ref[...] = jnp.full_like(pos_ref, -1)
    for k in range(top):
        gate_ref[k : k + 1, :] = gates[k]
        pos_ref[k : k + 1, :] = position[k]
    spot = jnp.zeros((8, slots), F32)
    for k in range(top):
        spread = (
            lax.broadcasted_iota(I32, (tok, slots), 1)
            == lax.broadcasted_iota(I32, (tok, slots), 0) * top + k
        ).astype(BF)
        kept = position[k] >= 0
        parts = [
            jnp.where(kept, jnp.right_shift(position[k], 5), 0),
            jnp.where(kept, jnp.bitwise_and(position[k], 31), 0),
            jnp.where(kept, 1, 0),
            member[k],
        ]
        stacked = jnp.concatenate(
            [p.astype(F32) for p in parts] + [jnp.zeros((4, tok), F32)], axis=0
        ).astype(BF)
        spot = spot + jnp.dot(stacked, spread, preferred_element_type=F32)
    spot = spot.astype(I32)
    slot_pos = jnp.where(spot[2:3] > 0, spot[0:1] * 32 + spot[1:2], -1)
    slot_ref[...] = jnp.broadcast_to(slot_pos, slot_ref.shape)
    take = lax.broadcasted_iota(I32, (places, slots), 0) == slot_pos
    placed = jnp.sum(jnp.where(take, spot[3:4].astype(F32), 0.0), axis=1, keepdims=True)
    depth = og_ref.shape[1]
    send_ref[:, depth + width :] = jnp.broadcast_to(placed, (places, 128)).astype(BF)
    take = take.astype(BF)
    for n in range(0, width, TILE):
        rows = jnp.dot(take, hid_ref[:, n : n + TILE], preferred_element_type=F32)
        send_ref[:, depth + n : depth + n + TILE] = rows.astype(BF)
    takes = [
        (lax.broadcasted_iota(I32, (places, tok), 0) == position[k]).astype(BF) for k in range(top)
    ]
    columns = [column(g) for g in gates]
    for n in range(0, depth, TILE):
        og = og_ref[:, n : n + TILE].astype(F32)
        rows = jnp.zeros((places, TILE), F32)
        for k in range(top):
            rows = rows + jnp.dot(takes[k], (columns[k] * og).astype(BF), preferred_element_type=F32)
        send_ref[:, n : n + TILE] = rows.astype(BF)


def route(xt, rwt, router_b, idx_t, merge_map, hid, og, after, capacity, lanes):
    slots, width = hid.shape
    tok = idx_t.shape[1]
    return pl.pallas_call(
        functools.partial(route_kernel, capacity, lanes),
        in_specs=[vmem_spec()] * 7 + [any_spec()],
        out_specs=[vmem_spec()] * 4,
        out_shape=[
            jax.ShapeDtypeStruct((lanes * capacity, og.shape[1] + width + 128), BF),
            jax.ShapeDtypeStruct((8, tok), F32),
            jax.ShapeDtypeStruct((8, tok), I32),
            jax.ShapeDtypeStruct((8, slots), I32),
        ],
        compiler_params=params(56),
        cost_estimate=BRIEF,
        name="route",
    )(xt, rwt, router_b[None, :], idx_t, merge_map[None, :], hid, og, after)


def load_weights(core_ref, mine, other, w_ref, sems):
    core = core_ref[0]
    copies = []
    for m in range(len(mine)):
        blocks, rows, half = mine[m].shape
        for n, part in enumerate((mine[m], other[m])):
            for c in range(blocks):
                to = w_ref.at[core if n == 0 else 1 - core, m, pl.ds(c * rows, rows), :]
                copies.append(pltpu.make_async_copy(part.at[c], to, sems.at[len(copies)]))
    for copy in copies:
        copy.start()
    for copy in copies:
        copy.wait()


def forward_kernel(core_ref, rows_ref, flag_ref, *refs):
    out_ref, w_ref, sems = refs[-3:]
    load_weights(core_ref, refs[:2], refs[2:4], w_ref, sems)
    half = w_ref.shape[3]
    member = flag_ref[:, :1].astype(F32)

    for n in range(0, w_ref.shape[2], TILE):
        at = slice(n, n + TILE)
        both = [
            dot(rows_ref[:, :half], w_ref[0, m, at, :], ((1,), (1,)))
            + dot(rows_ref[:, half : 2 * half], w_ref[1, m, at, :], ((1,), (1,)))
            for m in range(2)
        ]
        out_ref[:, at] = jnp.where(member == 0.0, both[0], both[1]).astype(BF)


def backward_kernel(core_ref, rows_ref, flag_ref, *refs):
    out_ref, w_ref, sems = refs[-3:]
    load_weights(core_ref, refs[:2], refs[2:4], w_ref, sems)
    half = w_ref.shape[3]
    member = flag_ref[:, :1].astype(F32)
    for h in range(2):
        for n in range(0, half, TILE):
            at = slice(n, n + TILE)
            both = [dot(rows_ref[...], w_ref[h, m, :, at], ((1,), (0,))) for m in range(2)]
            both = jnp.where(member == 0.0, both[0], both[1])
            out_ref[:, h * half + n : h * half + n + TILE] = both.astype(BF)


def run_lane(kernel, core, rows, which, mine, other, name):
    blocks, share, half = mine[0].shape
    members = len(mine)
    depth = share * blocks
    count = rows.shape[0]
    wide = (rows.shape[1] - 128) // 2
    return pl.pallas_call(
        kernel,
        grid=(1,),
        in_specs=[
            smem_spec(),
            pl.BlockSpec((count, wide), lambda i: (0, which)),
            pl.BlockSpec((count, 128), lambda i: (0, 2 * wide // 128)),
        ]
        + [any_spec()] * (2 * members),
        out_specs=pl.BlockSpec((count, wide), lambda i: (0, 0)),
        out_shape=jax.ShapeDtypeStruct((count, wide), BF),
        scratch_shapes=[
            pltpu.VMEM((2, members, depth, half), BF),
            pltpu.SemaphoreType.DMA((2 * members * blocks,)),
        ],
        compiler_params=params(56),
        cost_estimate=BRIEF,
        name=name,
    )(core, rows, rows, *mine, *other)


def lane_grad_kernel(member, has_other, _, grd_ref, hid_ref, flag_ref, *refs):
    out_ref = refs[-1]
    chosen = flag_ref[:, :1].astype(F32) == float(member)
    hid = jnp.where(chosen, hid_ref[...], jnp.zeros_like(hid_ref))
    blocks, _, rows, cols = out_ref.shape
    each = 2 if blocks % 2 == 0 and 2 * rows % 128 == 0 else blocks
    for n in range(0, blocks, each):
        part = dot(grd_ref[:, n * rows : (n + each) * rows], hid, ((0,), (0,)))
        part = part.reshape(each, rows, cols)
        if has_other:
            part = part + refs[0][n : n + each, 0].astype(F32)
        out_ref[n : n + each, 0] = part.astype(BF)


def lane_grads(core, rows, member, other, blocks, reps):
    count = rows.shape[0]
    width = (rows.shape[1] - 128) // 2
    cols = width // reps
    shape = (blocks, 2, width // blocks, cols)
    block = pl.BlockSpec((blocks, 1, width // blocks, cols), lambda y, s: (0, y, 0, 0))
    extra = [] if other is None else [other]
    return pl.pallas_call(
        functools.partial(lane_grad_kernel, member, other is not None),
        grid_spec=pltpu.PrefetchScalarGridSpec(
            num_scalar_prefetch=1,
            grid=(2,),
            in_specs=[
                pl.BlockSpec((count, width), lambda y, s: (0, 0)),
                pl.BlockSpec((count, cols), lambda y, s: (0, reps + 2 * y + s[0])),
                pl.BlockSpec((count, 128), lambda y, s: (0, 2 * width // 128)),
            ]
            + [block] * len(extra),
            out_specs=block,
        ),
        out_shape=jax.ShapeDtypeStruct(shape, BF),
        compiler_params=params(56),
        cost_estimate=BRIEF,
        name="lane_grads_add" if extra else "lane_grads_first",
    )(core, rows, rows, rows, *extra)


def combine_kernel(
    og_ref, gate_ref, pos_ref, idx_ref, rwt_ref, xt_ref, out_ref, mixed_ref, tg_ref, part_ref
):
    places, width = out_ref.shape
    top, tok = idx_ref.shape
    sources, features = rwt_ref.shape
    takes = [
        (lax.broadcasted_iota(I32, (places, tok), 0) == pos_ref[k : k + 1, :]).astype(BF)
        for k in range(top)
    ]
    gates = [gate_ref[k : k + 1, :] for k in range(top)]
    columns = [column(g) for g in gates]
    scores = [jnp.zeros((tok, 1), F32) for _ in range(top)]
    for n in range(0, width, TILE):
        og = og_ref[:, n : n + TILE].astype(F32)
        rows = out_ref[:, n : n + TILE]
        mixed = jnp.zeros((tok, TILE), F32)
        for k in range(top):
            slot_out = dot(takes[k], rows, ((0,), (0,)))
            mixed = mixed + columns[k] * slot_out
            scores[k] = scores[k] + jnp.sum(og * slot_out, axis=1, keepdims=True)
        mixed_ref[:, n : n + TILE] = mixed.astype(BF)
    scores = [to_row(s) for s in scores]
    middle = gates[0] * scores[0]
    for k in range(1, top):
        middle = middle + gates[k] * scores[k]
    logit_grad = jnp.zeros((sources, tok), F32)
    for k in range(top):
        chosen_grad = gates[k] * (scores[k] - middle)
        logit_grad = logit_grad + jnp.where(picks_of(idx_ref, k, sources), chosen_grad, 0.0)
    logit_half = logit_grad.astype(BF)
    tg_ref[...] = dot(rwt_ref[...], logit_half, ((0,), (0,))).astype(BF)
    part_ref[...] = jnp.zeros_like(part_ref)
    part_ref[:, :features] = dot(logit_half, xt_ref[...], ((1,), (1,)))
    bias = jnp.sum(logit_grad, axis=1, keepdims=True)
    last = part_ref.shape[1] - 128
    part_ref[:, last:] = jnp.broadcast_to(bias, (sources, 128))


def combine(home_out, og, gates, pos, idx_t, rwt, xt):
    sources, features = rwt.shape
    tok = idx_t.shape[1]
    return pl.pallas_call(
        combine_kernel,
        in_specs=[vmem_spec()] * 7,
        out_specs=[vmem_spec()] * 3,
        out_shape=[
            jax.ShapeDtypeStruct(og.shape, BF),
            jax.ShapeDtypeStruct((features, tok), BF),
            jax.ShapeDtypeStruct((sources, (features + 127) // 128 * 128 + 128), F32),
        ],
        compiler_params=params(56),
        cost_estimate=BRIEF,
        name="combine",
    )(og, gates, pos, idx_t, rwt, xt, home_out)


def unplace_kernel(slot_ref, back_ref, out_ref):
    places, width = back_ref.shape
    slots = slot_ref.shape[1]
    take = (lax.broadcasted_iota(I32, (places, slots), 0) == slot_ref[0:1, :]).astype(BF)
    for n in range(0, width, TILE):
        out_ref[:, n : n + TILE] = dot(take, back_ref[:, n : n + TILE], ((0,), (0,))).astype(BF)


def unplace(home_back, slot_pos):
    return pl.pallas_call(
        unplace_kernel,
        in_specs=[vmem_spec()] * 2,
        out_specs=vmem_spec(),
        out_shape=jax.ShapeDtypeStruct((slot_pos.shape[1], home_back.shape[1]), BF),
        compiler_params=params(56),
        cost_estimate=BRIEF,
        name="unplace",
    )(slot_pos, home_back)


def coef_kernel(rep_ref, map_ref, src_ref, *refs):
    parts, (out_ref, order_ref, count_ref, held, weights, sems) = refs[:-6], refs[-6:]
    count, rows, cols = weights.shape
    at = pl.ds(pl.multiple_of(rep_ref[0] * cols, cols), cols)
    copies = [pltpu.make_async_copy(src_ref.at[:, :, at], weights, sems.at[len(parts)])]
    for m, part in enumerate(parts):
        copies.append(pltpu.make_async_copy(part, held.at[m], sems.at[m]))
    for copy in copies:
        copy.start()
    expert_order(map_ref, order_ref, count_ref)
    for copy in copies:
        copy.wait()
    lane = lax.broadcasted_iota(I32, (8, 128), 1)

    def one(g, total):
        merged = held[jnp.bitwise_and(g, 1), jnp.right_shift(g, 1)].astype(F32)
        for n in range(2):
            expert = order_ref[2 * g + n]
            product = merged * weights[expert].astype(F32)
            folded = jnp.sum(product.reshape(rows // 8, 8, cols), axis=0)
            small = folded[:, :128]
            for c in range(128, cols, 128):
                small = small + folded[:, c : c + 128]
            small = jnp.sum(jnp.sum(small, axis=0, keepdims=True), axis=1, keepdims=True)
            total = total + jnp.where(lane == expert, small, 0.0)
        return total

    out_ref[...] = lax.fori_loop(0, count // 2, one, jnp.zeros((8, 128), F32))


def finish_kernel(scale, map_ref, coef_ref, _, *refs):
    parts, (out_ref, order_ref, count_ref, held, ready, sems, more) = refs[:-7], refs[-7:]
    count = ready.shape[0]
    copies = [
        pltpu.make_async_copy(part, held.at[m], sems.at[m]) for m, part in enumerate(parts)
    ]
    for copy in copies:
        copy.start()
    expert_order(map_ref, order_ref, count_ref)

    def send(i):
        return pltpu.make_async_copy(ready.at[i], out_ref.at[order_ref[i]], more.at[i])

    for m, copy in enumerate(copies):
        copy.wait()

        @pl.loop(0, count // 4)
        def _(lane, m=m):
            merged = held[m, lane].astype(F32)
            for n in range(2):
                i = 4 * lane + 2 * m + n
                ready[i] = merged * (coef_ref[order_ref[i]] * scale)
                send(i).start()

    @pl.loop(0, count)
    def _(i):
        send(i).wait()


def coef_dots(rep_index, merge_map, source_w, arrived):
    count = source_w.shape[0]
    _, rows, cols = arrived[0].shape
    return pl.pallas_call(
        coef_kernel,
        in_specs=[smem_spec(), smem_spec(), hbm_spec()] + [any_spec()] * len(arrived),
        out_specs=vmem_spec(),
        out_shape=jax.ShapeDtypeStruct((8, 128), F32),
        scratch_shapes=[
            pltpu.SMEM((count,), I32),
            pltpu.SMEM((count // 2,), I32),
            pltpu.VMEM((len(arrived),) + arrived[0].shape, BF),
            pltpu.VMEM((count, rows, cols), BF),
            pltpu.SemaphoreType.DMA((len(arrived) + 1,)),
        ],
        compiler_params=params(56),
        cost_estimate=BRIEF,
        name="coef_dots",
    )(rep_index, merge_map, source_w, *arrived)


def finish(merge_map, merge_coef, arrived, after, scale):
    count = merge_map.shape[0]
    _, rows, cols = arrived[0].shape
    return pl.pallas_call(
        functools.partial(finish_kernel, scale),
        in_specs=[smem_spec(), smem_spec(), any_spec()] + [any_spec()] * len(arrived),
        out_specs=hbm_spec(),
        out_shape=jax.ShapeDtypeStruct((count, rows, cols), F32),
        scratch_shapes=[
            pltpu.SMEM((count,), I32),
            pltpu.SMEM((count // 2,), I32),
            pltpu.VMEM((len(arrived),) + arrived[0].shape, BF),
            pltpu.VMEM((count, rows, cols), F32),
            pltpu.SemaphoreType.DMA((len(arrived),)),
            pltpu.SemaphoreType.DMA((count,)),
        ],
        compiler_params=params(56),
        cost_estimate=BRIEF,
        name="finish",
    )(merge_map, merge_coef, after, *arrived)


def add_up(x, bits):
    for axis, distance, bit in bits:
        x = x.reshape((2, x.shape[0] // 2) + x.shape[1:])
        keep = lax.dynamic_index_in_dim(x, bit, 0, keepdims=False)
        give = lax.dynamic_index_in_dim(x, 1 - bit, 0, keepdims=False)
        size = lax.axis_size(axis)
        x = keep + lax.ppermute(give, axis, [(i, i ^ distance) for i in range(size)])
    return x


def swap(x):
    return lax.ppermute(x, "core", [(0, 1), (1, 0)])


def on_pairs(
    tokens, router_w, router_b, hidden, teacher_idx, merge_map, merge_coef, source_w, out_grad
):
    places = lax.axis_size("place")
    blocks = 2 * places
    reps = 4
    tok = tokens.shape[1]
    features = tokens.shape[2]
    top = teacher_idx.shape[2]
    width = hidden.shape[3]
    depth = out_grad.shape[2]
    sources = router_w.shape[1]
    row_share = source_w.shape[1]
    lanes = 2 * places
    capacity = 5 * tok * top // (4 * blocks)
    scale = 1.0 / math.sqrt(tok * blocks * reps)
    half_i, place_i = lax.axis_index("half"), lax.axis_index("place")
    row_i, core_i = lax.axis_index("row"), lax.axis_index("core")
    ctx_i = half_i * places + place_i
    everyone = ("half", "place", "row", "core")
    devices = blocks * reps

    def stack(numbers):
        return jnp.stack([jnp.asarray(n, I32) for n in numbers])

    combos = merge_experts(stack([row_i, core_i]), merge_map, merge_coef, source_w, places)

    def trade(x, axes):
        return lax.all_to_all(x, axes, split_axis=0, concat_axis=0, tiled=True)

    shares = [trade(c, "place") for c in combos]
    mine = [lax.all_gather(x, "half", axis=0, tiled=True) for x in shares]

    xt = tokens.reshape(tok, features).T
    rwt = router_w.T
    idx_t = teacher_idx.reshape(tok, top).T
    og = out_grad.reshape(tok, depth)
    send_rows, gates, pos, slot_pos = route(
        xt, rwt, router_b, idx_t, merge_map, hidden.reshape(tok * top, width), og,
        combos[0], capacity, lanes,
    )

    def trade_rows(rows):
        parts = rows.reshape(lanes, capacity, rows.shape[1])
        return trade(parts, ("place", "row")).reshape(rows.shape)

    (send_rows,) = hold([send_rows], shares[1])
    rows = trade_rows(send_rows)
    here, there = stack([core_i]), stack([1 - core_i])
    firsts = [swap(lane_grads(there, rows, m, None, blocks, reps)) for m in range(2)]
    summed = [lane_grads(here, rows, m, firsts[m], blocks, reps) for m in range(2)]
    arrived = [
        lax.psum_scatter(
            part.reshape((2, lanes) + part.shape[2:]), "half", scatter_dimension=0, tiled=False
        )
        for part in summed
    ]

    mine = hold(mine, *summed)
    other = [swap(part) for part in mine]
    out_rows = run_lane(forward_kernel, here, rows, 1, mine, other, "lane_forward")
    home_out = trade_rows(out_rows)
    back_rows = run_lane(backward_kernel, here, rows, 0, mine, other, "lane_backward")
    mixed, token_grad, part = combine(home_out, og, gates, pos, idx_t, rwt, xt)
    hidden_grad = unplace(trade_rows(back_rows), slot_pos)

    part = add_up(
        part,
        [
            ("half", 1, half_i),
            ("place", 2, place_i // 2),
            ("place", 1, place_i % 2),
            ("row", 1, row_i),
            ("core", 1, core_i),
        ],
    )
    arrived = [trade(x, ("place", "row")) for x in hold(arrived, hidden_grad, part)]
    dots = coef_dots(stack([2 * row_i + core_i]), merge_map, source_w, arrived)
    news = jnp.concatenate([part, dots[:1]], axis=1)
    news = lax.all_to_all(
        jnp.broadcast_to(news[None], (devices,) + news.shape), everyone,
        split_axis=0, concat_axis=0, tiled=True,
    )
    source_w_grad = finish(merge_map, merge_coef, arrived, dots, scale)
    end = part.shape[1]
    return (
        mixed.reshape(1, tok, depth),
        hidden_grad.reshape(1, tok, top, width),
        token_grad.T.reshape(1, tok, features),
        news[:, 0, :features].T * scale,
        news[:, 0, end - 1] * scale,
        jnp.sum(news[:, 0, end : end + sources], axis=0) * scale,
        source_w_grad,
    )


def solution(mesh):
    if mesh.shape["ctx"] == 8 and mesh.shape["rep"] == 4:
        mesh = jax.sharding.Mesh(
            mesh.devices.reshape(2, 4, 2, 2), ("half", "place", "row", "core")
        )
        ctx, rep, body = ("half", "place"), ("row", "core"), on_pairs
    else:
        ctx, rep, body = "ctx", "rep", on_device
    in_specs = (
        P(rep, ctx, None),
        P(),
        P(),
        P(rep, ctx, None, None),
        P(rep, ctx, None),
        P(),
        P(),
        P(None, ctx, None),
        P(rep, ctx, None),
    )
    out_specs = (
        P(rep, ctx, None),
        P(rep, ctx, None, None),
        P(rep, ctx, None),
        P(),
        P(),
        P(),
        P(None, ctx, rep),
    )
    return jax.shard_map(
        body, mesh=mesh, in_specs=in_specs, out_specs=out_specs, check_vma=False
    )
```

```python
import functools
import math

import jax
import jax.numpy as jnp
from jax import lax
from jax.experimental import pallas as pl
from jax.experimental.pallas import tpu as pltpu
from jax.sharding import PartitionSpec as P

MERGED = 16


def expert_rows(rows_hidden, rows_grad, rows_member, lane_weights):
    row_count = rows_hidden.shape[0]
    out_rows = jnp.zeros((row_count, lane_weights.shape[1]), jnp.float32)
    back_rows = jnp.zeros((row_count, lane_weights.shape[2]), jnp.float32)
    grad_list = []
    for member_now in range(lane_weights.shape[0]):
        weight = lane_weights[member_now]
        selected = (rows_member == member_now)[:, None]
        forward = lax.dot_general(
            rows_hidden, weight, (((1,), (1,)), ((), ())), preferred_element_type=jnp.float32
        )
        out_rows = jnp.where(selected, forward, out_rows)
        backward = jnp.dot(rows_grad, weight, preferred_element_type=jnp.float32)
        back_rows = jnp.where(selected, backward, back_rows)
        masked = jnp.where(selected, rows_grad, jnp.zeros_like(rows_grad))
        grad_list.append(
            lax.dot_general(
                masked, rows_hidden, (((0,), (0,)), ((), ())), preferred_element_type=jnp.float32
            )
        )
    return (out_rows, back_rows, jnp.stack(grad_list))


def on_device(
    tokens, router_w, router_b, hidden, teacher_idx, merge_map, merge_coef, source_w, out_grad
):
    ctx_count = lax.axis_size("ctx")
    rep_count = lax.axis_size("rep")
    tok_count = tokens.shape[1]
    feature_count = tokens.shape[2]
    top_count = teacher_idx.shape[2]
    hidden_width = hidden.shape[3]
    out_width = out_grad.shape[2]
    source_count = router_w.shape[1]
    row_share = source_w.shape[1]
    per_lane = max(1, MERGED // ctx_count)
    copies = max(1, ctx_count // MERGED)
    capacity = 5 * tok_count * top_count // (4 * ctx_count)
    slot_count = tok_count * top_count
    grad_scale = 1.0 / math.sqrt(tok_count * ctx_count * rep_count)
    flat_x = tokens.reshape(tok_count, feature_count)
    logits = jnp.dot(flat_x, router_w, preferred_element_type=jnp.float32) + router_b
    choice_ids = teacher_idx.reshape(tok_count, top_count)
    pick_table = choice_ids[:, :, None] == jnp.arange(source_count, dtype=jnp.int32)[None, None, :]
    pick_float = pick_table.astype(jnp.float32)
    chosen = jnp.sum(pick_float * logits[:, None, :], axis=2)
    raised = jnp.exp(chosen)
    gate_probs = raised / jnp.sum(raised, axis=1, keepdims=True)
    merged_id = jnp.sum(jnp.where(pick_table, merge_map[None, None, :], 0), axis=2)
    position = lax.axis_index("ctx") * tok_count + jnp.arange(tok_count, dtype=jnp.int32)
    lane_id = merged_id // per_lane * copies + (position % copies)[:, None]
    member_id = (merged_id % per_lane).reshape(-1)
    lane_flat = lane_id.reshape(-1)
    onehot = (lane_flat[:, None] == jnp.arange(ctx_count, dtype=jnp.int32)[None, :]).astype(
        jnp.int32
    )
    before = jnp.cumsum(onehot, axis=0) - onehot
    slot_rank = jnp.sum(before * onehot, axis=1)
    is_kept = slot_rank < capacity
    slot_index = jnp.where(is_kept, lane_flat * capacity + slot_rank, ctx_count * capacity)
    slot_source = (
        jnp.full((ctx_count * capacity + 1,), slot_count, jnp.int32)
        .at[slot_index]
        .set(jnp.arange(slot_count, dtype=jnp.int32))[: ctx_count * capacity]
    )
    slot_grad = (gate_probs[:, :, None] * out_grad.reshape(tok_count, 1, out_width)).astype(
        jnp.bfloat16
    )
    pad_hidden = jnp.concatenate(
        [hidden.reshape(slot_count, hidden_width), jnp.zeros((1, hidden_width), jnp.bfloat16)],
        axis=0,
    )
    pad_grad = jnp.concatenate(
        [slot_grad.reshape(slot_count, out_width), jnp.zeros((1, out_width), jnp.bfloat16)], axis=0
    )
    pad_member = jnp.concatenate([member_id, jnp.zeros((1,), jnp.int32)], axis=0)
    send_hidden = pad_hidden[slot_source].reshape(ctx_count, capacity, hidden_width)
    send_grad = pad_grad[slot_source].reshape(ctx_count, capacity, out_width)
    send_member = pad_member[slot_source].reshape(ctx_count, capacity)
    lane_group = lax.axis_index("ctx") // copies
    same_group = merge_map[:, None] == merge_map[None, :]
    earlier = jnp.arange(source_count)[:, None] > jnp.arange(source_count)[None, :]
    member_rank = jnp.sum((same_group & earlier).astype(jnp.int32), axis=1)
    source_order = (
        jnp.zeros((source_count,), jnp.int32)
        .at[2 * merge_map + member_rank]
        .set(jnp.arange(source_count, dtype=jnp.int32))
    )
    picked = source_w[source_order].reshape(
        MERGED // per_lane, 2 * per_lane, row_share, hidden_width
    )
    outgoing = jnp.repeat(picked, copies, axis=0)
    arrived = lax.all_to_all(outgoing, "ctx", split_axis=0, concat_axis=2, tiled=True)
    pair_rows = arrived.reshape(per_lane, 2, row_share * ctx_count, hidden_width)
    coef_table = merge_coef[source_order].reshape(MERGED // per_lane, per_lane, 2)
    pair_coef = lax.dynamic_index_in_dim(coef_table, lane_group, 0, keepdims=False)
    lane_weights = (
        pair_coef[:, 0, None, None] * pair_rows[:, 0].astype(jnp.float32)
        + pair_coef[:, 1, None, None] * pair_rows[:, 1].astype(jnp.float32)
    ).astype(jnp.bfloat16)
    recv_hidden, recv_grad, recv_member = (
        lax.all_to_all(send_hidden, "ctx", split_axis=0, concat_axis=0, tiled=True),
        lax.all_to_all(send_grad, "ctx", split_axis=0, concat_axis=0, tiled=True),
        lax.all_to_all(send_member, "ctx", split_axis=0, concat_axis=0, tiled=True),
    )
    out_rows, back_rows, lane_grads = expert_rows(
        recv_hidden.reshape(-1, hidden_width),
        recv_grad.reshape(-1, out_width),
        recv_member.reshape(-1),
        lane_weights,
    )
    home_out, home_back = (
        lax.all_to_all(
            out_rows.astype(jnp.bfloat16).reshape(ctx_count, capacity, out_width),
            "ctx",
            split_axis=0,
            concat_axis=0,
            tiled=True,
        ),
        lax.all_to_all(
            back_rows.astype(jnp.bfloat16).reshape(ctx_count, capacity, hidden_width),
            "ctx",
            split_axis=0,
            concat_axis=0,
            tiled=True,
        ),
    )
    slot_out = jnp.concatenate(
        [home_out.reshape(-1, out_width), jnp.zeros((1, out_width), jnp.bfloat16)], axis=0
    )[slot_index].reshape(tok_count, top_count, out_width)
    hidden_grad = jnp.concatenate(
        [home_back.reshape(-1, hidden_width), jnp.zeros((1, hidden_width), jnp.bfloat16)], axis=0
    )[slot_index].reshape(1, tok_count, top_count, hidden_width)
    mixed = (
        jnp.sum(gate_probs[:, :, None] * slot_out.astype(jnp.float32), axis=1)
        .astype(jnp.bfloat16)
        .reshape(1, tok_count, out_width)
    )
    score_grad = jnp.einsum(
        "td,tkd->tk",
        out_grad.reshape(tok_count, out_width),
        slot_out,
        preferred_element_type=jnp.float32,
    )
    chosen_grad = gate_probs * (
        score_grad - jnp.sum(gate_probs * score_grad, axis=1, keepdims=True)
    )
    logit_grad = jnp.sum(pick_float * chosen_grad[:, :, None], axis=1)
    logit_half = logit_grad.astype(jnp.bfloat16)
    token_grad = (
        lax.dot_general(
            logit_half, router_w, (((1,), (1,)), ((), ())), preferred_element_type=jnp.float32
        )
        .astype(jnp.bfloat16)
        .reshape(1, tok_count, feature_count)
    )
    part_router_w = lax.dot_general(
        flat_x, logit_half, (((0,), (0,)), ((), ())), preferred_element_type=jnp.float32
    )
    part_router_b = jnp.sum(logit_grad, axis=0)
    arrived_grads = lax.all_to_all(
        lane_grads.reshape(per_lane, ctx_count, row_share, hidden_width),
        "ctx",
        split_axis=1,
        concat_axis=0,
        tiled=True,
    )
    merged_grad = (
        arrived_grads.reshape(MERGED // per_lane, copies, per_lane, row_share, hidden_width)
        .sum(axis=1)
        .reshape(MERGED, row_share, hidden_width)
    )
    source_grad = merged_grad[merge_map]
    coef_part = jnp.einsum(
        "edf,edf->e", source_grad, source_w.astype(jnp.float32), precision=lax.Precision.HIGHEST
    )
    summed = lax.psum_scatter(
        source_grad * merge_coef[:, None, None], "rep", scatter_dimension=2, tiled=True
    )
    source_w_grad = summed * grad_scale
    router_sum, bias_sum, coef_sum = lax.psum(
        (part_router_w, part_router_b, coef_part), ("ctx", "rep")
    )
    return (
        mixed,
        hidden_grad,
        token_grad,
        router_sum * grad_scale,
        bias_sum * grad_scale,
        coef_sum * grad_scale,
        source_w_grad,
    )


BF = jnp.bfloat16
F32 = jnp.float32
I32 = jnp.int32
TILE = 256


def cost(us):
    return pl.CostEstimate(flops=us * 10**9, bytes_accessed=us * 10**6, transcendentals=0)


def any_spec():
    return pl.BlockSpec(memory_space=pl.ANY)


def smem_spec():
    return pl.BlockSpec(memory_space=pltpu.SMEM)


def vmem_spec():
    return pl.BlockSpec(memory_space=pltpu.VMEM)


def params(mib):
    return pltpu.CompilerParams(vmem_limit_bytes=mib * 1024 * 1024)


def dot(a, b, dims):
    return lax.dot_general(a, b, (dims, ((), ())), preferred_element_type=F32)


def merge_kernel(rep_ref, map_ref, coef_ref, src_ref, out_ref, order_ref, count_ref, held, sems):
    combos, _, cols = out_ref.shape
    expert_order(map_ref, order_ref, count_ref)
    at = pl.ds(pl.multiple_of(rep_ref[0] * cols, cols), cols)
    copies = [
        pltpu.make_async_copy(src_ref.at[order_ref[i], :, at], held.at[i], sems.at[i])
        for i in range(2 * combos)
    ]
    for copy in copies:
        copy.start()
    for g in range(combos):
        copies[2 * g].wait()
        copies[2 * g + 1].wait()
        one, two = coef_ref[order_ref[2 * g]], coef_ref[order_ref[2 * g + 1]]
        merged = one * held[2 * g].astype(F32) + two * held[2 * g + 1].astype(F32)
        out_ref[g] = merged.astype(BF)


def expert_order(map_ref, order_ref, count_ref):
    @pl.loop(0, count_ref.shape[0])
    def _(g):
        count_ref[g] = 0

    @pl.loop(0, order_ref.shape[0])
    def _(e):
        g = map_ref[e]
        n = count_ref[g]
        order_ref[2 * g + n] = e
        count_ref[g] = n + 1


def merge_experts(rep_index, merge_map, merge_coef, source_w, reps):
    count, rows, width = source_w.shape
    cols = width // reps
    return pl.pallas_call(
        merge_kernel,
        in_specs=[smem_spec(), smem_spec(), smem_spec(), any_spec()],
        out_specs=vmem_spec(),
        out_shape=jax.ShapeDtypeStruct((count // 2, rows, cols), BF),
        scratch_shapes=[
            pltpu.SMEM((count,), I32),
            pltpu.SMEM((count // 2,), I32),
            pltpu.VMEM((count, rows, cols), BF),
            pltpu.SemaphoreType.DMA((count,)),
        ],
        compiler_params=params(56),
        cost_estimate=cost(5),
        name="merge_experts",
    )(rep_index, merge_map, merge_coef, source_w)


def hbm_spec():
    return pl.BlockSpec(memory_space=pltpu.HBM)


def hold(arrays, *after):
    count = len(arrays)
    return pl.pallas_call(
        lambda *refs: None,
        in_specs=[hbm_spec()] * count + [any_spec()] * len(after),
        out_specs=[hbm_spec()] * count,
        out_shape=[jax.ShapeDtypeStruct(a.shape, a.dtype) for a in arrays],
        input_output_aliases={i: i for i in range(count)},
        cost_estimate=cost(0),
        name="hold",
    )(*arrays, *after)


def column(row):
    size = row.shape[1]
    same = lax.broadcasted_iota(I32, (size, size), 0) == lax.broadcasted_iota(I32, (size, size), 1)
    return jnp.sum(jnp.where(same, row, jnp.zeros_like(row)), axis=1, keepdims=True)


def to_row(col):
    size = col.shape[0]
    same = lax.broadcasted_iota(I32, (size, size), 0) == lax.broadcasted_iota(I32, (size, size), 1)
    return jnp.sum(jnp.where(same, col, jnp.zeros_like(col)), axis=0, keepdims=True)


def picks_of(idx_ref, k, sources):
    tok = idx_ref.shape[1]
    return lax.broadcasted_iota(I32, (sources, tok), 0) == idx_ref[k : k + 1, :]


def route_kernel(
    capacity, lanes,
    xt_ref, rwt_ref, rb_ref, idx_ref, map_ref, hid_ref, og_ref, _,
    sh_ref, sg_ref, gate_ref, pos_ref, slot_ref,
):
    top, tok = idx_ref.shape
    sources = rwt_ref.shape[0]
    slots, width = hid_ref.shape
    places = lanes * capacity
    logits = jnp.dot(rwt_ref[...], xt_ref[...], preferred_element_type=F32) + column(rb_ref[...])
    raised, merged = [], []
    combos = column(map_ref[...])
    for k in range(top):
        pick = picks_of(idx_ref, k, sources)
        chosen = jnp.sum(jnp.where(pick, logits, 0.0), axis=0, keepdims=True)
        raised.append(jnp.exp(chosen))
        merged.append(jnp.sum(jnp.where(pick, combos, 0), axis=0, keepdims=True))
    total = raised[0]
    for k in range(1, top):
        total = total + raised[k]
    gates = [r / total for r in raised]
    lane = [jnp.right_shift(g, 1) for g in merged]
    member = [jnp.bitwise_and(g, 1) for g in merged]
    onehot = [(lax.broadcasted_iota(I32, (lanes, tok), 0) == l).astype(F32) for l in lane]
    all_hot = onehot[0]
    for k in range(1, top):
        all_hot = all_hot + onehot[k]
    earlier = (
        lax.broadcasted_iota(I32, (tok, tok), 0) < lax.broadcasted_iota(I32, (tok, tok), 1)
    ).astype(BF)
    before = jnp.dot(all_hot.astype(BF), earlier, preferred_element_type=F32)
    position = []
    for k in range(top):
        rank = jnp.sum(before * onehot[k], axis=0, keepdims=True).astype(I32)
        before = before + onehot[k]
        position.append(jnp.where(rank < capacity, lane[k] * capacity + rank, -1))
    gate_ref[...] = jnp.zeros_like(gate_ref)
    pos_ref[...] = jnp.full_like(pos_ref, -1)
    for k in range(top):
        gate_ref[k : k + 1, :] = gates[k]
        pos_ref[k : k + 1, :] = position[k]
    spot = jnp.zeros((8, slots), F32)
    for k in range(top):
        spread = (
            lax.broadcasted_iota(I32, (tok, slots), 1)
            == lax.broadcasted_iota(I32, (tok, slots), 0) * top + k
        ).astype(BF)
        kept = position[k] >= 0
        parts = [
            jnp.where(kept, jnp.right_shift(position[k], 5), 0),
            jnp.where(kept, jnp.bitwise_and(position[k], 31), 0),
            jnp.where(kept, 1, 0),
            member[k],
        ]
        stacked = jnp.concatenate(
            [p.astype(F32) for p in parts] + [jnp.zeros((4, tok), F32)], axis=0
        ).astype(BF)
        spot = spot + jnp.dot(stacked, spread, preferred_element_type=F32)
    spot = spot.astype(I32)
    slot_pos = jnp.where(spot[2:3] > 0, spot[0:1] * 32 + spot[1:2], -1)
    slot_ref[...] = jnp.broadcast_to(slot_pos, slot_ref.shape)
    take = lax.broadcasted_iota(I32, (places, slots), 0) == slot_pos
    placed = jnp.sum(jnp.where(take, spot[3:4].astype(F32), 0.0), axis=1, keepdims=True)
    sh_ref[:, width:] = jnp.broadcast_to(placed, (places, 128)).astype(BF)
    take = take.astype(BF)
    for n in range(0, width, TILE):
        rows = jnp.dot(take, hid_ref[:, n : n + TILE], preferred_element_type=F32)
        sh_ref[:, n : n + TILE] = rows.astype(BF)
    takes = [
        (lax.broadcasted_iota(I32, (places, tok), 0) == position[k]).astype(BF) for k in range(top)
    ]
    columns = [column(g) for g in gates]
    for n in range(0, og_ref.shape[1], TILE):
        og = og_ref[:, n : n + TILE].astype(F32)
        rows = jnp.zeros((places, TILE), F32)
        for k in range(top):
            rows = rows + jnp.dot(takes[k], (columns[k] * og).astype(BF), preferred_element_type=F32)
        sg_ref[:, n : n + TILE] = rows.astype(BF)


def route(xt, rwt, router_b, idx_t, merge_map, hid, og, after, capacity, lanes):
    slots, width = hid.shape
    tok = idx_t.shape[1]
    return pl.pallas_call(
        functools.partial(route_kernel, capacity, lanes),
        in_specs=[vmem_spec()] * 7 + [any_spec()],
        out_specs=[vmem_spec()] * 5,
        out_shape=[
            jax.ShapeDtypeStruct((lanes * capacity, width + 128), BF),
            jax.ShapeDtypeStruct((lanes * capacity, og.shape[1]), BF),
            jax.ShapeDtypeStruct((8, tok), F32),
            jax.ShapeDtypeStruct((8, tok), I32),
            jax.ShapeDtypeStruct((8, slots), I32),
        ],
        compiler_params=params(56),
        cost_estimate=cost(5),
        name="route",
    )(xt, rwt, router_b[None, :], idx_t, merge_map[None, :], hid, og, after)


def load_weights(rep_ref, pieces, w_ref, sems):
    copies = []
    for i, piece in enumerate(pieces):
        blocks, _, rows, cols = piece.shape
        owner = jnp.bitwise_xor(rep_ref[0], i)
        at = pl.ds(pl.multiple_of(owner * cols, cols), cols)
        for c in range(blocks):
            to = w_ref.at[:, pl.ds(c * rows, rows), at]
            copies.append(pltpu.make_async_copy(piece.at[c], to, sems.at[len(copies)]))
    for copy in copies:
        copy.start()
    for copy in copies:
        copy.wait()


def forward_kernel(rep_ref, rows_ref, flag_ref, *refs):
    out_ref, w_ref, sems = refs[-3:]
    load_weights(rep_ref, refs[:-3], w_ref, sems)
    member = flag_ref[:, :1].astype(F32)
    for n in range(0, w_ref.shape[1], TILE):
        at = slice(n, n + TILE)
        both = [dot(rows_ref[...], w_ref[m, at, :], ((1,), (1,))) for m in range(2)]
        out_ref[:, at] = jnp.where(member == 0.0, both[0], both[1]).astype(BF)


def backward_kernel(rep_ref, rows_ref, flag_ref, *refs):
    out_ref, w_ref, sems = refs[-3:]
    load_weights(rep_ref, refs[:-3], w_ref, sems)
    member = flag_ref[:, :1].astype(F32)
    for n in range(0, w_ref.shape[2], TILE):
        at = slice(n, n + TILE)
        both = [dot(rows_ref[...], w_ref[m, :, at], ((1,), (0,))) for m in range(2)]
        out_ref[:, at] = jnp.where(member == 0.0, both[0], both[1]).astype(BF)


def run_lane(kernel, rep_index, rows, hid, pieces, name):
    blocks, members, share, cols = pieces[0].shape
    depth, width = share * blocks, cols * len(pieces)
    count = rows.shape[0]
    return pl.pallas_call(
        kernel,
        grid=(1,),
        in_specs=[
            smem_spec(),
            pl.BlockSpec((count, width), lambda i: (0, 0)),
            pl.BlockSpec((count, 128), lambda i: (0, width // 128)),
        ]
        + [any_spec()] * len(pieces),
        out_specs=pl.BlockSpec((count, width), lambda i: (0, 0)),
        out_shape=jax.ShapeDtypeStruct((count, width), BF),
        scratch_shapes=[
            pltpu.VMEM((members, depth, width), BF),
            pltpu.SemaphoreType.DMA((blocks * len(pieces),)),
        ],
        compiler_params=params(56),
        cost_estimate=cost(12),
        name=name,
    )(rep_index, rows, hid, *pieces)


def lane_grad_kernel(has_other, _, grd_ref, hid_ref, flag_ref, *refs):
    out_ref = refs[-1]
    chosen = flag_ref[:, :1].astype(F32) == pl.program_id(0).astype(F32)
    hid = jnp.where(chosen, hid_ref[...], jnp.zeros_like(hid_ref))
    blocks, _, rows, cols = out_ref.shape
    each = 2 if blocks % 2 == 0 and 2 * rows % 128 == 0 else blocks
    for n in range(0, blocks, each):
        part = dot(grd_ref[:, n * rows : (n + each) * rows], hid, ((0,), (0,)))
        part = part.reshape(each, rows, cols)
        if has_other:
            part = part + refs[0][n : n + each, 0].astype(F32)
        out_ref[n : n + each, 0] = part.astype(BF)


def lane_grads(owner, grd, hid, other, blocks, reps):
    count, depth = grd.shape
    width = hid.shape[1] - 128
    cols = width // reps
    shape = (blocks, 2, depth // blocks, cols)
    block = pl.BlockSpec((blocks, 1, depth // blocks, cols), lambda m, s: (0, m, 0, 0))
    extra = [] if other is None else [other]
    return pl.pallas_call(
        functools.partial(lane_grad_kernel, other is not None),
        grid_spec=pltpu.PrefetchScalarGridSpec(
            num_scalar_prefetch=1,
            grid=(2,),
            in_specs=[
                pl.BlockSpec((count, depth), lambda m, s: (0, 0)),
                pl.BlockSpec((count, cols), lambda m, s: (0, s[0])),
                pl.BlockSpec((count, 128), lambda m, s: (0, width // 128)),
            ]
            + [block] * len(extra),
            out_specs=block,
        ),
        out_shape=jax.ShapeDtypeStruct(shape, BF),
        compiler_params=params(56),
        cost_estimate=cost(6),
        name="lane_grads_add" if extra else "lane_grads_first",
    )(owner, grd, hid, hid, *extra)


def combine_kernel(
    og_ref, gate_ref, pos_ref, idx_ref, rwt_ref, xt_ref, out_ref, mixed_ref, tg_ref, part_ref
):
    places, width = out_ref.shape
    top, tok = idx_ref.shape
    sources, features = rwt_ref.shape
    takes = [
        (lax.broadcasted_iota(I32, (places, tok), 0) == pos_ref[k : k + 1, :]).astype(BF)
        for k in range(top)
    ]
    gates = [gate_ref[k : k + 1, :] for k in range(top)]
    columns = [column(g) for g in gates]
    scores = [jnp.zeros((tok, 1), F32) for _ in range(top)]
    for n in range(0, width, TILE):
        og = og_ref[:, n : n + TILE].astype(F32)
        rows = out_ref[:, n : n + TILE]
        mixed = jnp.zeros((tok, TILE), F32)
        for k in range(top):
            slot_out = dot(takes[k], rows, ((0,), (0,)))
            mixed = mixed + columns[k] * slot_out
            scores[k] = scores[k] + jnp.sum(og * slot_out, axis=1, keepdims=True)
        mixed_ref[:, n : n + TILE] = mixed.astype(BF)
    scores = [to_row(s) for s in scores]
    middle = gates[0] * scores[0]
    for k in range(1, top):
        middle = middle + gates[k] * scores[k]
    logit_grad = jnp.zeros((sources, tok), F32)
    for k in range(top):
        chosen_grad = gates[k] * (scores[k] - middle)
        logit_grad = logit_grad + jnp.where(picks_of(idx_ref, k, sources), chosen_grad, 0.0)
    logit_half = logit_grad.astype(BF)
    tg_ref[...] = dot(rwt_ref[...], logit_half, ((0,), (0,))).astype(BF)
    part_ref[...] = jnp.zeros_like(part_ref)
    part_ref[:, :features] = dot(logit_half, xt_ref[...], ((1,), (1,)))
    bias = jnp.sum(logit_grad, axis=1, keepdims=True)
    last = part_ref.shape[1] - 128
    part_ref[:, last:] = jnp.broadcast_to(bias, (sources, 128))


def combine(home_out, og, gates, pos, idx_t, rwt, xt):
    sources, features = rwt.shape
    tok = idx_t.shape[1]
    return pl.pallas_call(
        combine_kernel,
        in_specs=[vmem_spec()] * 7,
        out_specs=[vmem_spec()] * 3,
        out_shape=[
            jax.ShapeDtypeStruct(og.shape, BF),
            jax.ShapeDtypeStruct((features, tok), BF),
            jax.ShapeDtypeStruct((sources, (features + 127) // 128 * 128 + 128), F32),
        ],
        compiler_params=params(56),
        cost_estimate=cost(5),
        name="combine",
    )(og, gates, pos, idx_t, rwt, xt, home_out)


def unplace_kernel(slot_ref, back_ref, out_ref):
    places, width = back_ref.shape
    slots = slot_ref.shape[1]
    take = (lax.broadcasted_iota(I32, (places, slots), 0) == slot_ref[0:1, :]).astype(BF)
    for n in range(0, width, TILE):
        out_ref[:, n : n + TILE] = dot(take, back_ref[:, n : n + TILE], ((0,), (0,))).astype(BF)


def unplace(home_back, slot_pos):
    return pl.pallas_call(
        unplace_kernel,
        in_specs=[vmem_spec()] * 2,
        out_specs=vmem_spec(),
        out_shape=jax.ShapeDtypeStruct((slot_pos.shape[1], home_back.shape[1]), BF),
        compiler_params=params(56),
        cost_estimate=cost(5),
        name="unplace",
    )(slot_pos, home_back)


def coef_kernel(rep_ref, map_ref, src_ref, got_ref, out_ref, order_ref, count_ref, held, weights, sems):
    count, rows, cols = weights.shape
    at = pl.ds(pl.multiple_of(rep_ref[0] * cols, cols), cols)
    copies = [
        pltpu.make_async_copy(src_ref.at[:, :, at], weights, sems.at[0]),
        pltpu.make_async_copy(got_ref, held, sems.at[1]),
    ]
    for copy in copies:
        copy.start()
    expert_order(map_ref, order_ref, count_ref)
    for copy in copies:
        copy.wait()
    lane = lax.broadcasted_iota(I32, (8, 128), 1)

    def one(g, total):
        merged = held[g].astype(F32)
        for n in range(2):
            expert = order_ref[2 * g + n]
            product = merged * weights[expert].astype(F32)
            folded = jnp.sum(product.reshape(rows // 8, 8, cols), axis=0)
            small = folded[:, :128]
            for c in range(128, cols, 128):
                small = small + folded[:, c : c + 128]
            small = jnp.sum(jnp.sum(small, axis=0, keepdims=True), axis=1, keepdims=True)
            total = total + jnp.where(lane == expert, small, 0.0)
        return total

    out_ref[...] = lax.fori_loop(0, count // 2, one, jnp.zeros((8, 128), F32))


def finish_kernel(
    scale, map_ref, coef_ref, _, got_ref, out_ref, order_ref, count_ref, held, ready, sems, more
):
    count = ready.shape[0]

    def load(g):
        return pltpu.make_async_copy(got_ref.at[g], held.at[g], sems.at[g])

    def send(i):
        return pltpu.make_async_copy(ready.at[i], out_ref.at[order_ref[i]], more.at[i])

    @pl.loop(0, count // 2)
    def _(g):
        load(g).start()

    expert_order(map_ref, order_ref, count_ref)

    @pl.loop(0, count // 2)
    def _(g):
        load(g).wait()
        merged = held[g].astype(F32)
        for n in range(2):
            i = 2 * g + n
            ready[i] = merged * (coef_ref[order_ref[i]] * scale)
            send(i).start()

    @pl.loop(0, count)
    def _(i):
        send(i).wait()


def coef_dots(rep_index, merge_map, source_w, arrived):
    count = source_w.shape[0]
    _, rows, cols = arrived.shape
    return pl.pallas_call(
        coef_kernel,
        in_specs=[smem_spec(), smem_spec(), hbm_spec(), any_spec()],
        out_specs=vmem_spec(),
        out_shape=jax.ShapeDtypeStruct((8, 128), F32),
        scratch_shapes=[
            pltpu.SMEM((count,), I32),
            pltpu.SMEM((count // 2,), I32),
            pltpu.VMEM(arrived.shape, BF),
            pltpu.VMEM((count, rows, cols), BF),
            pltpu.SemaphoreType.DMA((2,)),
        ],
        compiler_params=params(56),
        cost_estimate=cost(5),
        name="coef_dots",
    )(rep_index, merge_map, source_w, arrived)


def finish(merge_map, merge_coef, arrived, after, scale):
    count = merge_map.shape[0]
    _, rows, cols = arrived.shape
    return pl.pallas_call(
        functools.partial(finish_kernel, scale),
        in_specs=[smem_spec(), smem_spec(), any_spec(), any_spec()],
        out_specs=hbm_spec(),
        out_shape=jax.ShapeDtypeStruct((count, rows, cols), F32),
        scratch_shapes=[
            pltpu.SMEM((count,), I32),
            pltpu.SMEM((count // 2,), I32),
            pltpu.VMEM(arrived.shape, BF),
            pltpu.VMEM((count, rows, cols), F32),
            pltpu.SemaphoreType.DMA((count // 2,)),
            pltpu.SemaphoreType.DMA((count,)),
        ],
        compiler_params=params(56),
        cost_estimate=cost(5),
        name="finish",
    )(merge_map, merge_coef, after, arrived)


def add_up(x, bits):
    for axis, distance, bit in bits:
        x = x.reshape((2, x.shape[0] // 2) + x.shape[1:])
        keep = lax.dynamic_index_in_dim(x, bit, 0, keepdims=False)
        give = lax.dynamic_index_in_dim(x, 1 - bit, 0, keepdims=False)
        size = lax.axis_size(axis)
        x = keep + lax.ppermute(give, axis, [(i, i ^ distance) for i in range(size)])
    return x


def on_pairs(
    tokens, router_w, router_b, hidden, teacher_idx, merge_map, merge_coef, source_w, out_grad
):
    blocks = lax.axis_size("ctx")
    reps = lax.axis_size("row") * lax.axis_size("core")
    devices = blocks * reps
    tok = tokens.shape[1]
    features = tokens.shape[2]
    top = teacher_idx.shape[2]
    width = hidden.shape[3]
    depth = out_grad.shape[2]
    sources = router_w.shape[1]
    row_share = source_w.shape[1]
    lanes = blocks
    capacity = 5 * tok * top // (4 * blocks)
    scale = 1.0 / math.sqrt(tok * devices)
    ctx_i, row_i, core_i = lax.axis_index("ctx"), lax.axis_index("row"), lax.axis_index("core")
    rep_i = 2 * row_i + core_i

    def one(number):
        return jnp.asarray(number, I32)[None]

    def swap(x, axis):
        return lax.ppermute(x, axis, [(0, 1), (1, 0)])

    def trade(x):
        return lax.all_to_all(x, "ctx", split_axis=0, concat_axis=0, tiled=True)

    def trade_rows(rows):
        return trade(rows.reshape(lanes, capacity, rows.shape[1])).reshape(rows.shape)

    combos = merge_experts(one(rep_i), merge_map, merge_coef, source_w, reps)
    mine = trade(combos.reshape((lanes, 2) + combos.shape[1:]))

    xt = tokens.reshape(tok, features).T
    rwt = router_w.T
    idx_t = teacher_idx.reshape(tok, top).T
    og = out_grad.reshape(tok, depth)
    send_hid, send_grd, gates, pos, slot_pos = route(
        xt, rwt, router_b, idx_t, merge_map, hidden.reshape(tok * top, width), og,
        combos, capacity, lanes,
    )
    (send_hid,) = hold([send_hid], mine)
    hid = trade_rows(send_hid)
    far = swap(mine, "row")
    pieces = [mine, swap(mine, "core"), far, swap(far, "core")]
    (send_grd,) = hold([send_grd], hid)
    grd = trade_rows(send_grd)
    out_rows = run_lane(forward_kernel, one(rep_i), hid, hid, pieces, "lane_forward")
    grd, out_rows = hold([grd, out_rows])
    home_out = trade_rows(out_rows)

    def summed(row):
        first = lane_grads(one(2 * row + 1 - core_i), grd, hid, None, blocks, reps)
        return lane_grads(one(2 * row + core_i), grd, hid, swap(first, "core"), blocks, reps)

    distant, near = summed(1 - row_i), summed(row_i)
    away = swap(distant, "row")
    (last_grd,) = hold([grd], distant, near)
    back_rows = run_lane(backward_kernel, one(rep_i), last_grd, hid, pieces, "lane_backward")
    total = (near.astype(F32) + away.astype(F32)).astype(BF)

    mixed, token_grad, part = combine(home_out, og, gates, pos, idx_t, rwt, xt)
    home_back = trade_rows(back_rows)
    hidden_grad = unplace(home_back, slot_pos)

    (part,) = hold([part], back_rows)
    part = add_up(
        part,
        [
            ("ctx", 4, ctx_i // 4),
            ("ctx", 2, ctx_i // 2 % 2),
            ("ctx", 1, ctx_i % 2),
            ("row", 1, row_i),
            ("core", 1, core_i),
        ],
    )
    (total,) = hold([total], home_back)
    arrived = trade(total).reshape(2 * lanes, row_share, width // reps)
    (arrived,) = hold([arrived], hidden_grad, part)
    dots = coef_dots(one(rep_i), merge_map, source_w, arrived)
    news = jnp.concatenate([part, dots[:1]], axis=1)
    news = lax.all_to_all(
        jnp.broadcast_to(news[None], (devices,) + news.shape), ("ctx", "row", "core"),
        split_axis=0, concat_axis=0, tiled=True,
    )
    source_w_grad = finish(merge_map, merge_coef, arrived, dots, scale)
    end = part.shape[1]
    return (
        mixed.reshape(1, tok, depth),
        hidden_grad.reshape(1, tok, top, width),
        token_grad.T.reshape(1, tok, features),
        news[:, 0, :features].T * scale,
        news[:, 0, end - 1] * scale,
        jnp.sum(news[:, 0, end : end + sources], axis=0) * scale,
        source_w_grad,
    )


def solution(mesh):
    if mesh.shape["ctx"] == 8 and mesh.shape["rep"] == 4:
        mesh = jax.sharding.Mesh(mesh.devices.reshape(8, 2, 2), ("ctx", "row", "core"))
        ctx, rep, body = "ctx", ("row", "core"), on_pairs
    else:
        ctx, rep, body = "ctx", "rep", on_device
    in_specs = (
        P(rep, ctx, None),
        P(),
        P(),
        P(rep, ctx, None, None),
        P(rep, ctx, None),
        P(),
        P(),
        P(None, ctx, None),
        P(rep, ctx, None),
    )
    out_specs = (
        P(rep, ctx, None),
        P(rep, ctx, None, None),
        P(rep, ctx, None),
        P(),
        P(),
        P(),
        P(None, ctx, rep),
    )
    return jax.shard_map(
        body, mesh=mesh, in_specs=in_specs, out_specs=out_specs, check_vma=False
    )
```

```python
import functools
import math

import jax
import jax.numpy as jnp
from jax import lax
from jax.experimental import pallas as pl
from jax.experimental.pallas import tpu as pltpu
from jax.sharding import PartitionSpec as P

MERGED = 16


def expert_rows(rows_hidden, rows_grad, rows_member, lane_weights):
    row_count = rows_hidden.shape[0]
    out_rows = jnp.zeros((row_count, lane_weights.shape[1]), jnp.float32)
    back_rows = jnp.zeros((row_count, lane_weights.shape[2]), jnp.float32)
    grad_list = []
    for member_now in range(lane_weights.shape[0]):
        weight = lane_weights[member_now]
        selected = (rows_member == member_now)[:, None]
        forward = lax.dot_general(
            rows_hidden, weight, (((1,), (1,)), ((), ())), preferred_element_type=jnp.float32
        )
        out_rows = jnp.where(selected, forward, out_rows)
        backward = jnp.dot(rows_grad, weight, preferred_element_type=jnp.float32)
        back_rows = jnp.where(selected, backward, back_rows)
        masked = jnp.where(selected, rows_grad, jnp.zeros_like(rows_grad))
        grad_list.append(
            lax.dot_general(
                masked, rows_hidden, (((0,), (0,)), ((), ())), preferred_element_type=jnp.float32
            )
        )
    return (out_rows, back_rows, jnp.stack(grad_list))


def on_device(
    tokens, router_w, router_b, hidden, teacher_idx, merge_map, merge_coef, source_w, out_grad
):
    ctx_count = lax.axis_size("ctx")
    rep_count = lax.axis_size("rep")
    tok_count = tokens.shape[1]
    feature_count = tokens.shape[2]
    top_count = teacher_idx.shape[2]
    hidden_width = hidden.shape[3]
    out_width = out_grad.shape[2]
    source_count = router_w.shape[1]
    row_share = source_w.shape[1]
    per_lane = max(1, MERGED // ctx_count)
    copies = max(1, ctx_count // MERGED)
    capacity = 5 * tok_count * top_count // (4 * ctx_count)
    slot_count = tok_count * top_count
    grad_scale = 1.0 / math.sqrt(tok_count * ctx_count * rep_count)
    flat_x = tokens.reshape(tok_count, feature_count)
    logits = jnp.dot(flat_x, router_w, preferred_element_type=jnp.float32) + router_b
    choice_ids = teacher_idx.reshape(tok_count, top_count)
    pick_table = choice_ids[:, :, None] == jnp.arange(source_count, dtype=jnp.int32)[None, None, :]
    pick_float = pick_table.astype(jnp.float32)
    chosen = jnp.sum(pick_float * logits[:, None, :], axis=2)
    raised = jnp.exp(chosen)
    gate_probs = raised / jnp.sum(raised, axis=1, keepdims=True)
    merged_id = jnp.sum(jnp.where(pick_table, merge_map[None, None, :], 0), axis=2)
    position = lax.axis_index("ctx") * tok_count + jnp.arange(tok_count, dtype=jnp.int32)
    lane_id = merged_id // per_lane * copies + (position % copies)[:, None]
    member_id = (merged_id % per_lane).reshape(-1)
    lane_flat = lane_id.reshape(-1)
    onehot = (lane_flat[:, None] == jnp.arange(ctx_count, dtype=jnp.int32)[None, :]).astype(
        jnp.int32
    )
    before = jnp.cumsum(onehot, axis=0) - onehot
    slot_rank = jnp.sum(before * onehot, axis=1)
    is_kept = slot_rank < capacity
    slot_index = jnp.where(is_kept, lane_flat * capacity + slot_rank, ctx_count * capacity)
    slot_source = (
        jnp.full((ctx_count * capacity + 1,), slot_count, jnp.int32)
        .at[slot_index]
        .set(jnp.arange(slot_count, dtype=jnp.int32))[: ctx_count * capacity]
    )
    slot_grad = (gate_probs[:, :, None] * out_grad.reshape(tok_count, 1, out_width)).astype(
        jnp.bfloat16
    )
    pad_hidden = jnp.concatenate(
        [hidden.reshape(slot_count, hidden_width), jnp.zeros((1, hidden_width), jnp.bfloat16)],
        axis=0,
    )
    pad_grad = jnp.concatenate(
        [slot_grad.reshape(slot_count, out_width), jnp.zeros((1, out_width), jnp.bfloat16)], axis=0
    )
    pad_member = jnp.concatenate([member_id, jnp.zeros((1,), jnp.int32)], axis=0)
    send_hidden = pad_hidden[slot_source].reshape(ctx_count, capacity, hidden_width)
    send_grad = pad_grad[slot_source].reshape(ctx_count, capacity, out_width)
    send_member = pad_member[slot_source].reshape(ctx_count, capacity)
    lane_group = lax.axis_index("ctx") // copies
    same_group = merge_map[:, None] == merge_map[None, :]
    earlier = jnp.arange(source_count)[:, None] > jnp.arange(source_count)[None, :]
    member_rank = jnp.sum((same_group & earlier).astype(jnp.int32), axis=1)
    source_order = (
        jnp.zeros((source_count,), jnp.int32)
        .at[2 * merge_map + member_rank]
        .set(jnp.arange(source_count, dtype=jnp.int32))
    )
    picked = source_w[source_order].reshape(
        MERGED // per_lane, 2 * per_lane, row_share, hidden_width
    )
    outgoing = jnp.repeat(picked, copies, axis=0)
    arrived = lax.all_to_all(outgoing, "ctx", split_axis=0, concat_axis=2, tiled=True)
    pair_rows = arrived.reshape(per_lane, 2, row_share * ctx_count, hidden_width)
    coef_table = merge_coef[source_order].reshape(MERGED // per_lane, per_lane, 2)
    pair_coef = lax.dynamic_index_in_dim(coef_table, lane_group, 0, keepdims=False)
    lane_weights = (
        pair_coef[:, 0, None, None] * pair_rows[:, 0].astype(jnp.float32)
        + pair_coef[:, 1, None, None] * pair_rows[:, 1].astype(jnp.float32)
    ).astype(jnp.bfloat16)
    recv_hidden, recv_grad, recv_member = (
        lax.all_to_all(send_hidden, "ctx", split_axis=0, concat_axis=0, tiled=True),
        lax.all_to_all(send_grad, "ctx", split_axis=0, concat_axis=0, tiled=True),
        lax.all_to_all(send_member, "ctx", split_axis=0, concat_axis=0, tiled=True),
    )
    out_rows, back_rows, lane_grads = expert_rows(
        recv_hidden.reshape(-1, hidden_width),
        recv_grad.reshape(-1, out_width),
        recv_member.reshape(-1),
        lane_weights,
    )
    home_out, home_back = (
        lax.all_to_all(
            out_rows.astype(jnp.bfloat16).reshape(ctx_count, capacity, out_width),
            "ctx",
            split_axis=0,
            concat_axis=0,
            tiled=True,
        ),
        lax.all_to_all(
            back_rows.astype(jnp.bfloat16).reshape(ctx_count, capacity, hidden_width),
            "ctx",
            split_axis=0,
            concat_axis=0,
            tiled=True,
        ),
    )
    slot_out = jnp.concatenate(
        [home_out.reshape(-1, out_width), jnp.zeros((1, out_width), jnp.bfloat16)], axis=0
    )[slot_index].reshape(tok_count, top_count, out_width)
    hidden_grad = jnp.concatenate(
        [home_back.reshape(-1, hidden_width), jnp.zeros((1, hidden_width), jnp.bfloat16)], axis=0
    )[slot_index].reshape(1, tok_count, top_count, hidden_width)
    mixed = (
        jnp.sum(gate_probs[:, :, None] * slot_out.astype(jnp.float32), axis=1)
        .astype(jnp.bfloat16)
        .reshape(1, tok_count, out_width)
    )
    score_grad = jnp.einsum(
        "td,tkd->tk",
        out_grad.reshape(tok_count, out_width),
        slot_out,
        preferred_element_type=jnp.float32,
    )
    chosen_grad = gate_probs * (
        score_grad - jnp.sum(gate_probs * score_grad, axis=1, keepdims=True)
    )
    logit_grad = jnp.sum(pick_float * chosen_grad[:, :, None], axis=1)
    logit_half = logit_grad.astype(jnp.bfloat16)
    token_grad = (
        lax.dot_general(
            logit_half, router_w, (((1,), (1,)), ((), ())), preferred_element_type=jnp.float32
        )
        .astype(jnp.bfloat16)
        .reshape(1, tok_count, feature_count)
    )
    part_router_w = lax.dot_general(
        flat_x, logit_half, (((0,), (0,)), ((), ())), preferred_element_type=jnp.float32
    )
    part_router_b = jnp.sum(logit_grad, axis=0)
    arrived_grads = lax.all_to_all(
        lane_grads.reshape(per_lane, ctx_count, row_share, hidden_width),
        "ctx",
        split_axis=1,
        concat_axis=0,
        tiled=True,
    )
    merged_grad = (
        arrived_grads.reshape(MERGED // per_lane, copies, per_lane, row_share, hidden_width)
        .sum(axis=1)
        .reshape(MERGED, row_share, hidden_width)
    )
    source_grad = merged_grad[merge_map]
    coef_part = jnp.einsum(
        "edf,edf->e", source_grad, source_w.astype(jnp.float32), precision=lax.Precision.HIGHEST
    )
    summed = lax.psum_scatter(
        source_grad * merge_coef[:, None, None], "rep", scatter_dimension=2, tiled=True
    )
    source_w_grad = summed * grad_scale
    router_sum, bias_sum, coef_sum = lax.psum(
        (part_router_w, part_router_b, coef_part), ("ctx", "rep")
    )
    return (
        mixed,
        hidden_grad,
        token_grad,
        router_sum * grad_scale,
        bias_sum * grad_scale,
        coef_sum * grad_scale,
        source_w_grad,
    )


BF = jnp.bfloat16
F32 = jnp.float32
I32 = jnp.int32
TILE = 256


def cost(us):
    return pl.CostEstimate(flops=us * 10**9, bytes_accessed=us * 10**6, transcendentals=0)


def any_spec():
    return pl.BlockSpec(memory_space=pl.ANY)


def smem_spec():
    return pl.BlockSpec(memory_space=pltpu.SMEM)


def vmem_spec():
    return pl.BlockSpec(memory_space=pltpu.VMEM)


def params(mib):
    return pltpu.CompilerParams(vmem_limit_bytes=mib * 1024 * 1024)


def dot(a, b, dims):
    return lax.dot_general(a, b, (dims, ((), ())), preferred_element_type=F32)


def merge_kernel(rep_ref, map_ref, coef_ref, src_ref, out_ref, order_ref, count_ref, held, sems):
    combos, _, cols = out_ref.shape
    expert_order(map_ref, order_ref, count_ref)
    at = pl.ds(pl.multiple_of(rep_ref[0] * cols, cols), cols)
    copies = [
        pltpu.make_async_copy(src_ref.at[order_ref[i], :, at], held.at[i], sems.at[i])
        for i in range(2 * combos)
    ]
    for copy in copies:
        copy.start()
    for g in range(combos):
        copies[2 * g].wait()
        copies[2 * g + 1].wait()
        one, two = coef_ref[order_ref[2 * g]], coef_ref[order_ref[2 * g + 1]]
        merged = one * held[2 * g].astype(F32) + two * held[2 * g + 1].astype(F32)
        out_ref[g] = merged.astype(BF)


def expert_order(map_ref, order_ref, count_ref):
    @pl.loop(0, count_ref.shape[0])
    def _(g):
        count_ref[g] = 0

    @pl.loop(0, order_ref.shape[0])
    def _(e):
        g = map_ref[e]
        n = count_ref[g]
        order_ref[2 * g + n] = e
        count_ref[g] = n + 1


def merge_experts(rep_index, merge_map, merge_coef, source_w, reps):
    count, rows, width = source_w.shape
    cols = width // reps
    return pl.pallas_call(
        merge_kernel,
        in_specs=[smem_spec(), smem_spec(), smem_spec(), any_spec()],
        out_specs=vmem_spec(),
        out_shape=jax.ShapeDtypeStruct((count // 2, rows, cols), BF),
        scratch_shapes=[
            pltpu.SMEM((count,), I32),
            pltpu.SMEM((count // 2,), I32),
            pltpu.VMEM((count, rows, cols), BF),
            pltpu.SemaphoreType.DMA((count,)),
        ],
        compiler_params=params(56),
        cost_estimate=cost(5),
        name="merge_experts",
    )(rep_index, merge_map, merge_coef, source_w)


def hbm_spec():
    return pl.BlockSpec(memory_space=pltpu.HBM)


def hold(arrays, *after):
    count = len(arrays)
    return pl.pallas_call(
        lambda *refs: None,
        in_specs=[hbm_spec()] * count + [any_spec()] * len(after),
        out_specs=[hbm_spec()] * count,
        out_shape=[jax.ShapeDtypeStruct(a.shape, a.dtype) for a in arrays],
        input_output_aliases={i: i for i in range(count)},
        cost_estimate=cost(0),
        name="hold",
    )(*arrays, *after)


def column(row):
    size = row.shape[1]
    same = lax.broadcasted_iota(I32, (size, size), 0) == lax.broadcasted_iota(I32, (size, size), 1)
    return jnp.sum(jnp.where(same, row, jnp.zeros_like(row)), axis=1, keepdims=True)


def to_row(col):
    size = col.shape[0]
    same = lax.broadcasted_iota(I32, (size, size), 0) == lax.broadcasted_iota(I32, (size, size), 1)
    return jnp.sum(jnp.where(same, col, jnp.zeros_like(col)), axis=0, keepdims=True)


def picks_of(idx_ref, k, sources):
    tok = idx_ref.shape[1]
    return lax.broadcasted_iota(I32, (sources, tok), 0) == idx_ref[k : k + 1, :]


def place_rows(refs, at, rows):
    each = refs[0].shape[0]
    rows = rows.astype(BF)
    for d, ref in enumerate(refs):
        ref[:, at : at + rows.shape[1]] = rows[d * each : (d + 1) * each]


def assemble_kernel(me_ref, *refs):
    parts, (out_ref, sems) = refs[:-2], refs[-2:]
    each = parts[0].shape[0]
    copies = []
    for d, part in enumerate(parts):
        at = pl.ds(pl.multiple_of(jnp.bitwise_xor(me_ref[0], d) * each, each), each)
        copies.append(pltpu.make_async_copy(part, out_ref.at[at, :], sems.at[d]))
        copies[-1].start()
    for copy in copies:
        copy.wait()


def assemble(me, parts):
    each, width = parts[0].shape
    return pl.pallas_call(
        assemble_kernel,
        in_specs=[smem_spec()] + [any_spec()] * len(parts),
        out_specs=vmem_spec(),
        out_shape=jax.ShapeDtypeStruct((each * len(parts), width), BF),
        scratch_shapes=[pltpu.SemaphoreType.DMA((len(parts),))],
        compiler_params=params(56),
        cost_estimate=cost(2),
        name="assemble",
    )(me, *parts)


def route_kernel(
    capacity, lanes,
    me_ref, xt_ref, rwt_ref, rb_ref, idx_ref, map_ref, hid_ref, og_ref, _, *refs
):
    sends, (sg_ref, gate_ref, pos_ref, slot_ref) = refs[:-4], refs[-4:]
    top, tok = idx_ref.shape
    sources = rwt_ref.shape[0]
    slots, width = hid_ref.shape
    places = lanes * capacity
    logits = jnp.dot(rwt_ref[...], xt_ref[...], preferred_element_type=F32) + column(rb_ref[...])
    raised, merged = [], []
    combos = column(map_ref[...])
    for k in range(top):
        pick = picks_of(idx_ref, k, sources)
        chosen = jnp.sum(jnp.where(pick, logits, 0.0), axis=0, keepdims=True)
        raised.append(jnp.exp(chosen))
        merged.append(jnp.sum(jnp.where(pick, combos, 0), axis=0, keepdims=True))
    total = raised[0]
    for k in range(1, top):
        total = total + raised[k]
    gates = [r / total for r in raised]
    lane = [jnp.right_shift(g, 1) for g in merged]
    member = [jnp.bitwise_and(g, 1) for g in merged]
    onehot = [(lax.broadcasted_iota(I32, (lanes, tok), 0) == l).astype(F32) for l in lane]
    all_hot = onehot[0]
    for k in range(1, top):
        all_hot = all_hot + onehot[k]
    earlier = (
        lax.broadcasted_iota(I32, (tok, tok), 0) < lax.broadcasted_iota(I32, (tok, tok), 1)
    ).astype(BF)
    before = jnp.dot(all_hot.astype(BF), earlier, preferred_element_type=F32)
    position, ranks = [], []
    for k in range(top):
        rank = jnp.sum(before * onehot[k], axis=0, keepdims=True).astype(I32)
        ranks.append(rank)
        before = before + onehot[k]
        position.append(jnp.where(rank < capacity, lane[k] * capacity + rank, -1))
    gate_ref[...] = jnp.zeros_like(gate_ref)
    pos_ref[...] = jnp.full_like(pos_ref, -1)
    for k in range(top):
        gate_ref[k : k + 1, :] = gates[k]
        pos_ref[k : k + 1, :] = position[k]
    spot = jnp.zeros((8, slots), F32)
    for k in range(top):
        spread = (
            lax.broadcasted_iota(I32, (tok, slots), 1)
            == lax.broadcasted_iota(I32, (tok, slots), 0) * top + k
        ).astype(BF)
        kept = position[k] >= 0
        parts = [
            jnp.where(kept, lane[k], 0),
            jnp.where(kept, ranks[k], 0),
            jnp.where(kept, 1, 0),
            member[k],
        ]
        stacked = jnp.concatenate(
            [p.astype(F32) for p in parts] + [jnp.zeros((4, tok), F32)], axis=0
        ).astype(BF)
        spot = spot + jnp.dot(stacked, spread, preferred_element_type=F32)
    spot = spot.astype(I32)
    slot_pos = jnp.where(spot[2:3] > 0, spot[0:1] * capacity + spot[1:2], -1)
    slot_ref[...] = jnp.broadcast_to(slot_pos, slot_ref.shape)
    partner = jnp.bitwise_xor(spot[0:1], me_ref[0])
    part_pos = jnp.where(spot[2:3] > 0, partner * capacity + spot[1:2], -1)
    take = lax.broadcasted_iota(I32, (places, slots), 0) == part_pos
    placed = jnp.sum(jnp.where(take, spot[3:4].astype(F32), 0.0), axis=1, keepdims=True)
    place_rows(sends, width, jnp.broadcast_to(placed, (places, 128)))
    take = take.astype(BF)
    for n in range(0, width, TILE):
        rows = jnp.dot(take, hid_ref[:, n : n + TILE], preferred_element_type=F32)
        place_rows(sends, n, rows)
    takes = [
        (lax.broadcasted_iota(I32, (places, tok), 0) == position[k]).astype(BF) for k in range(top)
    ]
    columns = [column(g) for g in gates]
    for n in range(0, og_ref.shape[1], TILE):
        og = og_ref[:, n : n + TILE].astype(F32)
        rows = jnp.zeros((places, TILE), F32)
        for k in range(top):
            rows = rows + jnp.dot(takes[k], (columns[k] * og).astype(BF), preferred_element_type=F32)
        sg_ref[:, n : n + TILE] = rows.astype(BF)


def route(me, xt, rwt, router_b, idx_t, merge_map, hid, og, after, capacity, lanes):
    slots, width = hid.shape
    tok = idx_t.shape[1]
    return pl.pallas_call(
        functools.partial(route_kernel, capacity, lanes),
        in_specs=[smem_spec()] + [vmem_spec()] * 7 + [any_spec()],
        out_specs=[vmem_spec()] * (lanes + 4),
        out_shape=[jax.ShapeDtypeStruct((capacity, width + 128), BF)] * lanes
        + [
            jax.ShapeDtypeStruct((lanes * capacity, og.shape[1]), BF),
            jax.ShapeDtypeStruct((8, tok), F32),
            jax.ShapeDtypeStruct((8, tok), I32),
            jax.ShapeDtypeStruct((8, slots), I32),
        ],
        compiler_params=params(56),
        cost_estimate=cost(5),
        name="route",
    )(me, xt, rwt, router_b[None, :], idx_t, merge_map[None, :], hid, og, after)


def load_weights(rep_ref, pieces, w_ref, sems):
    copies = []
    for i, piece in enumerate(pieces):
        blocks, _, rows, cols = piece.shape
        owner = jnp.bitwise_xor(rep_ref[0], i)
        at = pl.ds(pl.multiple_of(owner * cols, cols), cols)
        for c in range(blocks):
            to = w_ref.at[:, pl.ds(c * rows, rows), at]
            copies.append(pltpu.make_async_copy(piece.at[c], to, sems.at[len(copies)]))
    for copy in copies:
        copy.start()
    for copy in copies:
        copy.wait()


def forward_kernel(rep_ref, me_ref, rows_ref, flag_ref, *refs):
    pieces, outs, (keep, w_ref, sems) = refs[:4], refs[4:-3], refs[-3:]
    load_weights(rep_ref, pieces, w_ref, sems)
    member = flag_ref[:, :1].astype(F32)
    for n in range(0, w_ref.shape[1], TILE):
        at = slice(n, n + TILE)
        both = [dot(rows_ref[...], w_ref[m, at, :], ((1,), (1,))) for m in range(2)]
        keep[:, at] = jnp.where(member == 0.0, both[0], both[1]).astype(BF)
    each = outs[0].shape[0]
    for d, out_ref in enumerate(outs):
        at = pl.ds(pl.multiple_of(jnp.bitwise_xor(me_ref[0], d) * each, each), each)
        out_ref[...] = keep[at, :]


def backward_kernel(rep_ref, _, rows_ref, flag_ref, *refs):
    pieces, (out_ref, w_ref, sems) = refs[:4], refs[4:]
    load_weights(rep_ref, pieces, w_ref, sems)
    member = flag_ref[:, :1].astype(F32)
    for n in range(0, w_ref.shape[2], TILE):
        at = slice(n, n + TILE)
        both = [dot(rows_ref[...], w_ref[m, :, at], ((1,), (0,))) for m in range(2)]
        out_ref[:, at] = jnp.where(member == 0.0, both[0], both[1]).astype(BF)


def run_lane(kernel, rep_index, me, rows, hid, pieces, lanes, name):
    blocks, members, share, cols = pieces[0].shape
    depth, width = share * blocks, cols * len(pieces)
    count = rows.shape[0]
    whole = pl.BlockSpec((count, width), lambda i: (0, 0))
    if lanes is None:
        out_specs, out_shape, keep = whole, jax.ShapeDtypeStruct((count, width), BF), []
    else:
        part = (count // lanes, width)
        out_specs = [pl.BlockSpec(part, lambda i: (0, 0))] * lanes
        out_shape = [jax.ShapeDtypeStruct(part, BF)] * lanes
        keep = [pltpu.VMEM((count, width), BF)]
    return pl.pallas_call(
        kernel,
        grid=(1,),
        in_specs=[smem_spec(), smem_spec(), whole]
        + [pl.BlockSpec((count, 128), lambda i: (0, width // 128))]
        + [any_spec()] * len(pieces),
        out_specs=out_specs,
        out_shape=out_shape,
        scratch_shapes=keep
        + [
            pltpu.VMEM((members, depth, width), BF),
            pltpu.SemaphoreType.DMA((blocks * len(pieces),)),
        ],
        compiler_params=params(56),
        cost_estimate=cost(12),
        name=name,
    )(rep_index, me, rows, hid, *pieces)


def lane_grad_kernel(has_other, _, grd_ref, hid_ref, flag_ref, *refs):
    out_ref = refs[-1]
    chosen = flag_ref[:, :1].astype(F32) == pl.program_id(0).astype(F32)
    hid = jnp.where(chosen, hid_ref[...], jnp.zeros_like(hid_ref))
    blocks, _, rows, cols = out_ref.shape
    each = 2 if blocks % 2 == 0 and 2 * rows % 128 == 0 else blocks
    for n in range(0, blocks, each):
        part = dot(grd_ref[:, n * rows : (n + each) * rows], hid, ((0,), (0,)))
        part = part.reshape(each, rows, cols)
        if has_other:
            part = part + refs[0][n : n + each, 0].astype(F32)
        out_ref[n : n + each, 0] = part.astype(BF)


def lane_grads(owner, grd, hid, other, blocks, reps):
    count, depth = grd.shape
    width = hid.shape[1] - 128
    cols = width // reps
    shape = (blocks, 2, depth // blocks, cols)
    block = pl.BlockSpec((blocks, 1, depth // blocks, cols), lambda m, s: (0, m, 0, 0))
    extra = [] if other is None else [other]
    return pl.pallas_call(
        functools.partial(lane_grad_kernel, other is not None),
        grid_spec=pltpu.PrefetchScalarGridSpec(
            num_scalar_prefetch=1,
            grid=(2,),
            in_specs=[
                pl.BlockSpec((count, depth), lambda m, s: (0, 0)),
                pl.BlockSpec((count, cols), lambda m, s: (0, s[0])),
                pl.BlockSpec((count, 128), lambda m, s: (0, width // 128)),
            ]
            + [block] * len(extra),
            out_specs=block,
        ),
        out_shape=jax.ShapeDtypeStruct(shape, BF),
        compiler_params=params(56),
        cost_estimate=cost(6),
        name="lane_grads_add" if extra else "lane_grads_first",
    )(owner, grd, hid, hid, *extra)


def combine_kernel(
    og_ref, gate_ref, pos_ref, idx_ref, rwt_ref, xt_ref, out_ref, mixed_ref, tg_ref, part_ref
):
    places, width = out_ref.shape
    top, tok = idx_ref.shape
    sources, features = rwt_ref.shape
    takes = [
        (lax.broadcasted_iota(I32, (places, tok), 0) == pos_ref[k : k + 1, :]).astype(BF)
        for k in range(top)
    ]
    gates = [gate_ref[k : k + 1, :] for k in range(top)]
    columns = [column(g) for g in gates]
    scores = [jnp.zeros((tok, 1), F32) for _ in range(top)]
    for n in range(0, width, TILE):
        og = og_ref[:, n : n + TILE].astype(F32)
        rows = out_ref[:, n : n + TILE]
        mixed = jnp.zeros((tok, TILE), F32)
        for k in range(top):
            slot_out = dot(takes[k], rows, ((0,), (0,)))
            mixed = mixed + columns[k] * slot_out
            scores[k] = scores[k] + jnp.sum(og * slot_out, axis=1, keepdims=True)
        mixed_ref[:, n : n + TILE] = mixed.astype(BF)
    scores = [to_row(s) for s in scores]
    middle = gates[0] * scores[0]
    for k in range(1, top):
        middle = middle + gates[k] * scores[k]
    logit_grad = jnp.zeros((sources, tok), F32)
    for k in range(top):
        chosen_grad = gates[k] * (scores[k] - middle)
        logit_grad = logit_grad + jnp.where(picks_of(idx_ref, k, sources), chosen_grad, 0.0)
    logit_half = logit_grad.astype(BF)
    tg_ref[...] = dot(rwt_ref[...], logit_half, ((0,), (0,))).astype(BF)
    part_ref[...] = jnp.zeros_like(part_ref)
    part_ref[:, :features] = dot(logit_half, xt_ref[...], ((1,), (1,)))
    bias = jnp.sum(logit_grad, axis=1, keepdims=True)
    last = part_ref.shape[1] - 128
    part_ref[:, last:] = jnp.broadcast_to(bias, (sources, 128))


def combine(home_out, og, gates, pos, idx_t, rwt, xt):
    sources, features = rwt.shape
    tok = idx_t.shape[1]
    return pl.pallas_call(
        combine_kernel,
        in_specs=[vmem_spec()] * 7,
        out_specs=[vmem_spec()] * 3,
        out_shape=[
            jax.ShapeDtypeStruct(og.shape, BF),
            jax.ShapeDtypeStruct((features, tok), BF),
            jax.ShapeDtypeStruct((sources, (features + 127) // 128 * 128 + 128), F32),
        ],
        compiler_params=params(56),
        cost_estimate=cost(5),
        name="combine",
    )(og, gates, pos, idx_t, rwt, xt, home_out)


def unplace_kernel(slot_ref, back_ref, out_ref):
    places, width = back_ref.shape
    slots = slot_ref.shape[1]
    take = (lax.broadcasted_iota(I32, (places, slots), 0) == slot_ref[0:1, :]).astype(BF)
    for n in range(0, width, TILE):
        out_ref[:, n : n + TILE] = dot(take, back_ref[:, n : n + TILE], ((0,), (0,))).astype(BF)


def unplace(home_back, slot_pos):
    return pl.pallas_call(
        unplace_kernel,
        in_specs=[vmem_spec()] * 2,
        out_specs=vmem_spec(),
        out_shape=jax.ShapeDtypeStruct((slot_pos.shape[1], home_back.shape[1]), BF),
        compiler_params=params(56),
        cost_estimate=cost(5),
        name="unplace",
    )(slot_pos, home_back)


def coef_kernel(
    rep_ref, map_ref, row_ref, src_ref, got_ref, out_ref, order_ref, count_ref, held, weights, sems
):
    count, rows, cols = weights.shape
    at = pl.ds(pl.multiple_of(rep_ref[0] * cols, cols), cols)
    copies = [
        pltpu.make_async_copy(src_ref.at[:, :, at], weights, sems.at[0]),
        pltpu.make_async_copy(got_ref, held, sems.at[1]),
    ]
    for copy in copies:
        copy.start()
    expert_order(map_ref, order_ref, count_ref)
    for copy in copies:
        copy.wait()
    lane = lax.broadcasted_iota(I32, (8, 128), 1)

    def one(g, total):
        merged = held[g].astype(F32)
        for n in range(2):
            expert = order_ref[2 * g + n]
            product = merged * weights[expert].astype(F32)
            folded = jnp.sum(product.reshape(rows // 8, 8, cols), axis=0)
            small = folded[:, :128]
            for c in range(128, cols, 128):
                small = small + folded[:, c : c + 128]
            small = jnp.sum(jnp.sum(small, axis=0, keepdims=True), axis=1, keepdims=True)
            total = total + jnp.where(lane == expert, small, 0.0)
        return total

    total = lax.fori_loop(0, count // 2, one, jnp.zeros((8, 128), F32))[:1]
    end = row_ref.shape[1]
    for n in range(out_ref.shape[0]):
        out_ref[n, :, :end] = row_ref[...]
        out_ref[n, :, end:] = total


def finish_kernel(
    scale, map_ref, coef_ref, _, got_ref, out_ref, order_ref, count_ref, held, ready, sems, more
):
    count = ready.shape[0]

    def load(g):
        return pltpu.make_async_copy(got_ref.at[g], held.at[g], sems.at[g])

    def send(i):
        return pltpu.make_async_copy(ready.at[i], out_ref.at[order_ref[i]], more.at[i])

    @pl.loop(0, count // 2)
    def _(g):
        load(g).start()

    expert_order(map_ref, order_ref, count_ref)

    @pl.loop(0, count // 2)
    def _(g):
        load(g).wait()
        merged = held[g].astype(F32)
        for n in range(2):
            i = 2 * g + n
            ready[i] = merged * (coef_ref[order_ref[i]] * scale)
            send(i).start()

    @pl.loop(0, count)
    def _(i):
        send(i).wait()


def coef_dots(rep_index, merge_map, row, source_w, arrived, devices):
    count = source_w.shape[0]
    _, rows, cols = arrived.shape
    return pl.pallas_call(
        coef_kernel,
        in_specs=[smem_spec(), smem_spec(), vmem_spec(), hbm_spec(), any_spec()],
        out_specs=vmem_spec(),
        out_shape=jax.ShapeDtypeStruct((devices, 1, row.shape[1] + 128), F32),
        scratch_shapes=[
            pltpu.SMEM((count,), I32),
            pltpu.SMEM((count // 2,), I32),
            pltpu.VMEM(arrived.shape, BF),
            pltpu.VMEM((count, rows, cols), BF),
            pltpu.SemaphoreType.DMA((2,)),
        ],
        compiler_params=params(56),
        cost_estimate=cost(5),
        name="coef_dots",
    )(rep_index, merge_map, row, source_w, arrived)


def finish(merge_map, merge_coef, arrived, after, scale):
    count = merge_map.shape[0]
    _, rows, cols = arrived.shape
    return pl.pallas_call(
        functools.partial(finish_kernel, scale),
        in_specs=[smem_spec(), smem_spec(), any_spec(), any_spec()],
        out_specs=hbm_spec(),
        out_shape=jax.ShapeDtypeStruct((count, rows, cols), F32),
        scratch_shapes=[
            pltpu.SMEM((count,), I32),
            pltpu.SMEM((count // 2,), I32),
            pltpu.VMEM(arrived.shape, BF),
            pltpu.VMEM((count, rows, cols), F32),
            pltpu.SemaphoreType.DMA((count // 2,)),
            pltpu.SemaphoreType.DMA((count,)),
        ],
        compiler_params=params(56),
        cost_estimate=cost(5),
        name="finish",
    )(merge_map, merge_coef, after, arrived)


def add_up(x, bits):
    for axis, distance, bit in bits:
        x = x.reshape((2, x.shape[0] // 2) + x.shape[1:])
        keep = lax.dynamic_index_in_dim(x, bit, 0, keepdims=False)
        give = lax.dynamic_index_in_dim(x, 1 - bit, 0, keepdims=False)
        size = lax.axis_size(axis)
        x = keep + lax.ppermute(give, axis, [(i, i ^ distance) for i in range(size)])
    return x


def on_pairs(
    tokens, router_w, router_b, hidden, teacher_idx, merge_map, merge_coef, source_w, out_grad
):
    blocks = lax.axis_size("ctx")
    reps = lax.axis_size("row") * lax.axis_size("core")
    devices = blocks * reps
    tok = tokens.shape[1]
    features = tokens.shape[2]
    top = teacher_idx.shape[2]
    width = hidden.shape[3]
    depth = out_grad.shape[2]
    sources = router_w.shape[1]
    row_share = source_w.shape[1]
    lanes = blocks
    capacity = 5 * tok * top // (4 * blocks)
    scale = 1.0 / math.sqrt(tok * devices)
    ctx_i, row_i, core_i = lax.axis_index("ctx"), lax.axis_index("row"), lax.axis_index("core")
    rep_i = 2 * row_i + core_i

    def one(number):
        return jnp.asarray(number, I32)[None]

    def swap(x, axis):
        return lax.ppermute(x, axis, [(0, 1), (1, 0)])

    def trade(x):
        return lax.all_to_all(x, "ctx", split_axis=0, concat_axis=0, tiled=True)

    def trade_rows(rows):
        return trade(rows.reshape(lanes, capacity, rows.shape[1])).reshape(rows.shape)

    combos = merge_experts(one(rep_i), merge_map, merge_coef, source_w, reps)
    mine = trade(combos.reshape((lanes, 2) + combos.shape[1:]))

    xt = tokens.reshape(tok, features).T
    rwt = router_w.T
    idx_t = teacher_idx.reshape(tok, top).T
    og = out_grad.reshape(tok, depth)
    *hid_parts, send_grd, gates, pos, slot_pos = route(
        one(ctx_i), xt, rwt, router_b, idx_t, merge_map, hidden.reshape(tok * top, width), og,
        combos, capacity, lanes,
    )

    def trade_parts(parts):
        return [parts[0]] + [
            lax.ppermute(parts[d], "ctx", [(i, i ^ d) for i in range(lanes)])
            for d in range(1, lanes)
        ]

    hid = assemble(one(ctx_i), trade_parts(hid_parts))
    far = swap(mine, "row")
    pieces = [mine, swap(mine, "core"), far, swap(far, "core")]
    (send_grd,) = hold([send_grd], mine)
    grd = trade_rows(send_grd)
    out_parts = run_lane(
        forward_kernel, one(rep_i), one(ctx_i), hid, hid, pieces, lanes, "lane_forward"
    )
    home_parts = trade_parts(out_parts)
    (grd,) = hold([grd], out_parts[0])

    def summed(row):
        first = lane_grads(one(2 * row + 1 - core_i), grd, hid, None, blocks, reps)
        return lane_grads(one(2 * row + core_i), grd, hid, swap(first, "core"), blocks, reps)

    distant, near = summed(1 - row_i), summed(row_i)
    away = swap(distant, "row")
    (last_grd,) = hold([grd], distant, near)
    back_rows = run_lane(
        backward_kernel, one(rep_i), one(ctx_i), last_grd, hid, pieces, None, "lane_backward"
    )
    home_out = assemble(one(ctx_i), hold(home_parts, back_rows))
    total = (near.astype(F32) + away.astype(F32)).astype(BF)

    mixed, token_grad, part = combine(home_out, og, gates, pos, idx_t, rwt, xt)
    home_back = trade_rows(back_rows)
    hidden_grad = unplace(home_back, slot_pos)

    (part,) = hold([part], away)
    part = add_up(
        part,
        [
            ("ctx", 4, ctx_i // 4),
            ("ctx", 2, ctx_i // 2 % 2),
            ("ctx", 1, ctx_i % 2),
            ("row", 1, row_i),
            ("core", 1, core_i),
        ],
    )
    (total,) = hold([total], home_back)
    arrived = trade(total).reshape(2 * lanes, row_share, width // reps)
    (arrived,) = hold([arrived], hidden_grad, part)
    dots = coef_dots(one(rep_i), merge_map, part, source_w, arrived, devices)
    news = lax.all_to_all(
        dots, ("ctx", "row", "core"), split_axis=0, concat_axis=0, tiled=True
    )
    source_w_grad = finish(merge_map, merge_coef, arrived, dots, scale)
    end = part.shape[1]
    return (
        mixed.reshape(1, tok, depth),
        hidden_grad.reshape(1, tok, top, width),
        token_grad.T.reshape(1, tok, features),
        news[:, 0, :features].T * scale,
        news[:, 0, end - 1] * scale,
        jnp.sum(news[:, 0, end : end + sources], axis=0) * scale,
        source_w_grad,
    )


def solution(mesh):
    if mesh.shape["ctx"] == 8 and mesh.shape["rep"] == 4:
        mesh = jax.sharding.Mesh(mesh.devices.reshape(8, 2, 2), ("ctx", "row", "core"))
        ctx, rep, body = "ctx", ("row", "core"), on_pairs
    else:
        ctx, rep, body = "ctx", "rep", on_device
    in_specs = (
        P(rep, ctx, None),
        P(),
        P(),
        P(rep, ctx, None, None),
        P(rep, ctx, None),
        P(),
        P(),
        P(None, ctx, None),
        P(rep, ctx, None),
    )
    out_specs = (
        P(rep, ctx, None),
        P(rep, ctx, None, None),
        P(rep, ctx, None),
        P(),
        P(),
        P(),
        P(None, ctx, rep),
    )
    return jax.shard_map(
        body, mesh=mesh, in_specs=in_specs, out_specs=out_specs, check_vma=False
    )
```

```python
import functools
import math

import jax
import jax.numpy as jnp
from jax import lax
from jax.experimental import pallas as pl
from jax.experimental.pallas import tpu as pltpu
from jax.sharding import PartitionSpec as P

MERGED = 16


def expert_rows(rows_hidden, rows_grad, rows_member, lane_weights):
    row_count = rows_hidden.shape[0]
    out_rows = jnp.zeros((row_count, lane_weights.shape[1]), jnp.float32)
    back_rows = jnp.zeros((row_count, lane_weights.shape[2]), jnp.float32)
    grad_list = []
    for member_now in range(lane_weights.shape[0]):
        weight = lane_weights[member_now]
        selected = (rows_member == member_now)[:, None]
        forward = lax.dot_general(
            rows_hidden, weight, (((1,), (1,)), ((), ())), preferred_element_type=jnp.float32
        )
        out_rows = jnp.where(selected, forward, out_rows)
        backward = jnp.dot(rows_grad, weight, preferred_element_type=jnp.float32)
        back_rows = jnp.where(selected, backward, back_rows)
        masked = jnp.where(selected, rows_grad, jnp.zeros_like(rows_grad))
        grad_list.append(
            lax.dot_general(
                masked, rows_hidden, (((0,), (0,)), ((), ())), preferred_element_type=jnp.float32
            )
        )
    return (out_rows, back_rows, jnp.stack(grad_list))


def on_device(
    tokens, router_w, router_b, hidden, teacher_idx, merge_map, merge_coef, source_w, out_grad
):
    ctx_count = lax.axis_size("ctx")
    rep_count = lax.axis_size("rep")
    tok_count = tokens.shape[1]
    feature_count = tokens.shape[2]
    top_count = teacher_idx.shape[2]
    hidden_width = hidden.shape[3]
    out_width = out_grad.shape[2]
    source_count = router_w.shape[1]
    row_share = source_w.shape[1]
    per_lane = max(1, MERGED // ctx_count)
    copies = max(1, ctx_count // MERGED)
    capacity = 5 * tok_count * top_count // (4 * ctx_count)
    slot_count = tok_count * top_count
    grad_scale = 1.0 / math.sqrt(tok_count * ctx_count * rep_count)
    flat_x = tokens.reshape(tok_count, feature_count)
    logits = jnp.dot(flat_x, router_w, preferred_element_type=jnp.float32) + router_b
    choice_ids = teacher_idx.reshape(tok_count, top_count)
    pick_table = choice_ids[:, :, None] == jnp.arange(source_count, dtype=jnp.int32)[None, None, :]
    pick_float = pick_table.astype(jnp.float32)
    chosen = jnp.sum(pick_float * logits[:, None, :], axis=2)
    raised = jnp.exp(chosen)
    gate_probs = raised / jnp.sum(raised, axis=1, keepdims=True)
    merged_id = jnp.sum(jnp.where(pick_table, merge_map[None, None, :], 0), axis=2)
    position = lax.axis_index("ctx") * tok_count + jnp.arange(tok_count, dtype=jnp.int32)
    lane_id = merged_id // per_lane * copies + (position % copies)[:, None]
    member_id = (merged_id % per_lane).reshape(-1)
    lane_flat = lane_id.reshape(-1)
    onehot = (lane_flat[:, None] == jnp.arange(ctx_count, dtype=jnp.int32)[None, :]).astype(
        jnp.int32
    )
    before = jnp.cumsum(onehot, axis=0) - onehot
    slot_rank = jnp.sum(before * onehot, axis=1)
    is_kept = slot_rank < capacity
    slot_index = jnp.where(is_kept, lane_flat * capacity + slot_rank, ctx_count * capacity)
    slot_source = (
        jnp.full((ctx_count * capacity + 1,), slot_count, jnp.int32)
        .at[slot_index]
        .set(jnp.arange(slot_count, dtype=jnp.int32))[: ctx_count * capacity]
    )
    slot_grad = (gate_probs[:, :, None] * out_grad.reshape(tok_count, 1, out_width)).astype(
        jnp.bfloat16
    )
    pad_hidden = jnp.concatenate(
        [hidden.reshape(slot_count, hidden_width), jnp.zeros((1, hidden_width), jnp.bfloat16)],
        axis=0,
    )
    pad_grad = jnp.concatenate(
        [slot_grad.reshape(slot_count, out_width), jnp.zeros((1, out_width), jnp.bfloat16)], axis=0
    )
    pad_member = jnp.concatenate([member_id, jnp.zeros((1,), jnp.int32)], axis=0)
    send_hidden = pad_hidden[slot_source].reshape(ctx_count, capacity, hidden_width)
    send_grad = pad_grad[slot_source].reshape(ctx_count, capacity, out_width)
    send_member = pad_member[slot_source].reshape(ctx_count, capacity)
    lane_group = lax.axis_index("ctx") // copies
    same_group = merge_map[:, None] == merge_map[None, :]
    earlier = jnp.arange(source_count)[:, None] > jnp.arange(source_count)[None, :]
    member_rank = jnp.sum((same_group & earlier).astype(jnp.int32), axis=1)
    source_order = (
        jnp.zeros((source_count,), jnp.int32)
        .at[2 * merge_map + member_rank]
        .set(jnp.arange(source_count, dtype=jnp.int32))
    )
    picked = source_w[source_order].reshape(
        MERGED // per_lane, 2 * per_lane, row_share, hidden_width
    )
    outgoing = jnp.repeat(picked, copies, axis=0)
    arrived = lax.all_to_all(outgoing, "ctx", split_axis=0, concat_axis=2, tiled=True)
    pair_rows = arrived.reshape(per_lane, 2, row_share * ctx_count, hidden_width)
    coef_table = merge_coef[source_order].reshape(MERGED // per_lane, per_lane, 2)
    pair_coef = lax.dynamic_index_in_dim(coef_table, lane_group, 0, keepdims=False)
    lane_weights = (
        pair_coef[:, 0, None, None] * pair_rows[:, 0].astype(jnp.float32)
        + pair_coef[:, 1, None, None] * pair_rows[:, 1].astype(jnp.float32)
    ).astype(jnp.bfloat16)
    recv_hidden, recv_grad, recv_member = (
        lax.all_to_all(send_hidden, "ctx", split_axis=0, concat_axis=0, tiled=True),
        lax.all_to_all(send_grad, "ctx", split_axis=0, concat_axis=0, tiled=True),
        lax.all_to_all(send_member, "ctx", split_axis=0, concat_axis=0, tiled=True),
    )
    out_rows, back_rows, lane_grads = expert_rows(
        recv_hidden.reshape(-1, hidden_width),
        recv_grad.reshape(-1, out_width),
        recv_member.reshape(-1),
        lane_weights,
    )
    home_out, home_back = (
        lax.all_to_all(
            out_rows.astype(jnp.bfloat16).reshape(ctx_count, capacity, out_width),
            "ctx",
            split_axis=0,
            concat_axis=0,
            tiled=True,
        ),
        lax.all_to_all(
            back_rows.astype(jnp.bfloat16).reshape(ctx_count, capacity, hidden_width),
            "ctx",
            split_axis=0,
            concat_axis=0,
            tiled=True,
        ),
    )
    slot_out = jnp.concatenate(
        [home_out.reshape(-1, out_width), jnp.zeros((1, out_width), jnp.bfloat16)], axis=0
    )[slot_index].reshape(tok_count, top_count, out_width)
    hidden_grad = jnp.concatenate(
        [home_back.reshape(-1, hidden_width), jnp.zeros((1, hidden_width), jnp.bfloat16)], axis=0
    )[slot_index].reshape(1, tok_count, top_count, hidden_width)
    mixed = (
        jnp.sum(gate_probs[:, :, None] * slot_out.astype(jnp.float32), axis=1)
        .astype(jnp.bfloat16)
        .reshape(1, tok_count, out_width)
    )
    score_grad = jnp.einsum(
        "td,tkd->tk",
        out_grad.reshape(tok_count, out_width),
        slot_out,
        preferred_element_type=jnp.float32,
    )
    chosen_grad = gate_probs * (
        score_grad - jnp.sum(gate_probs * score_grad, axis=1, keepdims=True)
    )
    logit_grad = jnp.sum(pick_float * chosen_grad[:, :, None], axis=1)
    logit_half = logit_grad.astype(jnp.bfloat16)
    token_grad = (
        lax.dot_general(
            logit_half, router_w, (((1,), (1,)), ((), ())), preferred_element_type=jnp.float32
        )
        .astype(jnp.bfloat16)
        .reshape(1, tok_count, feature_count)
    )
    part_router_w = lax.dot_general(
        flat_x, logit_half, (((0,), (0,)), ((), ())), preferred_element_type=jnp.float32
    )
    part_router_b = jnp.sum(logit_grad, axis=0)
    arrived_grads = lax.all_to_all(
        lane_grads.reshape(per_lane, ctx_count, row_share, hidden_width),
        "ctx",
        split_axis=1,
        concat_axis=0,
        tiled=True,
    )
    merged_grad = (
        arrived_grads.reshape(MERGED // per_lane, copies, per_lane, row_share, hidden_width)
        .sum(axis=1)
        .reshape(MERGED, row_share, hidden_width)
    )
    source_grad = merged_grad[merge_map]
    coef_part = jnp.einsum(
        "edf,edf->e", source_grad, source_w.astype(jnp.float32), precision=lax.Precision.HIGHEST
    )
    summed = lax.psum_scatter(
        source_grad * merge_coef[:, None, None], "rep", scatter_dimension=2, tiled=True
    )
    source_w_grad = summed * grad_scale
    router_sum, bias_sum, coef_sum = lax.psum(
        (part_router_w, part_router_b, coef_part), ("ctx", "rep")
    )
    return (
        mixed,
        hidden_grad,
        token_grad,
        router_sum * grad_scale,
        bias_sum * grad_scale,
        coef_sum * grad_scale,
        source_w_grad,
    )


BF = jnp.bfloat16
F32 = jnp.float32
I32 = jnp.int32
TILE = 256


def cost(us):
    return pl.CostEstimate(flops=us * 10**9, bytes_accessed=us * 10**6, transcendentals=0)


def any_spec():
    return pl.BlockSpec(memory_space=pl.ANY)


def smem_spec():
    return pl.BlockSpec(memory_space=pltpu.SMEM)


def vmem_spec():
    return pl.BlockSpec(memory_space=pltpu.VMEM)


def params(mib):
    return pltpu.CompilerParams(vmem_limit_bytes=mib * 1024 * 1024)


def dot(a, b, dims):
    return lax.dot_general(a, b, (dims, ((), ())), preferred_element_type=F32)


def merge_kernel(
    rep_ref, map_ref, coef_ref, src_ref, _, out_ref, order_ref, count_ref, held, sems
):
    combos, _, cols = out_ref.shape
    expert_order(map_ref, order_ref, count_ref)
    at = pl.ds(pl.multiple_of(rep_ref[0] * cols, cols), cols)
    copies = [
        pltpu.make_async_copy(src_ref.at[order_ref[i], :, at], held.at[i], sems.at[i])
        for i in range(2 * combos)
    ]
    for copy in copies:
        copy.start()
    for g in range(combos):
        copies[2 * g].wait()
        copies[2 * g + 1].wait()
        one, two = coef_ref[order_ref[2 * g]], coef_ref[order_ref[2 * g + 1]]
        merged = one * held[2 * g].astype(F32) + two * held[2 * g + 1].astype(F32)
        out_ref[g] = merged.astype(BF)


def expert_order(map_ref, order_ref, count_ref):
    @pl.loop(0, count_ref.shape[0])
    def _(g):
        count_ref[g] = 0

    @pl.loop(0, order_ref.shape[0])
    def _(e):
        g = map_ref[e]
        n = count_ref[g]
        order_ref[2 * g + n] = e
        count_ref[g] = n + 1


def merge_experts(rep_index, merge_map, merge_coef, source_w, after, reps):
    count, rows, width = source_w.shape
    cols = width // reps
    return pl.pallas_call(
        merge_kernel,
        in_specs=[smem_spec()] * 3 + [any_spec()] * 2,
        out_specs=vmem_spec(),
        out_shape=jax.ShapeDtypeStruct((count // 2, rows, cols), BF),
        scratch_shapes=[
            pltpu.SMEM((count,), I32),
            pltpu.SMEM((count // 2,), I32),
            pltpu.VMEM((count, rows, cols), BF),
            pltpu.SemaphoreType.DMA((count,)),
        ],
        compiler_params=params(56),
        cost_estimate=cost(5),
        name="merge_experts",
    )(rep_index, merge_map, merge_coef, source_w, after)


def hbm_spec():
    return pl.BlockSpec(memory_space=pltpu.HBM)


def hold(arrays, *after):
    count = len(arrays)
    return pl.pallas_call(
        lambda *refs: None,
        in_specs=[hbm_spec()] * count + [any_spec()] * len(after),
        out_specs=[hbm_spec()] * count,
        out_shape=[jax.ShapeDtypeStruct(a.shape, a.dtype) for a in arrays],
        input_output_aliases={i: i for i in range(count)},
        cost_estimate=cost(0),
        name="hold",
    )(*arrays, *after)


def column(row):
    size = row.shape[1]
    same = lax.broadcasted_iota(I32, (size, size), 0) == lax.broadcasted_iota(I32, (size, size), 1)
    return jnp.sum(jnp.where(same, row, jnp.zeros_like(row)), axis=1, keepdims=True)


def to_row(col):
    size = col.shape[0]
    same = lax.broadcasted_iota(I32, (size, size), 0) == lax.broadcasted_iota(I32, (size, size), 1)
    return jnp.sum(jnp.where(same, col, jnp.zeros_like(col)), axis=0, keepdims=True)


def picks_of(idx_ref, k, sources):
    tok = idx_ref.shape[1]
    return lax.broadcasted_iota(I32, (sources, tok), 0) == idx_ref[k : k + 1, :]


def route_kernel(
    capacity, lanes,
    xt_ref, rwt_ref, rb_ref, idx_ref, map_ref, hid_ref, og_ref,
    send_ref, gate_ref, pos_ref, slot_ref,
):
    top, tok = idx_ref.shape
    sources = rwt_ref.shape[0]
    slots, width = hid_ref.shape
    places = lanes * capacity
    logits = jnp.dot(rwt_ref[...], xt_ref[...], preferred_element_type=F32) + column(rb_ref[...])
    raised, merged = [], []
    combos = column(map_ref[...])
    for k in range(top):
        pick = picks_of(idx_ref, k, sources)
        chosen = jnp.sum(jnp.where(pick, logits, 0.0), axis=0, keepdims=True)
        raised.append(jnp.exp(chosen))
        merged.append(jnp.sum(jnp.where(pick, combos, 0), axis=0, keepdims=True))
    total = raised[0]
    for k in range(1, top):
        total = total + raised[k]
    gates = [r / total for r in raised]
    lane = [jnp.right_shift(g, 1) for g in merged]
    member = [jnp.bitwise_and(g, 1) for g in merged]
    onehot = [(lax.broadcasted_iota(I32, (lanes, tok), 0) == l).astype(F32) for l in lane]
    all_hot = onehot[0]
    for k in range(1, top):
        all_hot = all_hot + onehot[k]
    earlier = (
        lax.broadcasted_iota(I32, (tok, tok), 0) < lax.broadcasted_iota(I32, (tok, tok), 1)
    ).astype(BF)
    before = jnp.dot(all_hot.astype(BF), earlier, preferred_element_type=F32)
    position = []
    for k in range(top):
        rank = jnp.sum(before * onehot[k], axis=0, keepdims=True).astype(I32)
        before = before + onehot[k]
        position.append(jnp.where(rank < capacity, lane[k] * capacity + rank, -1))
    gate_ref[...] = jnp.zeros_like(gate_ref)
    pos_ref[...] = jnp.full_like(pos_ref, -1)
    for k in range(top):
        gate_ref[k : k + 1, :] = gates[k]
        pos_ref[k : k + 1, :] = position[k]
    spot = jnp.zeros((8, slots), F32)
    for k in range(top):
        spread = (
            lax.broadcasted_iota(I32, (tok, slots), 1)
            == lax.broadcasted_iota(I32, (tok, slots), 0) * top + k
        ).astype(BF)
        kept = position[k] >= 0
        parts = [
            jnp.where(kept, jnp.right_shift(position[k], 5), 0),
            jnp.where(kept, jnp.bitwise_and(position[k], 31), 0),
            jnp.where(kept, 1, 0),
            member[k],
        ]
        stacked = jnp.concatenate(
            [p.astype(F32) for p in parts] + [jnp.zeros((4, tok), F32)], axis=0
        ).astype(BF)
        spot = spot + jnp.dot(stacked, spread, preferred_element_type=F32)
    spot = spot.astype(I32)
    slot_pos = jnp.where(spot[2:3] > 0, spot[0:1] * 32 + spot[1:2], -1)
    slot_ref[...] = jnp.broadcast_to(slot_pos, slot_ref.shape)
    take = lax.broadcasted_iota(I32, (places, slots), 0) == slot_pos
    placed = jnp.sum(jnp.where(take, spot[3:4].astype(F32), 0.0), axis=1, keepdims=True)
    depth = og_ref.shape[1]
    send_ref[:, depth + width :] = jnp.broadcast_to(placed, (places, 128)).astype(BF)
    take = take.astype(BF)
    for n in range(0, width, TILE):
        rows = jnp.dot(take, hid_ref[:, n : n + TILE], preferred_element_type=F32)
        send_ref[:, depth + n : depth + n + TILE] = rows.astype(BF)
    takes = [
        (lax.broadcasted_iota(I32, (places, tok), 0) == position[k]).astype(BF) for k in range(top)
    ]
    columns = [column(g) for g in gates]
    for n in range(0, depth, TILE):
        og = og_ref[:, n : n + TILE].astype(F32)
        rows = jnp.zeros((places, TILE), F32)
        for k in range(top):
            rows = rows + jnp.dot(takes[k], (columns[k] * og).astype(BF), preferred_element_type=F32)
        send_ref[:, n : n + TILE] = rows.astype(BF)


def route(xt, rwt, router_b, idx_t, merge_map, hid, og, capacity, lanes):
    slots, width = hid.shape
    tok = idx_t.shape[1]
    return pl.pallas_call(
        functools.partial(route_kernel, capacity, lanes),
        in_specs=[vmem_spec()] * 7,
        out_specs=[vmem_spec()] * 4,
        out_shape=[
            jax.ShapeDtypeStruct((lanes * capacity, og.shape[1] + width + 128), BF),
            jax.ShapeDtypeStruct((8, tok), F32),
            jax.ShapeDtypeStruct((8, tok), I32),
            jax.ShapeDtypeStruct((8, slots), I32),
        ],
        compiler_params=params(56),
        cost_estimate=cost(5),
        name="route",
    )(xt, rwt, router_b[None, :], idx_t, merge_map[None, :], hid, og)


def load_weights(rep_ref, pieces, w_ref, sems):
    copies = []
    for i, piece in enumerate(pieces):
        blocks, _, rows, cols = piece.shape
        owner = jnp.bitwise_xor(rep_ref[0], i)
        at = pl.ds(pl.multiple_of(owner * cols, cols), cols)
        for c in range(blocks):
            to = w_ref.at[:, pl.ds(c * rows, rows), at]
            copies.append(pltpu.make_async_copy(piece.at[c], to, sems.at[len(copies)]))
    for copy in copies:
        copy.start()
    for copy in copies:
        copy.wait()


def forward_kernel(rep_ref, rows_ref, flag_ref, *refs):
    out_ref, w_ref, sems = refs[-3:]
    load_weights(rep_ref, refs[:-3], w_ref, sems)
    member = flag_ref[:, :1].astype(F32)
    for n in range(0, w_ref.shape[1], TILE):
        at = slice(n, n + TILE)
        both = [dot(rows_ref[...], w_ref[m, at, :], ((1,), (1,))) for m in range(2)]
        out_ref[:, at] = jnp.where(member == 0.0, both[0], both[1]).astype(BF)


def backward_kernel(rep_ref, rows_ref, flag_ref, *refs):
    out_ref, w_ref, sems = refs[-3:]
    load_weights(rep_ref, refs[:-3], w_ref, sems)
    member = flag_ref[:, :1].astype(F32)
    for n in range(0, w_ref.shape[2], TILE):
        at = slice(n, n + TILE)
        both = [dot(rows_ref[...], w_ref[m, :, at], ((1,), (0,))) for m in range(2)]
        out_ref[:, at] = jnp.where(member == 0.0, both[0], both[1]).astype(BF)


def run_lane(kernel, rep_index, rows, which, pieces, name):
    blocks, members, share, cols = pieces[0].shape
    depth, width = share * blocks, cols * len(pieces)
    count = rows.shape[0]
    return pl.pallas_call(
        kernel,
        grid=(1,),
        in_specs=[
            smem_spec(),
            pl.BlockSpec((count, width), lambda i: (0, which)),
            pl.BlockSpec((count, 128), lambda i: (0, 2 * width // 128)),
        ]
        + [any_spec()] * len(pieces),
        out_specs=pl.BlockSpec((count, width), lambda i: (0, 0)),
        out_shape=jax.ShapeDtypeStruct((count, width), BF),
        scratch_shapes=[
            pltpu.VMEM((members, depth, width), BF),
            pltpu.SemaphoreType.DMA((blocks * len(pieces),)),
        ],
        compiler_params=params(56),
        cost_estimate=cost(12),
        name=name,
    )(rep_index, rows, rows, *pieces)


def lane_grad_kernel(has_other, _, grd_ref, hid_ref, flag_ref, *refs):
    out_ref = refs[-1]
    chosen = flag_ref[:, :1].astype(F32) == pl.program_id(0).astype(F32)
    hid = jnp.where(chosen, hid_ref[...], jnp.zeros_like(hid_ref))
    blocks, _, rows, cols = out_ref.shape
    each = 2 if blocks % 2 == 0 and 2 * rows % 128 == 0 else blocks
    for n in range(0, blocks, each):
        part = dot(grd_ref[:, n * rows : (n + each) * rows], hid, ((0,), (0,)))
        part = part.reshape(each, rows, cols)
        if has_other:
            part = part + refs[0][n : n + each, 0].astype(F32)
        out_ref[n : n + each, 0] = part.astype(BF)


def lane_grads(owner, rows, other, blocks, reps):
    count = rows.shape[0]
    depth = width = (rows.shape[1] - 128) // 2
    cols = width // reps
    shape = (blocks, 2, depth // blocks, cols)
    block = pl.BlockSpec((blocks, 1, depth // blocks, cols), lambda m, s: (0, m, 0, 0))
    extra = [] if other is None else [other]
    return pl.pallas_call(
        functools.partial(lane_grad_kernel, other is not None),
        grid_spec=pltpu.PrefetchScalarGridSpec(
            num_scalar_prefetch=1,
            grid=(2,),
            in_specs=[
                pl.BlockSpec((count, depth), lambda m, s: (0, 0)),
                pl.BlockSpec((count, cols), lambda m, s: (0, reps + s[0])),
                pl.BlockSpec((count, 128), lambda m, s: (0, 2 * width // 128)),
            ]
            + [block] * len(extra),
            out_specs=block,
        ),
        out_shape=jax.ShapeDtypeStruct(shape, BF),
        compiler_params=params(56),
        cost_estimate=cost(6),
        name="lane_grads_add" if extra else "lane_grads_first",
    )(owner, rows, rows, rows, *extra)


def combine_kernel(
    og_ref, gate_ref, pos_ref, idx_ref, rwt_ref, xt_ref, out_ref, mixed_ref, tg_ref, part_ref
):
    places, width = out_ref.shape
    top, tok = idx_ref.shape
    sources, features = rwt_ref.shape
    takes = [
        (lax.broadcasted_iota(I32, (places, tok), 0) == pos_ref[k : k + 1, :]).astype(BF)
        for k in range(top)
    ]
    gates = [gate_ref[k : k + 1, :] for k in range(top)]
    columns = [column(g) for g in gates]
    scores = [jnp.zeros((tok, 1), F32) for _ in range(top)]
    for n in range(0, width, TILE):
        og = og_ref[:, n : n + TILE].astype(F32)
        rows = out_ref[:, n : n + TILE]
        mixed = jnp.zeros((tok, TILE), F32)
        for k in range(top):
            slot_out = dot(takes[k], rows, ((0,), (0,)))
            mixed = mixed + columns[k] * slot_out
            scores[k] = scores[k] + jnp.sum(og * slot_out, axis=1, keepdims=True)
        mixed_ref[:, n : n + TILE] = mixed.astype(BF)
    scores = [to_row(s) for s in scores]
    middle = gates[0] * scores[0]
    for k in range(1, top):
        middle = middle + gates[k] * scores[k]
    logit_grad = jnp.zeros((sources, tok), F32)
    for k in range(top):
        chosen_grad = gates[k] * (scores[k] - middle)
        logit_grad = logit_grad + jnp.where(picks_of(idx_ref, k, sources), chosen_grad, 0.0)
    logit_half = logit_grad.astype(BF)
    tg_ref[...] = dot(rwt_ref[...], logit_half, ((0,), (0,))).astype(BF)
    part_ref[...] = jnp.zeros_like(part_ref)
    part_ref[:, :features] = dot(logit_half, xt_ref[...], ((1,), (1,)))
    bias = jnp.sum(logit_grad, axis=1, keepdims=True)
    last = part_ref.shape[1] - 128
    part_ref[:, last:] = jnp.broadcast_to(bias, (sources, 128))


def combine(home_out, og, gates, pos, idx_t, rwt, xt):
    sources, features = rwt.shape
    tok = idx_t.shape[1]
    return pl.pallas_call(
        combine_kernel,
        in_specs=[vmem_spec()] * 7,
        out_specs=[vmem_spec()] * 3,
        out_shape=[
            jax.ShapeDtypeStruct(og.shape, BF),
            jax.ShapeDtypeStruct((features, tok), BF),
            jax.ShapeDtypeStruct((sources, (features + 127) // 128 * 128 + 128), F32),
        ],
        compiler_params=params(56),
        cost_estimate=cost(5),
        name="combine",
    )(og, gates, pos, idx_t, rwt, xt, home_out)


def unplace_kernel(slot_ref, back_ref, out_ref):
    places, width = back_ref.shape
    slots = slot_ref.shape[1]
    take = (lax.broadcasted_iota(I32, (places, slots), 0) == slot_ref[0:1, :]).astype(BF)
    for n in range(0, width, TILE):
        out_ref[:, n : n + TILE] = dot(take, back_ref[:, n : n + TILE], ((0,), (0,))).astype(BF)


def unplace(home_back, slot_pos):
    return pl.pallas_call(
        unplace_kernel,
        in_specs=[vmem_spec()] * 2,
        out_specs=vmem_spec(),
        out_shape=jax.ShapeDtypeStruct((slot_pos.shape[1], home_back.shape[1]), BF),
        compiler_params=params(56),
        cost_estimate=cost(5),
        name="unplace",
    )(slot_pos, home_back)


def coef_kernel(rep_ref, map_ref, src_ref, got_ref, out_ref, order_ref, count_ref, held, weights, sems):
    count, rows, cols = weights.shape
    at = pl.ds(pl.multiple_of(rep_ref[0] * cols, cols), cols)
    copies = [
        pltpu.make_async_copy(src_ref.at[:, :, at], weights, sems.at[0]),
        pltpu.make_async_copy(got_ref, held, sems.at[1]),
    ]
    for copy in copies:
        copy.start()
    expert_order(map_ref, order_ref, count_ref)
    for copy in copies:
        copy.wait()
    lane = lax.broadcasted_iota(I32, (8, 128), 1)

    def one(g, total):
        merged = held[g].astype(F32)
        for n in range(2):
            expert = order_ref[2 * g + n]
            product = merged * weights[expert].astype(F32)
            folded = jnp.sum(product.reshape(rows // 8, 8, cols), axis=0)
            small = folded[:, :128]
            for c in range(128, cols, 128):
                small = small + folded[:, c : c + 128]
            small = jnp.sum(jnp.sum(small, axis=0, keepdims=True), axis=1, keepdims=True)
            total = total + jnp.where(lane == expert, small, 0.0)
        return total

    out_ref[...] = lax.fori_loop(0, count // 2, one, jnp.zeros((8, 128), F32))


def finish_kernel(
    scale, map_ref, coef_ref, _, got_ref, out_ref, order_ref, count_ref, held, ready, sems, more
):
    count = ready.shape[0]

    def load(g):
        return pltpu.make_async_copy(got_ref.at[g], held.at[g], sems.at[g])

    def send(i):
        return pltpu.make_async_copy(ready.at[i], out_ref.at[order_ref[i]], more.at[i])

    @pl.loop(0, count // 2)
    def _(g):
        load(g).start()

    expert_order(map_ref, order_ref, count_ref)

    @pl.loop(0, count // 2)
    def _(g):
        load(g).wait()
        merged = held[g].astype(F32)
        for n in range(2):
            i = 2 * g + n
            ready[i] = merged * (coef_ref[order_ref[i]] * scale)
            send(i).start()

    @pl.loop(0, count)
    def _(i):
        send(i).wait()


def coef_dots(rep_index, merge_map, source_w, arrived):
    count = source_w.shape[0]
    _, rows, cols = arrived.shape
    return pl.pallas_call(
        coef_kernel,
        in_specs=[smem_spec(), smem_spec(), hbm_spec(), any_spec()],
        out_specs=vmem_spec(),
        out_shape=jax.ShapeDtypeStruct((8, 128), F32),
        scratch_shapes=[
            pltpu.SMEM((count,), I32),
            pltpu.SMEM((count // 2,), I32),
            pltpu.VMEM(arrived.shape, BF),
            pltpu.VMEM((count, rows, cols), BF),
            pltpu.SemaphoreType.DMA((2,)),
        ],
        compiler_params=params(56),
        cost_estimate=cost(5),
        name="coef_dots",
    )(rep_index, merge_map, source_w, arrived)


def finish(merge_map, merge_coef, arrived, after, scale):
    count = merge_map.shape[0]
    _, rows, cols = arrived.shape
    return pl.pallas_call(
        functools.partial(finish_kernel, scale),
        in_specs=[smem_spec(), smem_spec(), any_spec(), any_spec()],
        out_specs=hbm_spec(),
        out_shape=jax.ShapeDtypeStruct((count, rows, cols), F32),
        scratch_shapes=[
            pltpu.SMEM((count,), I32),
            pltpu.SMEM((count // 2,), I32),
            pltpu.VMEM(arrived.shape, BF),
            pltpu.VMEM((count, rows, cols), F32),
            pltpu.SemaphoreType.DMA((count // 2,)),
            pltpu.SemaphoreType.DMA((count,)),
        ],
        compiler_params=params(56),
        cost_estimate=cost(5),
        name="finish",
    )(merge_map, merge_coef, after, arrived)


def add_up(x, bits):
    for axis, distance, bit in bits:
        x = x.reshape((2, x.shape[0] // 2) + x.shape[1:])
        keep = lax.dynamic_index_in_dim(x, bit, 0, keepdims=False)
        give = lax.dynamic_index_in_dim(x, 1 - bit, 0, keepdims=False)
        size = lax.axis_size(axis)
        x = keep + lax.ppermute(give, axis, [(i, i ^ distance) for i in range(size)])
    return x


def on_pairs(
    tokens, router_w, router_b, hidden, teacher_idx, merge_map, merge_coef, source_w, out_grad
):
    blocks = lax.axis_size("ctx")
    reps = lax.axis_size("row") * lax.axis_size("core")
    devices = blocks * reps
    tok = tokens.shape[1]
    features = tokens.shape[2]
    top = teacher_idx.shape[2]
    width = hidden.shape[3]
    depth = out_grad.shape[2]
    sources = router_w.shape[1]
    row_share = source_w.shape[1]
    lanes = blocks
    capacity = 5 * tok * top // (4 * blocks)
    scale = 1.0 / math.sqrt(tok * devices)
    ctx_i, row_i, core_i = lax.axis_index("ctx"), lax.axis_index("row"), lax.axis_index("core")
    rep_i = 2 * row_i + core_i

    def one(number):
        return jnp.asarray(number, I32)[None]

    def swap(x, axis):
        return lax.ppermute(x, axis, [(0, 1), (1, 0)])

    def trade(x):
        return lax.all_to_all(x, "ctx", split_axis=0, concat_axis=0, tiled=True)

    def trade_rows(rows):
        return trade(rows.reshape(lanes, capacity, rows.shape[1])).reshape(rows.shape)

    def later(x):
        return swap(hold([jnp.zeros((8, 128), F32)], x)[0], "core")

    xt = tokens.reshape(tok, features).T
    rwt = router_w.T
    idx_t = teacher_idx.reshape(tok, top).T
    og = out_grad.reshape(tok, depth)
    send_rows, gates, pos, slot_pos = route(
        xt, rwt, router_b, idx_t, merge_map, hidden.reshape(tok * top, width), og,
        capacity, lanes,
    )
    combos = merge_experts(one(rep_i), merge_map, merge_coef, source_w, send_rows, reps)

    rows = trade_rows(send_rows)
    (combos,) = hold([combos], rows)
    mine = trade(combos.reshape((lanes, 2) + combos.shape[1:]))
    (rows,) = hold([rows], later(rows))

    def summed(row):
        first = lane_grads(one(2 * row + 1 - core_i), rows, None, blocks, reps)
        return lane_grads(one(2 * row + core_i), rows, swap(first, "core"), blocks, reps)

    distant, near = summed(1 - row_i), summed(row_i)
    away = swap(distant, "row")
    total = (near.astype(F32) + away.astype(F32)).astype(BF)
    (mine,) = hold([mine], near)
    (total,) = hold([total], mine)
    arrived = trade(total).reshape(2 * lanes, row_share, width // reps)

    far = swap(mine, "row")
    pieces = [mine, swap(mine, "core"), far, swap(far, "core")]
    out_rows = run_lane(forward_kernel, one(rep_i), rows, 1, pieces, "lane_forward")
    arrived, out_rows = hold([arrived, out_rows])
    home_out = trade_rows(out_rows)
    (last_rows,) = hold([rows], later(arrived))
    back_rows = run_lane(backward_kernel, one(rep_i), last_rows, 0, pieces, "lane_backward")
    (arrived,) = hold([arrived], back_rows)
    dots = coef_dots(one(rep_i), merge_map, source_w, arrived)
    source_w_grad = finish(merge_map, merge_coef, arrived, dots, scale)
    (home_out,) = hold([home_out], source_w_grad)
    (back_rows,) = hold([back_rows], home_out)
    home_back = trade_rows(back_rows)

    (home_out,) = hold([home_out], later(back_rows))
    mixed, token_grad, part = combine(home_out, og, gates, pos, idx_t, rwt, xt)
    part = part.reshape(blocks, 2, 2, part.shape[1]).transpose(2, 1, 0, 3).reshape(part.shape)
    part = add_up(
        part,
        [
            ("core", 1, core_i),
            ("row", 1, row_i),
            ("ctx", 4, ctx_i // 4),
            ("ctx", 2, ctx_i // 2 % 2),
            ("ctx", 1, ctx_i % 2),
        ],
    )
    news = jnp.concatenate([part, dots[:1]], axis=1)
    (news,) = hold([news], home_back)
    news = lax.all_to_all(
        jnp.broadcast_to(news[None], (devices,) + news.shape), ("ctx", "row", "core"),
        split_axis=0, concat_axis=0, tiled=True,
    )
    hidden_grad = unplace(home_back, slot_pos)
    end = part.shape[1]
    return (
        mixed.reshape(1, tok, depth),
        hidden_grad.reshape(1, tok, top, width),
        token_grad.T.reshape(1, tok, features),
        news[:, 0, :features].T * scale,
        news[:, 0, end - 1] * scale,
        jnp.sum(news[:, 0, end : end + sources], axis=0) * scale,
        source_w_grad,
    )


def solution(mesh):
    if mesh.shape["ctx"] == 8 and mesh.shape["rep"] == 4:
        mesh = jax.sharding.Mesh(mesh.devices.reshape(8, 2, 2), ("ctx", "row", "core"))
        ctx, rep, body = "ctx", ("row", "core"), on_pairs
    else:
        ctx, rep, body = "ctx", "rep", on_device
    in_specs = (
        P(rep, ctx, None),
        P(),
        P(),
        P(rep, ctx, None, None),
        P(rep, ctx, None),
        P(),
        P(),
        P(None, ctx, None),
        P(rep, ctx, None),
    )
    out_specs = (
        P(rep, ctx, None),
        P(rep, ctx, None, None),
        P(rep, ctx, None),
        P(),
        P(),
        P(),
        P(None, ctx, rep),
    )
    return jax.shard_map(
        body, mesh=mesh, in_specs=in_specs, out_specs=out_specs, check_vma=False
    )
```

```python
import functools
import math

import jax
import jax.numpy as jnp
from jax import lax
from jax.experimental import pallas as pl
from jax.experimental.pallas import tpu as pltpu
from jax.sharding import PartitionSpec as P

MERGED = 16


def expert_rows(rows_hidden, rows_grad, rows_member, lane_weights):
    row_count = rows_hidden.shape[0]
    out_rows = jnp.zeros((row_count, lane_weights.shape[1]), jnp.float32)
    back_rows = jnp.zeros((row_count, lane_weights.shape[2]), jnp.float32)
    grad_list = []
    for member_now in range(lane_weights.shape[0]):
        weight = lane_weights[member_now]
        selected = (rows_member == member_now)[:, None]
        forward = lax.dot_general(
            rows_hidden, weight, (((1,), (1,)), ((), ())), preferred_element_type=jnp.float32
        )
        out_rows = jnp.where(selected, forward, out_rows)
        backward = jnp.dot(rows_grad, weight, preferred_element_type=jnp.float32)
        back_rows = jnp.where(selected, backward, back_rows)
        masked = jnp.where(selected, rows_grad, jnp.zeros_like(rows_grad))
        grad_list.append(
            lax.dot_general(
                masked, rows_hidden, (((0,), (0,)), ((), ())), preferred_element_type=jnp.float32
            )
        )
    return (out_rows, back_rows, jnp.stack(grad_list))


def on_device(
    tokens, router_w, router_b, hidden, teacher_idx, merge_map, merge_coef, source_w, out_grad
):
    ctx_count = lax.axis_size("ctx")
    rep_count = lax.axis_size("rep")
    tok_count = tokens.shape[1]
    feature_count = tokens.shape[2]
    top_count = teacher_idx.shape[2]
    hidden_width = hidden.shape[3]
    out_width = out_grad.shape[2]
    source_count = router_w.shape[1]
    row_share = source_w.shape[1]
    per_lane = max(1, MERGED // ctx_count)
    copies = max(1, ctx_count // MERGED)
    capacity = 5 * tok_count * top_count // (4 * ctx_count)
    slot_count = tok_count * top_count
    grad_scale = 1.0 / math.sqrt(tok_count * ctx_count * rep_count)
    flat_x = tokens.reshape(tok_count, feature_count)
    logits = jnp.dot(flat_x, router_w, preferred_element_type=jnp.float32) + router_b
    choice_ids = teacher_idx.reshape(tok_count, top_count)
    pick_table = choice_ids[:, :, None] == jnp.arange(source_count, dtype=jnp.int32)[None, None, :]
    pick_float = pick_table.astype(jnp.float32)
    chosen = jnp.sum(pick_float * logits[:, None, :], axis=2)
    raised = jnp.exp(chosen)
    gate_probs = raised / jnp.sum(raised, axis=1, keepdims=True)
    merged_id = jnp.sum(jnp.where(pick_table, merge_map[None, None, :], 0), axis=2)
    position = lax.axis_index("ctx") * tok_count + jnp.arange(tok_count, dtype=jnp.int32)
    lane_id = merged_id // per_lane * copies + (position % copies)[:, None]
    member_id = (merged_id % per_lane).reshape(-1)
    lane_flat = lane_id.reshape(-1)
    onehot = (lane_flat[:, None] == jnp.arange(ctx_count, dtype=jnp.int32)[None, :]).astype(
        jnp.int32
    )
    before = jnp.cumsum(onehot, axis=0) - onehot
    slot_rank = jnp.sum(before * onehot, axis=1)
    is_kept = slot_rank < capacity
    slot_index = jnp.where(is_kept, lane_flat * capacity + slot_rank, ctx_count * capacity)
    slot_source = (
        jnp.full((ctx_count * capacity + 1,), slot_count, jnp.int32)
        .at[slot_index]
        .set(jnp.arange(slot_count, dtype=jnp.int32))[: ctx_count * capacity]
    )
    slot_grad = (gate_probs[:, :, None] * out_grad.reshape(tok_count, 1, out_width)).astype(
        jnp.bfloat16
    )
    pad_hidden = jnp.concatenate(
        [hidden.reshape(slot_count, hidden_width), jnp.zeros((1, hidden_width), jnp.bfloat16)],
        axis=0,
    )
    pad_grad = jnp.concatenate(
        [slot_grad.reshape(slot_count, out_width), jnp.zeros((1, out_width), jnp.bfloat16)], axis=0
    )
    pad_member = jnp.concatenate([member_id, jnp.zeros((1,), jnp.int32)], axis=0)
    send_hidden = pad_hidden[slot_source].reshape(ctx_count, capacity, hidden_width)
    send_grad = pad_grad[slot_source].reshape(ctx_count, capacity, out_width)
    send_member = pad_member[slot_source].reshape(ctx_count, capacity)
    lane_group = lax.axis_index("ctx") // copies
    same_group = merge_map[:, None] == merge_map[None, :]
    earlier = jnp.arange(source_count)[:, None] > jnp.arange(source_count)[None, :]
    member_rank = jnp.sum((same_group & earlier).astype(jnp.int32), axis=1)
    source_order = (
        jnp.zeros((source_count,), jnp.int32)
        .at[2 * merge_map + member_rank]
        .set(jnp.arange(source_count, dtype=jnp.int32))
    )
    picked = source_w[source_order].reshape(
        MERGED // per_lane, 2 * per_lane, row_share, hidden_width
    )
    outgoing = jnp.repeat(picked, copies, axis=0)
    arrived = lax.all_to_all(outgoing, "ctx", split_axis=0, concat_axis=2, tiled=True)
    pair_rows = arrived.reshape(per_lane, 2, row_share * ctx_count, hidden_width)
    coef_table = merge_coef[source_order].reshape(MERGED // per_lane, per_lane, 2)
    pair_coef = lax.dynamic_index_in_dim(coef_table, lane_group, 0, keepdims=False)
    lane_weights = (
        pair_coef[:, 0, None, None] * pair_rows[:, 0].astype(jnp.float32)
        + pair_coef[:, 1, None, None] * pair_rows[:, 1].astype(jnp.float32)
    ).astype(jnp.bfloat16)
    recv_hidden, recv_grad, recv_member = (
        lax.all_to_all(send_hidden, "ctx", split_axis=0, concat_axis=0, tiled=True),
        lax.all_to_all(send_grad, "ctx", split_axis=0, concat_axis=0, tiled=True),
        lax.all_to_all(send_member, "ctx", split_axis=0, concat_axis=0, tiled=True),
    )
    out_rows, back_rows, lane_grads = expert_rows(
        recv_hidden.reshape(-1, hidden_width),
        recv_grad.reshape(-1, out_width),
        recv_member.reshape(-1),
        lane_weights,
    )
    home_out, home_back = (
        lax.all_to_all(
            out_rows.astype(jnp.bfloat16).reshape(ctx_count, capacity, out_width),
            "ctx",
            split_axis=0,
            concat_axis=0,
            tiled=True,
        ),
        lax.all_to_all(
            back_rows.astype(jnp.bfloat16).reshape(ctx_count, capacity, hidden_width),
            "ctx",
            split_axis=0,
            concat_axis=0,
            tiled=True,
        ),
    )
    slot_out = jnp.concatenate(
        [home_out.reshape(-1, out_width), jnp.zeros((1, out_width), jnp.bfloat16)], axis=0
    )[slot_index].reshape(tok_count, top_count, out_width)
    hidden_grad = jnp.concatenate(
        [home_back.reshape(-1, hidden_width), jnp.zeros((1, hidden_width), jnp.bfloat16)], axis=0
    )[slot_index].reshape(1, tok_count, top_count, hidden_width)
    mixed = (
        jnp.sum(gate_probs[:, :, None] * slot_out.astype(jnp.float32), axis=1)
        .astype(jnp.bfloat16)
        .reshape(1, tok_count, out_width)
    )
    score_grad = jnp.einsum(
        "td,tkd->tk",
        out_grad.reshape(tok_count, out_width),
        slot_out,
        preferred_element_type=jnp.float32,
    )
    chosen_grad = gate_probs * (
        score_grad - jnp.sum(gate_probs * score_grad, axis=1, keepdims=True)
    )
    logit_grad = jnp.sum(pick_float * chosen_grad[:, :, None], axis=1)
    logit_half = logit_grad.astype(jnp.bfloat16)
    token_grad = (
        lax.dot_general(
            logit_half, router_w, (((1,), (1,)), ((), ())), preferred_element_type=jnp.float32
        )
        .astype(jnp.bfloat16)
        .reshape(1, tok_count, feature_count)
    )
    part_router_w = lax.dot_general(
        flat_x, logit_half, (((0,), (0,)), ((), ())), preferred_element_type=jnp.float32
    )
    part_router_b = jnp.sum(logit_grad, axis=0)
    arrived_grads = lax.all_to_all(
        lane_grads.reshape(per_lane, ctx_count, row_share, hidden_width),
        "ctx",
        split_axis=1,
        concat_axis=0,
        tiled=True,
    )
    merged_grad = (
        arrived_grads.reshape(MERGED // per_lane, copies, per_lane, row_share, hidden_width)
        .sum(axis=1)
        .reshape(MERGED, row_share, hidden_width)
    )
    source_grad = merged_grad[merge_map]
    coef_part = jnp.einsum(
        "edf,edf->e", source_grad, source_w.astype(jnp.float32), precision=lax.Precision.HIGHEST
    )
    summed = lax.psum_scatter(
        source_grad * merge_coef[:, None, None], "rep", scatter_dimension=2, tiled=True
    )
    source_w_grad = summed * grad_scale
    router_sum, bias_sum, coef_sum = lax.psum(
        (part_router_w, part_router_b, coef_part), ("ctx", "rep")
    )
    return (
        mixed,
        hidden_grad,
        token_grad,
        router_sum * grad_scale,
        bias_sum * grad_scale,
        coef_sum * grad_scale,
        source_w_grad,
    )


BF = jnp.bfloat16
F32 = jnp.float32
I32 = jnp.int32
TILE = 256


def cost(us):
    return pl.CostEstimate(flops=us * 10**9, bytes_accessed=us * 10**6, transcendentals=0)


def any_spec():
    return pl.BlockSpec(memory_space=pl.ANY)


def smem_spec():
    return pl.BlockSpec(memory_space=pltpu.SMEM)


def vmem_spec():
    return pl.BlockSpec(memory_space=pltpu.VMEM)


def params(mib):
    return pltpu.CompilerParams(vmem_limit_bytes=mib * 1024 * 1024)


def dot(a, b, dims):
    return lax.dot_general(a, b, (dims, ((), ())), preferred_element_type=F32)


def merge_kernel(rep_ref, map_ref, coef_ref, src_ref, out_ref, order_ref, count_ref, held, sems):
    combos, _, cols = out_ref.shape
    expert_order(map_ref, order_ref, count_ref)
    at = pl.ds(pl.multiple_of(rep_ref[0] * cols, cols), cols)
    copies = [
        pltpu.make_async_copy(src_ref.at[order_ref[i], :, at], held.at[i], sems.at[i])
        for i in range(2 * combos)
    ]
    for copy in copies:
        copy.start()
    for g in range(combos):
        copies[2 * g].wait()
        copies[2 * g + 1].wait()
        one, two = coef_ref[order_ref[2 * g]], coef_ref[order_ref[2 * g + 1]]
        merged = one * held[2 * g].astype(F32) + two * held[2 * g + 1].astype(F32)
        out_ref[g] = merged.astype(BF)


def expert_order(map_ref, order_ref, count_ref):
    @pl.loop(0, count_ref.shape[0])
    def _(g):
        count_ref[g] = 0

    @pl.loop(0, order_ref.shape[0])
    def _(e):
        g = map_ref[e]
        n = count_ref[g]
        order_ref[2 * g + n] = e
        count_ref[g] = n + 1


def merge_experts(rep_index, merge_map, merge_coef, source_w, reps):
    count, rows, width = source_w.shape
    cols = width // reps
    return pl.pallas_call(
        merge_kernel,
        in_specs=[smem_spec(), smem_spec(), smem_spec(), any_spec()],
        out_specs=vmem_spec(),
        out_shape=jax.ShapeDtypeStruct((count // 2, rows, cols), BF),
        scratch_shapes=[
            pltpu.SMEM((count,), I32),
            pltpu.SMEM((count // 2,), I32),
            pltpu.VMEM((count, rows, cols), BF),
            pltpu.SemaphoreType.DMA((count,)),
        ],
        compiler_params=params(56),
        cost_estimate=cost(5),
        name="merge_experts",
    )(rep_index, merge_map, merge_coef, source_w)


def hbm_spec():
    return pl.BlockSpec(memory_space=pltpu.HBM)


def hold(arrays, *after):
    count = len(arrays)
    return pl.pallas_call(
        lambda *refs: None,
        in_specs=[hbm_spec()] * count + [any_spec()] * len(after),
        out_specs=[hbm_spec()] * count,
        out_shape=[jax.ShapeDtypeStruct(a.shape, a.dtype) for a in arrays],
        input_output_aliases={i: i for i in range(count)},
        cost_estimate=cost(0),
        name="hold",
    )(*arrays, *after)


def column(row):
    size = row.shape[1]
    same = lax.broadcasted_iota(I32, (size, size), 0) == lax.broadcasted_iota(I32, (size, size), 1)
    return jnp.sum(jnp.where(same, row, jnp.zeros_like(row)), axis=1, keepdims=True)


def to_row(col):
    size = col.shape[0]
    same = lax.broadcasted_iota(I32, (size, size), 0) == lax.broadcasted_iota(I32, (size, size), 1)
    return jnp.sum(jnp.where(same, col, jnp.zeros_like(col)), axis=0, keepdims=True)


def picks_of(idx_ref, k, sources):
    tok = idx_ref.shape[1]
    return lax.broadcasted_iota(I32, (sources, tok), 0) == idx_ref[k : k + 1, :]


def route_kernel(
    capacity, lanes,
    xt_ref, rwt_ref, rb_ref, idx_ref, map_ref, hid_ref, og_ref, _,
    sh_ref, sg_ref, gate_ref, pos_ref, slot_ref,
):
    top, tok = idx_ref.shape
    sources = rwt_ref.shape[0]
    slots, width = hid_ref.shape
    places = lanes * capacity
    logits = jnp.dot(rwt_ref[...], xt_ref[...], preferred_element_type=F32) + column(rb_ref[...])
    raised, merged = [], []
    combos = column(map_ref[...])
    for k in range(top):
        pick = picks_of(idx_ref, k, sources)
        chosen = jnp.sum(jnp.where(pick, logits, 0.0), axis=0, keepdims=True)
        raised.append(jnp.exp(chosen))
        merged.append(jnp.sum(jnp.where(pick, combos, 0), axis=0, keepdims=True))
    total = raised[0]
    for k in range(1, top):
        total = total + raised[k]
    gates = [r / total for r in raised]
    lane = [jnp.right_shift(g, 1) for g in merged]
    member = [jnp.bitwise_and(g, 1) for g in merged]
    onehot = [(lax.broadcasted_iota(I32, (lanes, tok), 0) == l).astype(F32) for l in lane]
    all_hot = onehot[0]
    for k in range(1, top):
        all_hot = all_hot + onehot[k]
    earlier = (
        lax.broadcasted_iota(I32, (tok, tok), 0) < lax.broadcasted_iota(I32, (tok, tok), 1)
    ).astype(BF)
    before = jnp.dot(all_hot.astype(BF), earlier, preferred_element_type=F32)
    position = []
    for k in range(top):
        rank = jnp.sum(before * onehot[k], axis=0, keepdims=True).astype(I32)
        before = before + onehot[k]
        position.append(jnp.where(rank < capacity, lane[k] * capacity + rank, -1))
    gate_ref[...] = jnp.zeros_like(gate_ref)
    pos_ref[...] = jnp.full_like(pos_ref, -1)
    for k in range(top):
        gate_ref[k : k + 1, :] = gates[k]
        pos_ref[k : k + 1, :] = position[k]
    spot = jnp.zeros((8, slots), F32)
    for k in range(top):
        spread = (
            lax.broadcasted_iota(I32, (tok, slots), 1)
            == lax.broadcasted_iota(I32, (tok, slots), 0) * top + k
        ).astype(BF)
        kept = position[k] >= 0
        parts = [
            jnp.where(kept, jnp.right_shift(position[k], 5), 0),
            jnp.where(kept, jnp.bitwise_and(position[k], 31), 0),
            jnp.where(kept, 1, 0),
            member[k],
        ]
        stacked = jnp.concatenate(
            [p.astype(F32) for p in parts] + [jnp.zeros((4, tok), F32)], axis=0
        ).astype(BF)
        spot = spot + jnp.dot(stacked, spread, preferred_element_type=F32)
    spot = spot.astype(I32)
    slot_pos = jnp.where(spot[2:3] > 0, spot[0:1] * 32 + spot[1:2], -1)
    slot_ref[...] = jnp.broadcast_to(slot_pos, slot_ref.shape)
    take = lax.broadcasted_iota(I32, (places, slots), 0) == slot_pos
    placed = jnp.sum(jnp.where(take, spot[3:4].astype(F32), 0.0), axis=1, keepdims=True)
    sh_ref[:, width:] = jnp.broadcast_to(placed, (places, 128)).astype(BF)
    take = take.astype(BF)
    for n in range(0, width, TILE):
        rows = jnp.dot(take, hid_ref[:, n : n + TILE], preferred_element_type=F32)
        sh_ref[:, n : n + TILE] = rows.astype(BF)
    takes = [
        (lax.broadcasted_iota(I32, (places, tok), 0) == position[k]).astype(BF) for k in range(top)
    ]
    columns = [column(g) for g in gates]
    for n in range(0, og_ref.shape[1], TILE):
        og = og_ref[:, n : n + TILE].astype(F32)
        rows = jnp.zeros((places, TILE), F32)
        for k in range(top):
            rows = rows + jnp.dot(takes[k], (columns[k] * og).astype(BF), preferred_element_type=F32)
        sg_ref[:, n : n + TILE] = rows.astype(BF)


def route(xt, rwt, router_b, idx_t, merge_map, hid, og, after, capacity, lanes):
    slots, width = hid.shape
    tok = idx_t.shape[1]
    return pl.pallas_call(
        functools.partial(route_kernel, capacity, lanes),
        in_specs=[vmem_spec()] * 7 + [any_spec()],
        out_specs=[vmem_spec()] * 5,
        out_shape=[
            jax.ShapeDtypeStruct((lanes * capacity, width + 128), BF),
            jax.ShapeDtypeStruct((lanes * capacity, og.shape[1]), BF),
            jax.ShapeDtypeStruct((8, tok), F32),
            jax.ShapeDtypeStruct((8, tok), I32),
            jax.ShapeDtypeStruct((8, slots), I32),
        ],
        compiler_params=params(56),
        cost_estimate=cost(5),
        name="route",
    )(xt, rwt, router_b[None, :], idx_t, merge_map[None, :], hid, og, after)


def load_weights(rep_ref, pieces, w_ref, sems):
    copies = []
    for i, piece in enumerate(pieces):
        blocks, _, rows, cols = piece.shape
        owner = jnp.bitwise_xor(rep_ref[0], i)
        at = pl.ds(pl.multiple_of(owner * cols, cols), cols)
        for c in range(blocks):
            to = w_ref.at[:, pl.ds(c * rows, rows), at]
            copies.append(pltpu.make_async_copy(piece.at[c], to, sems.at[len(copies)]))
    for copy in copies:
        copy.start()
    for copy in copies:
        copy.wait()


def forward_kernel(rep_ref, rows_ref, flag_ref, *refs):
    out_ref, w_ref, sems = refs[-3:]
    load_weights(rep_ref, refs[:-3], w_ref, sems)
    member = flag_ref[:, :1].astype(F32)
    for n in range(0, w_ref.shape[1], TILE):
        at = slice(n, n + TILE)
        both = [dot(rows_ref[...], w_ref[m, at, :], ((1,), (1,))) for m in range(2)]
        out_ref[:, at] = jnp.where(member == 0.0, both[0], both[1]).astype(BF)


def backward_kernel(rep_ref, rows_ref, flag_ref, *refs):
    out_ref, w_ref, sems = refs[-3:]
    load_weights(rep_ref, refs[:-3], w_ref, sems)
    member = flag_ref[:, :1].astype(F32)
    for n in range(0, w_ref.shape[2], TILE):
        at = slice(n, n + TILE)
        both = [dot(rows_ref[...], w_ref[m, :, at], ((1,), (0,))) for m in range(2)]
        out_ref[:, at] = jnp.where(member == 0.0, both[0], both[1]).astype(BF)


def run_lane(kernel, rep_index, rows, hid, pieces, name):
    blocks, members, share, cols = pieces[0].shape
    depth, width = share * blocks, cols * len(pieces)
    count = rows.shape[0]
    return pl.pallas_call(
        kernel,
        grid=(1,),
        in_specs=[
            smem_spec(),
            pl.BlockSpec((count, width), lambda i: (0, 0)),
            pl.BlockSpec((count, 128), lambda i: (0, width // 128)),
        ]
        + [any_spec()] * len(pieces),
        out_specs=pl.BlockSpec((count, width), lambda i: (0, 0)),
        out_shape=jax.ShapeDtypeStruct((count, width), BF),
        scratch_shapes=[
            pltpu.VMEM((members, depth, width), BF),
            pltpu.SemaphoreType.DMA((blocks * len(pieces),)),
        ],
        compiler_params=params(56),
        cost_estimate=cost(12),
        name=name,
    )(rep_index, rows, hid, *pieces)


def lane_grad_kernel(has_other, _, grd_ref, hid_ref, flag_ref, *refs):
    out_ref = refs[-1]
    chosen = flag_ref[:, :1].astype(F32) == pl.program_id(0).astype(F32)
    hid = jnp.where(chosen, hid_ref[...], jnp.zeros_like(hid_ref))
    blocks, _, rows, cols = out_ref.shape
    each = 2 if blocks % 2 == 0 and 2 * rows % 128 == 0 else blocks
    for n in range(0, blocks, each):
        part = dot(grd_ref[:, n * rows : (n + each) * rows], hid, ((0,), (0,)))
        part = part.reshape(each, rows, cols)
        if has_other:
            part = part + refs[0][n : n + each, 0].astype(F32)
        out_ref[n : n + each, 0] = part.astype(BF)


def lane_grads(owner, grd, hid, other, blocks, reps):
    count, depth = grd.shape
    width = hid.shape[1] - 128
    cols = width // reps
    shape = (blocks, 2, depth // blocks, cols)
    block = pl.BlockSpec((blocks, 1, depth // blocks, cols), lambda m, s: (0, m, 0, 0))
    extra = [] if other is None else [other]
    return pl.pallas_call(
        functools.partial(lane_grad_kernel, other is not None),
        grid_spec=pltpu.PrefetchScalarGridSpec(
            num_scalar_prefetch=1,
            grid=(2,),
            in_specs=[
                pl.BlockSpec((count, depth), lambda m, s: (0, 0)),
                pl.BlockSpec((count, cols), lambda m, s: (0, s[0])),
                pl.BlockSpec((count, 128), lambda m, s: (0, width // 128)),
            ]
            + [block] * len(extra),
            out_specs=block,
        ),
        out_shape=jax.ShapeDtypeStruct(shape, BF),
        compiler_params=params(56),
        cost_estimate=cost(6),
        name="lane_grads_add" if extra else "lane_grads_first",
    )(owner, grd, hid, hid, *extra)


def combine_kernel(
    og_ref, gate_ref, pos_ref, idx_ref, rwt_ref, xt_ref, out_ref, mixed_ref, tg_ref, part_ref
):
    places, width = out_ref.shape
    top, tok = idx_ref.shape
    sources, features = rwt_ref.shape
    takes = [
        (lax.broadcasted_iota(I32, (places, tok), 0) == pos_ref[k : k + 1, :]).astype(BF)
        for k in range(top)
    ]
    gates = [gate_ref[k : k + 1, :] for k in range(top)]
    columns = [column(g) for g in gates]
    scores = [jnp.zeros((tok, 1), F32) for _ in range(top)]
    for n in range(0, width, TILE):
        og = og_ref[:, n : n + TILE].astype(F32)
        rows = out_ref[:, n : n + TILE]
        mixed = jnp.zeros((tok, TILE), F32)
        for k in range(top):
            slot_out = dot(takes[k], rows, ((0,), (0,)))
            mixed = mixed + columns[k] * slot_out
            scores[k] = scores[k] + jnp.sum(og * slot_out, axis=1, keepdims=True)
        mixed_ref[:, n : n + TILE] = mixed.astype(BF)
    scores = [to_row(s) for s in scores]
    middle = gates[0] * scores[0]
    for k in range(1, top):
        middle = middle + gates[k] * scores[k]
    logit_grad = jnp.zeros((sources, tok), F32)
    for k in range(top):
        chosen_grad = gates[k] * (scores[k] - middle)
        logit_grad = logit_grad + jnp.where(picks_of(idx_ref, k, sources), chosen_grad, 0.0)
    logit_half = logit_grad.astype(BF)
    tg_ref[...] = dot(rwt_ref[...], logit_half, ((0,), (0,))).astype(BF)
    part_ref[...] = jnp.zeros_like(part_ref)
    part_ref[:, :features] = dot(logit_half, xt_ref[...], ((1,), (1,)))
    bias = jnp.sum(logit_grad, axis=1, keepdims=True)
    last = part_ref.shape[1] - 128
    part_ref[:, last:] = jnp.broadcast_to(bias, (sources, 128))


def combine(home_out, og, gates, pos, idx_t, rwt, xt):
    sources, features = rwt.shape
    tok = idx_t.shape[1]
    return pl.pallas_call(
        combine_kernel,
        in_specs=[vmem_spec()] * 7,
        out_specs=[vmem_spec()] * 3,
        out_shape=[
            jax.ShapeDtypeStruct(og.shape, BF),
            jax.ShapeDtypeStruct((features, tok), BF),
            jax.ShapeDtypeStruct((sources, (features + 127) // 128 * 128 + 128), F32),
        ],
        compiler_params=params(56),
        cost_estimate=cost(5),
        name="combine",
    )(og, gates, pos, idx_t, rwt, xt, home_out)


def unplace_kernel(slot_ref, back_ref, out_ref):
    places, width = back_ref.shape
    slots = slot_ref.shape[1]
    take = (lax.broadcasted_iota(I32, (places, slots), 0) == slot_ref[0:1, :]).astype(BF)
    for n in range(0, width, TILE):
        out_ref[:, n : n + TILE] = dot(take, back_ref[:, n : n + TILE], ((0,), (0,))).astype(BF)


def unplace(home_back, slot_pos):
    return pl.pallas_call(
        unplace_kernel,
        in_specs=[vmem_spec()] * 2,
        out_specs=vmem_spec(),
        out_shape=jax.ShapeDtypeStruct((slot_pos.shape[1], home_back.shape[1]), BF),
        compiler_params=params(56),
        cost_estimate=cost(5),
        name="unplace",
    )(slot_pos, home_back)


def coef_kernel(
    rep_ref, map_ref, row_ref, src_ref, got_ref, out_ref, order_ref, count_ref, held, weights, sems
):
    count, rows, cols = weights.shape
    at = pl.ds(pl.multiple_of(rep_ref[0] * cols, cols), cols)
    copies = [
        pltpu.make_async_copy(src_ref.at[:, :, at], weights, sems.at[0]),
        pltpu.make_async_copy(got_ref, held, sems.at[1]),
    ]
    for copy in copies:
        copy.start()
    expert_order(map_ref, order_ref, count_ref)
    for copy in copies:
        copy.wait()
    lane = lax.broadcasted_iota(I32, (8, 128), 1)

    def one(g, total):
        merged = held[g].astype(F32)
        for n in range(2):
            expert = order_ref[2 * g + n]
            product = merged * weights[expert].astype(F32)
            folded = jnp.sum(product.reshape(rows // 8, 8, cols), axis=0)
            small = folded[:, :128]
            for c in range(128, cols, 128):
                small = small + folded[:, c : c + 128]
            small = jnp.sum(jnp.sum(small, axis=0, keepdims=True), axis=1, keepdims=True)
            total = total + jnp.where(lane == expert, small, 0.0)
        return total

    total = lax.fori_loop(0, count // 2, one, jnp.zeros((8, 128), F32))[:1]
    end = row_ref.shape[1]
    for n in range(out_ref.shape[0]):
        out_ref[n, :, :end] = row_ref[...]
        out_ref[n, :, end:] = total


def finish_kernel(
    scale, map_ref, coef_ref, _, got_ref, out_ref, order_ref, count_ref, held, ready, sems, more
):
    count = ready.shape[0]

    def load(g):
        return pltpu.make_async_copy(got_ref.at[g], held.at[g], sems.at[g])

    def send(i):
        return pltpu.make_async_copy(ready.at[i], out_ref.at[order_ref[i]], more.at[i])

    @pl.loop(0, count // 2)
    def _(g):
        load(g).start()

    expert_order(map_ref, order_ref, count_ref)

    @pl.loop(0, count // 2)
    def _(g):
        load(g).wait()
        merged = held[g].astype(F32)
        for n in range(2):
            i = 2 * g + n
            ready[i] = merged * (coef_ref[order_ref[i]] * scale)
            send(i).start()

    @pl.loop(0, count)
    def _(i):
        send(i).wait()


def coef_dots(rep_index, merge_map, row, source_w, arrived, devices):
    count = source_w.shape[0]
    _, rows, cols = arrived.shape
    return pl.pallas_call(
        coef_kernel,
        in_specs=[smem_spec(), smem_spec(), vmem_spec(), hbm_spec(), any_spec()],
        out_specs=vmem_spec(),
        out_shape=jax.ShapeDtypeStruct((devices, 1, row.shape[1] + 128), F32),
        scratch_shapes=[
            pltpu.SMEM((count,), I32),
            pltpu.SMEM((count // 2,), I32),
            pltpu.VMEM(arrived.shape, BF),
            pltpu.VMEM((count, rows, cols), BF),
            pltpu.SemaphoreType.DMA((2,)),
        ],
        compiler_params=params(56),
        cost_estimate=cost(5),
        name="coef_dots",
    )(rep_index, merge_map, row, source_w, arrived)


def finish(merge_map, merge_coef, arrived, after, scale):
    count = merge_map.shape[0]
    _, rows, cols = arrived.shape
    return pl.pallas_call(
        functools.partial(finish_kernel, scale),
        in_specs=[smem_spec(), smem_spec(), any_spec(), any_spec()],
        out_specs=hbm_spec(),
        out_shape=jax.ShapeDtypeStruct((count, rows, cols), F32),
        scratch_shapes=[
            pltpu.SMEM((count,), I32),
            pltpu.SMEM((count // 2,), I32),
            pltpu.VMEM(arrived.shape, BF),
            pltpu.VMEM((count, rows, cols), F32),
            pltpu.SemaphoreType.DMA((count // 2,)),
            pltpu.SemaphoreType.DMA((count,)),
        ],
        compiler_params=params(56),
        cost_estimate=cost(5),
        name="finish",
    )(merge_map, merge_coef, after, arrived)


def add_up(x, bits):
    for axis, distance, bit in bits:
        x = x.reshape((2, x.shape[0] // 2) + x.shape[1:])
        keep = lax.dynamic_index_in_dim(x, bit, 0, keepdims=False)
        give = lax.dynamic_index_in_dim(x, 1 - bit, 0, keepdims=False)
        size = lax.axis_size(axis)
        x = keep + lax.ppermute(give, axis, [(i, i ^ distance) for i in range(size)])
    return x


def on_pairs(
    tokens, router_w, router_b, hidden, teacher_idx, merge_map, merge_coef, source_w, out_grad
):
    blocks = lax.axis_size("ctx")
    reps = lax.axis_size("row") * lax.axis_size("core")
    devices = blocks * reps
    tok = tokens.shape[1]
    features = tokens.shape[2]
    top = teacher_idx.shape[2]
    width = hidden.shape[3]
    depth = out_grad.shape[2]
    sources = router_w.shape[1]
    row_share = source_w.shape[1]
    lanes = blocks
    capacity = 5 * tok * top // (4 * blocks)
    scale = 1.0 / math.sqrt(tok * devices)
    ctx_i, row_i, core_i = lax.axis_index("ctx"), lax.axis_index("row"), lax.axis_index("core")
    rep_i = 2 * row_i + core_i

    def one(number):
        return jnp.asarray(number, I32)[None]

    def swap(x, axis):
        return lax.ppermute(x, axis, [(0, 1), (1, 0)])

    def trade(x):
        return lax.all_to_all(x, "ctx", split_axis=0, concat_axis=0, tiled=True)

    def trade_rows(rows):
        return trade(rows.reshape(lanes, capacity, rows.shape[1])).reshape(rows.shape)

    def later(*x):
        return swap(hold([jnp.zeros((8, 128), F32)], *x)[0], "core")

    combos = merge_experts(one(rep_i), merge_map, merge_coef, source_w, reps)
    mine = trade(combos.reshape((lanes, 2) + combos.shape[1:]))

    xt = tokens.reshape(tok, features).T
    rwt = router_w.T
    idx_t = teacher_idx.reshape(tok, top).T
    og = out_grad.reshape(tok, depth)
    send_hid, send_grd, gates, pos, slot_pos = route(
        xt, rwt, router_b, idx_t, merge_map, hidden.reshape(tok * top, width), og,
        combos, capacity, lanes,
    )
    (send_hid,) = hold([send_hid], mine)
    hid = trade_rows(send_hid)
    far = swap(mine, "row")
    (send_grd,) = hold([send_grd], hid)
    grd = trade_rows(send_grd)
    (far,) = hold([far], later(hid))
    pieces = [mine, swap(mine, "core"), far, swap(far, "core")]
    out_rows = run_lane(forward_kernel, one(rep_i), hid, hid, pieces, "lane_forward")
    grd, out_rows = hold([grd, out_rows])
    home_out = trade_rows(out_rows)
    (grd,) = hold([grd], later(out_rows))

    def summed(row):
        first = lane_grads(one(2 * row + 1 - core_i), grd, hid, None, blocks, reps)
        return lane_grads(one(2 * row + core_i), grd, hid, swap(first, "core"), blocks, reps)

    distant, near = summed(1 - row_i), summed(row_i)
    away = swap(distant, "row")
    (last_grd,) = hold([grd], later(distant, near))
    back_rows = run_lane(backward_kernel, one(rep_i), last_grd, hid, pieces, "lane_backward")
    (away,) = hold([away], later(back_rows))
    home_back = trade_rows(back_rows)

    mixed, token_grad, part = combine(home_out, og, gates, pos, idx_t, rwt, xt)
    total = (near.astype(F32) + away.astype(F32)).astype(BF)
    (part,) = hold([part], total)
    part = part.reshape(blocks, 2, 2, part.shape[1]).transpose(2, 1, 0, 3).reshape(part.shape)
    part = add_up(
        part,
        [
            ("core", 1, core_i),
            ("row", 1, row_i),
            ("ctx", 4, ctx_i // 4),
            ("ctx", 2, ctx_i // 2 % 2),
            ("ctx", 1, ctx_i % 2),
        ],
    )
    (total,) = hold([total], home_back)
    arrived = trade(total).reshape(2 * lanes, row_share, width // reps)
    hidden_grad = unplace(home_back, slot_pos)
    (arrived,) = hold([arrived], hidden_grad, part)
    dots = coef_dots(one(rep_i), merge_map, part, source_w, arrived, devices)
    news = lax.all_to_all(
        dots, ("ctx", "row", "core"), split_axis=0, concat_axis=0, tiled=True
    )
    source_w_grad = finish(merge_map, merge_coef, arrived, dots, scale)
    end = part.shape[1]
    return (
        mixed.reshape(1, tok, depth),
        hidden_grad.reshape(1, tok, top, width),
        token_grad.T.reshape(1, tok, features),
        news[:, 0, :features].T * scale,
        news[:, 0, end - 1] * scale,
        jnp.sum(news[:, 0, end : end + sources], axis=0) * scale,
        source_w_grad,
    )


def solution(mesh):
    if mesh.shape["ctx"] == 8 and mesh.shape["rep"] == 4:
        mesh = jax.sharding.Mesh(mesh.devices.reshape(8, 2, 2), ("ctx", "row", "core"))
        ctx, rep, body = "ctx", ("row", "core"), on_pairs
    else:
        ctx, rep, body = "ctx", "rep", on_device
    in_specs = (
        P(rep, ctx, None),
        P(),
        P(),
        P(rep, ctx, None, None),
        P(rep, ctx, None),
        P(),
        P(),
        P(None, ctx, None),
        P(rep, ctx, None),
    )
    out_specs = (
        P(rep, ctx, None),
        P(rep, ctx, None, None),
        P(rep, ctx, None),
        P(),
        P(),
        P(),
        P(None, ctx, rep),
    )
    return jax.shard_map(
        body, mesh=mesh, in_specs=in_specs, out_specs=out_specs, check_vma=False
    )
```

```python
import functools
import math

import jax
import jax.numpy as jnp
from jax import lax
from jax.experimental import pallas as pl
from jax.experimental.pallas import tpu as pltpu
from jax.sharding import PartitionSpec as P

MERGED = 16


def expert_rows(rows_hidden, rows_grad, rows_member, lane_weights):
    row_count = rows_hidden.shape[0]
    out_rows = jnp.zeros((row_count, lane_weights.shape[1]), jnp.float32)
    back_rows = jnp.zeros((row_count, lane_weights.shape[2]), jnp.float32)
    grad_list = []
    for member_now in range(lane_weights.shape[0]):
        weight = lane_weights[member_now]
        selected = (rows_member == member_now)[:, None]
        forward = lax.dot_general(
            rows_hidden, weight, (((1,), (1,)), ((), ())), preferred_element_type=jnp.float32
        )
        out_rows = jnp.where(selected, forward, out_rows)
        backward = jnp.dot(rows_grad, weight, preferred_element_type=jnp.float32)
        back_rows = jnp.where(selected, backward, back_rows)
        masked = jnp.where(selected, rows_grad, jnp.zeros_like(rows_grad))
        grad_list.append(
            lax.dot_general(
                masked, rows_hidden, (((0,), (0,)), ((), ())), preferred_element_type=jnp.float32
            )
        )
    return (out_rows, back_rows, jnp.stack(grad_list))


def on_device(
    tokens, router_w, router_b, hidden, teacher_idx, merge_map, merge_coef, source_w, out_grad
):
    ctx_count = lax.axis_size("ctx")
    rep_count = lax.axis_size("rep")
    tok_count = tokens.shape[1]
    feature_count = tokens.shape[2]
    top_count = teacher_idx.shape[2]
    hidden_width = hidden.shape[3]
    out_width = out_grad.shape[2]
    source_count = router_w.shape[1]
    row_share = source_w.shape[1]
    per_lane = max(1, MERGED // ctx_count)
    copies = max(1, ctx_count // MERGED)
    capacity = 5 * tok_count * top_count // (4 * ctx_count)
    slot_count = tok_count * top_count
    grad_scale = 1.0 / math.sqrt(tok_count * ctx_count * rep_count)
    flat_x = tokens.reshape(tok_count, feature_count)
    logits = jnp.dot(flat_x, router_w, preferred_element_type=jnp.float32) + router_b
    choice_ids = teacher_idx.reshape(tok_count, top_count)
    pick_table = choice_ids[:, :, None] == jnp.arange(source_count, dtype=jnp.int32)[None, None, :]
    pick_float = pick_table.astype(jnp.float32)
    chosen = jnp.sum(pick_float * logits[:, None, :], axis=2)
    raised = jnp.exp(chosen)
    gate_probs = raised / jnp.sum(raised, axis=1, keepdims=True)
    merged_id = jnp.sum(jnp.where(pick_table, merge_map[None, None, :], 0), axis=2)
    position = lax.axis_index("ctx") * tok_count + jnp.arange(tok_count, dtype=jnp.int32)
    lane_id = merged_id // per_lane * copies + (position % copies)[:, None]
    member_id = (merged_id % per_lane).reshape(-1)
    lane_flat = lane_id.reshape(-1)
    onehot = (lane_flat[:, None] == jnp.arange(ctx_count, dtype=jnp.int32)[None, :]).astype(
        jnp.int32
    )
    before = jnp.cumsum(onehot, axis=0) - onehot
    slot_rank = jnp.sum(before * onehot, axis=1)
    is_kept = slot_rank < capacity
    slot_index = jnp.where(is_kept, lane_flat * capacity + slot_rank, ctx_count * capacity)
    slot_source = (
        jnp.full((ctx_count * capacity + 1,), slot_count, jnp.int32)
        .at[slot_index]
        .set(jnp.arange(slot_count, dtype=jnp.int32))[: ctx_count * capacity]
    )
    slot_grad = (gate_probs[:, :, None] * out_grad.reshape(tok_count, 1, out_width)).astype(
        jnp.bfloat16
    )
    pad_hidden = jnp.concatenate(
        [hidden.reshape(slot_count, hidden_width), jnp.zeros((1, hidden_width), jnp.bfloat16)],
        axis=0,
    )
    pad_grad = jnp.concatenate(
        [slot_grad.reshape(slot_count, out_width), jnp.zeros((1, out_width), jnp.bfloat16)], axis=0
    )
    pad_member = jnp.concatenate([member_id, jnp.zeros((1,), jnp.int32)], axis=0)
    send_hidden = pad_hidden[slot_source].reshape(ctx_count, capacity, hidden_width)
    send_grad = pad_grad[slot_source].reshape(ctx_count, capacity, out_width)
    send_member = pad_member[slot_source].reshape(ctx_count, capacity)
    lane_group = lax.axis_index("ctx") // copies
    same_group = merge_map[:, None] == merge_map[None, :]
    earlier = jnp.arange(source_count)[:, None] > jnp.arange(source_count)[None, :]
    member_rank = jnp.sum((same_group & earlier).astype(jnp.int32), axis=1)
    source_order = (
        jnp.zeros((source_count,), jnp.int32)
        .at[2 * merge_map + member_rank]
        .set(jnp.arange(source_count, dtype=jnp.int32))
    )
    picked = source_w[source_order].reshape(
        MERGED // per_lane, 2 * per_lane, row_share, hidden_width
    )
    outgoing = jnp.repeat(picked, copies, axis=0)
    arrived = lax.all_to_all(outgoing, "ctx", split_axis=0, concat_axis=2, tiled=True)
    pair_rows = arrived.reshape(per_lane, 2, row_share * ctx_count, hidden_width)
    coef_table = merge_coef[source_order].reshape(MERGED // per_lane, per_lane, 2)
    pair_coef = lax.dynamic_index_in_dim(coef_table, lane_group, 0, keepdims=False)
    lane_weights = (
        pair_coef[:, 0, None, None] * pair_rows[:, 0].astype(jnp.float32)
        + pair_coef[:, 1, None, None] * pair_rows[:, 1].astype(jnp.float32)
    ).astype(jnp.bfloat16)
    recv_hidden, recv_grad, recv_member = (
        lax.all_to_all(send_hidden, "ctx", split_axis=0, concat_axis=0, tiled=True),
        lax.all_to_all(send_grad, "ctx", split_axis=0, concat_axis=0, tiled=True),
        lax.all_to_all(send_member, "ctx", split_axis=0, concat_axis=0, tiled=True),
    )
    out_rows, back_rows, lane_grads = expert_rows(
        recv_hidden.reshape(-1, hidden_width),
        recv_grad.reshape(-1, out_width),
        recv_member.reshape(-1),
        lane_weights,
    )
    home_out, home_back = (
        lax.all_to_all(
            out_rows.astype(jnp.bfloat16).reshape(ctx_count, capacity, out_width),
            "ctx",
            split_axis=0,
            concat_axis=0,
            tiled=True,
        ),
        lax.all_to_all(
            back_rows.astype(jnp.bfloat16).reshape(ctx_count, capacity, hidden_width),
            "ctx",
            split_axis=0,
            concat_axis=0,
            tiled=True,
        ),
    )
    slot_out = jnp.concatenate(
        [home_out.reshape(-1, out_width), jnp.zeros((1, out_width), jnp.bfloat16)], axis=0
    )[slot_index].reshape(tok_count, top_count, out_width)
    hidden_grad = jnp.concatenate(
        [home_back.reshape(-1, hidden_width), jnp.zeros((1, hidden_width), jnp.bfloat16)], axis=0
    )[slot_index].reshape(1, tok_count, top_count, hidden_width)
    mixed = (
        jnp.sum(gate_probs[:, :, None] * slot_out.astype(jnp.float32), axis=1)
        .astype(jnp.bfloat16)
        .reshape(1, tok_count, out_width)
    )
    score_grad = jnp.einsum(
        "td,tkd->tk",
        out_grad.reshape(tok_count, out_width),
        slot_out,
        preferred_element_type=jnp.float32,
    )
    chosen_grad = gate_probs * (
        score_grad - jnp.sum(gate_probs * score_grad, axis=1, keepdims=True)
    )
    logit_grad = jnp.sum(pick_float * chosen_grad[:, :, None], axis=1)
    logit_half = logit_grad.astype(jnp.bfloat16)
    token_grad = (
        lax.dot_general(
            logit_half, router_w, (((1,), (1,)), ((), ())), preferred_element_type=jnp.float32
        )
        .astype(jnp.bfloat16)
        .reshape(1, tok_count, feature_count)
    )
    part_router_w = lax.dot_general(
        flat_x, logit_half, (((0,), (0,)), ((), ())), preferred_element_type=jnp.float32
    )
    part_router_b = jnp.sum(logit_grad, axis=0)
    arrived_grads = lax.all_to_all(
        lane_grads.reshape(per_lane, ctx_count, row_share, hidden_width),
        "ctx",
        split_axis=1,
        concat_axis=0,
        tiled=True,
    )
    merged_grad = (
        arrived_grads.reshape(MERGED // per_lane, copies, per_lane, row_share, hidden_width)
        .sum(axis=1)
        .reshape(MERGED, row_share, hidden_width)
    )
    source_grad = merged_grad[merge_map]
    coef_part = jnp.einsum(
        "edf,edf->e", source_grad, source_w.astype(jnp.float32), precision=lax.Precision.HIGHEST
    )
    summed = lax.psum_scatter(
        source_grad * merge_coef[:, None, None], "rep", scatter_dimension=2, tiled=True
    )
    source_w_grad = summed * grad_scale
    router_sum, bias_sum, coef_sum = lax.psum(
        (part_router_w, part_router_b, coef_part), ("ctx", "rep")
    )
    return (
        mixed,
        hidden_grad,
        token_grad,
        router_sum * grad_scale,
        bias_sum * grad_scale,
        coef_sum * grad_scale,
        source_w_grad,
    )


BF = jnp.bfloat16
F32 = jnp.float32
I32 = jnp.int32
TILE = 256


def cost(us):
    return pl.CostEstimate(flops=us * 10**9, bytes_accessed=us * 10**6, transcendentals=0)


def any_spec():
    return pl.BlockSpec(memory_space=pl.ANY)


def smem_spec():
    return pl.BlockSpec(memory_space=pltpu.SMEM)


def vmem_spec():
    return pl.BlockSpec(memory_space=pltpu.VMEM)


def params(mib):
    return pltpu.CompilerParams(vmem_limit_bytes=mib * 1024 * 1024)


def dot(a, b, dims):
    return lax.dot_general(a, b, (dims, ((), ())), preferred_element_type=F32)


def merge_start(map_ref, place_ref, src_ref, places, order_ref, count_ref, held, sems):
    half = held.shape[2]
    expert_order(map_ref, order_ref, count_ref)
    at = pl.ds(pl.multiple_of(place_ref[1] * half, half), half)
    copies, experts = [], []
    for j in range(places):
        for m in range(2):
            combo = 4 * j + 2 * place_ref[0] + m
            for n in range(2):
                expert = order_ref[2 * combo + n]
                experts.append(expert)
                i = len(copies)
                copies.append(
                    pltpu.make_async_copy(src_ref.at[expert, :, at], held.at[i], sems.at[i])
                )
                copies[-1].start()
    return copies, experts


def merge_finish(copies, experts, coef_ref, held, out_ref):
    halves, places = out_ref.shape[:2]
    for j in range(places):
        for m in range(2):
            i = 4 * j + 2 * m
            copies[i].wait()
            copies[i + 1].wait()
            one, two = coef_ref[experts[i]], coef_ref[experts[i + 1]]
            merged = (one * held[i].astype(F32) + two * held[i + 1].astype(F32)).astype(BF)
            for h in range(halves):
                out_ref[h, j, m] = merged


def expert_order(map_ref, order_ref, count_ref):
    @pl.loop(0, count_ref.shape[0])
    def _(g):
        count_ref[g] = 0

    @pl.loop(0, order_ref.shape[0])
    def _(e):
        g = map_ref[e]
        n = count_ref[g]
        order_ref[2 * g + n] = e
        count_ref[g] = n + 1


def hbm_spec():
    return pl.BlockSpec(memory_space=pltpu.HBM)


def hold(arrays, *after):
    count = len(arrays)
    return pl.pallas_call(
        lambda *refs: None,
        in_specs=[hbm_spec()] * count + [any_spec()] * len(after),
        out_specs=[hbm_spec()] * count,
        out_shape=[jax.ShapeDtypeStruct(a.shape, a.dtype) for a in arrays],
        input_output_aliases={i: i for i in range(count)},
        name="hold",
    )(*arrays, *after)


def column(row):
    size = row.shape[1]
    same = lax.broadcasted_iota(I32, (size, size), 0) == lax.broadcasted_iota(I32, (size, size), 1)
    return jnp.sum(jnp.where(same, row, jnp.zeros_like(row)), axis=1, keepdims=True)


def to_row(col):
    size = col.shape[0]
    same = lax.broadcasted_iota(I32, (size, size), 0) == lax.broadcasted_iota(I32, (size, size), 1)
    return jnp.sum(jnp.where(same, col, jnp.zeros_like(col)), axis=0, keepdims=True)


def picks_of(idx_ref, k, sources):
    tok = idx_ref.shape[1]
    return lax.broadcasted_iota(I32, (sources, tok), 0) == idx_ref[k : k + 1, :]


def prepare_kernel(
    capacity, lanes,
    combo_ref, coef_ref, place_ref, src_ref,
    xt_ref, rwt_ref, rb_ref, idx_ref, map_ref, hid_ref, og_ref,
    merged_ref, send_ref, gate_ref, pos_ref, slot_ref,
    order_ref, count_ref, held, sems,
):
    copies, experts = merge_start(
        combo_ref, place_ref, src_ref, merged_ref.shape[1], order_ref, count_ref, held, sems
    )
    top, tok = idx_ref.shape
    sources = rwt_ref.shape[0]
    slots, width = hid_ref.shape
    places = lanes * capacity
    logits = jnp.dot(rwt_ref[...], xt_ref[...], preferred_element_type=F32) + column(rb_ref[...])
    raised, merged = [], []
    combos = column(map_ref[...])
    for k in range(top):
        pick = picks_of(idx_ref, k, sources)
        chosen = jnp.sum(jnp.where(pick, logits, 0.0), axis=0, keepdims=True)
        raised.append(jnp.exp(chosen))
        merged.append(jnp.sum(jnp.where(pick, combos, 0), axis=0, keepdims=True))
    total = raised[0]
    for k in range(1, top):
        total = total + raised[k]
    gates = [r / total for r in raised]
    lane = [jnp.right_shift(g, 1) for g in merged]
    member = [jnp.bitwise_and(g, 1) for g in merged]
    onehot = [(lax.broadcasted_iota(I32, (lanes, tok), 0) == l).astype(F32) for l in lane]
    all_hot = onehot[0]
    for k in range(1, top):
        all_hot = all_hot + onehot[k]
    earlier = (
        lax.broadcasted_iota(I32, (tok, tok), 0) < lax.broadcasted_iota(I32, (tok, tok), 1)
    ).astype(BF)
    before = jnp.dot(all_hot.astype(BF), earlier, preferred_element_type=F32)
    position = []
    for k in range(top):
        rank = jnp.sum(before * onehot[k], axis=0, keepdims=True).astype(I32)
        before = before + onehot[k]
        position.append(jnp.where(rank < capacity, lane[k] * capacity + rank, -1))
    gate_ref[...] = jnp.zeros_like(gate_ref)
    pos_ref[...] = jnp.full_like(pos_ref, -1)
    for k in range(top):
        gate_ref[k : k + 1, :] = gates[k]
        pos_ref[k : k + 1, :] = position[k]
    spot = jnp.zeros((8, slots), F32)
    for k in range(top):
        spread = (
            lax.broadcasted_iota(I32, (tok, slots), 1)
            == lax.broadcasted_iota(I32, (tok, slots), 0) * top + k
        ).astype(BF)
        kept = position[k] >= 0
        parts = [
            jnp.where(kept, jnp.right_shift(position[k], 5), 0),
            jnp.where(kept, jnp.bitwise_and(position[k], 31), 0),
            jnp.where(kept, 1, 0),
            member[k],
        ]
        stacked = jnp.concatenate(
            [p.astype(F32) for p in parts] + [jnp.zeros((4, tok), F32)], axis=0
        ).astype(BF)
        spot = spot + jnp.dot(stacked, spread, preferred_element_type=F32)
    spot = spot.astype(I32)
    slot_pos = jnp.where(spot[2:3] > 0, spot[0:1] * 32 + spot[1:2], -1)
    slot_ref[...] = jnp.broadcast_to(slot_pos, slot_ref.shape)
    take = lax.broadcasted_iota(I32, (places, slots), 0) == slot_pos
    placed = jnp.sum(jnp.where(take, spot[3:4].astype(F32), 0.0), axis=1, keepdims=True)
    depth = og_ref.shape[1]
    send_ref[:, depth + width :] = jnp.broadcast_to(placed, (places, 128)).astype(BF)
    take = take.astype(BF)
    for n in range(0, width, TILE):
        rows = jnp.dot(take, hid_ref[:, n : n + TILE], preferred_element_type=F32)
        send_ref[:, depth + n : depth + n + TILE] = rows.astype(BF)
    takes = [
        (lax.broadcasted_iota(I32, (places, tok), 0) == position[k]).astype(BF) for k in range(top)
    ]
    columns = [column(g) for g in gates]
    for n in range(0, depth, TILE):
        og = og_ref[:, n : n + TILE].astype(F32)
        rows = jnp.zeros((places, TILE), F32)
        for k in range(top):
            rows = rows + jnp.dot(takes[k], (columns[k] * og).astype(BF), preferred_element_type=F32)
        send_ref[:, n : n + TILE] = rows.astype(BF)
    merge_finish(copies, experts, coef_ref, held, merged_ref)


def prepare(
    place, merge_map, merge_coef, source_w, xt, rwt, router_b, idx_t, hid, og, capacity, lanes
):
    count, rows, whole = source_w.shape
    slots, width = hid.shape
    tok = idx_t.shape[1]
    half, places = whole // 2, lanes // 2
    return pl.pallas_call(
        functools.partial(prepare_kernel, capacity, lanes),
        in_specs=[smem_spec()] * 3 + [any_spec()] + [vmem_spec()] * 7,
        out_specs=[vmem_spec()] * 5,
        out_shape=[
            jax.ShapeDtypeStruct((2, places, 2, rows, half), BF),
            jax.ShapeDtypeStruct((lanes * capacity, og.shape[1] + width + 128), BF),
            jax.ShapeDtypeStruct((8, tok), F32),
            jax.ShapeDtypeStruct((8, tok), I32),
            jax.ShapeDtypeStruct((8, slots), I32),
        ],
        scratch_shapes=[
            pltpu.SMEM((count,), I32),
            pltpu.SMEM((count // 2,), I32),
            pltpu.VMEM((4 * places, rows, half), BF),
            pltpu.SemaphoreType.DMA((4 * places,)),
        ],
        compiler_params=params(56),
        cost_estimate=cost(10),
        name="prepare",
    )(
        merge_map, merge_coef, place, source_w,
        xt, rwt, router_b[None, :], idx_t, merge_map[None, :], hid, og,
    )


def assemble_kernel(me_ref, *refs):
    parts, (out_ref, sems) = refs[:-2], refs[-2:]
    each = parts[0].shape[0]
    copies = []
    for d, part in enumerate(parts):
        at = pl.ds(pl.multiple_of(jnp.bitwise_xor(me_ref[0], d) * each, each), each)
        copies.append(pltpu.make_async_copy(part, out_ref.at[at, :], sems.at[d]))
        copies[-1].start()
    for copy in copies:
        copy.wait()


def assemble(me, parts):
    each, width = parts[0].shape
    return pl.pallas_call(
        assemble_kernel,
        in_specs=[smem_spec()] + [any_spec()] * len(parts),
        out_specs=vmem_spec(),
        out_shape=jax.ShapeDtypeStruct((each * len(parts), width), BF),
        scratch_shapes=[pltpu.SemaphoreType.DMA((len(parts),))],
        compiler_params=params(56),
        cost_estimate=cost(2),
        name="assemble",
    )(me, *parts)


def load_weights(core_ref, mine, other, w_ref, sems):
    core = core_ref[0]
    blocks, _, rows, _ = mine.shape
    copies = []
    for c in range(blocks):
        at = pl.ds(c * rows, rows)
        for n, part in enumerate((mine, other)):
            to = core if n == 0 else 1 - core
            i = 2 * c + n
            copies.append(
                pltpu.make_async_copy(part.at[c], w_ref.at[to, :, at, :], sems.at[i])
            )
    for copy in copies:
        copy.start()
    for copy in copies:
        copy.wait()


def lane_kernel(
    core_ref, me_ref, grd_ref, hid_ref, flag_ref, mine, other, *refs
):
    outs, (keep, w_ref, sems) = refs[:-3], refs[-3:]
    load_weights(core_ref, mine, other, w_ref, sems)
    half, depth = w_ref.shape[3], w_ref.shape[2]
    first = flag_ref[:, :1].astype(F32) == 0.0
    for n in range(0, depth, TILE):
        at = slice(n, n + TILE)
        both = [
            dot(hid_ref[:, :half], w_ref[0, m, at, :], ((1,), (1,)))
            + dot(hid_ref[:, half:], w_ref[1, m, at, :], ((1,), (1,)))
            for m in range(2)
        ]
        keep[:, at] = jnp.where(first, both[0], both[1]).astype(BF)
    for h in range(2):
        for n in range(0, half, TILE):
            at = slice(n, n + TILE)
            both = [dot(grd_ref[...], w_ref[h, m, :, at], ((1,), (0,))) for m in range(2)]
            to = depth + h * half + n
            keep[:, to : to + TILE] = jnp.where(first, both[0], both[1]).astype(BF)
    each = outs[0].shape[0]
    for d, out_ref in enumerate(outs):
        at = pl.ds(pl.multiple_of(jnp.bitwise_xor(me_ref[0], d) * each, each), each)
        out_ref[...] = keep[at, :]


def run_lane(core, me, rows, mine, other, lanes):
    blocks, members, share, half = mine.shape
    depth = share * blocks
    count = rows.shape[0]
    wide = (rows.shape[1] - 128) // 2
    part = (count // lanes, 2 * wide)
    return pl.pallas_call(
        lane_kernel,
        grid=(1,),
        in_specs=[
            smem_spec(),
            smem_spec(),
            pl.BlockSpec((count, wide), lambda i: (0, 0)),
            pl.BlockSpec((count, wide), lambda i: (0, 1)),
            pl.BlockSpec((count, 128), lambda i: (0, 2 * wide // 128)),
            any_spec(),
            any_spec(),
        ],
        out_specs=[pl.BlockSpec(part, lambda i: (0, 0))] * lanes,
        out_shape=[jax.ShapeDtypeStruct(part, BF)] * lanes,
        scratch_shapes=[
            pltpu.VMEM((count, 2 * wide), BF),
            pltpu.VMEM((2, members, depth, half), BF),
            pltpu.SemaphoreType.DMA((2 * blocks,)),
        ],
        compiler_params=params(60),
        cost_estimate=cost(20),
        name="lane_products",
    )(core, me, rows, rows, rows, mine, other)


def lane_grad_kernel(has_other, _, grd_ref, hid_ref, flag_ref, *refs):
    out_ref = refs[-1]
    chosen = flag_ref[:, :1].astype(F32) == pl.program_id(1).astype(F32)
    hid = jnp.where(chosen, hid_ref[...], jnp.zeros_like(hid_ref))
    blocks, _, _, rows, cols = out_ref.shape
    each = 2 if blocks % 2 == 0 and 2 * rows % 128 == 0 else blocks
    for n in range(0, blocks, each):
        part = dot(grd_ref[:, n * rows : (n + each) * rows], hid, ((0,), (0,)))
        part = part.reshape(each, rows, cols)
        if has_other:
            part = part + refs[0][n : n + each, 0, 0].astype(F32)
        out_ref[n : n + each, 0, 0] = part.astype(BF)


def lane_grads(core, rows, other, blocks, reps):
    count = rows.shape[0]
    width = (rows.shape[1] - 128) // 2
    cols = width // reps
    shape = (blocks, 2, 2, width // blocks, cols)
    block = pl.BlockSpec((blocks, 1, 1, width // blocks, cols), lambda y, m, s: (0, y, m, 0, 0))
    extra = [] if other is None else [other]
    return pl.pallas_call(
        functools.partial(lane_grad_kernel, other is not None),
        grid_spec=pltpu.PrefetchScalarGridSpec(
            num_scalar_prefetch=1,
            grid=(2, 2),
            in_specs=[
                pl.BlockSpec((count, width), lambda y, m, s: (0, 0)),
                pl.BlockSpec((count, cols), lambda y, m, s: (0, reps + 2 * y + s[0])),
                pl.BlockSpec((count, 128), lambda y, m, s: (0, 2 * width // 128)),
            ]
            + [block] * len(extra),
            out_specs=block,
        ),
        out_shape=jax.ShapeDtypeStruct(shape, BF),
        compiler_params=params(56),
        cost_estimate=cost(8),
        name="lane_grads_add" if extra else "lane_grads_first",
    )(core, rows, rows, rows, *extra)


def combine_kernel(
    og_ref, gate_ref, pos_ref, idx_ref, rwt_ref, xt_ref, out_ref, mixed_ref, tg_ref, part_ref
):
    places, width = out_ref.shape
    top, tok = idx_ref.shape
    sources, features = rwt_ref.shape
    takes = [
        (lax.broadcasted_iota(I32, (places, tok), 0) == pos_ref[k : k + 1, :]).astype(BF)
        for k in range(top)
    ]
    gates = [gate_ref[k : k + 1, :] for k in range(top)]
    columns = [column(g) for g in gates]
    scores = [jnp.zeros((tok, 1), F32) for _ in range(top)]
    for n in range(0, width, TILE):
        og = og_ref[:, n : n + TILE].astype(F32)
        rows = out_ref[:, n : n + TILE]
        mixed = jnp.zeros((tok, TILE), F32)
        for k in range(top):
            slot_out = dot(takes[k], rows, ((0,), (0,)))
            mixed = mixed + columns[k] * slot_out
            scores[k] = scores[k] + jnp.sum(og * slot_out, axis=1, keepdims=True)
        mixed_ref[:, n : n + TILE] = mixed.astype(BF)
    scores = [to_row(s) for s in scores]
    middle = gates[0] * scores[0]
    for k in range(1, top):
        middle = middle + gates[k] * scores[k]
    logit_grad = jnp.zeros((sources, tok), F32)
    for k in range(top):
        chosen_grad = gates[k] * (scores[k] - middle)
        logit_grad = logit_grad + jnp.where(picks_of(idx_ref, k, sources), chosen_grad, 0.0)
    logit_half = logit_grad.astype(BF)
    tg_ref[...] = dot(rwt_ref[...], logit_half, ((0,), (0,))).astype(BF)
    part_ref[...] = jnp.zeros_like(part_ref)
    part_ref[:, :features] = dot(logit_half, xt_ref[...], ((1,), (1,)))
    bias = jnp.sum(logit_grad, axis=1, keepdims=True)
    last = part_ref.shape[1] - 128
    part_ref[:, last:] = jnp.broadcast_to(bias, (sources, 128))


def combine(home, og, gates, pos, idx_t, rwt, xt):
    sources, features = rwt.shape
    tok, width = og.shape
    whole = lambda a: pl.BlockSpec(a.shape, lambda i: (0, 0))
    outs = [
        jax.ShapeDtypeStruct(og.shape, BF),
        jax.ShapeDtypeStruct((features, tok), BF),
        jax.ShapeDtypeStruct((sources, (features + 127) // 128 * 128 + 128), F32),
    ]
    return pl.pallas_call(
        combine_kernel,
        grid=(1,),
        in_specs=[whole(a) for a in (og, gates, pos, idx_t, rwt, xt)]
        + [pl.BlockSpec((home.shape[0], width), lambda i: (0, 0))],
        out_specs=[whole(a) for a in outs],
        out_shape=outs,
        compiler_params=params(56),
        cost_estimate=cost(5),
        name="combine",
    )(og, gates, pos, idx_t, rwt, xt, home)


def unplace_kernel(slot_ref, back_ref, out_ref):
    places, width = back_ref.shape
    slots = slot_ref.shape[1]
    take = (lax.broadcasted_iota(I32, (places, slots), 0) == slot_ref[0:1, :]).astype(BF)
    for n in range(0, width, TILE):
        out_ref[:, n : n + TILE] = dot(take, back_ref[:, n : n + TILE], ((0,), (0,))).astype(BF)


def unplace(home, slot_pos):
    places, width = home.shape[0], home.shape[1] // 2
    slots = slot_pos.shape[1]
    return pl.pallas_call(
        unplace_kernel,
        grid=(1,),
        in_specs=[
            pl.BlockSpec(slot_pos.shape, lambda i: (0, 0)),
            pl.BlockSpec((places, width), lambda i: (0, 1)),
        ],
        out_specs=pl.BlockSpec((slots, width), lambda i: (0, 0)),
        out_shape=jax.ShapeDtypeStruct((slots, width), BF),
        compiler_params=params(56),
        cost_estimate=cost(4),
        name="unplace",
    )(slot_pos, home)


def coef_kernel(rep_ref, map_ref, src_ref, got_ref, out_ref, order_ref, count_ref, held, weights, sems):
    count, rows, cols = weights.shape
    at = pl.ds(pl.multiple_of(rep_ref[0] * cols, cols), cols)
    copies = [
        pltpu.make_async_copy(src_ref.at[:, :, at], weights, sems.at[0]),
        pltpu.make_async_copy(got_ref, held, sems.at[1]),
    ]
    for copy in copies:
        copy.start()
    expert_order(map_ref, order_ref, count_ref)
    for copy in copies:
        copy.wait()
    lane = lax.broadcasted_iota(I32, (8, 128), 1)

    def one(g, total):
        merged = held[0, g].astype(F32) + held[1, g].astype(F32)
        for n in range(2):
            expert = order_ref[2 * g + n]
            product = merged * weights[expert].astype(F32)
            folded = jnp.sum(product.reshape(rows // 8, 8, cols), axis=0)
            small = folded[:, :128]
            for c in range(128, cols, 128):
                small = small + folded[:, c : c + 128]
            small = jnp.sum(jnp.sum(small, axis=0, keepdims=True), axis=1, keepdims=True)
            total = total + jnp.where(lane == expert, small, 0.0)
        return total

    out_ref[...] = lax.fori_loop(0, count // 2, one, jnp.zeros((8, 128), F32))


def finish_kernel(scale, map_ref, coef_ref, got_ref, out_ref, order_ref, count_ref, held, ready, sems, more):
    count = ready.shape[0]

    def load(g):
        return pltpu.make_async_copy(got_ref.at[:, g], held.at[:, g], sems.at[g])

    def send(i):
        return pltpu.make_async_copy(ready.at[i], out_ref.at[order_ref[i]], more.at[i])

    @pl.loop(0, count // 2)
    def _(g):
        load(g).start()

    expert_order(map_ref, order_ref, count_ref)

    @pl.loop(0, count // 2)
    def _(g):
        load(g).wait()
        merged = held[0, g].astype(F32) + held[1, g].astype(F32)
        for n in range(2):
            i = 2 * g + n
            ready[i] = merged * (coef_ref[order_ref[i]] * scale)
            send(i).start()

    @pl.loop(0, count)
    def _(i):
        send(i).wait()


def coef_dots(rep_index, merge_map, source_w, arrived):
    count = source_w.shape[0]
    _, _, rows, cols = arrived.shape
    return pl.pallas_call(
        coef_kernel,
        in_specs=[smem_spec(), smem_spec(), hbm_spec(), hbm_spec()],
        out_specs=vmem_spec(),
        out_shape=jax.ShapeDtypeStruct((8, 128), F32),
        scratch_shapes=[
            pltpu.SMEM((count,), I32),
            pltpu.SMEM((count // 2,), I32),
            pltpu.VMEM(arrived.shape, BF),
            pltpu.VMEM((count, rows, cols), BF),
            pltpu.SemaphoreType.DMA((2,)),
        ],
        compiler_params=params(56),
        name="coef_dots",
    )(rep_index, merge_map, source_w, arrived)


def finish(merge_map, merge_coef, arrived, after, scale):
    count = merge_map.shape[0]
    _, _, rows, cols = arrived.shape
    return pl.pallas_call(
        lambda a, b, c, _, *refs: finish_kernel(scale, a, b, c, *refs),
        in_specs=[smem_spec(), smem_spec(), hbm_spec(), any_spec()],
        out_specs=hbm_spec(),
        out_shape=jax.ShapeDtypeStruct((count, rows, cols), F32),
        scratch_shapes=[
            pltpu.SMEM((count,), I32),
            pltpu.SMEM((count // 2,), I32),
            pltpu.VMEM(arrived.shape, BF),
            pltpu.VMEM((count, rows, cols), F32),
            pltpu.SemaphoreType.DMA((count // 2,)),
            pltpu.SemaphoreType.DMA((count,)),
        ],
        compiler_params=params(56),
        cost_estimate=cost(8),
        name="finish",
    )(merge_map, merge_coef, arrived, after)


def swap(x):
    return lax.ppermute(x, "core", [(0, 1), (1, 0)])


def on_pairs(
    tokens, router_w, router_b, hidden, teacher_idx, merge_map, merge_coef, source_w, out_grad
):
    places = lax.axis_size("place")
    blocks = 2 * places
    reps = 4
    tok = tokens.shape[1]
    features = tokens.shape[2]
    top = teacher_idx.shape[2]
    width = hidden.shape[3]
    depth = out_grad.shape[2]
    sources = router_w.shape[1]
    row_share = source_w.shape[1]
    lanes = 2 * places
    capacity = 5 * tok * top // (4 * blocks)
    scale = 1.0 / math.sqrt(tok * blocks * reps)
    half_i, place_i = lax.axis_index("half"), lax.axis_index("place")
    row_i, core_i = lax.axis_index("row"), lax.axis_index("core")
    ctx_i = half_i * places + place_i
    everyone = ("half", "place", "row", "core")
    devices = blocks * reps

    def stack(numbers):
        return jnp.stack([jnp.asarray(n, I32) for n in numbers])

    def later(*x):
        return swap(hold([jnp.zeros((8, 128), F32)], *x)[0])

    def trade(x, axes):
        return lax.all_to_all(x, axes, split_axis=0, concat_axis=0, tiled=True)

    xt = tokens.reshape(tok, features).T
    rwt = router_w.T
    idx_t = teacher_idx.reshape(tok, top).T
    og = out_grad.reshape(tok, depth)
    combos, send_rows, gates, pos, slot_pos = prepare(
        stack([row_i, core_i]), merge_map, merge_coef, source_w,
        xt, rwt, router_b, idx_t, hidden.reshape(tok * top, width), og, capacity, lanes,
    )
    rows = trade(send_rows.reshape(lanes, capacity, send_rows.shape[1]), ("place", "row"))
    rows = rows.reshape(send_rows.shape)
    (combos,) = hold([combos.reshape((blocks,) + combos.shape[2:])], rows)
    mine = trade(combos, ("half", "place"))
    (rows,) = hold([rows], later(rows))
    here = stack([core_i])
    first = lane_grads(stack([1 - core_i]), rows, None, blocks, reps)
    summed = lane_grads(here, rows, swap(first), blocks, reps)
    (mine,) = hold([mine], summed)
    (summed,) = hold([summed], mine)
    arrived = trade(
        summed.reshape(2 * blocks, 2, row_share, width // reps), ("half", "place", "row")
    )

    other = swap(mine)
    me = stack([2 * place_i + row_i])
    (rows,) = hold([rows], later(summed))
    parts = run_lane(here, me, rows, mine, other, lanes)
    home = assemble(
        me,
        [parts[0]]
        + [
            lax.ppermute(parts[d], ("place", "row"), [(i, i ^ d) for i in range(lanes)])
            for d in range(1, lanes)
        ],
    )
    mixed, token_grad, part = combine(home, og, gates, pos, idx_t, rwt, xt)
    part, arrived = hold([part, arrived])
    part = jnp.sum(trade(part[:, None, :], everyone), axis=0)
    hidden_grad = unplace(home, slot_pos)
    arrived = arrived.reshape(2, 2 * lanes, row_share, width // reps)
    dots = coef_dots(stack([2 * row_i + core_i]), merge_map, source_w, arrived)
    news = jnp.concatenate([part, dots[:1]], axis=1)
    news = trade(jnp.broadcast_to(news[None], (devices,) + news.shape), everyone)
    source_w_grad = finish(merge_map, merge_coef, arrived, dots, scale)
    end = part.shape[1]
    return (
        mixed.reshape(1, tok, depth),
        hidden_grad.reshape(1, tok, top, width),
        token_grad.T.reshape(1, tok, features),
        news[:, 0, :features].T * scale,
        news[:, 0, end - 1] * scale,
        jnp.sum(news[:, 0, end : end + sources], axis=0) * scale,
        source_w_grad,
    )


def solution(mesh):
    if mesh.shape["ctx"] == 8 and mesh.shape["rep"] == 4:
        mesh = jax.sharding.Mesh(
            mesh.devices.reshape(2, 4, 2, 2), ("half", "place", "row", "core")
        )
        ctx, rep, body = ("half", "place"), ("row", "core"), on_pairs
    else:
        ctx, rep, body = "ctx", "rep", on_device
    in_specs = (
        P(rep, ctx, None),
        P(),
        P(),
        P(rep, ctx, None, None),
        P(rep, ctx, None),
        P(),
        P(),
        P(None, ctx, None),
        P(rep, ctx, None),
    )
    out_specs = (
        P(rep, ctx, None),
        P(rep, ctx, None, None),
        P(rep, ctx, None),
        P(),
        P(),
        P(),
        P(None, ctx, rep),
    )
    return jax.shard_map(
        body, mesh=mesh, in_specs=in_specs, out_specs=out_specs, check_vma=False
    )
```

```python
import functools
import math

import jax
import jax.numpy as jnp
from jax import lax
from jax.experimental import pallas as pl
from jax.experimental.pallas import tpu as pltpu
from jax.sharding import PartitionSpec as P

MERGED = 16


def expert_rows(rows_hidden, rows_grad, rows_member, lane_weights):
    row_count = rows_hidden.shape[0]
    out_rows = jnp.zeros((row_count, lane_weights.shape[1]), jnp.float32)
    back_rows = jnp.zeros((row_count, lane_weights.shape[2]), jnp.float32)
    grad_list = []
    for member_now in range(lane_weights.shape[0]):
        weight = lane_weights[member_now]
        selected = (rows_member == member_now)[:, None]
        forward = lax.dot_general(
            rows_hidden, weight, (((1,), (1,)), ((), ())), preferred_element_type=jnp.float32
        )
        out_rows = jnp.where(selected, forward, out_rows)
        backward = jnp.dot(rows_grad, weight, preferred_element_type=jnp.float32)
        back_rows = jnp.where(selected, backward, back_rows)
        masked = jnp.where(selected, rows_grad, jnp.zeros_like(rows_grad))
        grad_list.append(
            lax.dot_general(
                masked, rows_hidden, (((0,), (0,)), ((), ())), preferred_element_type=jnp.float32
            )
        )
    return (out_rows, back_rows, jnp.stack(grad_list))


def on_device(
    tokens, router_w, router_b, hidden, teacher_idx, merge_map, merge_coef, source_w, out_grad
):
    ctx_count = lax.axis_size("ctx")
    rep_count = lax.axis_size("rep")
    tok_count = tokens.shape[1]
    feature_count = tokens.shape[2]
    top_count = teacher_idx.shape[2]
    hidden_width = hidden.shape[3]
    out_width = out_grad.shape[2]
    source_count = router_w.shape[1]
    row_share = source_w.shape[1]
    per_lane = max(1, MERGED // ctx_count)
    copies = max(1, ctx_count // MERGED)
    capacity = 5 * tok_count * top_count // (4 * ctx_count)
    slot_count = tok_count * top_count
    grad_scale = 1.0 / math.sqrt(tok_count * ctx_count * rep_count)
    flat_x = tokens.reshape(tok_count, feature_count)
    logits = jnp.dot(flat_x, router_w, preferred_element_type=jnp.float32) + router_b
    choice_ids = teacher_idx.reshape(tok_count, top_count)
    pick_table = choice_ids[:, :, None] == jnp.arange(source_count, dtype=jnp.int32)[None, None, :]
    pick_float = pick_table.astype(jnp.float32)
    chosen = jnp.sum(pick_float * logits[:, None, :], axis=2)
    raised = jnp.exp(chosen)
    gate_probs = raised / jnp.sum(raised, axis=1, keepdims=True)
    merged_id = jnp.sum(jnp.where(pick_table, merge_map[None, None, :], 0), axis=2)
    position = lax.axis_index("ctx") * tok_count + jnp.arange(tok_count, dtype=jnp.int32)
    lane_id = merged_id // per_lane * copies + (position % copies)[:, None]
    member_id = (merged_id % per_lane).reshape(-1)
    lane_flat = lane_id.reshape(-1)
    onehot = (lane_flat[:, None] == jnp.arange(ctx_count, dtype=jnp.int32)[None, :]).astype(
        jnp.int32
    )
    before = jnp.cumsum(onehot, axis=0) - onehot
    slot_rank = jnp.sum(before * onehot, axis=1)
    is_kept = slot_rank < capacity
    slot_index = jnp.where(is_kept, lane_flat * capacity + slot_rank, ctx_count * capacity)
    slot_source = (
        jnp.full((ctx_count * capacity + 1,), slot_count, jnp.int32)
        .at[slot_index]
        .set(jnp.arange(slot_count, dtype=jnp.int32))[: ctx_count * capacity]
    )
    slot_grad = (gate_probs[:, :, None] * out_grad.reshape(tok_count, 1, out_width)).astype(
        jnp.bfloat16
    )
    pad_hidden = jnp.concatenate(
        [hidden.reshape(slot_count, hidden_width), jnp.zeros((1, hidden_width), jnp.bfloat16)],
        axis=0,
    )
    pad_grad = jnp.concatenate(
        [slot_grad.reshape(slot_count, out_width), jnp.zeros((1, out_width), jnp.bfloat16)], axis=0
    )
    pad_member = jnp.concatenate([member_id, jnp.zeros((1,), jnp.int32)], axis=0)
    send_hidden = pad_hidden[slot_source].reshape(ctx_count, capacity, hidden_width)
    send_grad = pad_grad[slot_source].reshape(ctx_count, capacity, out_width)
    send_member = pad_member[slot_source].reshape(ctx_count, capacity)
    lane_group = lax.axis_index("ctx") // copies
    same_group = merge_map[:, None] == merge_map[None, :]
    earlier = jnp.arange(source_count)[:, None] > jnp.arange(source_count)[None, :]
    member_rank = jnp.sum((same_group & earlier).astype(jnp.int32), axis=1)
    source_order = (
        jnp.zeros((source_count,), jnp.int32)
        .at[2 * merge_map + member_rank]
        .set(jnp.arange(source_count, dtype=jnp.int32))
    )
    picked = source_w[source_order].reshape(
        MERGED // per_lane, 2 * per_lane, row_share, hidden_width
    )
    outgoing = jnp.repeat(picked, copies, axis=0)
    arrived = lax.all_to_all(outgoing, "ctx", split_axis=0, concat_axis=2, tiled=True)
    pair_rows = arrived.reshape(per_lane, 2, row_share * ctx_count, hidden_width)
    coef_table = merge_coef[source_order].reshape(MERGED // per_lane, per_lane, 2)
    pair_coef = lax.dynamic_index_in_dim(coef_table, lane_group, 0, keepdims=False)
    lane_weights = (
        pair_coef[:, 0, None, None] * pair_rows[:, 0].astype(jnp.float32)
        + pair_coef[:, 1, None, None] * pair_rows[:, 1].astype(jnp.float32)
    ).astype(jnp.bfloat16)
    recv_hidden, recv_grad, recv_member = (
        lax.all_to_all(send_hidden, "ctx", split_axis=0, concat_axis=0, tiled=True),
        lax.all_to_all(send_grad, "ctx", split_axis=0, concat_axis=0, tiled=True),
        lax.all_to_all(send_member, "ctx", split_axis=0, concat_axis=0, tiled=True),
    )
    out_rows, back_rows, lane_grads = expert_rows(
        recv_hidden.reshape(-1, hidden_width),
        recv_grad.reshape(-1, out_width),
        recv_member.reshape(-1),
        lane_weights,
    )
    home_out, home_back = (
        lax.all_to_all(
            out_rows.astype(jnp.bfloat16).reshape(ctx_count, capacity, out_width),
            "ctx",
            split_axis=0,
            concat_axis=0,
            tiled=True,
        ),
        lax.all_to_all(
            back_rows.astype(jnp.bfloat16).reshape(ctx_count, capacity, hidden_width),
            "ctx",
            split_axis=0,
            concat_axis=0,
            tiled=True,
        ),
    )
    slot_out = jnp.concatenate(
        [home_out.reshape(-1, out_width), jnp.zeros((1, out_width), jnp.bfloat16)], axis=0
    )[slot_index].reshape(tok_count, top_count, out_width)
    hidden_grad = jnp.concatenate(
        [home_back.reshape(-1, hidden_width), jnp.zeros((1, hidden_width), jnp.bfloat16)], axis=0
    )[slot_index].reshape(1, tok_count, top_count, hidden_width)
    mixed = (
        jnp.sum(gate_probs[:, :, None] * slot_out.astype(jnp.float32), axis=1)
        .astype(jnp.bfloat16)
        .reshape(1, tok_count, out_width)
    )
    score_grad = jnp.einsum(
        "td,tkd->tk",
        out_grad.reshape(tok_count, out_width),
        slot_out,
        preferred_element_type=jnp.float32,
    )
    chosen_grad = gate_probs * (
        score_grad - jnp.sum(gate_probs * score_grad, axis=1, keepdims=True)
    )
    logit_grad = jnp.sum(pick_float * chosen_grad[:, :, None], axis=1)
    logit_half = logit_grad.astype(jnp.bfloat16)
    token_grad = (
        lax.dot_general(
            logit_half, router_w, (((1,), (1,)), ((), ())), preferred_element_type=jnp.float32
        )
        .astype(jnp.bfloat16)
        .reshape(1, tok_count, feature_count)
    )
    part_router_w = lax.dot_general(
        flat_x, logit_half, (((0,), (0,)), ((), ())), preferred_element_type=jnp.float32
    )
    part_router_b = jnp.sum(logit_grad, axis=0)
    arrived_grads = lax.all_to_all(
        lane_grads.reshape(per_lane, ctx_count, row_share, hidden_width),
        "ctx",
        split_axis=1,
        concat_axis=0,
        tiled=True,
    )
    merged_grad = (
        arrived_grads.reshape(MERGED // per_lane, copies, per_lane, row_share, hidden_width)
        .sum(axis=1)
        .reshape(MERGED, row_share, hidden_width)
    )
    source_grad = merged_grad[merge_map]
    coef_part = jnp.einsum(
        "edf,edf->e", source_grad, source_w.astype(jnp.float32), precision=lax.Precision.HIGHEST
    )
    summed = lax.psum_scatter(
        source_grad * merge_coef[:, None, None], "rep", scatter_dimension=2, tiled=True
    )
    source_w_grad = summed * grad_scale
    router_sum, bias_sum, coef_sum = lax.psum(
        (part_router_w, part_router_b, coef_part), ("ctx", "rep")
    )
    return (
        mixed,
        hidden_grad,
        token_grad,
        router_sum * grad_scale,
        bias_sum * grad_scale,
        coef_sum * grad_scale,
        source_w_grad,
    )


BF = jnp.bfloat16
F32 = jnp.float32
I32 = jnp.int32
TILE = 256


def cost(us):
    return pl.CostEstimate(flops=us * 10**9, bytes_accessed=us * 10**6, transcendentals=0)


def any_spec():
    return pl.BlockSpec(memory_space=pl.ANY)


def smem_spec():
    return pl.BlockSpec(memory_space=pltpu.SMEM)


def vmem_spec():
    return pl.BlockSpec(memory_space=pltpu.VMEM)


def params(mib):
    return pltpu.CompilerParams(vmem_limit_bytes=mib * 1024 * 1024)


def dot(a, b, dims):
    return lax.dot_general(a, b, (dims, ((), ())), preferred_element_type=F32)


def merge_start(map_ref, place_ref, src_ref, places, order_ref, count_ref, held, sems):
    half = held.shape[2]
    expert_order(map_ref, order_ref, count_ref)
    at = pl.ds(pl.multiple_of(place_ref[1] * half, half), half)
    copies, experts = [], []
    for j in range(places):
        for m in range(2):
            combo = 4 * j + 2 * place_ref[0] + m
            for n in range(2):
                expert = order_ref[2 * combo + n]
                experts.append(expert)
                i = len(copies)
                copies.append(
                    pltpu.make_async_copy(src_ref.at[expert, :, at], held.at[i], sems.at[i])
                )
                copies[-1].start()
    return copies, experts


def merge_finish(copies, experts, coef_ref, held, out_ref):
    halves, places = out_ref.shape[:2]
    for j in range(places):
        for m in range(2):
            i = 4 * j + 2 * m
            copies[i].wait()
            copies[i + 1].wait()
            one, two = coef_ref[experts[i]], coef_ref[experts[i + 1]]
            merged = (one * held[i].astype(F32) + two * held[i + 1].astype(F32)).astype(BF)
            for h in range(halves):
                out_ref[h, j, m] = merged


def expert_order(map_ref, order_ref, count_ref):
    @pl.loop(0, count_ref.shape[0])
    def _(g):
        count_ref[g] = 0

    @pl.loop(0, order_ref.shape[0])
    def _(e):
        g = map_ref[e]
        n = count_ref[g]
        order_ref[2 * g + n] = e
        count_ref[g] = n + 1


def hbm_spec():
    return pl.BlockSpec(memory_space=pltpu.HBM)


def hold(arrays, *after):
    count = len(arrays)
    return pl.pallas_call(
        lambda *refs: None,
        in_specs=[hbm_spec()] * count + [any_spec()] * len(after),
        out_specs=[hbm_spec()] * count,
        out_shape=[jax.ShapeDtypeStruct(a.shape, a.dtype) for a in arrays],
        input_output_aliases={i: i for i in range(count)},
        name="hold",
    )(*arrays, *after)


def column(row):
    size = row.shape[1]
    same = lax.broadcasted_iota(I32, (size, size), 0) == lax.broadcasted_iota(I32, (size, size), 1)
    return jnp.sum(jnp.where(same, row, jnp.zeros_like(row)), axis=1, keepdims=True)


def to_row(col):
    size = col.shape[0]
    same = lax.broadcasted_iota(I32, (size, size), 0) == lax.broadcasted_iota(I32, (size, size), 1)
    return jnp.sum(jnp.where(same, col, jnp.zeros_like(col)), axis=0, keepdims=True)


def picks_of(idx_ref, k, sources):
    tok = idx_ref.shape[1]
    return lax.broadcasted_iota(I32, (sources, tok), 0) == idx_ref[k : k + 1, :]


def prepare_kernel(
    capacity, lanes,
    combo_ref, coef_ref, place_ref, src_ref,
    xt_ref, rwt_ref, rb_ref, idx_ref, map_ref, hid_ref, og_ref,
    merged_ref, send_ref, gate_ref, pos_ref, slot_ref,
    order_ref, count_ref, held, sems,
):
    copies, experts = merge_start(
        combo_ref, place_ref, src_ref, merged_ref.shape[1], order_ref, count_ref, held, sems
    )
    top, tok = idx_ref.shape
    sources = rwt_ref.shape[0]
    slots, width = hid_ref.shape
    places = lanes * capacity
    logits = jnp.dot(rwt_ref[...], xt_ref[...], preferred_element_type=F32) + column(rb_ref[...])
    raised, merged = [], []
    combos = column(map_ref[...])
    for k in range(top):
        pick = picks_of(idx_ref, k, sources)
        chosen = jnp.sum(jnp.where(pick, logits, 0.0), axis=0, keepdims=True)
        raised.append(jnp.exp(chosen))
        merged.append(jnp.sum(jnp.where(pick, combos, 0), axis=0, keepdims=True))
    total = raised[0]
    for k in range(1, top):
        total = total + raised[k]
    gates = [r / total for r in raised]
    lane = [jnp.right_shift(g, 1) for g in merged]
    member = [jnp.bitwise_and(g, 1) for g in merged]
    onehot = [(lax.broadcasted_iota(I32, (lanes, tok), 0) == l).astype(F32) for l in lane]
    all_hot = onehot[0]
    for k in range(1, top):
        all_hot = all_hot + onehot[k]
    earlier = (
        lax.broadcasted_iota(I32, (tok, tok), 0) < lax.broadcasted_iota(I32, (tok, tok), 1)
    ).astype(BF)
    before = jnp.dot(all_hot.astype(BF), earlier, preferred_element_type=F32)
    position, back = [], []
    for k in range(top):
        rank = jnp.sum(before * onehot[k], axis=0, keepdims=True).astype(I32)
        before = before + onehot[k]
        position.append(jnp.where(rank < capacity, lane[k] * capacity + rank, -1))
        partner = jnp.bitwise_xor(lane[k], place_ref[2])
        back.append(jnp.where(rank < capacity, partner * capacity + rank, -1))
    gate_ref[...] = jnp.zeros_like(gate_ref)
    pos_ref[...] = jnp.full_like(pos_ref, -1)
    for k in range(top):
        gate_ref[k : k + 1, :] = gates[k]
        pos_ref[k : k + 1, :] = back[k]
    spot = jnp.zeros((8, slots), F32)
    for k in range(top):
        spread = (
            lax.broadcasted_iota(I32, (tok, slots), 1)
            == lax.broadcasted_iota(I32, (tok, slots), 0) * top + k
        ).astype(BF)
        kept = position[k] >= 0
        parts = [
            jnp.where(kept, lane[k], 0),
            jnp.where(kept, position[k] - lane[k] * capacity, 0),
            jnp.where(kept, 1, 0),
            member[k],
        ]
        stacked = jnp.concatenate(
            [p.astype(F32) for p in parts] + [jnp.zeros((4, tok), F32)], axis=0
        ).astype(BF)
        spot = spot + jnp.dot(stacked, spread, preferred_element_type=F32)
    spot = spot.astype(I32)
    slot_pos = jnp.where(spot[2:3] > 0, spot[0:1] * capacity + spot[1:2], -1)
    partner = jnp.bitwise_xor(spot[0:1], place_ref[2])
    slot_back = jnp.where(spot[2:3] > 0, partner * capacity + spot[1:2], -1)
    slot_ref[...] = jnp.broadcast_to(slot_back, slot_ref.shape)
    take = lax.broadcasted_iota(I32, (places, slots), 0) == slot_pos
    placed = jnp.sum(jnp.where(take, spot[3:4].astype(F32), 0.0), axis=1, keepdims=True)
    depth = og_ref.shape[1]
    send_ref[:, depth + width :] = jnp.broadcast_to(placed, (places, 128)).astype(BF)
    take = take.astype(BF)
    for n in range(0, width, TILE):
        rows = jnp.dot(take, hid_ref[:, n : n + TILE], preferred_element_type=F32)
        send_ref[:, depth + n : depth + n + TILE] = rows.astype(BF)
    takes = [
        (lax.broadcasted_iota(I32, (places, tok), 0) == position[k]).astype(BF) for k in range(top)
    ]
    columns = [column(g) for g in gates]
    for n in range(0, depth, TILE):
        og = og_ref[:, n : n + TILE].astype(F32)
        rows = jnp.zeros((places, TILE), F32)
        for k in range(top):
            rows = rows + jnp.dot(takes[k], (columns[k] * og).astype(BF), preferred_element_type=F32)
        send_ref[:, n : n + TILE] = rows.astype(BF)
    merge_finish(copies, experts, coef_ref, held, merged_ref)


def prepare(
    place, merge_map, merge_coef, source_w, xt, rwt, router_b, idx_t, hid, og, capacity, lanes
):
    count, rows, whole = source_w.shape
    slots, width = hid.shape
    tok = idx_t.shape[1]
    half, places = whole // 2, lanes // 2
    return pl.pallas_call(
        functools.partial(prepare_kernel, capacity, lanes),
        in_specs=[smem_spec()] * 3 + [any_spec()] + [vmem_spec()] * 7,
        out_specs=[vmem_spec()] * 5,
        out_shape=[
            jax.ShapeDtypeStruct((2, places, 2, rows, half), BF),
            jax.ShapeDtypeStruct((lanes * capacity, og.shape[1] + width + 128), BF),
            jax.ShapeDtypeStruct((8, tok), F32),
            jax.ShapeDtypeStruct((8, tok), I32),
            jax.ShapeDtypeStruct((8, slots), I32),
        ],
        scratch_shapes=[
            pltpu.SMEM((count,), I32),
            pltpu.SMEM((count // 2,), I32),
            pltpu.VMEM((4 * places, rows, half), BF),
            pltpu.SemaphoreType.DMA((4 * places,)),
        ],
        compiler_params=params(56),
        cost_estimate=cost(10),
        name="prepare",
    )(
        merge_map, merge_coef, place, source_w,
        xt, rwt, router_b[None, :], idx_t, merge_map[None, :], hid, og,
    )


def gather_rows(refs, keep):
    each = refs[0].shape[0]
    for d, ref in enumerate(refs):
        keep[d * each : (d + 1) * each, :] = ref[...]


def load_weights(core_ref, mine, other, w_ref, sems):
    core = core_ref[0]
    blocks, _, rows, _ = mine.shape
    copies = []
    for c in range(blocks):
        at = pl.ds(c * rows, rows)
        for n, part in enumerate((mine, other)):
            to = core if n == 0 else 1 - core
            i = 2 * c + n
            copies.append(
                pltpu.make_async_copy(part.at[c], w_ref.at[to, :, at, :], sems.at[i])
            )
    for copy in copies:
        copy.start()
    for copy in copies:
        copy.wait()


def lane_kernel(
    core_ref, me_ref, grd_ref, hid_ref, flag_ref, mine, other, *refs
):
    outs, (keep, w_ref, sems) = refs[:-3], refs[-3:]
    load_weights(core_ref, mine, other, w_ref, sems)
    half, depth = w_ref.shape[3], w_ref.shape[2]
    first = flag_ref[:, :1].astype(F32) == 0.0
    for n in range(0, depth, TILE):
        at = slice(n, n + TILE)
        both = [
            dot(hid_ref[:, :half], w_ref[0, m, at, :], ((1,), (1,)))
            + dot(hid_ref[:, half:], w_ref[1, m, at, :], ((1,), (1,)))
            for m in range(2)
        ]
        keep[:, at] = jnp.where(first, both[0], both[1]).astype(BF)
    for h in range(2):
        for n in range(0, half, TILE):
            at = slice(n, n + TILE)
            both = [dot(grd_ref[...], w_ref[h, m, :, at], ((1,), (0,))) for m in range(2)]
            to = depth + h * half + n
            keep[:, to : to + TILE] = jnp.where(first, both[0], both[1]).astype(BF)
    each = outs[0].shape[0]
    for d, out_ref in enumerate(outs):
        at = pl.ds(pl.multiple_of(jnp.bitwise_xor(me_ref[0], d) * each, each), each)
        out_ref[...] = keep[at, :]


def run_lane(core, me, rows, mine, other, lanes):
    blocks, members, share, half = mine.shape
    depth = share * blocks
    count = rows.shape[0]
    wide = (rows.shape[1] - 128) // 2
    part = (count // lanes, 2 * wide)
    return pl.pallas_call(
        lane_kernel,
        grid=(1,),
        in_specs=[
            smem_spec(),
            smem_spec(),
            pl.BlockSpec((count, wide), lambda i: (0, 0)),
            pl.BlockSpec((count, wide), lambda i: (0, 1)),
            pl.BlockSpec((count, 128), lambda i: (0, 2 * wide // 128)),
            any_spec(),
            any_spec(),
        ],
        out_specs=[pl.BlockSpec(part, lambda i: (0, 0))] * lanes,
        out_shape=[jax.ShapeDtypeStruct(part, BF)] * lanes,
        scratch_shapes=[
            pltpu.VMEM((count, 2 * wide), BF),
            pltpu.VMEM((2, members, depth, half), BF),
            pltpu.SemaphoreType.DMA((2 * blocks,)),
        ],
        compiler_params=params(60),
        cost_estimate=cost(20),
        name="lane_products",
    )(core, me, rows, rows, rows, mine, other)


def lane_grad_kernel(has_other, _, grd_ref, hid_ref, flag_ref, *refs):
    out_ref = refs[-1]
    chosen = flag_ref[:, :1].astype(F32) == pl.program_id(1).astype(F32)
    hid = jnp.where(chosen, hid_ref[...], jnp.zeros_like(hid_ref))
    blocks, _, _, rows, cols = out_ref.shape
    each = 2 if blocks % 2 == 0 and 2 * rows % 128 == 0 else blocks
    for n in range(0, blocks, each):
        part = dot(grd_ref[:, n * rows : (n + each) * rows], hid, ((0,), (0,)))
        part = part.reshape(each, rows, cols)
        if has_other:
            part = part + refs[0][n : n + each, 0, 0].astype(F32)
        out_ref[n : n + each, 0, 0] = part.astype(BF)


def lane_grads(core, rows, other, blocks, reps):
    count = rows.shape[0]
    width = (rows.shape[1] - 128) // 2
    cols = width // reps
    shape = (blocks, 2, 2, width // blocks, cols)
    block = pl.BlockSpec((blocks, 1, 1, width // blocks, cols), lambda y, m, s: (0, y, m, 0, 0))
    extra = [] if other is None else [other]
    return pl.pallas_call(
        functools.partial(lane_grad_kernel, other is not None),
        grid_spec=pltpu.PrefetchScalarGridSpec(
            num_scalar_prefetch=1,
            grid=(2, 2),
            in_specs=[
                pl.BlockSpec((count, width), lambda y, m, s: (0, 0)),
                pl.BlockSpec((count, cols), lambda y, m, s: (0, reps + 2 * y + s[0])),
                pl.BlockSpec((count, 128), lambda y, m, s: (0, 2 * width // 128)),
            ]
            + [block] * len(extra),
            out_specs=block,
        ),
        out_shape=jax.ShapeDtypeStruct(shape, BF),
        compiler_params=params(56),
        cost_estimate=cost(8),
        name="lane_grads_add" if extra else "lane_grads_first",
    )(core, rows, rows, rows, *extra)


def combine_kernel(og_ref, gate_ref, pos_ref, idx_ref, rwt_ref, xt_ref, *refs):
    homes, (mixed_ref, tg_ref, part_ref, out_ref) = refs[:-4], refs[-4:]
    gather_rows(homes, out_ref)
    places, width = out_ref.shape
    top, tok = idx_ref.shape
    sources, features = rwt_ref.shape
    takes = [
        (lax.broadcasted_iota(I32, (places, tok), 0) == pos_ref[k : k + 1, :]).astype(BF)
        for k in range(top)
    ]
    gates = [gate_ref[k : k + 1, :] for k in range(top)]
    columns = [column(g) for g in gates]
    scores = [jnp.zeros((tok, 1), F32) for _ in range(top)]
    for n in range(0, width, TILE):
        og = og_ref[:, n : n + TILE].astype(F32)
        rows = out_ref[:, n : n + TILE]
        mixed = jnp.zeros((tok, TILE), F32)
        for k in range(top):
            slot_out = dot(takes[k], rows, ((0,), (0,)))
            mixed = mixed + columns[k] * slot_out
            scores[k] = scores[k] + jnp.sum(og * slot_out, axis=1, keepdims=True)
        mixed_ref[:, n : n + TILE] = mixed.astype(BF)
    scores = [to_row(s) for s in scores]
    middle = gates[0] * scores[0]
    for k in range(1, top):
        middle = middle + gates[k] * scores[k]
    logit_grad = jnp.zeros((sources, tok), F32)
    for k in range(top):
        chosen_grad = gates[k] * (scores[k] - middle)
        logit_grad = logit_grad + jnp.where(picks_of(idx_ref, k, sources), chosen_grad, 0.0)
    logit_half = logit_grad.astype(BF)
    tg_ref[...] = dot(rwt_ref[...], logit_half, ((0,), (0,))).astype(BF)
    part_ref[...] = jnp.zeros_like(part_ref)
    part_ref[:, 0, :features] = dot(logit_half, xt_ref[...], ((1,), (1,)))
    bias = jnp.sum(logit_grad, axis=1, keepdims=True)
    last = part_ref.shape[2] - 128
    part_ref[:, 0, last:] = jnp.broadcast_to(bias, (sources, 128))


def combine(homes, og, gates, pos, idx_t, rwt, xt):
    sources, features = rwt.shape
    tok, width = og.shape
    each = homes[0].shape[0]
    whole = lambda a: pl.BlockSpec(a.shape, lambda i: (0,) * len(a.shape))
    outs = [
        jax.ShapeDtypeStruct(og.shape, BF),
        jax.ShapeDtypeStruct((features, tok), BF),
        jax.ShapeDtypeStruct((sources, 1, (features + 127) // 128 * 128 + 128), F32),
    ]
    return pl.pallas_call(
        combine_kernel,
        grid=(1,),
        in_specs=[whole(a) for a in (og, gates, pos, idx_t, rwt, xt)]
        + [pl.BlockSpec((each, width), lambda i: (0, 0))] * len(homes),
        out_specs=[whole(a) for a in outs],
        out_shape=outs,
        scratch_shapes=[pltpu.VMEM((len(homes) * each, width), BF)],
        compiler_params=params(56),
        cost_estimate=cost(5),
        name="combine",
    )(og, gates, pos, idx_t, rwt, xt, *homes)


def unplace_kernel(slot_ref, *refs):
    homes, (out_ref, back_ref) = refs[:-2], refs[-2:]
    gather_rows(homes, back_ref)
    places, width = back_ref.shape
    slots = slot_ref.shape[1]
    take = (lax.broadcasted_iota(I32, (places, slots), 0) == slot_ref[0:1, :]).astype(BF)
    for n in range(0, width, TILE):
        out_ref[:, n : n + TILE] = dot(take, back_ref[:, n : n + TILE], ((0,), (0,))).astype(BF)


def unplace(homes, slot_pos):
    each, width = homes[0].shape[0], homes[0].shape[1] // 2
    slots = slot_pos.shape[1]
    return pl.pallas_call(
        unplace_kernel,
        grid=(1,),
        in_specs=[pl.BlockSpec(slot_pos.shape, lambda i: (0, 0))]
        + [pl.BlockSpec((each, width), lambda i: (0, 1))] * len(homes),
        out_specs=pl.BlockSpec((slots, width), lambda i: (0, 0)),
        out_shape=jax.ShapeDtypeStruct((slots, width), BF),
        scratch_shapes=[pltpu.VMEM((len(homes) * each, width), BF)],
        compiler_params=params(56),
        cost_estimate=cost(4),
        name="unplace",
    )(slot_pos, *homes)


def coef_kernel(rep_ref, map_ref, src_ref, got_ref, out_ref, order_ref, count_ref, held, weights, sems):
    count, rows, cols = weights.shape
    at = pl.ds(pl.multiple_of(rep_ref[0] * cols, cols), cols)
    copies = [
        pltpu.make_async_copy(src_ref.at[:, :, at], weights, sems.at[0]),
        pltpu.make_async_copy(got_ref, held, sems.at[1]),
    ]
    for copy in copies:
        copy.start()
    expert_order(map_ref, order_ref, count_ref)
    for copy in copies:
        copy.wait()
    lane = lax.broadcasted_iota(I32, (8, 128), 1)

    def one(g, total):
        merged = held[0, g].astype(F32) + held[1, g].astype(F32)
        for n in range(2):
            expert = order_ref[2 * g + n]
            product = merged * weights[expert].astype(F32)
            folded = jnp.sum(product.reshape(rows // 8, 8, cols), axis=0)
            small = folded[:, :128]
            for c in range(128, cols, 128):
                small = small + folded[:, c : c + 128]
            small = jnp.sum(jnp.sum(small, axis=0, keepdims=True), axis=1, keepdims=True)
            total = total + jnp.where(lane == expert, small, 0.0)
        return total

    out_ref[...] = lax.fori_loop(0, count // 2, one, jnp.zeros((8, 128), F32))


def finish_kernel(scale, map_ref, coef_ref, got_ref, out_ref, order_ref, count_ref, held, ready, sems, more):
    count = ready.shape[0]

    def load(g):
        return pltpu.make_async_copy(got_ref.at[:, g], held.at[:, g], sems.at[g])

    def send(i):
        return pltpu.make_async_copy(ready.at[i], out_ref.at[order_ref[i]], more.at[i])

    @pl.loop(0, count // 2)
    def _(g):
        load(g).start()

    expert_order(map_ref, order_ref, count_ref)

    @pl.loop(0, count // 2)
    def _(g):
        load(g).wait()
        merged = held[0, g].astype(F32) + held[1, g].astype(F32)
        for n in range(2):
            i = 2 * g + n
            ready[i] = merged * (coef_ref[order_ref[i]] * scale)
            send(i).start()

    @pl.loop(0, count)
    def _(i):
        send(i).wait()


def coef_dots(rep_index, merge_map, source_w, arrived):
    count = source_w.shape[0]
    _, _, rows, cols = arrived.shape
    return pl.pallas_call(
        coef_kernel,
        in_specs=[smem_spec(), smem_spec(), hbm_spec(), hbm_spec()],
        out_specs=vmem_spec(),
        out_shape=jax.ShapeDtypeStruct((8, 128), F32),
        scratch_shapes=[
            pltpu.SMEM((count,), I32),
            pltpu.SMEM((count // 2,), I32),
            pltpu.VMEM(arrived.shape, BF),
            pltpu.VMEM((count, rows, cols), BF),
            pltpu.SemaphoreType.DMA((2,)),
        ],
        compiler_params=params(56),
        name="coef_dots",
    )(rep_index, merge_map, source_w, arrived)


def finish(merge_map, merge_coef, arrived, after, scale):
    count = merge_map.shape[0]
    _, _, rows, cols = arrived.shape
    return pl.pallas_call(
        lambda a, b, c, _, *refs: finish_kernel(scale, a, b, c, *refs),
        in_specs=[smem_spec(), smem_spec(), hbm_spec(), any_spec()],
        out_specs=hbm_spec(),
        out_shape=jax.ShapeDtypeStruct((count, rows, cols), F32),
        scratch_shapes=[
            pltpu.SMEM((count,), I32),
            pltpu.SMEM((count // 2,), I32),
            pltpu.VMEM(arrived.shape, BF),
            pltpu.VMEM((count, rows, cols), F32),
            pltpu.SemaphoreType.DMA((count // 2,)),
            pltpu.SemaphoreType.DMA((count,)),
        ],
        compiler_params=params(56),
        cost_estimate=cost(8),
        name="finish",
    )(merge_map, merge_coef, arrived, after)


def swap(x):
    return lax.ppermute(x, "core", [(0, 1), (1, 0)])


def on_pairs(
    tokens, router_w, router_b, hidden, teacher_idx, merge_map, merge_coef, source_w, out_grad
):
    places = lax.axis_size("place")
    blocks = 2 * places
    reps = 4
    tok = tokens.shape[1]
    features = tokens.shape[2]
    top = teacher_idx.shape[2]
    width = hidden.shape[3]
    depth = out_grad.shape[2]
    sources = router_w.shape[1]
    row_share = source_w.shape[1]
    lanes = 2 * places
    capacity = 5 * tok * top // (4 * blocks)
    scale = 1.0 / math.sqrt(tok * blocks * reps)
    half_i, place_i = lax.axis_index("half"), lax.axis_index("place")
    row_i, core_i = lax.axis_index("row"), lax.axis_index("core")
    ctx_i = half_i * places + place_i
    everyone = ("half", "place", "row", "core")
    devices = blocks * reps

    def stack(numbers):
        return jnp.stack([jnp.asarray(n, I32) for n in numbers])

    def later(*x):
        return swap(hold([jnp.zeros((8, 128), F32)], *x)[0])

    def trade(x, axes):
        return lax.all_to_all(x, axes, split_axis=0, concat_axis=0, tiled=True)

    xt = tokens.reshape(tok, features).T
    rwt = router_w.T
    idx_t = teacher_idx.reshape(tok, top).T
    og = out_grad.reshape(tok, depth)
    combos, send_rows, gates, pos, slot_pos = prepare(
        stack([row_i, core_i, 2 * place_i + row_i]), merge_map, merge_coef, source_w,
        xt, rwt, router_b, idx_t, hidden.reshape(tok * top, width), og, capacity, lanes,
    )
    rows = trade(send_rows.reshape(lanes, capacity, send_rows.shape[1]), ("place", "row"))
    rows = rows.reshape(send_rows.shape)
    (combos,) = hold([combos.reshape((blocks,) + combos.shape[2:])], rows)
    mine = trade(combos, ("half", "place"))
    (rows,) = hold([rows], later(rows))
    here = stack([core_i])
    first = lane_grads(stack([1 - core_i]), rows, None, blocks, reps)
    summed = lane_grads(here, rows, swap(first), blocks, reps)
    (mine,) = hold([mine], summed)
    (summed,) = hold([summed], mine)
    arrived = trade(
        summed.reshape(2 * blocks, 2, row_share, width // reps), ("half", "place", "row")
    )

    other = swap(mine)
    me = stack([2 * place_i + row_i])
    (rows,) = hold([rows], later(summed))
    parts = run_lane(here, me, rows, mine, other, lanes)
    home = [parts[0]] + [
        lax.ppermute(parts[d], ("place", "row"), [(i, i ^ d) for i in range(lanes)])
        for d in range(1, lanes)
    ]
    mixed, token_grad, part = combine(home, og, gates, pos, idx_t, rwt, xt)
    part, arrived = hold([part, arrived])
    part = jnp.sum(trade(part, everyone), axis=0)
    hidden_grad = unplace(home, slot_pos).reshape(1, tok, top, width)
    arrived = arrived.reshape(2, 2 * lanes, row_share, width // reps)
    dots = coef_dots(stack([2 * row_i + core_i]), merge_map, source_w, arrived)
    news = jnp.concatenate([part, dots[:1]], axis=1)
    (news,) = hold([news], hidden_grad)
    news = trade(jnp.broadcast_to(news[None], (devices,) + news.shape), everyone)
    source_w_grad = finish(merge_map, merge_coef, arrived, dots, scale)
    end = part.shape[1]
    return (
        mixed.reshape(1, tok, depth),
        hidden_grad,
        token_grad.T.reshape(1, tok, features),
        news[:, 0, :features].T * scale,
        news[:, 0, end - 1] * scale,
        jnp.sum(news[:, 0, end : end + sources], axis=0) * scale,
        source_w_grad,
    )


def solution(mesh):
    if mesh.shape["ctx"] == 8 and mesh.shape["rep"] == 4:
        mesh = jax.sharding.Mesh(
            mesh.devices.reshape(2, 4, 2, 2), ("half", "place", "row", "core")
        )
        ctx, rep, body = ("half", "place"), ("row", "core"), on_pairs
    else:
        ctx, rep, body = "ctx", "rep", on_device
    in_specs = (
        P(rep, ctx, None),
        P(),
        P(),
        P(rep, ctx, None, None),
        P(rep, ctx, None),
        P(),
        P(),
        P(None, ctx, None),
        P(rep, ctx, None),
    )
    out_specs = (
        P(rep, ctx, None),
        P(rep, ctx, None, None),
        P(rep, ctx, None),
        P(),
        P(),
        P(),
        P(None, ctx, rep),
    )
    return jax.shard_map(
        body, mesh=mesh, in_specs=in_specs, out_specs=out_specs, check_vma=False
    )
```

```python
import functools
import math

import jax
import jax.numpy as jnp
from jax import lax
from jax.experimental import pallas as pl
from jax.experimental.pallas import tpu as pltpu
from jax.sharding import PartitionSpec as P

MERGED = 16


def expert_rows(rows_hidden, rows_grad, rows_member, lane_weights):
    row_count = rows_hidden.shape[0]
    out_rows = jnp.zeros((row_count, lane_weights.shape[1]), jnp.float32)
    back_rows = jnp.zeros((row_count, lane_weights.shape[2]), jnp.float32)
    grad_list = []
    for member_now in range(lane_weights.shape[0]):
        weight = lane_weights[member_now]
        selected = (rows_member == member_now)[:, None]
        forward = lax.dot_general(
            rows_hidden, weight, (((1,), (1,)), ((), ())), preferred_element_type=jnp.float32
        )
        out_rows = jnp.where(selected, forward, out_rows)
        backward = jnp.dot(rows_grad, weight, preferred_element_type=jnp.float32)
        back_rows = jnp.where(selected, backward, back_rows)
        masked = jnp.where(selected, rows_grad, jnp.zeros_like(rows_grad))
        grad_list.append(
            lax.dot_general(
                masked, rows_hidden, (((0,), (0,)), ((), ())), preferred_element_type=jnp.float32
            )
        )
    return (out_rows, back_rows, jnp.stack(grad_list))


def on_device(
    tokens, router_w, router_b, hidden, teacher_idx, merge_map, merge_coef, source_w, out_grad
):
    ctx_count = lax.axis_size("ctx")
    rep_count = lax.axis_size("rep")
    tok_count = tokens.shape[1]
    feature_count = tokens.shape[2]
    top_count = teacher_idx.shape[2]
    hidden_width = hidden.shape[3]
    out_width = out_grad.shape[2]
    source_count = router_w.shape[1]
    row_share = source_w.shape[1]
    per_lane = max(1, MERGED // ctx_count)
    copies = max(1, ctx_count // MERGED)
    capacity = 5 * tok_count * top_count // (4 * ctx_count)
    slot_count = tok_count * top_count
    grad_scale = 1.0 / math.sqrt(tok_count * ctx_count * rep_count)
    flat_x = tokens.reshape(tok_count, feature_count)
    logits = jnp.dot(flat_x, router_w, preferred_element_type=jnp.float32) + router_b
    choice_ids = teacher_idx.reshape(tok_count, top_count)
    pick_table = choice_ids[:, :, None] == jnp.arange(source_count, dtype=jnp.int32)[None, None, :]
    pick_float = pick_table.astype(jnp.float32)
    chosen = jnp.sum(pick_float * logits[:, None, :], axis=2)
    raised = jnp.exp(chosen)
    gate_probs = raised / jnp.sum(raised, axis=1, keepdims=True)
    merged_id = jnp.sum(jnp.where(pick_table, merge_map[None, None, :], 0), axis=2)
    position = lax.axis_index("ctx") * tok_count + jnp.arange(tok_count, dtype=jnp.int32)
    lane_id = merged_id // per_lane * copies + (position % copies)[:, None]
    member_id = (merged_id % per_lane).reshape(-1)
    lane_flat = lane_id.reshape(-1)
    onehot = (lane_flat[:, None] == jnp.arange(ctx_count, dtype=jnp.int32)[None, :]).astype(
        jnp.int32
    )
    before = jnp.cumsum(onehot, axis=0) - onehot
    slot_rank = jnp.sum(before * onehot, axis=1)
    is_kept = slot_rank < capacity
    slot_index = jnp.where(is_kept, lane_flat * capacity + slot_rank, ctx_count * capacity)
    slot_source = (
        jnp.full((ctx_count * capacity + 1,), slot_count, jnp.int32)
        .at[slot_index]
        .set(jnp.arange(slot_count, dtype=jnp.int32))[: ctx_count * capacity]
    )
    slot_grad = (gate_probs[:, :, None] * out_grad.reshape(tok_count, 1, out_width)).astype(
        jnp.bfloat16
    )
    pad_hidden = jnp.concatenate(
        [hidden.reshape(slot_count, hidden_width), jnp.zeros((1, hidden_width), jnp.bfloat16)],
        axis=0,
    )
    pad_grad = jnp.concatenate(
        [slot_grad.reshape(slot_count, out_width), jnp.zeros((1, out_width), jnp.bfloat16)], axis=0
    )
    pad_member = jnp.concatenate([member_id, jnp.zeros((1,), jnp.int32)], axis=0)
    send_hidden = pad_hidden[slot_source].reshape(ctx_count, capacity, hidden_width)
    send_grad = pad_grad[slot_source].reshape(ctx_count, capacity, out_width)
    send_member = pad_member[slot_source].reshape(ctx_count, capacity)
    lane_group = lax.axis_index("ctx") // copies
    same_group = merge_map[:, None] == merge_map[None, :]
    earlier = jnp.arange(source_count)[:, None] > jnp.arange(source_count)[None, :]
    member_rank = jnp.sum((same_group & earlier).astype(jnp.int32), axis=1)
    source_order = (
        jnp.zeros((source_count,), jnp.int32)
        .at[2 * merge_map + member_rank]
        .set(jnp.arange(source_count, dtype=jnp.int32))
    )
    picked = source_w[source_order].reshape(
        MERGED // per_lane, 2 * per_lane, row_share, hidden_width
    )
    outgoing = jnp.repeat(picked, copies, axis=0)
    arrived = lax.all_to_all(outgoing, "ctx", split_axis=0, concat_axis=2, tiled=True)
    pair_rows = arrived.reshape(per_lane, 2, row_share * ctx_count, hidden_width)
    coef_table = merge_coef[source_order].reshape(MERGED // per_lane, per_lane, 2)
    pair_coef = lax.dynamic_index_in_dim(coef_table, lane_group, 0, keepdims=False)
    lane_weights = (
        pair_coef[:, 0, None, None] * pair_rows[:, 0].astype(jnp.float32)
        + pair_coef[:, 1, None, None] * pair_rows[:, 1].astype(jnp.float32)
    ).astype(jnp.bfloat16)
    recv_hidden, recv_grad, recv_member = (
        lax.all_to_all(send_hidden, "ctx", split_axis=0, concat_axis=0, tiled=True),
        lax.all_to_all(send_grad, "ctx", split_axis=0, concat_axis=0, tiled=True),
        lax.all_to_all(send_member, "ctx", split_axis=0, concat_axis=0, tiled=True),
    )
    out_rows, back_rows, lane_grads = expert_rows(
        recv_hidden.reshape(-1, hidden_width),
        recv_grad.reshape(-1, out_width),
        recv_member.reshape(-1),
        lane_weights,
    )
    home_out, home_back = (
        lax.all_to_all(
            out_rows.astype(jnp.bfloat16).reshape(ctx_count, capacity, out_width),
            "ctx",
            split_axis=0,
            concat_axis=0,
            tiled=True,
        ),
        lax.all_to_all(
            back_rows.astype(jnp.bfloat16).reshape(ctx_count, capacity, hidden_width),
            "ctx",
            split_axis=0,
            concat_axis=0,
            tiled=True,
        ),
    )
    slot_out = jnp.concatenate(
        [home_out.reshape(-1, out_width), jnp.zeros((1, out_width), jnp.bfloat16)], axis=0
    )[slot_index].reshape(tok_count, top_count, out_width)
    hidden_grad = jnp.concatenate(
        [home_back.reshape(-1, hidden_width), jnp.zeros((1, hidden_width), jnp.bfloat16)], axis=0
    )[slot_index].reshape(1, tok_count, top_count, hidden_width)
    mixed = (
        jnp.sum(gate_probs[:, :, None] * slot_out.astype(jnp.float32), axis=1)
        .astype(jnp.bfloat16)
        .reshape(1, tok_count, out_width)
    )
    score_grad = jnp.einsum(
        "td,tkd->tk",
        out_grad.reshape(tok_count, out_width),
        slot_out,
        preferred_element_type=jnp.float32,
    )
    chosen_grad = gate_probs * (
        score_grad - jnp.sum(gate_probs * score_grad, axis=1, keepdims=True)
    )
    logit_grad = jnp.sum(pick_float * chosen_grad[:, :, None], axis=1)
    logit_half = logit_grad.astype(jnp.bfloat16)
    token_grad = (
        lax.dot_general(
            logit_half, router_w, (((1,), (1,)), ((), ())), preferred_element_type=jnp.float32
        )
        .astype(jnp.bfloat16)
        .reshape(1, tok_count, feature_count)
    )
    part_router_w = lax.dot_general(
        flat_x, logit_half, (((0,), (0,)), ((), ())), preferred_element_type=jnp.float32
    )
    part_router_b = jnp.sum(logit_grad, axis=0)
    arrived_grads = lax.all_to_all(
        lane_grads.reshape(per_lane, ctx_count, row_share, hidden_width),
        "ctx",
        split_axis=1,
        concat_axis=0,
        tiled=True,
    )
    merged_grad = (
        arrived_grads.reshape(MERGED // per_lane, copies, per_lane, row_share, hidden_width)
        .sum(axis=1)
        .reshape(MERGED, row_share, hidden_width)
    )
    source_grad = merged_grad[merge_map]
    coef_part = jnp.einsum(
        "edf,edf->e", source_grad, source_w.astype(jnp.float32), precision=lax.Precision.HIGHEST
    )
    summed = lax.psum_scatter(
        source_grad * merge_coef[:, None, None], "rep", scatter_dimension=2, tiled=True
    )
    source_w_grad = summed * grad_scale
    router_sum, bias_sum, coef_sum = lax.psum(
        (part_router_w, part_router_b, coef_part), ("ctx", "rep")
    )
    return (
        mixed,
        hidden_grad,
        token_grad,
        router_sum * grad_scale,
        bias_sum * grad_scale,
        coef_sum * grad_scale,
        source_w_grad,
    )


BF = jnp.bfloat16
F32 = jnp.float32
I32 = jnp.int32
TILE = 256


def cost(us):
    return pl.CostEstimate(flops=us * 10**9, bytes_accessed=us * 10**6, transcendentals=0)


def any_spec():
    return pl.BlockSpec(memory_space=pl.ANY)


def smem_spec():
    return pl.BlockSpec(memory_space=pltpu.SMEM)


def vmem_spec():
    return pl.BlockSpec(memory_space=pltpu.VMEM)


def params(mib):
    return pltpu.CompilerParams(vmem_limit_bytes=mib * 1024 * 1024)


def dot(a, b, dims):
    return lax.dot_general(a, b, (dims, ((), ())), preferred_element_type=F32)


def merge_start(map_ref, place_ref, src_ref, places, order_ref, count_ref, held, sems):
    half = held.shape[2]
    expert_order(map_ref, order_ref, count_ref)
    at = pl.ds(pl.multiple_of(place_ref[1] * half, half), half)
    copies, experts = [], []
    for j in range(places):
        for m in range(2):
            combo = 4 * j + 2 * place_ref[0] + m
            for n in range(2):
                expert = order_ref[2 * combo + n]
                experts.append(expert)
                i = len(copies)
                copies.append(
                    pltpu.make_async_copy(src_ref.at[expert, :, at], held.at[i], sems.at[i])
                )
                copies[-1].start()
    return copies, experts


def merge_finish(copies, experts, coef_ref, held, out_ref):
    halves, places = out_ref.shape[:2]
    for j in range(places):
        for m in range(2):
            i = 4 * j + 2 * m
            copies[i].wait()
            copies[i + 1].wait()
            one, two = coef_ref[experts[i]], coef_ref[experts[i + 1]]
            merged = (one * held[i].astype(F32) + two * held[i + 1].astype(F32)).astype(BF)
            for h in range(halves):
                out_ref[h, j, m] = merged


def expert_order(map_ref, order_ref, count_ref):
    @pl.loop(0, count_ref.shape[0])
    def _(g):
        count_ref[g] = 0

    @pl.loop(0, order_ref.shape[0])
    def _(e):
        g = map_ref[e]
        n = count_ref[g]
        order_ref[2 * g + n] = e
        count_ref[g] = n + 1


def hbm_spec():
    return pl.BlockSpec(memory_space=pltpu.HBM)


def hold(arrays, *after):
    count = len(arrays)
    return pl.pallas_call(
        lambda *refs: None,
        in_specs=[hbm_spec()] * count + [any_spec()] * len(after),
        out_specs=[hbm_spec()] * count,
        out_shape=[jax.ShapeDtypeStruct(a.shape, a.dtype) for a in arrays],
        input_output_aliases={i: i for i in range(count)},
        name="hold",
    )(*arrays, *after)


def column(row):
    size = row.shape[1]
    same = lax.broadcasted_iota(I32, (size, size), 0) == lax.broadcasted_iota(I32, (size, size), 1)
    return jnp.sum(jnp.where(same, row, jnp.zeros_like(row)), axis=1, keepdims=True)


def to_row(col):
    size = col.shape[0]
    same = lax.broadcasted_iota(I32, (size, size), 0) == lax.broadcasted_iota(I32, (size, size), 1)
    return jnp.sum(jnp.where(same, col, jnp.zeros_like(col)), axis=0, keepdims=True)


def picks_of(idx_ref, k, sources):
    tok = idx_ref.shape[1]
    return lax.broadcasted_iota(I32, (sources, tok), 0) == idx_ref[k : k + 1, :]


def prepare_kernel(
    capacity, lanes,
    combo_ref, coef_ref, place_ref, src_ref,
    xt_ref, rwt_ref, rb_ref, idx_ref, map_ref, hid_ref, og_ref,
    merged_ref, send_ref, gate_ref, pos_ref, slot_ref,
    order_ref, count_ref, held, sems,
):
    copies, experts = merge_start(
        combo_ref, place_ref, src_ref, merged_ref.shape[1], order_ref, count_ref, held, sems
    )
    top, tok = idx_ref.shape
    sources = rwt_ref.shape[0]
    slots, width = hid_ref.shape
    places = lanes * capacity
    logits = jnp.dot(rwt_ref[...], xt_ref[...], preferred_element_type=F32) + column(rb_ref[...])
    raised, merged = [], []
    combos = column(map_ref[...])
    for k in range(top):
        pick = picks_of(idx_ref, k, sources)
        chosen = jnp.sum(jnp.where(pick, logits, 0.0), axis=0, keepdims=True)
        raised.append(jnp.exp(chosen))
        merged.append(jnp.sum(jnp.where(pick, combos, 0), axis=0, keepdims=True))
    total = raised[0]
    for k in range(1, top):
        total = total + raised[k]
    gates = [r / total for r in raised]
    lane = [jnp.right_shift(g, 1) for g in merged]
    member = [jnp.bitwise_and(g, 1) for g in merged]
    onehot = [(lax.broadcasted_iota(I32, (lanes, tok), 0) == l).astype(F32) for l in lane]
    all_hot = onehot[0]
    for k in range(1, top):
        all_hot = all_hot + onehot[k]
    earlier = (
        lax.broadcasted_iota(I32, (tok, tok), 0) < lax.broadcasted_iota(I32, (tok, tok), 1)
    ).astype(BF)
    before = jnp.dot(all_hot.astype(BF), earlier, preferred_element_type=F32)
    position, back = [], []
    for k in range(top):
        rank = jnp.sum(before * onehot[k], axis=0, keepdims=True).astype(I32)
        before = before + onehot[k]
        position.append(jnp.where(rank < capacity, lane[k] * capacity + rank, -1))
        partner = jnp.bitwise_xor(lane[k], place_ref[2])
        back.append(jnp.where(rank < capacity, partner * capacity + rank, -1))
    gate_ref[...] = jnp.zeros_like(gate_ref)
    pos_ref[...] = jnp.full_like(pos_ref, -1)
    for k in range(top):
        gate_ref[k : k + 1, :] = gates[k]
        pos_ref[k : k + 1, :] = back[k]
    spot = jnp.zeros((8, slots), F32)
    for k in range(top):
        spread = (
            lax.broadcasted_iota(I32, (tok, slots), 1)
            == lax.broadcasted_iota(I32, (tok, slots), 0) * top + k
        ).astype(BF)
        kept = position[k] >= 0
        parts = [
            jnp.where(kept, lane[k], 0),
            jnp.where(kept, position[k] - lane[k] * capacity, 0),
            jnp.where(kept, 1, 0),
            member[k],
        ]
        stacked = jnp.concatenate(
            [p.astype(F32) for p in parts] + [jnp.zeros((4, tok), F32)], axis=0
        ).astype(BF)
        spot = spot + jnp.dot(stacked, spread, preferred_element_type=F32)
    spot = spot.astype(I32)
    slot_pos = jnp.where(spot[2:3] > 0, spot[0:1] * capacity + spot[1:2], -1)
    partner = jnp.bitwise_xor(spot[0:1], place_ref[2])
    slot_back = jnp.where(spot[2:3] > 0, partner * capacity + spot[1:2], -1)
    slot_ref[...] = jnp.broadcast_to(slot_back, slot_ref.shape)
    take = lax.broadcasted_iota(I32, (places, slots), 0) == slot_pos
    placed = jnp.sum(jnp.where(take, spot[3:4].astype(F32), 0.0), axis=1, keepdims=True)
    depth = og_ref.shape[1]
    send_ref[:, depth + width :] = jnp.broadcast_to(placed, (places, 128)).astype(BF)
    take = take.astype(BF)
    for n in range(0, width, TILE):
        rows = jnp.dot(take, hid_ref[:, n : n + TILE], preferred_element_type=F32)
        send_ref[:, depth + n : depth + n + TILE] = rows.astype(BF)
    takes = [
        (lax.broadcasted_iota(I32, (places, tok), 0) == position[k]).astype(BF) for k in range(top)
    ]
    columns = [column(g) for g in gates]
    for n in range(0, depth, TILE):
        og = og_ref[:, n : n + TILE].astype(F32)
        rows = jnp.zeros((places, TILE), F32)
        for k in range(top):
            rows = rows + jnp.dot(takes[k], (columns[k] * og).astype(BF), preferred_element_type=F32)
        send_ref[:, n : n + TILE] = rows.astype(BF)
    merge_finish(copies, experts, coef_ref, held, merged_ref)


def prepare(
    place, merge_map, merge_coef, source_w, xt, rwt, router_b, idx_t, hid, og, capacity, lanes
):
    count, rows, whole = source_w.shape
    slots, width = hid.shape
    tok = idx_t.shape[1]
    half, places = whole // 2, lanes // 2
    return pl.pallas_call(
        functools.partial(prepare_kernel, capacity, lanes),
        in_specs=[smem_spec()] * 3 + [any_spec()] + [vmem_spec()] * 7,
        out_specs=[vmem_spec()] * 5,
        out_shape=[
            jax.ShapeDtypeStruct((2, places, 2, rows, half), BF),
            jax.ShapeDtypeStruct((lanes * capacity, og.shape[1] + width + 128), BF),
            jax.ShapeDtypeStruct((8, tok), F32),
            jax.ShapeDtypeStruct((8, tok), I32),
            jax.ShapeDtypeStruct((8, slots), I32),
        ],
        scratch_shapes=[
            pltpu.SMEM((count,), I32),
            pltpu.SMEM((count // 2,), I32),
            pltpu.VMEM((4 * places, rows, half), BF),
            pltpu.SemaphoreType.DMA((4 * places,)),
        ],
        compiler_params=params(56),
        cost_estimate=cost(10),
        name="prepare",
    )(
        merge_map, merge_coef, place, source_w,
        xt, rwt, router_b[None, :], idx_t, merge_map[None, :], hid, og,
    )


def gather_rows(refs, keep):
    each = refs[0].shape[0]
    for d, ref in enumerate(refs):
        keep[d * each : (d + 1) * each, :] = ref[...]


def load_weights(core_ref, mine, other, w_ref, sems):
    core = core_ref[0]
    blocks, _, rows, _ = mine.shape
    copies = []
    for c in range(blocks):
        at = pl.ds(c * rows, rows)
        for n, part in enumerate((mine, other)):
            to = core if n == 0 else 1 - core
            i = 2 * c + n
            copies.append(
                pltpu.make_async_copy(part.at[c], w_ref.at[to, :, at, :], sems.at[i])
            )
    for copy in copies:
        copy.start()
    for copy in copies:
        copy.wait()


def lane_kernel(
    core_ref, me_ref, grd_ref, hid_ref, flag_ref, mine, other, *refs
):
    outs, (keep, w_ref, sems) = refs[:-3], refs[-3:]
    load_weights(core_ref, mine, other, w_ref, sems)
    half, depth = w_ref.shape[3], w_ref.shape[2]
    first = flag_ref[:, :1].astype(F32) == 0.0
    for n in range(0, depth, TILE):
        at = slice(n, n + TILE)
        both = [
            dot(hid_ref[:, :half], w_ref[0, m, at, :], ((1,), (1,)))
            + dot(hid_ref[:, half:], w_ref[1, m, at, :], ((1,), (1,)))
            for m in range(2)
        ]
        keep[:, at] = jnp.where(first, both[0], both[1]).astype(BF)
    for h in range(2):
        for n in range(0, half, TILE):
            at = slice(n, n + TILE)
            both = [dot(grd_ref[...], w_ref[h, m, :, at], ((1,), (0,))) for m in range(2)]
            to = depth + h * half + n
            keep[:, to : to + TILE] = jnp.where(first, both[0], both[1]).astype(BF)
    each = outs[0].shape[0]
    for d, out_ref in enumerate(outs):
        at = pl.ds(pl.multiple_of(jnp.bitwise_xor(me_ref[0], d) * each, each), each)
        out_ref[...] = keep[at, :]


def run_lane(core, me, rows, mine, other, lanes):
    blocks, members, share, half = mine.shape
    depth = share * blocks
    count = rows.shape[0]
    wide = (rows.shape[1] - 128) // 2
    part = (count // lanes, 2 * wide)
    return pl.pallas_call(
        lane_kernel,
        grid=(1,),
        in_specs=[
            smem_spec(),
            smem_spec(),
            pl.BlockSpec((count, wide), lambda i: (0, 0)),
            pl.BlockSpec((count, wide), lambda i: (0, 1)),
            pl.BlockSpec((count, 128), lambda i: (0, 2 * wide // 128)),
            any_spec(),
            any_spec(),
        ],
        out_specs=[pl.BlockSpec(part, lambda i: (0, 0))] * lanes,
        out_shape=[jax.ShapeDtypeStruct(part, BF)] * lanes,
        scratch_shapes=[
            pltpu.VMEM((count, 2 * wide), BF),
            pltpu.VMEM((2, members, depth, half), BF),
            pltpu.SemaphoreType.DMA((2 * blocks,)),
        ],
        compiler_params=params(60),
        cost_estimate=cost(20),
        name="lane_products",
    )(core, me, rows, rows, rows, mine, other)


def lane_grad_kernel(has_other, _, grd_ref, hid_ref, flag_ref, *refs):
    out_ref = refs[-1]
    chosen = flag_ref[:, :1].astype(F32) == pl.program_id(1).astype(F32)
    hid = jnp.where(chosen, hid_ref[...], jnp.zeros_like(hid_ref))
    blocks, _, _, rows, cols = out_ref.shape
    each = 2 if blocks % 2 == 0 and 2 * rows % 128 == 0 else blocks
    for n in range(0, blocks, each):
        part = dot(grd_ref[:, n * rows : (n + each) * rows], hid, ((0,), (0,)))
        part = part.reshape(each, rows, cols)
        if has_other:
            part = part + refs[0][n : n + each, 0, 0].astype(F32)
        out_ref[n : n + each, 0, 0] = part.astype(BF)


def lane_grads(core, rows, other, blocks, reps):
    count = rows.shape[0]
    width = (rows.shape[1] - 128) // 2
    cols = width // reps
    shape = (blocks, 2, 2, width // blocks, cols)
    block = pl.BlockSpec((blocks, 1, 1, width // blocks, cols), lambda y, m, s: (0, y, m, 0, 0))
    extra = [] if other is None else [other]
    return pl.pallas_call(
        functools.partial(lane_grad_kernel, other is not None),
        grid_spec=pltpu.PrefetchScalarGridSpec(
            num_scalar_prefetch=1,
            grid=(2, 2),
            in_specs=[
                pl.BlockSpec((count, width), lambda y, m, s: (0, 0)),
                pl.BlockSpec((count, cols), lambda y, m, s: (0, reps + 2 * y + s[0])),
                pl.BlockSpec((count, 128), lambda y, m, s: (0, 2 * width // 128)),
            ]
            + [block] * len(extra),
            out_specs=block,
        ),
        out_shape=jax.ShapeDtypeStruct(shape, BF),
        compiler_params=params(56),
        cost_estimate=cost(8),
        name="lane_grads_add" if extra else "lane_grads_first",
    )(core, rows, rows, rows, *extra)


def combine_kernel(og_ref, gate_ref, pos_ref, idx_ref, rwt_ref, xt_ref, *refs):
    homes, (mixed_ref, tg_ref, part_ref, out_ref) = refs[:-4], refs[-4:]
    gather_rows(homes, out_ref)
    places, width = out_ref.shape
    top, tok = idx_ref.shape
    sources, features = rwt_ref.shape
    takes = [
        (lax.broadcasted_iota(I32, (places, tok), 0) == pos_ref[k : k + 1, :]).astype(BF)
        for k in range(top)
    ]
    gates = [gate_ref[k : k + 1, :] for k in range(top)]
    columns = [column(g) for g in gates]
    scores = [jnp.zeros((tok, 1), F32) for _ in range(top)]
    for n in range(0, width, TILE):
        og = og_ref[:, n : n + TILE].astype(F32)
        rows = out_ref[:, n : n + TILE]
        mixed = jnp.zeros((tok, TILE), F32)
        for k in range(top):
            slot_out = dot(takes[k], rows, ((0,), (0,)))
            mixed = mixed + columns[k] * slot_out
            scores[k] = scores[k] + jnp.sum(og * slot_out, axis=1, keepdims=True)
        mixed_ref[:, n : n + TILE] = mixed.astype(BF)
    scores = [to_row(s) for s in scores]
    middle = gates[0] * scores[0]
    for k in range(1, top):
        middle = middle + gates[k] * scores[k]
    logit_grad = jnp.zeros((sources, tok), F32)
    for k in range(top):
        chosen_grad = gates[k] * (scores[k] - middle)
        logit_grad = logit_grad + jnp.where(picks_of(idx_ref, k, sources), chosen_grad, 0.0)
    logit_half = logit_grad.astype(BF)
    tg_ref[...] = dot(rwt_ref[...], logit_half, ((0,), (0,))).astype(BF)
    part_ref[...] = jnp.zeros_like(part_ref)
    part_ref[:, 0, :features] = dot(logit_half, xt_ref[...], ((1,), (1,)))
    bias = jnp.sum(logit_grad, axis=1, keepdims=True)
    last = part_ref.shape[2] - 128
    part_ref[:, 0, last:] = jnp.broadcast_to(bias, (sources, 128))


def combine(homes, og, gates, pos, idx_t, rwt, xt):
    sources, features = rwt.shape
    tok, width = og.shape
    each = homes[0].shape[0]
    whole = lambda a: pl.BlockSpec(a.shape, lambda i: (0,) * len(a.shape))
    outs = [
        jax.ShapeDtypeStruct(og.shape, BF),
        jax.ShapeDtypeStruct((features, tok), BF),
        jax.ShapeDtypeStruct((sources, 1, (features + 127) // 128 * 128 + 128), F32),
    ]
    return pl.pallas_call(
        combine_kernel,
        grid=(1,),
        in_specs=[whole(a) for a in (og, gates, pos, idx_t, rwt, xt)]
        + [pl.BlockSpec((each, width), lambda i: (0, 0))] * len(homes),
        out_specs=[whole(a) for a in outs],
        out_shape=outs,
        scratch_shapes=[pltpu.VMEM((len(homes) * each, width), BF)],
        compiler_params=params(56),
        cost_estimate=cost(5),
        name="combine",
    )(og, gates, pos, idx_t, rwt, xt, *homes)


def unplace_kernel(slot_ref, *refs):
    homes, (out_ref, back_ref) = refs[:-2], refs[-2:]
    gather_rows(homes, back_ref)
    places, width = back_ref.shape
    slots = slot_ref.shape[1]
    take = (lax.broadcasted_iota(I32, (places, slots), 0) == slot_ref[0:1, :]).astype(BF)
    for n in range(0, width, TILE):
        out_ref[:, n : n + TILE] = dot(take, back_ref[:, n : n + TILE], ((0,), (0,))).astype(BF)


def unplace(homes, slot_pos):
    each, width = homes[0].shape[0], homes[0].shape[1] // 2
    slots = slot_pos.shape[1]
    return pl.pallas_call(
        unplace_kernel,
        grid=(1,),
        in_specs=[pl.BlockSpec(slot_pos.shape, lambda i: (0, 0))]
        + [pl.BlockSpec((each, width), lambda i: (0, 1))] * len(homes),
        out_specs=pl.BlockSpec((slots, width), lambda i: (0, 0)),
        out_shape=jax.ShapeDtypeStruct((slots, width), BF),
        scratch_shapes=[pltpu.VMEM((len(homes) * each, width), BF)],
        compiler_params=params(56),
        cost_estimate=cost(4),
        name="unplace",
    )(slot_pos, *homes)


def coef_kernel(rep_ref, map_ref, src_ref, got_ref, out_ref, order_ref, count_ref, held, weights, sems):
    count, rows, cols = weights.shape
    at = pl.ds(pl.multiple_of(rep_ref[0] * cols, cols), cols)
    copies = [
        pltpu.make_async_copy(src_ref.at[:, :, at], weights, sems.at[0]),
        pltpu.make_async_copy(got_ref, held, sems.at[1]),
    ]
    for copy in copies:
        copy.start()
    expert_order(map_ref, order_ref, count_ref)
    for copy in copies:
        copy.wait()
    lane = lax.broadcasted_iota(I32, (8, 128), 1)

    def one(g, total):
        merged = held[0, g].astype(F32) + held[1, g].astype(F32)
        for n in range(2):
            expert = order_ref[2 * g + n]
            product = merged * weights[expert].astype(F32)
            folded = jnp.sum(product.reshape(rows // 8, 8, cols), axis=0)
            small = folded[:, :128]
            for c in range(128, cols, 128):
                small = small + folded[:, c : c + 128]
            small = jnp.sum(jnp.sum(small, axis=0, keepdims=True), axis=1, keepdims=True)
            total = total + jnp.where(lane == expert, small, 0.0)
        return total

    out_ref[...] = lax.fori_loop(0, count // 2, one, jnp.zeros((8, 128), F32))


def finish_kernel(scale, map_ref, coef_ref, got_ref, out_ref, order_ref, count_ref, held, ready, sems, more):
    count = ready.shape[0]

    def load(g):
        return pltpu.make_async_copy(got_ref.at[:, g], held.at[:, g], sems.at[g])

    def send(i):
        return pltpu.make_async_copy(ready.at[i], out_ref.at[order_ref[i]], more.at[i])

    @pl.loop(0, count // 2)
    def _(g):
        load(g).start()

    expert_order(map_ref, order_ref, count_ref)

    @pl.loop(0, count // 2)
    def _(g):
        load(g).wait()
        merged = held[0, g].astype(F32) + held[1, g].astype(F32)
        for n in range(2):
            i = 2 * g + n
            ready[i] = merged * (coef_ref[order_ref[i]] * scale)
            send(i).start()

    @pl.loop(0, count)
    def _(i):
        send(i).wait()


def coef_dots(rep_index, merge_map, source_w, arrived):
    count = source_w.shape[0]
    _, _, rows, cols = arrived.shape
    return pl.pallas_call(
        coef_kernel,
        in_specs=[smem_spec(), smem_spec(), hbm_spec(), hbm_spec()],
        out_specs=vmem_spec(),
        out_shape=jax.ShapeDtypeStruct((8, 128), F32),
        scratch_shapes=[
            pltpu.SMEM((count,), I32),
            pltpu.SMEM((count // 2,), I32),
            pltpu.VMEM(arrived.shape, BF),
            pltpu.VMEM((count, rows, cols), BF),
            pltpu.SemaphoreType.DMA((2,)),
        ],
        compiler_params=params(56),
        name="coef_dots",
    )(rep_index, merge_map, source_w, arrived)


def finish(merge_map, merge_coef, arrived, after, scale):
    count = merge_map.shape[0]
    _, _, rows, cols = arrived.shape
    return pl.pallas_call(
        lambda a, b, c, _, *refs: finish_kernel(scale, a, b, c, *refs),
        in_specs=[smem_spec(), smem_spec(), hbm_spec(), any_spec()],
        out_specs=hbm_spec(),
        out_shape=jax.ShapeDtypeStruct((count, rows, cols), F32),
        scratch_shapes=[
            pltpu.SMEM((count,), I32),
            pltpu.SMEM((count // 2,), I32),
            pltpu.VMEM(arrived.shape, BF),
            pltpu.VMEM((count, rows, cols), F32),
            pltpu.SemaphoreType.DMA((count // 2,)),
            pltpu.SemaphoreType.DMA((count,)),
        ],
        compiler_params=params(56),
        cost_estimate=cost(8),
        name="finish",
    )(merge_map, merge_coef, arrived, after)


def swap(x):
    return lax.ppermute(x, "core", [(0, 1), (1, 0)])


def on_pairs(
    tokens, router_w, router_b, hidden, teacher_idx, merge_map, merge_coef, source_w, out_grad
):
    places = lax.axis_size("place")
    blocks = 2 * places
    reps = 4
    tok = tokens.shape[1]
    features = tokens.shape[2]
    top = teacher_idx.shape[2]
    width = hidden.shape[3]
    depth = out_grad.shape[2]
    sources = router_w.shape[1]
    row_share = source_w.shape[1]
    lanes = 2 * places
    capacity = 5 * tok * top // (4 * blocks)
    scale = 1.0 / math.sqrt(tok * blocks * reps)
    half_i, place_i = lax.axis_index("half"), lax.axis_index("place")
    row_i, core_i = lax.axis_index("row"), lax.axis_index("core")
    ctx_i = half_i * places + place_i
    everyone = ("half", "place", "row", "core")
    devices = blocks * reps

    def stack(numbers):
        return jnp.stack([jnp.asarray(n, I32) for n in numbers])

    def later(*x):
        return swap(hold([jnp.zeros((8, 128), F32)], *x)[0])

    def trade(x, axes):
        return lax.all_to_all(x, axes, split_axis=0, concat_axis=0, tiled=True)

    xt = tokens.reshape(tok, features).T
    rwt = router_w.T
    idx_t = teacher_idx.reshape(tok, top).T
    og = out_grad.reshape(tok, depth)
    combos, send_rows, gates, pos, slot_pos = prepare(
        stack([row_i, core_i, 2 * place_i + row_i]), merge_map, merge_coef, source_w,
        xt, rwt, router_b, idx_t, hidden.reshape(tok * top, width), og, capacity, lanes,
    )
    rows = trade(send_rows.reshape(lanes, capacity, send_rows.shape[1]), ("place", "row"))
    rows = rows.reshape(send_rows.shape)
    (combos,) = hold([combos.reshape((blocks,) + combos.shape[2:])], rows)
    mine = trade(combos, ("half", "place"))
    (rows,) = hold([rows], later(rows))
    here = stack([core_i])
    first = lane_grads(stack([1 - core_i]), rows, None, blocks, reps)
    summed = lane_grads(here, rows, swap(first), blocks, reps)
    (mine,) = hold([mine], summed)
    (summed,) = hold([summed], mine)
    arrived = trade(
        summed.reshape(2 * blocks, 2, row_share, width // reps), ("half", "place", "row")
    )

    other = swap(mine)
    me = stack([2 * place_i + row_i])
    (rows,) = hold([rows], later(summed))
    parts = run_lane(here, me, rows, mine, other, lanes)
    home = [parts[0]] + [
        lax.ppermute(parts[d], ("place", "row"), [(i, i ^ d) for i in range(lanes)])
        for d in range(1, lanes)
    ]
    arrived = arrived.reshape(2, 2 * lanes, row_share, width // reps)
    dots = coef_dots(stack([2 * row_i + core_i]), merge_map, source_w, arrived)
    source_w_grad = finish(merge_map, merge_coef, arrived, dots, scale)
    home = hold(home, source_w_grad)
    mixed, token_grad, part = combine(home, og, gates, pos, idx_t, rwt, xt)
    part = jnp.sum(trade(part, everyone), axis=0)
    hidden_grad = unplace(home, slot_pos).reshape(1, tok, top, width)
    news = jnp.concatenate([part, dots[:1]], axis=1)
    (news,) = hold([news], hidden_grad)
    news = trade(jnp.broadcast_to(news[None], (devices,) + news.shape), everyone)
    end = part.shape[1]
    return (
        mixed.reshape(1, tok, depth),
        hidden_grad,
        token_grad.T.reshape(1, tok, features),
        news[:, 0, :features].T * scale,
        news[:, 0, end - 1] * scale,
        jnp.sum(news[:, 0, end : end + sources], axis=0) * scale,
        source_w_grad,
    )


def solution(mesh):
    if mesh.shape["ctx"] == 8 and mesh.shape["rep"] == 4:
        mesh = jax.sharding.Mesh(
            mesh.devices.reshape(2, 4, 2, 2), ("half", "place", "row", "core")
        )
        ctx, rep, body = ("half", "place"), ("row", "core"), on_pairs
    else:
        ctx, rep, body = "ctx", "rep", on_device
    in_specs = (
        P(rep, ctx, None),
        P(),
        P(),
        P(rep, ctx, None, None),
        P(rep, ctx, None),
        P(),
        P(),
        P(None, ctx, None),
        P(rep, ctx, None),
    )
    out_specs = (
        P(rep, ctx, None),
        P(rep, ctx, None, None),
        P(rep, ctx, None),
        P(),
        P(),
        P(),
        P(None, ctx, rep),
    )
    return jax.shard_map(
        body, mesh=mesh, in_specs=in_specs, out_specs=out_specs, check_vma=False
    )
```

```python
import functools
import math

import jax
import jax.numpy as jnp
from jax import lax
from jax.experimental import pallas as pl
from jax.experimental.pallas import tpu as pltpu
from jax.sharding import PartitionSpec as P

MERGED = 16


def expert_rows(rows_hidden, rows_grad, rows_member, lane_weights):
    row_count = rows_hidden.shape[0]
    out_rows = jnp.zeros((row_count, lane_weights.shape[1]), jnp.float32)
    back_rows = jnp.zeros((row_count, lane_weights.shape[2]), jnp.float32)
    grad_list = []
    for member_now in range(lane_weights.shape[0]):
        weight = lane_weights[member_now]
        selected = (rows_member == member_now)[:, None]
        forward = lax.dot_general(
            rows_hidden, weight, (((1,), (1,)), ((), ())), preferred_element_type=jnp.float32
        )
        out_rows = jnp.where(selected, forward, out_rows)
        backward = jnp.dot(rows_grad, weight, preferred_element_type=jnp.float32)
        back_rows = jnp.where(selected, backward, back_rows)
        masked = jnp.where(selected, rows_grad, jnp.zeros_like(rows_grad))
        grad_list.append(
            lax.dot_general(
                masked, rows_hidden, (((0,), (0,)), ((), ())), preferred_element_type=jnp.float32
            )
        )
    return (out_rows, back_rows, jnp.stack(grad_list))


def on_device(
    tokens, router_w, router_b, hidden, teacher_idx, merge_map, merge_coef, source_w, out_grad
):
    ctx_count = lax.axis_size("ctx")
    rep_count = lax.axis_size("rep")
    tok_count = tokens.shape[1]
    feature_count = tokens.shape[2]
    top_count = teacher_idx.shape[2]
    hidden_width = hidden.shape[3]
    out_width = out_grad.shape[2]
    source_count = router_w.shape[1]
    row_share = source_w.shape[1]
    per_lane = max(1, MERGED // ctx_count)
    copies = max(1, ctx_count // MERGED)
    capacity = 5 * tok_count * top_count // (4 * ctx_count)
    slot_count = tok_count * top_count
    grad_scale = 1.0 / math.sqrt(tok_count * ctx_count * rep_count)
    flat_x = tokens.reshape(tok_count, feature_count)
    logits = jnp.dot(flat_x, router_w, preferred_element_type=jnp.float32) + router_b
    choice_ids = teacher_idx.reshape(tok_count, top_count)
    pick_table = choice_ids[:, :, None] == jnp.arange(source_count, dtype=jnp.int32)[None, None, :]
    pick_float = pick_table.astype(jnp.float32)
    chosen = jnp.sum(pick_float * logits[:, None, :], axis=2)
    raised = jnp.exp(chosen)
    gate_probs = raised / jnp.sum(raised, axis=1, keepdims=True)
    merged_id = jnp.sum(jnp.where(pick_table, merge_map[None, None, :], 0), axis=2)
    position = lax.axis_index("ctx") * tok_count + jnp.arange(tok_count, dtype=jnp.int32)
    lane_id = merged_id // per_lane * copies + (position % copies)[:, None]
    member_id = (merged_id % per_lane).reshape(-1)
    lane_flat = lane_id.reshape(-1)
    onehot = (lane_flat[:, None] == jnp.arange(ctx_count, dtype=jnp.int32)[None, :]).astype(
        jnp.int32
    )
    before = jnp.cumsum(onehot, axis=0) - onehot
    slot_rank = jnp.sum(before * onehot, axis=1)
    is_kept = slot_rank < capacity
    slot_index = jnp.where(is_kept, lane_flat * capacity + slot_rank, ctx_count * capacity)
    slot_source = (
        jnp.full((ctx_count * capacity + 1,), slot_count, jnp.int32)
        .at[slot_index]
        .set(jnp.arange(slot_count, dtype=jnp.int32))[: ctx_count * capacity]
    )
    slot_grad = (gate_probs[:, :, None] * out_grad.reshape(tok_count, 1, out_width)).astype(
        jnp.bfloat16
    )
    pad_hidden = jnp.concatenate(
        [hidden.reshape(slot_count, hidden_width), jnp.zeros((1, hidden_width), jnp.bfloat16)],
        axis=0,
    )
    pad_grad = jnp.concatenate(
        [slot_grad.reshape(slot_count, out_width), jnp.zeros((1, out_width), jnp.bfloat16)], axis=0
    )
    pad_member = jnp.concatenate([member_id, jnp.zeros((1,), jnp.int32)], axis=0)
    send_hidden = pad_hidden[slot_source].reshape(ctx_count, capacity, hidden_width)
    send_grad = pad_grad[slot_source].reshape(ctx_count, capacity, out_width)
    send_member = pad_member[slot_source].reshape(ctx_count, capacity)
    lane_group = lax.axis_index("ctx") // copies
    same_group = merge_map[:, None] == merge_map[None, :]
    earlier = jnp.arange(source_count)[:, None] > jnp.arange(source_count)[None, :]
    member_rank = jnp.sum((same_group & earlier).astype(jnp.int32), axis=1)
    source_order = (
        jnp.zeros((source_count,), jnp.int32)
        .at[2 * merge_map + member_rank]
        .set(jnp.arange(source_count, dtype=jnp.int32))
    )
    picked = source_w[source_order].reshape(
        MERGED // per_lane, 2 * per_lane, row_share, hidden_width
    )
    outgoing = jnp.repeat(picked, copies, axis=0)
    arrived = lax.all_to_all(outgoing, "ctx", split_axis=0, concat_axis=2, tiled=True)
    pair_rows = arrived.reshape(per_lane, 2, row_share * ctx_count, hidden_width)
    coef_table = merge_coef[source_order].reshape(MERGED // per_lane, per_lane, 2)
    pair_coef = lax.dynamic_index_in_dim(coef_table, lane_group, 0, keepdims=False)
    lane_weights = (
        pair_coef[:, 0, None, None] * pair_rows[:, 0].astype(jnp.float32)
        + pair_coef[:, 1, None, None] * pair_rows[:, 1].astype(jnp.float32)
    ).astype(jnp.bfloat16)
    recv_hidden, recv_grad, recv_member = (
        lax.all_to_all(send_hidden, "ctx", split_axis=0, concat_axis=0, tiled=True),
        lax.all_to_all(send_grad, "ctx", split_axis=0, concat_axis=0, tiled=True),
        lax.all_to_all(send_member, "ctx", split_axis=0, concat_axis=0, tiled=True),
    )
    out_rows, back_rows, lane_grads = expert_rows(
        recv_hidden.reshape(-1, hidden_width),
        recv_grad.reshape(-1, out_width),
        recv_member.reshape(-1),
        lane_weights,
    )
    home_out, home_back = (
        lax.all_to_all(
            out_rows.astype(jnp.bfloat16).reshape(ctx_count, capacity, out_width),
            "ctx",
            split_axis=0,
            concat_axis=0,
            tiled=True,
        ),
        lax.all_to_all(
            back_rows.astype(jnp.bfloat16).reshape(ctx_count, capacity, hidden_width),
            "ctx",
            split_axis=0,
            concat_axis=0,
            tiled=True,
        ),
    )
    slot_out = jnp.concatenate(
        [home_out.reshape(-1, out_width), jnp.zeros((1, out_width), jnp.bfloat16)], axis=0
    )[slot_index].reshape(tok_count, top_count, out_width)
    hidden_grad = jnp.concatenate(
        [home_back.reshape(-1, hidden_width), jnp.zeros((1, hidden_width), jnp.bfloat16)], axis=0
    )[slot_index].reshape(1, tok_count, top_count, hidden_width)
    mixed = (
        jnp.sum(gate_probs[:, :, None] * slot_out.astype(jnp.float32), axis=1)
        .astype(jnp.bfloat16)
        .reshape(1, tok_count, out_width)
    )
    score_grad = jnp.einsum(
        "td,tkd->tk",
        out_grad.reshape(tok_count, out_width),
        slot_out,
        preferred_element_type=jnp.float32,
    )
    chosen_grad = gate_probs * (
        score_grad - jnp.sum(gate_probs * score_grad, axis=1, keepdims=True)
    )
    logit_grad = jnp.sum(pick_float * chosen_grad[:, :, None], axis=1)
    logit_half = logit_grad.astype(jnp.bfloat16)
    token_grad = (
        lax.dot_general(
            logit_half, router_w, (((1,), (1,)), ((), ())), preferred_element_type=jnp.float32
        )
        .astype(jnp.bfloat16)
        .reshape(1, tok_count, feature_count)
    )
    part_router_w = lax.dot_general(
        flat_x, logit_half, (((0,), (0,)), ((), ())), preferred_element_type=jnp.float32
    )
    part_router_b = jnp.sum(logit_grad, axis=0)
    arrived_grads = lax.all_to_all(
        lane_grads.reshape(per_lane, ctx_count, row_share, hidden_width),
        "ctx",
        split_axis=1,
        concat_axis=0,
        tiled=True,
    )
    merged_grad = (
        arrived_grads.reshape(MERGED // per_lane, copies, per_lane, row_share, hidden_width)
        .sum(axis=1)
        .reshape(MERGED, row_share, hidden_width)
    )
    source_grad = merged_grad[merge_map]
    coef_part = jnp.einsum(
        "edf,edf->e", source_grad, source_w.astype(jnp.float32), precision=lax.Precision.HIGHEST
    )
    summed = lax.psum_scatter(
        source_grad * merge_coef[:, None, None], "rep", scatter_dimension=2, tiled=True
    )
    source_w_grad = summed * grad_scale
    router_sum, bias_sum, coef_sum = lax.psum(
        (part_router_w, part_router_b, coef_part), ("ctx", "rep")
    )
    return (
        mixed,
        hidden_grad,
        token_grad,
        router_sum * grad_scale,
        bias_sum * grad_scale,
        coef_sum * grad_scale,
        source_w_grad,
    )


BF = jnp.bfloat16
F32 = jnp.float32
I32 = jnp.int32
TILE = 256


def cost(us):
    return pl.CostEstimate(flops=us * 10**9, bytes_accessed=us * 10**6, transcendentals=0)


def any_spec():
    return pl.BlockSpec(memory_space=pl.ANY)


def smem_spec():
    return pl.BlockSpec(memory_space=pltpu.SMEM)


def vmem_spec():
    return pl.BlockSpec(memory_space=pltpu.VMEM)


def params(mib):
    return pltpu.CompilerParams(vmem_limit_bytes=mib * 1024 * 1024)


def dot(a, b, dims):
    return lax.dot_general(a, b, (dims, ((), ())), preferred_element_type=F32)


def merge_start(map_ref, place_ref, src_ref, places, order_ref, count_ref, held, sems):
    half = held.shape[2]
    expert_order(map_ref, order_ref, count_ref)
    at = pl.ds(pl.multiple_of(place_ref[1] * half, half), half)
    copies, experts = [], []
    for j in range(places):
        for m in range(2):
            combo = 4 * j + 2 * place_ref[0] + m
            for n in range(2):
                expert = order_ref[2 * combo + n]
                experts.append(expert)
                i = len(copies)
                copies.append(
                    pltpu.make_async_copy(src_ref.at[expert, :, at], held.at[i], sems.at[i])
                )
                copies[-1].start()
    return copies, experts


def merge_finish(copies, experts, coef_ref, held, out_ref):
    halves, places = out_ref.shape[:2]
    for j in range(places):
        for m in range(2):
            i = 4 * j + 2 * m
            copies[i].wait()
            copies[i + 1].wait()
            one, two = coef_ref[experts[i]], coef_ref[experts[i + 1]]
            merged = (one * held[i].astype(F32) + two * held[i + 1].astype(F32)).astype(BF)
            for h in range(halves):
                out_ref[h, j, m] = merged


def expert_order(map_ref, order_ref, count_ref):
    @pl.loop(0, count_ref.shape[0])
    def _(g):
        count_ref[g] = 0

    @pl.loop(0, order_ref.shape[0])
    def _(e):
        g = map_ref[e]
        n = count_ref[g]
        order_ref[2 * g + n] = e
        count_ref[g] = n + 1


def hbm_spec():
    return pl.BlockSpec(memory_space=pltpu.HBM)


def hold(arrays, *after):
    count = len(arrays)
    return pl.pallas_call(
        lambda *refs: None,
        in_specs=[hbm_spec()] * count + [any_spec()] * len(after),
        out_specs=[hbm_spec()] * count,
        out_shape=[jax.ShapeDtypeStruct(a.shape, a.dtype) for a in arrays],
        input_output_aliases={i: i for i in range(count)},
        name="hold",
    )(*arrays, *after)


def column(row):
    size = row.shape[1]
    same = lax.broadcasted_iota(I32, (size, size), 0) == lax.broadcasted_iota(I32, (size, size), 1)
    return jnp.sum(jnp.where(same, row, jnp.zeros_like(row)), axis=1, keepdims=True)


def to_row(col):
    size = col.shape[0]
    same = lax.broadcasted_iota(I32, (size, size), 0) == lax.broadcasted_iota(I32, (size, size), 1)
    return jnp.sum(jnp.where(same, col, jnp.zeros_like(col)), axis=0, keepdims=True)


def picks_of(idx_ref, k, sources):
    tok = idx_ref.shape[1]
    return lax.broadcasted_iota(I32, (sources, tok), 0) == idx_ref[k : k + 1, :]


def prepare_kernel(
    capacity, lanes,
    combo_ref, coef_ref, place_ref, src_ref,
    xt_ref, rwt_ref, rb_ref, idx_ref, map_ref, hid_ref, og_ref,
    merged_ref, send_ref, gate_ref, pos_ref, slot_ref,
    order_ref, count_ref, held, sems,
):
    copies, experts = merge_start(
        combo_ref, place_ref, src_ref, merged_ref.shape[1], order_ref, count_ref, held, sems
    )
    top, tok = idx_ref.shape
    sources = rwt_ref.shape[0]
    slots, width = hid_ref.shape
    places = lanes * capacity
    logits = jnp.dot(rwt_ref[...], xt_ref[...], preferred_element_type=F32) + column(rb_ref[...])
    raised, merged = [], []
    combos = column(map_ref[...])
    for k in range(top):
        pick = picks_of(idx_ref, k, sources)
        chosen = jnp.sum(jnp.where(pick, logits, 0.0), axis=0, keepdims=True)
        raised.append(jnp.exp(chosen))
        merged.append(jnp.sum(jnp.where(pick, combos, 0), axis=0, keepdims=True))
    total = raised[0]
    for k in range(1, top):
        total = total + raised[k]
    gates = [r / total for r in raised]
    lane = [jnp.right_shift(g, 1) for g in merged]
    member = [jnp.bitwise_and(g, 1) for g in merged]
    onehot = [(lax.broadcasted_iota(I32, (lanes, tok), 0) == l).astype(F32) for l in lane]
    all_hot = onehot[0]
    for k in range(1, top):
        all_hot = all_hot + onehot[k]
    earlier = (
        lax.broadcasted_iota(I32, (tok, tok), 0) < lax.broadcasted_iota(I32, (tok, tok), 1)
    ).astype(BF)
    before = jnp.dot(all_hot.astype(BF), earlier, preferred_element_type=F32)
    position, back = [], []
    for k in range(top):
        rank = jnp.sum(before * onehot[k], axis=0, keepdims=True).astype(I32)
        before = before + onehot[k]
        position.append(jnp.where(rank < capacity, lane[k] * capacity + rank, -1))
        partner = jnp.bitwise_xor(lane[k], place_ref[2])
        back.append(jnp.where(rank < capacity, partner * capacity + rank, -1))
    gate_ref[...] = jnp.zeros_like(gate_ref)
    pos_ref[...] = jnp.full_like(pos_ref, -1)
    for k in range(top):
        gate_ref[k : k + 1, :] = gates[k]
        pos_ref[k : k + 1, :] = back[k]
    spot = jnp.zeros((8, slots), F32)
    for k in range(top):
        spread = (
            lax.broadcasted_iota(I32, (tok, slots), 1)
            == lax.broadcasted_iota(I32, (tok, slots), 0) * top + k
        ).astype(BF)
        kept = position[k] >= 0
        parts = [
            jnp.where(kept, lane[k], 0),
            jnp.where(kept, position[k] - lane[k] * capacity, 0),
            jnp.where(kept, 1, 0),
            member[k],
        ]
        stacked = jnp.concatenate(
            [p.astype(F32) for p in parts] + [jnp.zeros((4, tok), F32)], axis=0
        ).astype(BF)
        spot = spot + jnp.dot(stacked, spread, preferred_element_type=F32)
    spot = spot.astype(I32)
    slot_pos = jnp.where(spot[2:3] > 0, spot[0:1] * capacity + spot[1:2], -1)
    partner = jnp.bitwise_xor(spot[0:1], place_ref[2])
    slot_back = jnp.where(spot[2:3] > 0, partner * capacity + spot[1:2], -1)
    slot_ref[...] = jnp.broadcast_to(slot_back, slot_ref.shape)
    take = lax.broadcasted_iota(I32, (places, slots), 0) == slot_pos
    placed = jnp.sum(jnp.where(take, spot[3:4].astype(F32), 0.0), axis=1, keepdims=True)
    depth = og_ref.shape[1]
    send_ref[:, depth + width :] = jnp.broadcast_to(placed, (places, 128)).astype(BF)
    take = take.astype(BF)
    for n in range(0, width, TILE):
        rows = jnp.dot(take, hid_ref[:, n : n + TILE], preferred_element_type=F32)
        send_ref[:, depth + n : depth + n + TILE] = rows.astype(BF)
    takes = [
        (lax.broadcasted_iota(I32, (places, tok), 0) == position[k]).astype(BF) for k in range(top)
    ]
    columns = [column(g) for g in gates]
    for n in range(0, depth, TILE):
        og = og_ref[:, n : n + TILE].astype(F32)
        rows = jnp.zeros((places, TILE), F32)
        for k in range(top):
            rows = rows + jnp.dot(takes[k], (columns[k] * og).astype(BF), preferred_element_type=F32)
        send_ref[:, n : n + TILE] = rows.astype(BF)
    merge_finish(copies, experts, coef_ref, held, merged_ref)


def prepare(
    place, merge_map, merge_coef, source_w, xt, rwt, router_b, idx_t, hid, og, capacity, lanes
):
    count, rows, whole = source_w.shape
    slots, width = hid.shape
    tok = idx_t.shape[1]
    half, places = whole // 2, lanes // 2
    return pl.pallas_call(
        functools.partial(prepare_kernel, capacity, lanes),
        in_specs=[smem_spec()] * 3 + [any_spec()] + [vmem_spec()] * 7,
        out_specs=[vmem_spec()] * 5,
        out_shape=[
            jax.ShapeDtypeStruct((2, places, 2, rows, half), BF),
            jax.ShapeDtypeStruct((lanes * capacity, og.shape[1] + width + 128), BF),
            jax.ShapeDtypeStruct((8, tok), F32),
            jax.ShapeDtypeStruct((8, tok), I32),
            jax.ShapeDtypeStruct((8, slots), I32),
        ],
        scratch_shapes=[
            pltpu.SMEM((count,), I32),
            pltpu.SMEM((count // 2,), I32),
            pltpu.VMEM((4 * places, rows, half), BF),
            pltpu.SemaphoreType.DMA((4 * places,)),
        ],
        compiler_params=params(56),
        cost_estimate=cost(10),
        name="prepare",
    )(
        merge_map, merge_coef, place, source_w,
        xt, rwt, router_b[None, :], idx_t, merge_map[None, :], hid, og,
    )


def gather_rows(refs, keep):
    each = refs[0].shape[0]
    for d, ref in enumerate(refs):
        keep[d * each : (d + 1) * each, :] = ref[...]


def load_weights(core_ref, mine, other, w_ref, sems):
    core = core_ref[0]
    blocks, _, rows, _ = mine.shape
    copies = []
    for c in range(blocks):
        at = pl.ds(c * rows, rows)
        for n, part in enumerate((mine, other)):
            to = core if n == 0 else 1 - core
            i = 2 * c + n
            copies.append(
                pltpu.make_async_copy(part.at[c], w_ref.at[to, :, at, :], sems.at[i])
            )
    for copy in copies:
        copy.start()
    for copy in copies:
        copy.wait()


def lane_kernel(
    core_ref, me_ref, grd_ref, hid_ref, flag_ref, mine, other, *refs
):
    outs, (keep, w_ref, sems) = refs[:-3], refs[-3:]
    load_weights(core_ref, mine, other, w_ref, sems)
    half, depth = w_ref.shape[3], w_ref.shape[2]
    first = flag_ref[:, :1].astype(F32) == 0.0
    for n in range(0, depth, TILE):
        at = slice(n, n + TILE)
        both = [
            dot(hid_ref[:, :half], w_ref[0, m, at, :], ((1,), (1,)))
            + dot(hid_ref[:, half:], w_ref[1, m, at, :], ((1,), (1,)))
            for m in range(2)
        ]
        keep[:, at] = jnp.where(first, both[0], both[1]).astype(BF)
    for h in range(2):
        for n in range(0, half, TILE):
            at = slice(n, n + TILE)
            both = [dot(grd_ref[...], w_ref[h, m, :, at], ((1,), (0,))) for m in range(2)]
            to = depth + h * half + n
            keep[:, to : to + TILE] = jnp.where(first, both[0], both[1]).astype(BF)
    each = outs[0].shape[0]
    for d, out_ref in enumerate(outs):
        at = pl.ds(pl.multiple_of(jnp.bitwise_xor(me_ref[0], d) * each, each), each)
        out_ref[...] = keep[at, :]


def run_lane(core, me, rows, mine, other, lanes):
    blocks, members, share, half = mine.shape
    depth = share * blocks
    count = rows.shape[0]
    wide = (rows.shape[1] - 128) // 2
    part = (count // lanes, 2 * wide)
    return pl.pallas_call(
        lane_kernel,
        grid=(1,),
        in_specs=[
            smem_spec(),
            smem_spec(),
            pl.BlockSpec((count, wide), lambda i: (0, 0)),
            pl.BlockSpec((count, wide), lambda i: (0, 1)),
            pl.BlockSpec((count, 128), lambda i: (0, 2 * wide // 128)),
            any_spec(),
            any_spec(),
        ],
        out_specs=[pl.BlockSpec(part, lambda i: (0, 0))] * lanes,
        out_shape=[jax.ShapeDtypeStruct(part, BF)] * lanes,
        scratch_shapes=[
            pltpu.VMEM((count, 2 * wide), BF),
            pltpu.VMEM((2, members, depth, half), BF),
            pltpu.SemaphoreType.DMA((2 * blocks,)),
        ],
        compiler_params=params(60),
        cost_estimate=cost(20),
        name="lane_products",
    )(core, me, rows, rows, rows, mine, other)


def lane_grad_kernel(has_other, _, grd_ref, hid_ref, flag_ref, *refs):
    out_ref = refs[-1]
    chosen = flag_ref[:, :1].astype(F32) == pl.program_id(1).astype(F32)
    hid = jnp.where(chosen, hid_ref[...], jnp.zeros_like(hid_ref))
    blocks, _, _, rows, cols = out_ref.shape
    each = 2 if blocks % 2 == 0 and 2 * rows % 128 == 0 else blocks
    for n in range(0, blocks, each):
        part = dot(grd_ref[:, n * rows : (n + each) * rows], hid, ((0,), (0,)))
        part = part.reshape(each, rows, cols)
        if has_other:
            part = part + refs[0][n : n + each, 0, 0].astype(F32)
        out_ref[n : n + each, 0, 0] = part.astype(BF)


def lane_grads(core, rows, other, blocks, reps):
    count = rows.shape[0]
    width = (rows.shape[1] - 128) // 2
    cols = width // reps
    shape = (blocks, 2, 2, width // blocks, cols)
    block = pl.BlockSpec((blocks, 1, 1, width // blocks, cols), lambda y, m, s: (0, y, m, 0, 0))
    extra = [] if other is None else [other]
    return pl.pallas_call(
        functools.partial(lane_grad_kernel, other is not None),
        grid_spec=pltpu.PrefetchScalarGridSpec(
            num_scalar_prefetch=1,
            grid=(2, 2),
            in_specs=[
                pl.BlockSpec((count, width), lambda y, m, s: (0, 0)),
                pl.BlockSpec((count, cols), lambda y, m, s: (0, reps + 2 * y + s[0])),
                pl.BlockSpec((count, 128), lambda y, m, s: (0, 2 * width // 128)),
            ]
            + [block] * len(extra),
            out_specs=block,
        ),
        out_shape=jax.ShapeDtypeStruct(shape, BF),
        compiler_params=params(56),
        cost_estimate=cost(8),
        name="lane_grads_add" if extra else "lane_grads_first",
    )(core, rows, rows, rows, *extra)


def combine_kernel(og_ref, gate_ref, pos_ref, idx_ref, rwt_ref, xt_ref, *refs):
    homes, (mixed_ref, tg_ref, part_ref, out_ref) = refs[:-4], refs[-4:]
    gather_rows(homes, out_ref)
    places, width = out_ref.shape
    top, tok = idx_ref.shape
    sources, features = rwt_ref.shape
    takes = [
        (lax.broadcasted_iota(I32, (places, tok), 0) == pos_ref[k : k + 1, :]).astype(BF)
        for k in range(top)
    ]
    gates = [gate_ref[k : k + 1, :] for k in range(top)]
    columns = [column(g) for g in gates]
    scores = [jnp.zeros((tok, 1), F32) for _ in range(top)]
    for n in range(0, width, TILE):
        og = og_ref[:, n : n + TILE].astype(F32)
        rows = out_ref[:, n : n + TILE]
        mixed = jnp.zeros((tok, TILE), F32)
        for k in range(top):
            slot_out = dot(takes[k], rows, ((0,), (0,)))
            mixed = mixed + columns[k] * slot_out
            scores[k] = scores[k] + jnp.sum(og * slot_out, axis=1, keepdims=True)
        mixed_ref[:, n : n + TILE] = mixed.astype(BF)
    scores = [to_row(s) for s in scores]
    middle = gates[0] * scores[0]
    for k in range(1, top):
        middle = middle + gates[k] * scores[k]
    logit_grad = jnp.zeros((sources, tok), F32)
    for k in range(top):
        chosen_grad = gates[k] * (scores[k] - middle)
        logit_grad = logit_grad + jnp.where(picks_of(idx_ref, k, sources), chosen_grad, 0.0)
    logit_half = logit_grad.astype(BF)
    tg_ref[...] = dot(rwt_ref[...], logit_half, ((0,), (0,))).astype(BF)
    part_ref[...] = jnp.zeros_like(part_ref)
    part_ref[:, 0, :features] = dot(logit_half, xt_ref[...], ((1,), (1,)))
    bias = jnp.sum(logit_grad, axis=1, keepdims=True)
    last = part_ref.shape[2] - 128
    part_ref[:, 0, last:] = jnp.broadcast_to(bias, (sources, 128))


def combine(homes, og, gates, pos, idx_t, rwt, xt):
    sources, features = rwt.shape
    tok, width = og.shape
    each = homes[0].shape[0]
    whole = lambda a: pl.BlockSpec(a.shape, lambda i: (0,) * len(a.shape))
    outs = [
        jax.ShapeDtypeStruct(og.shape, BF),
        jax.ShapeDtypeStruct((features, tok), BF),
        jax.ShapeDtypeStruct((sources, 1, (features + 127) // 128 * 128 + 128), F32),
    ]
    return pl.pallas_call(
        combine_kernel,
        grid=(1,),
        in_specs=[whole(a) for a in (og, gates, pos, idx_t, rwt, xt)]
        + [pl.BlockSpec((each, width), lambda i: (0, 0))] * len(homes),
        out_specs=[whole(a) for a in outs],
        out_shape=outs,
        scratch_shapes=[pltpu.VMEM((len(homes) * each, width), BF)],
        compiler_params=params(56),
        cost_estimate=cost(5),
        name="combine",
    )(og, gates, pos, idx_t, rwt, xt, *homes)


def unplace_kernel(slot_ref, *refs):
    homes, (out_ref, back_ref) = refs[:-2], refs[-2:]
    gather_rows(homes, back_ref)
    places, width = back_ref.shape
    slots = slot_ref.shape[1]
    take = (lax.broadcasted_iota(I32, (places, slots), 0) == slot_ref[0:1, :]).astype(BF)
    for n in range(0, width, TILE):
        out_ref[:, n : n + TILE] = dot(take, back_ref[:, n : n + TILE], ((0,), (0,))).astype(BF)


def unplace(homes, slot_pos):
    each, width = homes[0].shape[0], homes[0].shape[1] // 2
    slots = slot_pos.shape[1]
    return pl.pallas_call(
        unplace_kernel,
        grid=(1,),
        in_specs=[pl.BlockSpec(slot_pos.shape, lambda i: (0, 0))]
        + [pl.BlockSpec((each, width), lambda i: (0, 1))] * len(homes),
        out_specs=pl.BlockSpec((slots, width), lambda i: (0, 0)),
        out_shape=jax.ShapeDtypeStruct((slots, width), BF),
        scratch_shapes=[pltpu.VMEM((len(homes) * each, width), BF)],
        compiler_params=params(56),
        cost_estimate=cost(4),
        name="unplace",
    )(slot_pos, *homes)


def coef_kernel(rep_ref, map_ref, src_ref, got_ref, out_ref, order_ref, count_ref, held, weights, sems):
    count, rows, cols = weights.shape
    at = pl.ds(pl.multiple_of(rep_ref[0] * cols, cols), cols)
    copies = [
        pltpu.make_async_copy(src_ref.at[:, :, at], weights, sems.at[0]),
        pltpu.make_async_copy(got_ref, held, sems.at[1]),
    ]
    for copy in copies:
        copy.start()
    expert_order(map_ref, order_ref, count_ref)
    for copy in copies:
        copy.wait()
    lane = lax.broadcasted_iota(I32, (8, 128), 1)

    def one(g, total):
        merged = held[0, g].astype(F32) + held[1, g].astype(F32)
        for n in range(2):
            expert = order_ref[2 * g + n]
            product = merged * weights[expert].astype(F32)
            folded = jnp.sum(product.reshape(rows // 8, 8, cols), axis=0)
            small = folded[:, :128]
            for c in range(128, cols, 128):
                small = small + folded[:, c : c + 128]
            small = jnp.sum(jnp.sum(small, axis=0, keepdims=True), axis=1, keepdims=True)
            total = total + jnp.where(lane == expert, small, 0.0)
        return total

    out_ref[...] = lax.fori_loop(0, count // 2, one, jnp.zeros((8, 128), F32))


def finish_kernel(scale, map_ref, coef_ref, got_ref, out_ref, order_ref, count_ref, held, ready, sems, more):
    count = ready.shape[0]

    def load(g):
        return pltpu.make_async_copy(got_ref.at[:, g], held.at[:, g], sems.at[g])

    def send(i):
        return pltpu.make_async_copy(ready.at[i], out_ref.at[order_ref[i]], more.at[i])

    @pl.loop(0, count // 2)
    def _(g):
        load(g).start()

    expert_order(map_ref, order_ref, count_ref)

    @pl.loop(0, count // 2)
    def _(g):
        load(g).wait()
        merged = held[0, g].astype(F32) + held[1, g].astype(F32)
        for n in range(2):
            i = 2 * g + n
            ready[i] = merged * (coef_ref[order_ref[i]] * scale)
            send(i).start()

    @pl.loop(0, count)
    def _(i):
        send(i).wait()


def coef_dots(rep_index, merge_map, source_w, arrived):
    count = source_w.shape[0]
    _, _, rows, cols = arrived.shape
    return pl.pallas_call(
        coef_kernel,
        in_specs=[smem_spec(), smem_spec(), hbm_spec(), hbm_spec()],
        out_specs=vmem_spec(),
        out_shape=jax.ShapeDtypeStruct((8, 128), F32),
        scratch_shapes=[
            pltpu.SMEM((count,), I32),
            pltpu.SMEM((count // 2,), I32),
            pltpu.VMEM(arrived.shape, BF),
            pltpu.VMEM((count, rows, cols), BF),
            pltpu.SemaphoreType.DMA((2,)),
        ],
        compiler_params=params(56),
        name="coef_dots",
    )(rep_index, merge_map, source_w, arrived)


def finish(merge_map, merge_coef, arrived, after, scale):
    count = merge_map.shape[0]
    _, _, rows, cols = arrived.shape
    return pl.pallas_call(
        lambda a, b, c, _, *refs: finish_kernel(scale, a, b, c, *refs),
        in_specs=[smem_spec(), smem_spec(), hbm_spec(), any_spec()],
        out_specs=hbm_spec(),
        out_shape=jax.ShapeDtypeStruct((count, rows, cols), F32),
        scratch_shapes=[
            pltpu.SMEM((count,), I32),
            pltpu.SMEM((count // 2,), I32),
            pltpu.VMEM(arrived.shape, BF),
            pltpu.VMEM((count, rows, cols), F32),
            pltpu.SemaphoreType.DMA((count // 2,)),
            pltpu.SemaphoreType.DMA((count,)),
        ],
        compiler_params=params(56),
        cost_estimate=cost(8),
        name="finish",
    )(merge_map, merge_coef, arrived, after)


def swap(x):
    return lax.ppermute(x, "core", [(0, 1), (1, 0)])


def on_pairs(
    tokens, router_w, router_b, hidden, teacher_idx, merge_map, merge_coef, source_w, out_grad
):
    places = lax.axis_size("place")
    blocks = 2 * places
    reps = 4
    tok = tokens.shape[1]
    features = tokens.shape[2]
    top = teacher_idx.shape[2]
    width = hidden.shape[3]
    depth = out_grad.shape[2]
    sources = router_w.shape[1]
    row_share = source_w.shape[1]
    lanes = 2 * places
    capacity = 5 * tok * top // (4 * blocks)
    scale = 1.0 / math.sqrt(tok * blocks * reps)
    half_i, place_i = lax.axis_index("half"), lax.axis_index("place")
    row_i, core_i = lax.axis_index("row"), lax.axis_index("core")
    ctx_i = half_i * places + place_i
    everyone = ("half", "place", "row", "core")
    devices = blocks * reps

    def stack(numbers):
        return jnp.stack([jnp.asarray(n, I32) for n in numbers])

    def later(*x):
        return swap(hold([jnp.zeros((8, 128), F32)], *x)[0])

    def trade(x, axes):
        return lax.all_to_all(x, axes, split_axis=0, concat_axis=0, tiled=True)

    xt = tokens.reshape(tok, features).T
    rwt = router_w.T
    idx_t = teacher_idx.reshape(tok, top).T
    og = out_grad.reshape(tok, depth)
    combos, send_rows, gates, pos, slot_pos = prepare(
        stack([row_i, core_i, 2 * place_i + row_i]), merge_map, merge_coef, source_w,
        xt, rwt, router_b, idx_t, hidden.reshape(tok * top, width), og, capacity, lanes,
    )
    rows = trade(send_rows.reshape(lanes, capacity, send_rows.shape[1]), ("place", "row"))
    rows = rows.reshape(send_rows.shape)
    (combos,) = hold([combos.reshape((blocks,) + combos.shape[2:])], rows)
    mine = trade(combos, ("half", "place"))
    (rows,) = hold([rows], later(rows))
    here = stack([core_i])
    first = lane_grads(stack([1 - core_i]), rows, None, blocks, reps)
    summed = lane_grads(here, rows, swap(first), blocks, reps)
    (mine,) = hold([mine], summed)
    (summed,) = hold([summed], mine)
    arrived = trade(
        summed.reshape(2 * blocks, 2, row_share, width // reps), ("half", "place", "row")
    )

    other = swap(mine)
    me = stack([2 * place_i + row_i])
    (rows,) = hold([rows], later(summed))
    parts = run_lane(here, me, rows, mine, other, lanes)

    def give(part, d):
        return lax.ppermute(part, ("place", "row"), [(i, i ^ d) for i in range(lanes)])

    home = {d: give(parts[d], d) for d in range(4, lanes)}
    home[0], home[1] = parts[0], give(parts[1], 1)
    for d in (2, 3):
        home[d] = give(hold([parts[d]], home[d - 1])[0], d)
    home = [home[d] for d in range(lanes)]
    (arrived,) = hold([arrived], home[3])
    arrived = arrived.reshape(2, 2 * lanes, row_share, width // reps)
    dots = coef_dots(stack([2 * row_i + core_i]), merge_map, source_w, arrived)
    source_w_grad = finish(merge_map, merge_coef, arrived, dots, scale)
    home = hold(home, source_w_grad)
    mixed, token_grad, part = combine(home, og, gates, pos, idx_t, rwt, xt)
    part = jnp.sum(trade(part, everyone), axis=0)
    hidden_grad = unplace(home, slot_pos).reshape(1, tok, top, width)
    news = jnp.concatenate([part, dots[:1]], axis=1)
    (news,) = hold([news], hidden_grad)
    news = trade(jnp.broadcast_to(news[None], (devices,) + news.shape), everyone)
    end = part.shape[1]
    return (
        mixed.reshape(1, tok, depth),
        hidden_grad,
        token_grad.T.reshape(1, tok, features),
        news[:, 0, :features].T * scale,
        news[:, 0, end - 1] * scale,
        jnp.sum(news[:, 0, end : end + sources], axis=0) * scale,
        source_w_grad,
    )


def solution(mesh):
    if mesh.shape["ctx"] == 8 and mesh.shape["rep"] == 4:
        mesh = jax.sharding.Mesh(
            mesh.devices.reshape(2, 4, 2, 2), ("half", "place", "row", "core")
        )
        ctx, rep, body = ("half", "place"), ("row", "core"), on_pairs
    else:
        ctx, rep, body = "ctx", "rep", on_device
    in_specs = (
        P(rep, ctx, None),
        P(),
        P(),
        P(rep, ctx, None, None),
        P(rep, ctx, None),
        P(),
        P(),
        P(None, ctx, None),
        P(rep, ctx, None),
    )
    out_specs = (
        P(rep, ctx, None),
        P(rep, ctx, None, None),
        P(rep, ctx, None),
        P(),
        P(),
        P(),
        P(None, ctx, rep),
    )
    return jax.shard_map(
        body, mesh=mesh, in_specs=in_specs, out_specs=out_specs, check_vma=False
    )
```

```python
import functools
import math

import jax
import jax.numpy as jnp
from jax import lax
from jax.experimental import pallas as pl
from jax.experimental.pallas import tpu as pltpu
from jax.sharding import PartitionSpec as P

MERGED = 16


def expert_rows(rows_hidden, rows_grad, rows_member, lane_weights):
    row_count = rows_hidden.shape[0]
    out_rows = jnp.zeros((row_count, lane_weights.shape[1]), jnp.float32)
    back_rows = jnp.zeros((row_count, lane_weights.shape[2]), jnp.float32)
    grad_list = []
    for member_now in range(lane_weights.shape[0]):
        weight = lane_weights[member_now]
        selected = (rows_member == member_now)[:, None]
        forward = lax.dot_general(
            rows_hidden, weight, (((1,), (1,)), ((), ())), preferred_element_type=jnp.float32
        )
        out_rows = jnp.where(selected, forward, out_rows)
        backward = jnp.dot(rows_grad, weight, preferred_element_type=jnp.float32)
        back_rows = jnp.where(selected, backward, back_rows)
        masked = jnp.where(selected, rows_grad, jnp.zeros_like(rows_grad))
        grad_list.append(
            lax.dot_general(
                masked, rows_hidden, (((0,), (0,)), ((), ())), preferred_element_type=jnp.float32
            )
        )
    return (out_rows, back_rows, jnp.stack(grad_list))


def on_device(
    tokens, router_w, router_b, hidden, teacher_idx, merge_map, merge_coef, source_w, out_grad
):
    ctx_count = lax.axis_size("ctx")
    rep_count = lax.axis_size("rep")
    tok_count = tokens.shape[1]
    feature_count = tokens.shape[2]
    top_count = teacher_idx.shape[2]
    hidden_width = hidden.shape[3]
    out_width = out_grad.shape[2]
    source_count = router_w.shape[1]
    row_share = source_w.shape[1]
    per_lane = max(1, MERGED // ctx_count)
    copies = max(1, ctx_count // MERGED)
    capacity = 5 * tok_count * top_count // (4 * ctx_count)
    slot_count = tok_count * top_count
    grad_scale = 1.0 / math.sqrt(tok_count * ctx_count * rep_count)
    flat_x = tokens.reshape(tok_count, feature_count)
    logits = jnp.dot(flat_x, router_w, preferred_element_type=jnp.float32) + router_b
    choice_ids = teacher_idx.reshape(tok_count, top_count)
    pick_table = choice_ids[:, :, None] == jnp.arange(source_count, dtype=jnp.int32)[None, None, :]
    pick_float = pick_table.astype(jnp.float32)
    chosen = jnp.sum(pick_float * logits[:, None, :], axis=2)
    raised = jnp.exp(chosen)
    gate_probs = raised / jnp.sum(raised, axis=1, keepdims=True)
    merged_id = jnp.sum(jnp.where(pick_table, merge_map[None, None, :], 0), axis=2)
    position = lax.axis_index("ctx") * tok_count + jnp.arange(tok_count, dtype=jnp.int32)
    lane_id = merged_id // per_lane * copies + (position % copies)[:, None]
    member_id = (merged_id % per_lane).reshape(-1)
    lane_flat = lane_id.reshape(-1)
    onehot = (lane_flat[:, None] == jnp.arange(ctx_count, dtype=jnp.int32)[None, :]).astype(
        jnp.int32
    )
    before = jnp.cumsum(onehot, axis=0) - onehot
    slot_rank = jnp.sum(before * onehot, axis=1)
    is_kept = slot_rank < capacity
    slot_index = jnp.where(is_kept, lane_flat * capacity + slot_rank, ctx_count * capacity)
    slot_source = (
        jnp.full((ctx_count * capacity + 1,), slot_count, jnp.int32)
        .at[slot_index]
        .set(jnp.arange(slot_count, dtype=jnp.int32))[: ctx_count * capacity]
    )
    slot_grad = (gate_probs[:, :, None] * out_grad.reshape(tok_count, 1, out_width)).astype(
        jnp.bfloat16
    )
    pad_hidden = jnp.concatenate(
        [hidden.reshape(slot_count, hidden_width), jnp.zeros((1, hidden_width), jnp.bfloat16)],
        axis=0,
    )
    pad_grad = jnp.concatenate(
        [slot_grad.reshape(slot_count, out_width), jnp.zeros((1, out_width), jnp.bfloat16)], axis=0
    )
    pad_member = jnp.concatenate([member_id, jnp.zeros((1,), jnp.int32)], axis=0)
    send_hidden = pad_hidden[slot_source].reshape(ctx_count, capacity, hidden_width)
    send_grad = pad_grad[slot_source].reshape(ctx_count, capacity, out_width)
    send_member = pad_member[slot_source].reshape(ctx_count, capacity)
    lane_group = lax.axis_index("ctx") // copies
    same_group = merge_map[:, None] == merge_map[None, :]
    earlier = jnp.arange(source_count)[:, None] > jnp.arange(source_count)[None, :]
    member_rank = jnp.sum((same_group & earlier).astype(jnp.int32), axis=1)
    source_order = (
        jnp.zeros((source_count,), jnp.int32)
        .at[2 * merge_map + member_rank]
        .set(jnp.arange(source_count, dtype=jnp.int32))
    )
    picked = source_w[source_order].reshape(
        MERGED // per_lane, 2 * per_lane, row_share, hidden_width
    )
    outgoing = jnp.repeat(picked, copies, axis=0)
    arrived = lax.all_to_all(outgoing, "ctx", split_axis=0, concat_axis=2, tiled=True)
    pair_rows = arrived.reshape(per_lane, 2, row_share * ctx_count, hidden_width)
    coef_table = merge_coef[source_order].reshape(MERGED // per_lane, per_lane, 2)
    pair_coef = lax.dynamic_index_in_dim(coef_table, lane_group, 0, keepdims=False)
    lane_weights = (
        pair_coef[:, 0, None, None] * pair_rows[:, 0].astype(jnp.float32)
        + pair_coef[:, 1, None, None] * pair_rows[:, 1].astype(jnp.float32)
    ).astype(jnp.bfloat16)
    recv_hidden, recv_grad, recv_member = (
        lax.all_to_all(send_hidden, "ctx", split_axis=0, concat_axis=0, tiled=True),
        lax.all_to_all(send_grad, "ctx", split_axis=0, concat_axis=0, tiled=True),
        lax.all_to_all(send_member, "ctx", split_axis=0, concat_axis=0, tiled=True),
    )
    out_rows, back_rows, lane_grads = expert_rows(
        recv_hidden.reshape(-1, hidden_width),
        recv_grad.reshape(-1, out_width),
        recv_member.reshape(-1),
        lane_weights,
    )
    home_out, home_back = (
        lax.all_to_all(
            out_rows.astype(jnp.bfloat16).reshape(ctx_count, capacity, out_width),
            "ctx",
            split_axis=0,
            concat_axis=0,
            tiled=True,
        ),
        lax.all_to_all(
            back_rows.astype(jnp.bfloat16).reshape(ctx_count, capacity, hidden_width),
            "ctx",
            split_axis=0,
            concat_axis=0,
            tiled=True,
        ),
    )
    slot_out = jnp.concatenate(
        [home_out.reshape(-1, out_width), jnp.zeros((1, out_width), jnp.bfloat16)], axis=0
    )[slot_index].reshape(tok_count, top_count, out_width)
    hidden_grad = jnp.concatenate(
        [home_back.reshape(-1, hidden_width), jnp.zeros((1, hidden_width), jnp.bfloat16)], axis=0
    )[slot_index].reshape(1, tok_count, top_count, hidden_width)
    mixed = (
        jnp.sum(gate_probs[:, :, None] * slot_out.astype(jnp.float32), axis=1)
        .astype(jnp.bfloat16)
        .reshape(1, tok_count, out_width)
    )
    score_grad = jnp.einsum(
        "td,tkd->tk",
        out_grad.reshape(tok_count, out_width),
        slot_out,
        preferred_element_type=jnp.float32,
    )
    chosen_grad = gate_probs * (
        score_grad - jnp.sum(gate_probs * score_grad, axis=1, keepdims=True)
    )
    logit_grad = jnp.sum(pick_float * chosen_grad[:, :, None], axis=1)
    logit_half = logit_grad.astype(jnp.bfloat16)
    token_grad = (
        lax.dot_general(
            logit_half, router_w, (((1,), (1,)), ((), ())), preferred_element_type=jnp.float32
        )
        .astype(jnp.bfloat16)
        .reshape(1, tok_count, feature_count)
    )
    part_router_w = lax.dot_general(
        flat_x, logit_half, (((0,), (0,)), ((), ())), preferred_element_type=jnp.float32
    )
    part_router_b = jnp.sum(logit_grad, axis=0)
    arrived_grads = lax.all_to_all(
        lane_grads.reshape(per_lane, ctx_count, row_share, hidden_width),
        "ctx",
        split_axis=1,
        concat_axis=0,
        tiled=True,
    )
    merged_grad = (
        arrived_grads.reshape(MERGED // per_lane, copies, per_lane, row_share, hidden_width)
        .sum(axis=1)
        .reshape(MERGED, row_share, hidden_width)
    )
    source_grad = merged_grad[merge_map]
    coef_part = jnp.einsum(
        "edf,edf->e", source_grad, source_w.astype(jnp.float32), precision=lax.Precision.HIGHEST
    )
    summed = lax.psum_scatter(
        source_grad * merge_coef[:, None, None], "rep", scatter_dimension=2, tiled=True
    )
    source_w_grad = summed * grad_scale
    router_sum, bias_sum, coef_sum = lax.psum(
        (part_router_w, part_router_b, coef_part), ("ctx", "rep")
    )
    return (
        mixed,
        hidden_grad,
        token_grad,
        router_sum * grad_scale,
        bias_sum * grad_scale,
        coef_sum * grad_scale,
        source_w_grad,
    )


BF = jnp.bfloat16
F32 = jnp.float32
I32 = jnp.int32
TILE = 256


def cost(us):
    return pl.CostEstimate(flops=us * 10**9, bytes_accessed=us * 10**6, transcendentals=0)


def any_spec():
    return pl.BlockSpec(memory_space=pl.ANY)


def smem_spec():
    return pl.BlockSpec(memory_space=pltpu.SMEM)


def vmem_spec():
    return pl.BlockSpec(memory_space=pltpu.VMEM)


def params(mib):
    return pltpu.CompilerParams(vmem_limit_bytes=mib * 1024 * 1024)


def dot(a, b, dims):
    return lax.dot_general(a, b, (dims, ((), ())), preferred_element_type=F32)


def merge_start(map_ref, place_ref, src_ref, places, order_ref, count_ref, held, sems):
    half = held.shape[2]
    expert_order(map_ref, order_ref, count_ref)
    at = pl.ds(pl.multiple_of(place_ref[1] * half, half), half)
    copies, experts = [], []
    for j in range(places):
        for m in range(2):
            combo = 4 * j + 2 * place_ref[0] + m
            for n in range(2):
                expert = order_ref[2 * combo + n]
                experts.append(expert)
                i = len(copies)
                copies.append(
                    pltpu.make_async_copy(src_ref.at[expert, :, at], held.at[i], sems.at[i])
                )
                copies[-1].start()
    return copies, experts


def merge_finish(copies, experts, coef_ref, held, out_ref):
    halves, places = out_ref.shape[:2]
    for j in range(places):
        for m in range(2):
            i = 4 * j + 2 * m
            copies[i].wait()
            copies[i + 1].wait()
            one, two = coef_ref[experts[i]], coef_ref[experts[i + 1]]
            merged = (one * held[i].astype(F32) + two * held[i + 1].astype(F32)).astype(BF)
            for h in range(halves):
                out_ref[h, j, m] = merged


def expert_order(map_ref, order_ref, count_ref):
    @pl.loop(0, count_ref.shape[0])
    def _(g):
        count_ref[g] = 0

    @pl.loop(0, order_ref.shape[0])
    def _(e):
        g = map_ref[e]
        n = count_ref[g]
        order_ref[2 * g + n] = e
        count_ref[g] = n + 1


def hbm_spec():
    return pl.BlockSpec(memory_space=pltpu.HBM)


def hold(arrays, *after):
    count = len(arrays)
    return pl.pallas_call(
        lambda *refs: None,
        in_specs=[hbm_spec()] * count + [any_spec()] * len(after),
        out_specs=[hbm_spec()] * count,
        out_shape=[jax.ShapeDtypeStruct(a.shape, a.dtype) for a in arrays],
        input_output_aliases={i: i for i in range(count)},
        name="hold",
    )(*arrays, *after)


def column(row):
    size = row.shape[1]
    same = lax.broadcasted_iota(I32, (size, size), 0) == lax.broadcasted_iota(I32, (size, size), 1)
    return jnp.sum(jnp.where(same, row, jnp.zeros_like(row)), axis=1, keepdims=True)


def to_row(col):
    size = col.shape[0]
    same = lax.broadcasted_iota(I32, (size, size), 0) == lax.broadcasted_iota(I32, (size, size), 1)
    return jnp.sum(jnp.where(same, col, jnp.zeros_like(col)), axis=0, keepdims=True)


def picks_of(idx_ref, k, sources):
    tok = idx_ref.shape[1]
    return lax.broadcasted_iota(I32, (sources, tok), 0) == idx_ref[k : k + 1, :]


def prepare_kernel(
    capacity, lanes,
    combo_ref, coef_ref, place_ref, src_ref,
    xt_ref, rwt_ref, rb_ref, idx_ref, map_ref, hid_ref, og_ref,
    merged_ref, send_ref, gate_ref, pos_ref, slot_ref,
    order_ref, count_ref, held, sems,
):
    copies, experts = merge_start(
        combo_ref, place_ref, src_ref, merged_ref.shape[1], order_ref, count_ref, held, sems
    )
    top, tok = idx_ref.shape
    sources = rwt_ref.shape[0]
    slots, width = hid_ref.shape
    places = lanes * capacity
    logits = jnp.dot(rwt_ref[...], xt_ref[...], preferred_element_type=F32) + column(rb_ref[...])
    raised, merged = [], []
    combos = column(map_ref[...])
    for k in range(top):
        pick = picks_of(idx_ref, k, sources)
        chosen = jnp.sum(jnp.where(pick, logits, 0.0), axis=0, keepdims=True)
        raised.append(jnp.exp(chosen))
        merged.append(jnp.sum(jnp.where(pick, combos, 0), axis=0, keepdims=True))
    total = raised[0]
    for k in range(1, top):
        total = total + raised[k]
    gates = [r / total for r in raised]
    lane = [jnp.right_shift(g, 1) for g in merged]
    member = [jnp.bitwise_and(g, 1) for g in merged]
    onehot = [(lax.broadcasted_iota(I32, (lanes, tok), 0) == l).astype(F32) for l in lane]
    all_hot = onehot[0]
    for k in range(1, top):
        all_hot = all_hot + onehot[k]
    earlier = (
        lax.broadcasted_iota(I32, (tok, tok), 0) < lax.broadcasted_iota(I32, (tok, tok), 1)
    ).astype(BF)
    before = jnp.dot(all_hot.astype(BF), earlier, preferred_element_type=F32)
    position, back = [], []
    for k in range(top):
        rank = jnp.sum(before * onehot[k], axis=0, keepdims=True).astype(I32)
        before = before + onehot[k]
        position.append(jnp.where(rank < capacity, lane[k] * capacity + rank, -1))
        partner = jnp.bitwise_xor(lane[k], place_ref[2])
        back.append(jnp.where(rank < capacity, partner * capacity + rank, -1))
    gate_ref[...] = jnp.zeros_like(gate_ref)
    pos_ref[...] = jnp.full_like(pos_ref, -1)
    for k in range(top):
        gate_ref[k : k + 1, :] = gates[k]
        pos_ref[k : k + 1, :] = back[k]
    spot = jnp.zeros((8, slots), F32)
    for k in range(top):
        spread = (
            lax.broadcasted_iota(I32, (tok, slots), 1)
            == lax.broadcasted_iota(I32, (tok, slots), 0) * top + k
        ).astype(BF)
        kept = position[k] >= 0
        parts = [
            jnp.where(kept, lane[k], 0),
            jnp.where(kept, position[k] - lane[k] * capacity, 0),
            jnp.where(kept, 1, 0),
            member[k],
        ]
        stacked = jnp.concatenate(
            [p.astype(F32) for p in parts] + [jnp.zeros((4, tok), F32)], axis=0
        ).astype(BF)
        spot = spot + jnp.dot(stacked, spread, preferred_element_type=F32)
    spot = spot.astype(I32)
    slot_pos = jnp.where(spot[2:3] > 0, spot[0:1] * capacity + spot[1:2], -1)
    slot_ref[...] = jnp.broadcast_to(slot_pos, slot_ref.shape)
    take = lax.broadcasted_iota(I32, (places, slots), 0) == slot_pos
    placed = jnp.sum(jnp.where(take, spot[3:4].astype(F32), 0.0), axis=1, keepdims=True)
    depth = og_ref.shape[1]
    send_ref[:, depth + width :] = jnp.broadcast_to(placed, (places, 128)).astype(BF)
    take = take.astype(BF)
    for n in range(0, width, TILE):
        rows = jnp.dot(take, hid_ref[:, n : n + TILE], preferred_element_type=F32)
        send_ref[:, depth + n : depth + n + TILE] = rows.astype(BF)
    takes = [
        (lax.broadcasted_iota(I32, (places, tok), 0) == position[k]).astype(BF) for k in range(top)
    ]
    columns = [column(g) for g in gates]
    for n in range(0, depth, TILE):
        og = og_ref[:, n : n + TILE].astype(F32)
        rows = jnp.zeros((places, TILE), F32)
        for k in range(top):
            rows = rows + jnp.dot(takes[k], (columns[k] * og).astype(BF), preferred_element_type=F32)
        send_ref[:, n : n + TILE] = rows.astype(BF)
    merge_finish(copies, experts, coef_ref, held, merged_ref)


def prepare(
    place, merge_map, merge_coef, source_w, xt, rwt, router_b, idx_t, hid, og, capacity, lanes
):
    count, rows, whole = source_w.shape
    slots, width = hid.shape
    tok = idx_t.shape[1]
    half, places = whole // 2, lanes // 2
    return pl.pallas_call(
        functools.partial(prepare_kernel, capacity, lanes),
        in_specs=[smem_spec()] * 3 + [any_spec()] + [vmem_spec()] * 7,
        out_specs=[vmem_spec()] * 5,
        out_shape=[
            jax.ShapeDtypeStruct((2, places, 2, rows, half), BF),
            jax.ShapeDtypeStruct((lanes * capacity, og.shape[1] + width + 128), BF),
            jax.ShapeDtypeStruct((8, tok), F32),
            jax.ShapeDtypeStruct((8, tok), I32),
            jax.ShapeDtypeStruct((8, slots), I32),
        ],
        scratch_shapes=[
            pltpu.SMEM((count,), I32),
            pltpu.SMEM((count // 2,), I32),
            pltpu.VMEM((4 * places, rows, half), BF),
            pltpu.SemaphoreType.DMA((4 * places,)),
        ],
        compiler_params=params(56),
        cost_estimate=cost(10),
        name="prepare",
    )(
        merge_map, merge_coef, place, source_w,
        xt, rwt, router_b[None, :], idx_t, merge_map[None, :], hid, og,
    )


def gather_rows(refs, keep):
    each = refs[0].shape[0]
    for d, ref in enumerate(refs):
        keep[d * each : (d + 1) * each, :] = ref[...]


def load_weights(core_ref, mine, other, w_ref, sems):
    core = core_ref[0]
    blocks, _, rows, _ = mine.shape
    copies = []
    for c in range(blocks):
        at = pl.ds(c * rows, rows)
        for n, part in enumerate((mine, other)):
            to = core if n == 0 else 1 - core
            i = 2 * c + n
            copies.append(
                pltpu.make_async_copy(part.at[c], w_ref.at[to, :, at, :], sems.at[i])
            )
    for copy in copies:
        copy.start()
    for copy in copies:
        copy.wait()


def lane_kernel(
    core_ref, me_ref, grd_ref, hid_ref, flag_ref, mine, other, *refs
):
    outs, (back_ref, keep, w_ref, sems) = refs[:-4], refs[-4:]
    load_weights(core_ref, mine, other, w_ref, sems)
    half, depth = w_ref.shape[3], w_ref.shape[2]
    first = flag_ref[:, :1].astype(F32) == 0.0
    for n in range(0, depth, TILE):
        at = slice(n, n + TILE)
        both = [
            dot(hid_ref[:, :half], w_ref[0, m, at, :], ((1,), (1,)))
            + dot(hid_ref[:, half:], w_ref[1, m, at, :], ((1,), (1,)))
            for m in range(2)
        ]
        keep[:, at] = jnp.where(first, both[0], both[1]).astype(BF)
    for h in range(2):
        for n in range(0, half, TILE):
            at = slice(n, n + TILE)
            both = [dot(grd_ref[...], w_ref[h, m, :, at], ((1,), (0,))) for m in range(2)]
            to = h * half + n
            back_ref[:, to : to + TILE] = jnp.where(first, both[0], both[1]).astype(BF)
    each = outs[0].shape[0]
    for d, out_ref in enumerate(outs):
        at = pl.ds(pl.multiple_of(jnp.bitwise_xor(me_ref[0], d) * each, each), each)
        out_ref[...] = keep[at, :]


def run_lane(core, me, rows, mine, other, lanes):
    blocks, members, share, half = mine.shape
    depth = share * blocks
    count = rows.shape[0]
    wide = (rows.shape[1] - 128) // 2
    part = (count // lanes, wide)
    return pl.pallas_call(
        lane_kernel,
        grid=(1,),
        in_specs=[
            smem_spec(),
            smem_spec(),
            pl.BlockSpec((count, wide), lambda i: (0, 0)),
            pl.BlockSpec((count, wide), lambda i: (0, 1)),
            pl.BlockSpec((count, 128), lambda i: (0, 2 * wide // 128)),
            any_spec(),
            any_spec(),
        ],
        out_specs=[pl.BlockSpec(part, lambda i: (0, 0))] * lanes
        + [pl.BlockSpec((count, wide), lambda i: (0, 0))],
        out_shape=[jax.ShapeDtypeStruct(part, BF)] * lanes
        + [jax.ShapeDtypeStruct((count, wide), BF)],
        scratch_shapes=[
            pltpu.VMEM((count, wide), BF),
            pltpu.VMEM((2, members, depth, half), BF),
            pltpu.SemaphoreType.DMA((2 * blocks,)),
        ],
        compiler_params=params(60),
        cost_estimate=cost(20),
        name="lane_products",
    )(core, me, rows, rows, rows, mine, other)


def lane_grad_kernel(has_other, _, grd_ref, hid_ref, flag_ref, *refs):
    out_ref = refs[-1]
    chosen = flag_ref[:, :1].astype(F32) == pl.program_id(1).astype(F32)
    hid = jnp.where(chosen, hid_ref[...], jnp.zeros_like(hid_ref))
    blocks, _, _, rows, cols = out_ref.shape
    each = 2 if blocks % 2 == 0 and 2 * rows % 128 == 0 else blocks
    for n in range(0, blocks, each):
        part = dot(grd_ref[:, n * rows : (n + each) * rows], hid, ((0,), (0,)))
        part = part.reshape(each, rows, cols)
        if has_other:
            part = part + refs[0][n : n + each, 0, 0].astype(F32)
        out_ref[n : n + each, 0, 0] = part.astype(BF)


def lane_grads(core, rows, other, blocks, reps):
    count = rows.shape[0]
    width = (rows.shape[1] - 128) // 2
    cols = width // reps
    shape = (blocks, 2, 2, width // blocks, cols)
    block = pl.BlockSpec((blocks, 1, 1, width // blocks, cols), lambda y, m, s: (0, y, m, 0, 0))
    extra = [] if other is None else [other]
    return pl.pallas_call(
        functools.partial(lane_grad_kernel, other is not None),
        grid_spec=pltpu.PrefetchScalarGridSpec(
            num_scalar_prefetch=1,
            grid=(2, 2),
            in_specs=[
                pl.BlockSpec((count, width), lambda y, m, s: (0, 0)),
                pl.BlockSpec((count, cols), lambda y, m, s: (0, reps + 2 * y + s[0])),
                pl.BlockSpec((count, 128), lambda y, m, s: (0, 2 * width // 128)),
            ]
            + [block] * len(extra),
            out_specs=block,
        ),
        out_shape=jax.ShapeDtypeStruct(shape, BF),
        compiler_params=params(56),
        cost_estimate=cost(8),
        name="lane_grads_add" if extra else "lane_grads_first",
    )(core, rows, rows, rows, *extra)


def combine_kernel(og_ref, gate_ref, pos_ref, idx_ref, rwt_ref, xt_ref, *refs):
    homes, (mixed_ref, tg_ref, part_ref, out_ref) = refs[:-4], refs[-4:]
    gather_rows(homes, out_ref)
    places, width = out_ref.shape
    top, tok = idx_ref.shape
    sources, features = rwt_ref.shape
    takes = [
        (lax.broadcasted_iota(I32, (places, tok), 0) == pos_ref[k : k + 1, :]).astype(BF)
        for k in range(top)
    ]
    gates = [gate_ref[k : k + 1, :] for k in range(top)]
    columns = [column(g) for g in gates]
    scores = [jnp.zeros((tok, 1), F32) for _ in range(top)]
    for n in range(0, width, TILE):
        og = og_ref[:, n : n + TILE].astype(F32)
        rows = out_ref[:, n : n + TILE]
        mixed = jnp.zeros((tok, TILE), F32)
        for k in range(top):
            slot_out = dot(takes[k], rows, ((0,), (0,)))
            mixed = mixed + columns[k] * slot_out
            scores[k] = scores[k] + jnp.sum(og * slot_out, axis=1, keepdims=True)
        mixed_ref[:, n : n + TILE] = mixed.astype(BF)
    scores = [to_row(s) for s in scores]
    middle = gates[0] * scores[0]
    for k in range(1, top):
        middle = middle + gates[k] * scores[k]
    logit_grad = jnp.zeros((sources, tok), F32)
    for k in range(top):
        chosen_grad = gates[k] * (scores[k] - middle)
        logit_grad = logit_grad + jnp.where(picks_of(idx_ref, k, sources), chosen_grad, 0.0)
    logit_half = logit_grad.astype(BF)
    tg_ref[...] = dot(rwt_ref[...], logit_half, ((0,), (0,))).astype(BF)
    part_ref[...] = jnp.zeros_like(part_ref)
    part_ref[:, 0, :features] = dot(logit_half, xt_ref[...], ((1,), (1,)))
    bias = jnp.sum(logit_grad, axis=1, keepdims=True)
    last = part_ref.shape[2] - 128
    part_ref[:, 0, last:] = jnp.broadcast_to(bias, (sources, 128))


def combine(homes, og, gates, pos, idx_t, rwt, xt):
    sources, features = rwt.shape
    tok, width = og.shape
    each = homes[0].shape[0]
    whole = lambda a: pl.BlockSpec(a.shape, lambda i: (0,) * len(a.shape))
    outs = [
        jax.ShapeDtypeStruct(og.shape, BF),
        jax.ShapeDtypeStruct((features, tok), BF),
        jax.ShapeDtypeStruct((sources, 1, (features + 127) // 128 * 128 + 128), F32),
    ]
    return pl.pallas_call(
        combine_kernel,
        grid=(1,),
        in_specs=[whole(a) for a in (og, gates, pos, idx_t, rwt, xt)]
        + [pl.BlockSpec((each, width), lambda i: (0, 0))] * len(homes),
        out_specs=[whole(a) for a in outs],
        out_shape=outs,
        scratch_shapes=[pltpu.VMEM((len(homes) * each, width), BF)],
        compiler_params=params(56),
        cost_estimate=cost(5),
        name="combine",
    )(og, gates, pos, idx_t, rwt, xt, *homes)


def unplace_kernel(slot_ref, back_ref, out_ref):
    places, width = back_ref.shape
    slots = slot_ref.shape[1]
    take = (lax.broadcasted_iota(I32, (places, slots), 0) == slot_ref[0:1, :]).astype(BF)
    for n in range(0, width, TILE):
        out_ref[:, n : n + TILE] = dot(take, back_ref[:, n : n + TILE], ((0,), (0,))).astype(BF)


def unplace(home, slot_pos):
    return pl.pallas_call(
        unplace_kernel,
        in_specs=[vmem_spec()] * 2,
        out_specs=vmem_spec(),
        out_shape=jax.ShapeDtypeStruct((slot_pos.shape[1], home.shape[1]), BF),
        compiler_params=params(56),
        cost_estimate=cost(4),
        name="unplace",
    )(slot_pos, home)


def coef_kernel(rep_ref, map_ref, src_ref, got_ref, out_ref, order_ref, count_ref, held, weights, sems):
    count, rows, cols = weights.shape
    at = pl.ds(pl.multiple_of(rep_ref[0] * cols, cols), cols)
    copies = [
        pltpu.make_async_copy(src_ref.at[:, :, at], weights, sems.at[0]),
        pltpu.make_async_copy(got_ref, held, sems.at[1]),
    ]
    for copy in copies:
        copy.start()
    expert_order(map_ref, order_ref, count_ref)
    for copy in copies:
        copy.wait()
    lane = lax.broadcasted_iota(I32, (8, 128), 1)

    def one(g, total):
        merged = held[0, g].astype(F32) + held[1, g].astype(F32)
        for n in range(2):
            expert = order_ref[2 * g + n]
            product = merged * weights[expert].astype(F32)
            folded = jnp.sum(product.reshape(rows // 8, 8, cols), axis=0)
            small = folded[:, :128]
            for c in range(128, cols, 128):
                small = small + folded[:, c : c + 128]
            small = jnp.sum(jnp.sum(small, axis=0, keepdims=True), axis=1, keepdims=True)
            total = total + jnp.where(lane == expert, small, 0.0)
        return total

    out_ref[...] = lax.fori_loop(0, count // 2, one, jnp.zeros((8, 128), F32))


def finish_kernel(scale, map_ref, coef_ref, got_ref, out_ref, order_ref, count_ref, held, ready, sems, more):
    count = ready.shape[0]

    def load(g):
        return pltpu.make_async_copy(got_ref.at[:, g], held.at[:, g], sems.at[g])

    def send(i):
        return pltpu.make_async_copy(ready.at[i], out_ref.at[order_ref[i]], more.at[i])

    @pl.loop(0, count // 2)
    def _(g):
        load(g).start()

    expert_order(map_ref, order_ref, count_ref)

    @pl.loop(0, count // 2)
    def _(g):
        load(g).wait()
        merged = held[0, g].astype(F32) + held[1, g].astype(F32)
        for n in range(2):
            i = 2 * g + n
            ready[i] = merged * (coef_ref[order_ref[i]] * scale)
            send(i).start()

    @pl.loop(0, count)
    def _(i):
        send(i).wait()


def coef_dots(rep_index, merge_map, source_w, arrived):
    count = source_w.shape[0]
    _, _, rows, cols = arrived.shape
    return pl.pallas_call(
        coef_kernel,
        in_specs=[smem_spec(), smem_spec(), hbm_spec(), hbm_spec()],
        out_specs=vmem_spec(),
        out_shape=jax.ShapeDtypeStruct((8, 128), F32),
        scratch_shapes=[
            pltpu.SMEM((count,), I32),
            pltpu.SMEM((count // 2,), I32),
            pltpu.VMEM(arrived.shape, BF),
            pltpu.VMEM((count, rows, cols), BF),
            pltpu.SemaphoreType.DMA((2,)),
        ],
        compiler_params=params(56),
        name="coef_dots",
    )(rep_index, merge_map, source_w, arrived)


def finish(merge_map, merge_coef, arrived, after, scale):
    count = merge_map.shape[0]
    _, _, rows, cols = arrived.shape
    return pl.pallas_call(
        lambda a, b, c, _, *refs: finish_kernel(scale, a, b, c, *refs),
        in_specs=[smem_spec(), smem_spec(), hbm_spec(), any_spec()],
        out_specs=hbm_spec(),
        out_shape=jax.ShapeDtypeStruct((count, rows, cols), F32),
        scratch_shapes=[
            pltpu.SMEM((count,), I32),
            pltpu.SMEM((count // 2,), I32),
            pltpu.VMEM(arrived.shape, BF),
            pltpu.VMEM((count, rows, cols), F32),
            pltpu.SemaphoreType.DMA((count // 2,)),
            pltpu.SemaphoreType.DMA((count,)),
        ],
        compiler_params=params(56),
        cost_estimate=cost(8),
        name="finish",
    )(merge_map, merge_coef, arrived, after)


def swap(x):
    return lax.ppermute(x, "core", [(0, 1), (1, 0)])


def on_pairs(
    tokens, router_w, router_b, hidden, teacher_idx, merge_map, merge_coef, source_w, out_grad
):
    places = lax.axis_size("place")
    blocks = 2 * places
    reps = 4
    tok = tokens.shape[1]
    features = tokens.shape[2]
    top = teacher_idx.shape[2]
    width = hidden.shape[3]
    depth = out_grad.shape[2]
    sources = router_w.shape[1]
    row_share = source_w.shape[1]
    lanes = 2 * places
    capacity = 5 * tok * top // (4 * blocks)
    scale = 1.0 / math.sqrt(tok * blocks * reps)
    half_i, place_i = lax.axis_index("half"), lax.axis_index("place")
    row_i, core_i = lax.axis_index("row"), lax.axis_index("core")
    ctx_i = half_i * places + place_i
    everyone = ("half", "place", "row", "core")
    devices = blocks * reps

    def stack(numbers):
        return jnp.stack([jnp.asarray(n, I32) for n in numbers])

    def later(*x):
        return swap(hold([jnp.zeros((8, 128), F32)], *x)[0])

    def trade(x, axes):
        return lax.all_to_all(x, axes, split_axis=0, concat_axis=0, tiled=True)

    xt = tokens.reshape(tok, features).T
    rwt = router_w.T
    idx_t = teacher_idx.reshape(tok, top).T
    og = out_grad.reshape(tok, depth)
    combos, send_rows, gates, pos, slot_pos = prepare(
        stack([row_i, core_i, 2 * place_i + row_i]), merge_map, merge_coef, source_w,
        xt, rwt, router_b, idx_t, hidden.reshape(tok * top, width), og, capacity, lanes,
    )
    def trade_rows(rows):
        cut = rows.reshape(lanes, capacity, rows.shape[1])
        return trade(cut, ("place", "row")).reshape(rows.shape)

    rows = trade_rows(send_rows)
    (combos,) = hold([combos.reshape((blocks,) + combos.shape[2:])], rows)
    mine = trade(combos, ("half", "place"))
    (rows,) = hold([rows], later(rows))
    here = stack([core_i])
    first = lane_grads(stack([1 - core_i]), rows, None, blocks, reps)
    summed = lane_grads(here, rows, swap(first), blocks, reps)
    (mine,) = hold([mine], summed)
    (summed,) = hold([summed], mine)
    arrived = trade(
        summed.reshape(2 * blocks, 2, row_share, width // reps), ("half", "place", "row")
    )

    other = swap(mine)
    me = stack([2 * place_i + row_i])
    (rows,) = hold([rows], later(summed))
    *parts, back_rows = run_lane(here, me, rows, mine, other, lanes)
    home = [parts[0]] + [
        lax.ppermute(parts[d], ("place", "row"), [(i, i ^ d) for i in range(lanes)])
        for d in range(1, lanes)
    ]
    (back_rows,) = hold([back_rows], arrived)
    home_back = trade_rows(back_rows)
    (arrived,) = hold([arrived], later(arrived))
    arrived = arrived.reshape(2, 2 * lanes, row_share, width // reps)
    dots = coef_dots(stack([2 * row_i + core_i]), merge_map, source_w, arrived)
    source_w_grad = finish(merge_map, merge_coef, arrived, dots, scale)
    home = hold(home, source_w_grad)
    mixed, token_grad, part = combine(home, og, gates, pos, idx_t, rwt, xt)
    part = jnp.sum(trade(part, everyone), axis=0)
    hidden_grad = unplace(home_back, slot_pos).reshape(1, tok, top, width)
    news = jnp.concatenate([part, dots[:1]], axis=1)
    (news,) = hold([news], hidden_grad)
    news = trade(jnp.broadcast_to(news[None], (devices,) + news.shape), everyone)
    end = part.shape[1]
    return (
        mixed.reshape(1, tok, depth),
        hidden_grad,
        token_grad.T.reshape(1, tok, features),
        news[:, 0, :features].T * scale,
        news[:, 0, end - 1] * scale,
        jnp.sum(news[:, 0, end : end + sources], axis=0) * scale,
        source_w_grad,
    )


def solution(mesh):
    if mesh.shape["ctx"] == 8 and mesh.shape["rep"] == 4:
        mesh = jax.sharding.Mesh(
            mesh.devices.reshape(2, 4, 2, 2), ("half", "place", "row", "core")
        )
        ctx, rep, body = ("half", "place"), ("row", "core"), on_pairs
    else:
        ctx, rep, body = "ctx", "rep", on_device
    in_specs = (
        P(rep, ctx, None),
        P(),
        P(),
        P(rep, ctx, None, None),
        P(rep, ctx, None),
        P(),
        P(),
        P(None, ctx, None),
        P(rep, ctx, None),
    )
    out_specs = (
        P(rep, ctx, None),
        P(rep, ctx, None, None),
        P(rep, ctx, None),
        P(),
        P(),
        P(),
        P(None, ctx, rep),
    )
    return jax.shard_map(
        body, mesh=mesh, in_specs=in_specs, out_specs=out_specs, check_vma=False
    )
```

```python
import functools
import math

import jax
import jax.numpy as jnp
from jax import lax
from jax.experimental import pallas as pl
from jax.experimental.pallas import tpu as pltpu
from jax.sharding import PartitionSpec as P

MERGED = 16


def expert_rows(rows_hidden, rows_grad, rows_member, lane_weights):
    row_count = rows_hidden.shape[0]
    out_rows = jnp.zeros((row_count, lane_weights.shape[1]), jnp.float32)
    back_rows = jnp.zeros((row_count, lane_weights.shape[2]), jnp.float32)
    grad_list = []
    for member_now in range(lane_weights.shape[0]):
        weight = lane_weights[member_now]
        selected = (rows_member == member_now)[:, None]
        forward = lax.dot_general(
            rows_hidden, weight, (((1,), (1,)), ((), ())), preferred_element_type=jnp.float32
        )
        out_rows = jnp.where(selected, forward, out_rows)
        backward = jnp.dot(rows_grad, weight, preferred_element_type=jnp.float32)
        back_rows = jnp.where(selected, backward, back_rows)
        masked = jnp.where(selected, rows_grad, jnp.zeros_like(rows_grad))
        grad_list.append(
            lax.dot_general(
                masked, rows_hidden, (((0,), (0,)), ((), ())), preferred_element_type=jnp.float32
            )
        )
    return (out_rows, back_rows, jnp.stack(grad_list))


def on_device(
    tokens, router_w, router_b, hidden, teacher_idx, merge_map, merge_coef, source_w, out_grad
):
    ctx_count = lax.axis_size("ctx")
    rep_count = lax.axis_size("rep")
    tok_count = tokens.shape[1]
    feature_count = tokens.shape[2]
    top_count = teacher_idx.shape[2]
    hidden_width = hidden.shape[3]
    out_width = out_grad.shape[2]
    source_count = router_w.shape[1]
    row_share = source_w.shape[1]
    per_lane = max(1, MERGED // ctx_count)
    copies = max(1, ctx_count // MERGED)
    capacity = 5 * tok_count * top_count // (4 * ctx_count)
    slot_count = tok_count * top_count
    grad_scale = 1.0 / math.sqrt(tok_count * ctx_count * rep_count)
    flat_x = tokens.reshape(tok_count, feature_count)
    logits = jnp.dot(flat_x, router_w, preferred_element_type=jnp.float32) + router_b
    choice_ids = teacher_idx.reshape(tok_count, top_count)
    pick_table = choice_ids[:, :, None] == jnp.arange(source_count, dtype=jnp.int32)[None, None, :]
    pick_float = pick_table.astype(jnp.float32)
    chosen = jnp.sum(pick_float * logits[:, None, :], axis=2)
    raised = jnp.exp(chosen)
    gate_probs = raised / jnp.sum(raised, axis=1, keepdims=True)
    merged_id = jnp.sum(jnp.where(pick_table, merge_map[None, None, :], 0), axis=2)
    position = lax.axis_index("ctx") * tok_count + jnp.arange(tok_count, dtype=jnp.int32)
    lane_id = merged_id // per_lane * copies + (position % copies)[:, None]
    member_id = (merged_id % per_lane).reshape(-1)
    lane_flat = lane_id.reshape(-1)
    onehot = (lane_flat[:, None] == jnp.arange(ctx_count, dtype=jnp.int32)[None, :]).astype(
        jnp.int32
    )
    before = jnp.cumsum(onehot, axis=0) - onehot
    slot_rank = jnp.sum(before * onehot, axis=1)
    is_kept = slot_rank < capacity
    slot_index = jnp.where(is_kept, lane_flat * capacity + slot_rank, ctx_count * capacity)
    slot_source = (
        jnp.full((ctx_count * capacity + 1,), slot_count, jnp.int32)
        .at[slot_index]
        .set(jnp.arange(slot_count, dtype=jnp.int32))[: ctx_count * capacity]
    )
    slot_grad = (gate_probs[:, :, None] * out_grad.reshape(tok_count, 1, out_width)).astype(
        jnp.bfloat16
    )
    pad_hidden = jnp.concatenate(
        [hidden.reshape(slot_count, hidden_width), jnp.zeros((1, hidden_width), jnp.bfloat16)],
        axis=0,
    )
    pad_grad = jnp.concatenate(
        [slot_grad.reshape(slot_count, out_width), jnp.zeros((1, out_width), jnp.bfloat16)], axis=0
    )
    pad_member = jnp.concatenate([member_id, jnp.zeros((1,), jnp.int32)], axis=0)
    send_hidden = pad_hidden[slot_source].reshape(ctx_count, capacity, hidden_width)
    send_grad = pad_grad[slot_source].reshape(ctx_count, capacity, out_width)
    send_member = pad_member[slot_source].reshape(ctx_count, capacity)
    lane_group = lax.axis_index("ctx") // copies
    same_group = merge_map[:, None] == merge_map[None, :]
    earlier = jnp.arange(source_count)[:, None] > jnp.arange(source_count)[None, :]
    member_rank = jnp.sum((same_group & earlier).astype(jnp.int32), axis=1)
    source_order = (
        jnp.zeros((source_count,), jnp.int32)
        .at[2 * merge_map + member_rank]
        .set(jnp.arange(source_count, dtype=jnp.int32))
    )
    picked = source_w[source_order].reshape(
        MERGED // per_lane, 2 * per_lane, row_share, hidden_width
    )
    outgoing = jnp.repeat(picked, copies, axis=0)
    arrived = lax.all_to_all(outgoing, "ctx", split_axis=0, concat_axis=2, tiled=True)
    pair_rows = arrived.reshape(per_lane, 2, row_share * ctx_count, hidden_width)
    coef_table = merge_coef[source_order].reshape(MERGED // per_lane, per_lane, 2)
    pair_coef = lax.dynamic_index_in_dim(coef_table, lane_group, 0, keepdims=False)
    lane_weights = (
        pair_coef[:, 0, None, None] * pair_rows[:, 0].astype(jnp.float32)
        + pair_coef[:, 1, None, None] * pair_rows[:, 1].astype(jnp.float32)
    ).astype(jnp.bfloat16)
    recv_hidden, recv_grad, recv_member = (
        lax.all_to_all(send_hidden, "ctx", split_axis=0, concat_axis=0, tiled=True),
        lax.all_to_all(send_grad, "ctx", split_axis=0, concat_axis=0, tiled=True),
        lax.all_to_all(send_member, "ctx", split_axis=0, concat_axis=0, tiled=True),
    )
    out_rows, back_rows, lane_grads = expert_rows(
        recv_hidden.reshape(-1, hidden_width),
        recv_grad.reshape(-1, out_width),
        recv_member.reshape(-1),
        lane_weights,
    )
    home_out, home_back = (
        lax.all_to_all(
            out_rows.astype(jnp.bfloat16).reshape(ctx_count, capacity, out_width),
            "ctx",
            split_axis=0,
            concat_axis=0,
            tiled=True,
        ),
        lax.all_to_all(
            back_rows.astype(jnp.bfloat16).reshape(ctx_count, capacity, hidden_width),
            "ctx",
            split_axis=0,
            concat_axis=0,
            tiled=True,
        ),
    )
    slot_out = jnp.concatenate(
        [home_out.reshape(-1, out_width), jnp.zeros((1, out_width), jnp.bfloat16)], axis=0
    )[slot_index].reshape(tok_count, top_count, out_width)
    hidden_grad = jnp.concatenate(
        [home_back.reshape(-1, hidden_width), jnp.zeros((1, hidden_width), jnp.bfloat16)], axis=0
    )[slot_index].reshape(1, tok_count, top_count, hidden_width)
    mixed = (
        jnp.sum(gate_probs[:, :, None] * slot_out.astype(jnp.float32), axis=1)
        .astype(jnp.bfloat16)
        .reshape(1, tok_count, out_width)
    )
    score_grad = jnp.einsum(
        "td,tkd->tk",
        out_grad.reshape(tok_count, out_width),
        slot_out,
        preferred_element_type=jnp.float32,
    )
    chosen_grad = gate_probs * (
        score_grad - jnp.sum(gate_probs * score_grad, axis=1, keepdims=True)
    )
    logit_grad = jnp.sum(pick_float * chosen_grad[:, :, None], axis=1)
    logit_half = logit_grad.astype(jnp.bfloat16)
    token_grad = (
        lax.dot_general(
            logit_half, router_w, (((1,), (1,)), ((), ())), preferred_element_type=jnp.float32
        )
        .astype(jnp.bfloat16)
        .reshape(1, tok_count, feature_count)
    )
    part_router_w = lax.dot_general(
        flat_x, logit_half, (((0,), (0,)), ((), ())), preferred_element_type=jnp.float32
    )
    part_router_b = jnp.sum(logit_grad, axis=0)
    arrived_grads = lax.all_to_all(
        lane_grads.reshape(per_lane, ctx_count, row_share, hidden_width),
        "ctx",
        split_axis=1,
        concat_axis=0,
        tiled=True,
    )
    merged_grad = (
        arrived_grads.reshape(MERGED // per_lane, copies, per_lane, row_share, hidden_width)
        .sum(axis=1)
        .reshape(MERGED, row_share, hidden_width)
    )
    source_grad = merged_grad[merge_map]
    coef_part = jnp.einsum(
        "edf,edf->e", source_grad, source_w.astype(jnp.float32), precision=lax.Precision.HIGHEST
    )
    summed = lax.psum_scatter(
        source_grad * merge_coef[:, None, None], "rep", scatter_dimension=2, tiled=True
    )
    source_w_grad = summed * grad_scale
    router_sum, bias_sum, coef_sum = lax.psum(
        (part_router_w, part_router_b, coef_part), ("ctx", "rep")
    )
    return (
        mixed,
        hidden_grad,
        token_grad,
        router_sum * grad_scale,
        bias_sum * grad_scale,
        coef_sum * grad_scale,
        source_w_grad,
    )


BF = jnp.bfloat16
F32 = jnp.float32
I32 = jnp.int32
TILE = 256


def cost(us):
    return pl.CostEstimate(flops=us * 10**9, bytes_accessed=us * 10**6, transcendentals=0)


def any_spec():
    return pl.BlockSpec(memory_space=pl.ANY)


def smem_spec():
    return pl.BlockSpec(memory_space=pltpu.SMEM)


def vmem_spec():
    return pl.BlockSpec(memory_space=pltpu.VMEM)


def params(mib):
    return pltpu.CompilerParams(vmem_limit_bytes=mib * 1024 * 1024)


def dot(a, b, dims):
    return lax.dot_general(a, b, (dims, ((), ())), preferred_element_type=F32)


def merge_start(map_ref, place_ref, src_ref, places, order_ref, count_ref, held, sems):
    half = held.shape[2]
    expert_order(map_ref, order_ref, count_ref)
    at = pl.ds(pl.multiple_of(place_ref[1] * half, half), half)
    copies, experts = [], []
    for j in range(places):
        for m in range(2):
            combo = 4 * j + 2 * place_ref[0] + m
            for n in range(2):
                expert = order_ref[2 * combo + n]
                experts.append(expert)
                i = len(copies)
                copies.append(
                    pltpu.make_async_copy(src_ref.at[expert, :, at], held.at[i], sems.at[i])
                )
                copies[-1].start()
    return copies, experts


def merge_finish(copies, experts, coef_ref, held, out_ref):
    halves, places = out_ref.shape[:2]
    for j in range(places):
        for m in range(2):
            i = 4 * j + 2 * m
            copies[i].wait()
            copies[i + 1].wait()
            one, two = coef_ref[experts[i]], coef_ref[experts[i + 1]]
            merged = (one * held[i].astype(F32) + two * held[i + 1].astype(F32)).astype(BF)
            for h in range(halves):
                out_ref[h, j, m] = merged


def expert_order(map_ref, order_ref, count_ref):
    @pl.loop(0, count_ref.shape[0])
    def _(g):
        count_ref[g] = 0

    @pl.loop(0, order_ref.shape[0])
    def _(e):
        g = map_ref[e]
        n = count_ref[g]
        order_ref[2 * g + n] = e
        count_ref[g] = n + 1


def hbm_spec():
    return pl.BlockSpec(memory_space=pltpu.HBM)


def hold(arrays, *after):
    count = len(arrays)
    return pl.pallas_call(
        lambda *refs: None,
        in_specs=[hbm_spec()] * count + [any_spec()] * len(after),
        out_specs=[hbm_spec()] * count,
        out_shape=[jax.ShapeDtypeStruct(a.shape, a.dtype) for a in arrays],
        input_output_aliases={i: i for i in range(count)},
        name="hold",
    )(*arrays, *after)


def column(row):
    size = row.shape[1]
    same = lax.broadcasted_iota(I32, (size, size), 0) == lax.broadcasted_iota(I32, (size, size), 1)
    return jnp.sum(jnp.where(same, row, jnp.zeros_like(row)), axis=1, keepdims=True)


def to_row(col):
    size = col.shape[0]
    same = lax.broadcasted_iota(I32, (size, size), 0) == lax.broadcasted_iota(I32, (size, size), 1)
    return jnp.sum(jnp.where(same, col, jnp.zeros_like(col)), axis=0, keepdims=True)


def picks_of(idx_ref, k, sources):
    tok = idx_ref.shape[1]
    return lax.broadcasted_iota(I32, (sources, tok), 0) == idx_ref[k : k + 1, :]


def prepare_kernel(
    capacity, lanes,
    combo_ref, coef_ref, place_ref, src_ref,
    xt_ref, rwt_ref, rb_ref, idx_ref, map_ref, hid_ref, og_ref,
    merged_ref, send_ref, gate_ref, pos_ref, slot_ref,
    order_ref, count_ref, held, sems,
):
    copies, experts = merge_start(
        combo_ref, place_ref, src_ref, merged_ref.shape[1], order_ref, count_ref, held, sems
    )
    top, tok = idx_ref.shape
    sources = rwt_ref.shape[0]
    slots, width = hid_ref.shape
    places = lanes * capacity
    logits = jnp.dot(rwt_ref[...], xt_ref[...], preferred_element_type=F32) + column(rb_ref[...])
    raised, merged = [], []
    combos = column(map_ref[...])
    for k in range(top):
        pick = picks_of(idx_ref, k, sources)
        chosen = jnp.sum(jnp.where(pick, logits, 0.0), axis=0, keepdims=True)
        raised.append(jnp.exp(chosen))
        merged.append(jnp.sum(jnp.where(pick, combos, 0), axis=0, keepdims=True))
    total = raised[0]
    for k in range(1, top):
        total = total + raised[k]
    gates = [r / total for r in raised]
    lane = [jnp.right_shift(g, 1) for g in merged]
    member = [jnp.bitwise_and(g, 1) for g in merged]
    onehot = [(lax.broadcasted_iota(I32, (lanes, tok), 0) == l).astype(F32) for l in lane]
    all_hot = onehot[0]
    for k in range(1, top):
        all_hot = all_hot + onehot[k]
    earlier = (
        lax.broadcasted_iota(I32, (tok, tok), 0) < lax.broadcasted_iota(I32, (tok, tok), 1)
    ).astype(BF)
    before = jnp.dot(all_hot.astype(BF), earlier, preferred_element_type=F32)
    position, back = [], []
    for k in range(top):
        rank = jnp.sum(before * onehot[k], axis=0, keepdims=True).astype(I32)
        before = before + onehot[k]
        position.append(jnp.where(rank < capacity, lane[k] * capacity + rank, -1))
        partner = jnp.bitwise_xor(lane[k], place_ref[2])
        back.append(jnp.where(rank < capacity, partner * capacity + rank, -1))
    gate_ref[...] = jnp.zeros_like(gate_ref)
    pos_ref[...] = jnp.full_like(pos_ref, -1)
    for k in range(top):
        gate_ref[k : k + 1, :] = gates[k]
        pos_ref[k : k + 1, :] = back[k]
    spot = jnp.zeros((8, slots), F32)
    for k in range(top):
        spread = (
            lax.broadcasted_iota(I32, (tok, slots), 1)
            == lax.broadcasted_iota(I32, (tok, slots), 0) * top + k
        ).astype(BF)
        kept = position[k] >= 0
        parts = [
            jnp.where(kept, lane[k], 0),
            jnp.where(kept, position[k] - lane[k] * capacity, 0),
            jnp.where(kept, 1, 0),
            member[k],
        ]
        stacked = jnp.concatenate(
            [p.astype(F32) for p in parts] + [jnp.zeros((4, tok), F32)], axis=0
        ).astype(BF)
        spot = spot + jnp.dot(stacked, spread, preferred_element_type=F32)
    spot = spot.astype(I32)
    slot_pos = jnp.where(spot[2:3] > 0, spot[0:1] * capacity + spot[1:2], -1)
    partner = jnp.bitwise_xor(spot[0:1], place_ref[2])
    slot_back = jnp.where(spot[2:3] > 0, partner * capacity + spot[1:2], -1)
    slot_ref[...] = jnp.broadcast_to(slot_back, slot_ref.shape)
    take = lax.broadcasted_iota(I32, (places, slots), 0) == slot_pos
    placed = jnp.sum(jnp.where(take, spot[3:4].astype(F32), 0.0), axis=1, keepdims=True)
    depth = og_ref.shape[1]
    send_ref[:, depth + width :] = jnp.broadcast_to(placed, (places, 128)).astype(BF)
    take = take.astype(BF)
    for n in range(0, width, TILE):
        rows = jnp.dot(take, hid_ref[:, n : n + TILE], preferred_element_type=F32)
        send_ref[:, depth + n : depth + n + TILE] = rows.astype(BF)
    takes = [
        (lax.broadcasted_iota(I32, (places, tok), 0) == position[k]).astype(BF) for k in range(top)
    ]
    columns = [column(g) for g in gates]
    for n in range(0, depth, TILE):
        og = og_ref[:, n : n + TILE].astype(F32)
        rows = jnp.zeros((places, TILE), F32)
        for k in range(top):
            rows = rows + jnp.dot(takes[k], (columns[k] * og).astype(BF), preferred_element_type=F32)
        send_ref[:, n : n + TILE] = rows.astype(BF)
    merge_finish(copies, experts, coef_ref, held, merged_ref)


def prepare(
    place, merge_map, merge_coef, source_w, xt, rwt, router_b, idx_t, hid, og, capacity, lanes
):
    count, rows, whole = source_w.shape
    slots, width = hid.shape
    tok = idx_t.shape[1]
    half, places = whole // 2, lanes // 2
    return pl.pallas_call(
        functools.partial(prepare_kernel, capacity, lanes),
        in_specs=[smem_spec()] * 3 + [any_spec()] + [vmem_spec()] * 7,
        out_specs=[vmem_spec()] * 5,
        out_shape=[
            jax.ShapeDtypeStruct((2, places, 2, rows, half), BF),
            jax.ShapeDtypeStruct((lanes * capacity, og.shape[1] + width + 128), BF),
            jax.ShapeDtypeStruct((8, tok), F32),
            jax.ShapeDtypeStruct((8, tok), I32),
            jax.ShapeDtypeStruct((8, slots), I32),
        ],
        scratch_shapes=[
            pltpu.SMEM((count,), I32),
            pltpu.SMEM((count // 2,), I32),
            pltpu.VMEM((4 * places, rows, half), BF),
            pltpu.SemaphoreType.DMA((4 * places,)),
        ],
        compiler_params=params(56),
        cost_estimate=cost(10),
        name="prepare",
    )(
        merge_map, merge_coef, place, source_w,
        xt, rwt, router_b[None, :], idx_t, merge_map[None, :], hid, og,
    )


def gather_rows(refs, keep):
    each = refs[0].shape[0]
    for d, ref in enumerate(refs):
        keep[d * each : (d + 1) * each, :] = ref[...]


def load_weights(core_ref, mine, other, w_ref, sems):
    core = core_ref[0]
    blocks, _, rows, _ = mine.shape
    copies = []
    for c in range(blocks):
        at = pl.ds(c * rows, rows)
        for n, part in enumerate((mine, other)):
            to = core if n == 0 else 1 - core
            i = 2 * c + n
            copies.append(
                pltpu.make_async_copy(part.at[c], w_ref.at[to, :, at, :], sems.at[i])
            )
    for copy in copies:
        copy.start()
    for copy in copies:
        copy.wait()


def lane_kernel(
    core_ref, me_ref, grd_ref, hid_ref, flag_ref, mine, other, *refs
):
    outs, (keep, w_ref, sems) = refs[:-3], refs[-3:]
    load_weights(core_ref, mine, other, w_ref, sems)
    half, depth = w_ref.shape[3], w_ref.shape[2]
    first = flag_ref[:, :1].astype(F32) == 0.0
    for n in range(0, depth, TILE):
        at = slice(n, n + TILE)
        both = [
            dot(hid_ref[:, :half], w_ref[0, m, at, :], ((1,), (1,)))
            + dot(hid_ref[:, half:], w_ref[1, m, at, :], ((1,), (1,)))
            for m in range(2)
        ]
        keep[:, at] = jnp.where(first, both[0], both[1]).astype(BF)
    for h in range(2):
        for n in range(0, half, TILE):
            at = slice(n, n + TILE)
            both = [dot(grd_ref[...], w_ref[h, m, :, at], ((1,), (0,))) for m in range(2)]
            to = depth + h * half + n
            keep[:, to : to + TILE] = jnp.where(first, both[0], both[1]).astype(BF)
    each = outs[0].shape[0]
    for d, out_ref in enumerate(outs):
        at = pl.ds(pl.multiple_of(jnp.bitwise_xor(me_ref[0], d) * each, each), each)
        out_ref[...] = keep[at, :]


def run_lane(core, me, rows, mine, other, lanes):
    blocks, members, share, half = mine.shape
    depth = share * blocks
    count = rows.shape[0]
    wide = (rows.shape[1] - 128) // 2
    part = (count // lanes, 2 * wide)
    return pl.pallas_call(
        lane_kernel,
        grid=(1,),
        in_specs=[
            smem_spec(),
            smem_spec(),
            pl.BlockSpec((count, wide), lambda i: (0, 0)),
            pl.BlockSpec((count, wide), lambda i: (0, 1)),
            pl.BlockSpec((count, 128), lambda i: (0, 2 * wide // 128)),
            any_spec(),
            any_spec(),
        ],
        out_specs=[pl.BlockSpec(part, lambda i: (0, 0))] * lanes,
        out_shape=[jax.ShapeDtypeStruct(part, BF)] * lanes,
        scratch_shapes=[
            pltpu.VMEM((count, 2 * wide), BF),
            pltpu.VMEM((2, members, depth, half), BF),
            pltpu.SemaphoreType.DMA((2 * blocks,)),
        ],
        compiler_params=params(60),
        cost_estimate=cost(20),
        name="lane_products",
    )(core, me, rows, rows, rows, mine, other)


def lane_grad_kernel(has_other, _, grd_ref, hid_ref, flag_ref, *refs):
    out_ref = refs[-1]
    chosen = flag_ref[:, :1].astype(F32) == pl.program_id(1).astype(F32)
    hid = jnp.where(chosen, hid_ref[...], jnp.zeros_like(hid_ref))
    blocks, _, _, rows, cols = out_ref.shape
    each = 2 if blocks % 2 == 0 and 2 * rows % 128 == 0 else blocks
    for n in range(0, blocks, each):
        part = dot(grd_ref[:, n * rows : (n + each) * rows], hid, ((0,), (0,)))
        part = part.reshape(each, rows, cols)
        if has_other:
            part = part + refs[0][n : n + each, 0, 0].astype(F32)
        out_ref[n : n + each, 0, 0] = part.astype(BF)


def lane_grads(core, rows, other, blocks, reps):
    count = rows.shape[0]
    width = (rows.shape[1] - 128) // 2
    cols = width // reps
    shape = (blocks, 2, 2, width // blocks, cols)
    block = pl.BlockSpec((blocks, 1, 1, width // blocks, cols), lambda y, m, s: (0, y, m, 0, 0))
    extra = [] if other is None else [other]
    return pl.pallas_call(
        functools.partial(lane_grad_kernel, other is not None),
        grid_spec=pltpu.PrefetchScalarGridSpec(
            num_scalar_prefetch=1,
            grid=(2, 2),
            in_specs=[
                pl.BlockSpec((count, width), lambda y, m, s: (0, 0)),
                pl.BlockSpec((count, cols), lambda y, m, s: (0, reps + 2 * y + s[0])),
                pl.BlockSpec((count, 128), lambda y, m, s: (0, 2 * width // 128)),
            ]
            + [block] * len(extra),
            out_specs=block,
        ),
        out_shape=jax.ShapeDtypeStruct(shape, BF),
        compiler_params=params(56),
        cost_estimate=cost(8),
        name="lane_grads_add" if extra else "lane_grads_first",
    )(core, rows, rows, rows, *extra)


def combine_kernel(og_ref, gate_ref, pos_ref, idx_ref, rwt_ref, xt_ref, *refs):
    homes, (mixed_ref, tg_ref, part_ref, out_ref) = refs[:-4], refs[-4:]
    gather_rows(homes, out_ref)
    places, width = out_ref.shape
    top, tok = idx_ref.shape
    sources, features = rwt_ref.shape
    takes = [
        (lax.broadcasted_iota(I32, (places, tok), 0) == pos_ref[k : k + 1, :]).astype(BF)
        for k in range(top)
    ]
    gates = [gate_ref[k : k + 1, :] for k in range(top)]
    columns = [column(g) for g in gates]
    scores = [jnp.zeros((tok, 1), F32) for _ in range(top)]
    for n in range(0, width, TILE):
        og = og_ref[:, n : n + TILE].astype(F32)
        rows = out_ref[:, n : n + TILE]
        mixed = jnp.zeros((tok, TILE), F32)
        for k in range(top):
            slot_out = dot(takes[k], rows, ((0,), (0,)))
            mixed = mixed + columns[k] * slot_out
            scores[k] = scores[k] + jnp.sum(og * slot_out, axis=1, keepdims=True)
        mixed_ref[:, n : n + TILE] = mixed.astype(BF)
    scores = [to_row(s) for s in scores]
    middle = gates[0] * scores[0]
    for k in range(1, top):
        middle = middle + gates[k] * scores[k]
    logit_grad = jnp.zeros((sources, tok), F32)
    for k in range(top):
        chosen_grad = gates[k] * (scores[k] - middle)
        logit_grad = logit_grad + jnp.where(picks_of(idx_ref, k, sources), chosen_grad, 0.0)
    logit_half = logit_grad.astype(BF)
    tg_ref[...] = dot(rwt_ref[...], logit_half, ((0,), (0,))).astype(BF)
    part_ref[...] = jnp.zeros_like(part_ref)
    part_ref[:, 0, :features] = dot(logit_half, xt_ref[...], ((1,), (1,)))
    bias = jnp.sum(logit_grad, axis=1, keepdims=True)
    last = part_ref.shape[2] - 128
    part_ref[:, 0, last:] = jnp.broadcast_to(bias, (sources, 128))


def combine(homes, og, gates, pos, idx_t, rwt, xt):
    sources, features = rwt.shape
    tok, width = og.shape
    each = homes[0].shape[0]
    whole = lambda a: pl.BlockSpec(a.shape, lambda i: (0,) * len(a.shape))
    outs = [
        jax.ShapeDtypeStruct(og.shape, BF),
        jax.ShapeDtypeStruct((features, tok), BF),
        jax.ShapeDtypeStruct((sources, 1, (features + 127) // 128 * 128 + 128), F32),
    ]
    return pl.pallas_call(
        combine_kernel,
        grid=(1,),
        in_specs=[whole(a) for a in (og, gates, pos, idx_t, rwt, xt)]
        + [pl.BlockSpec((each, width), lambda i: (0, 0))] * len(homes),
        out_specs=[whole(a) for a in outs],
        out_shape=outs,
        scratch_shapes=[pltpu.VMEM((len(homes) * each, width), BF)],
        compiler_params=params(56),
        cost_estimate=cost(5),
        name="combine",
    )(og, gates, pos, idx_t, rwt, xt, *homes)


def unplace_kernel(slot_ref, *refs):
    homes, (out_ref, back_ref) = refs[:-2], refs[-2:]
    gather_rows(homes, back_ref)
    places, width = back_ref.shape
    slots = slot_ref.shape[1]
    take = (lax.broadcasted_iota(I32, (places, slots), 0) == slot_ref[0:1, :]).astype(BF)
    for n in range(0, width, TILE):
        out_ref[:, n : n + TILE] = dot(take, back_ref[:, n : n + TILE], ((0,), (0,))).astype(BF)


def unplace(homes, slot_pos):
    each, width = homes[0].shape[0], homes[0].shape[1] // 2
    slots = slot_pos.shape[1]
    return pl.pallas_call(
        unplace_kernel,
        grid=(1,),
        in_specs=[pl.BlockSpec(slot_pos.shape, lambda i: (0, 0))]
        + [pl.BlockSpec((each, width), lambda i: (0, 1))] * len(homes),
        out_specs=pl.BlockSpec((slots, width), lambda i: (0, 0)),
        out_shape=jax.ShapeDtypeStruct((slots, width), BF),
        scratch_shapes=[pltpu.VMEM((len(homes) * each, width), BF)],
        compiler_params=params(56),
        cost_estimate=cost(4),
        name="unplace",
    )(slot_pos, *homes)


def coef_kernel(rep_ref, map_ref, src_ref, got_ref, out_ref, order_ref, count_ref, held, weights, sems):
    count, rows, cols = weights.shape
    at = pl.ds(pl.multiple_of(rep_ref[0] * cols, cols), cols)
    copies = [
        pltpu.make_async_copy(src_ref.at[:, :, at], weights, sems.at[0]),
        pltpu.make_async_copy(got_ref, held, sems.at[1]),
    ]
    for copy in copies:
        copy.start()
    expert_order(map_ref, order_ref, count_ref)
    for copy in copies:
        copy.wait()
    lane = lax.broadcasted_iota(I32, (8, 128), 1)

    def one(g, total):
        merged = held[0, g].astype(F32) + held[1, g].astype(F32)
        for n in range(2):
            expert = order_ref[2 * g + n]
            product = merged * weights[expert].astype(F32)
            folded = jnp.sum(product.reshape(rows // 8, 8, cols), axis=0)
            small = folded[:, :128]
            for c in range(128, cols, 128):
                small = small + folded[:, c : c + 128]
            small = jnp.sum(jnp.sum(small, axis=0, keepdims=True), axis=1, keepdims=True)
            total = total + jnp.where(lane == expert, small, 0.0)
        return total

    out_ref[...] = lax.fori_loop(0, count // 2, one, jnp.zeros((8, 128), F32))


def finish_kernel(scale, map_ref, coef_ref, got_ref, out_ref, order_ref, count_ref, held, ready, sems, more):
    count = ready.shape[0]

    def load(g):
        return pltpu.make_async_copy(got_ref.at[:, g], held.at[:, g], sems.at[g])

    def send(i):
        return pltpu.make_async_copy(ready.at[i], out_ref.at[order_ref[i]], more.at[i])

    @pl.loop(0, count // 2)
    def _(g):
        load(g).start()

    expert_order(map_ref, order_ref, count_ref)

    @pl.loop(0, count // 2)
    def _(g):
        load(g).wait()
        merged = held[0, g].astype(F32) + held[1, g].astype(F32)
        for n in range(2):
            i = 2 * g + n
            ready[i] = merged * (coef_ref[order_ref[i]] * scale)
            send(i).start()

    @pl.loop(0, count)
    def _(i):
        send(i).wait()


def coef_dots(rep_index, merge_map, source_w, arrived):
    count = source_w.shape[0]
    _, _, rows, cols = arrived.shape
    return pl.pallas_call(
        coef_kernel,
        in_specs=[smem_spec(), smem_spec(), hbm_spec(), hbm_spec()],
        out_specs=vmem_spec(),
        out_shape=jax.ShapeDtypeStruct((8, 128), F32),
        scratch_shapes=[
            pltpu.SMEM((count,), I32),
            pltpu.SMEM((count // 2,), I32),
            pltpu.VMEM(arrived.shape, BF),
            pltpu.VMEM((count, rows, cols), BF),
            pltpu.SemaphoreType.DMA((2,)),
        ],
        compiler_params=params(56),
        cost_estimate=cost(0),
        name="coef_dots",
    )(rep_index, merge_map, source_w, arrived)


def finish(merge_map, merge_coef, arrived, after, scale):
    count = merge_map.shape[0]
    _, _, rows, cols = arrived.shape
    return pl.pallas_call(
        lambda a, b, c, _, *refs: finish_kernel(scale, a, b, c, *refs),
        in_specs=[smem_spec(), smem_spec(), hbm_spec(), any_spec()],
        out_specs=hbm_spec(),
        out_shape=jax.ShapeDtypeStruct((count, rows, cols), F32),
        scratch_shapes=[
            pltpu.SMEM((count,), I32),
            pltpu.SMEM((count // 2,), I32),
            pltpu.VMEM(arrived.shape, BF),
            pltpu.VMEM((count, rows, cols), F32),
            pltpu.SemaphoreType.DMA((count // 2,)),
            pltpu.SemaphoreType.DMA((count,)),
        ],
        compiler_params=params(56),
        cost_estimate=cost(0),
        name="finish",
    )(merge_map, merge_coef, arrived, after)


def swap(x):
    return lax.ppermute(x, "core", [(0, 1), (1, 0)])


def on_pairs(
    tokens, router_w, router_b, hidden, teacher_idx, merge_map, merge_coef, source_w, out_grad
):
    places = lax.axis_size("place")
    blocks = 2 * places
    reps = 4
    tok = tokens.shape[1]
    features = tokens.shape[2]
    top = teacher_idx.shape[2]
    width = hidden.shape[3]
    depth = out_grad.shape[2]
    sources = router_w.shape[1]
    row_share = source_w.shape[1]
    lanes = 2 * places
    capacity = 5 * tok * top // (4 * blocks)
    scale = 1.0 / math.sqrt(tok * blocks * reps)
    half_i, place_i = lax.axis_index("half"), lax.axis_index("place")
    row_i, core_i = lax.axis_index("row"), lax.axis_index("core")
    ctx_i = half_i * places + place_i
    everyone = ("half", "place", "row", "core")
    devices = blocks * reps

    def stack(numbers):
        return jnp.stack([jnp.asarray(n, I32) for n in numbers])

    def later(*x):
        return swap(hold([jnp.zeros((8, 128), F32)], *x)[0])

    def trade(x, axes):
        return lax.all_to_all(x, axes, split_axis=0, concat_axis=0, tiled=True)

    xt = tokens.reshape(tok, features).T
    rwt = router_w.T
    idx_t = teacher_idx.reshape(tok, top).T
    og = out_grad.reshape(tok, depth)
    combos, send_rows, gates, pos, slot_pos = prepare(
        stack([row_i, core_i, 2 * place_i + row_i]), merge_map, merge_coef, source_w,
        xt, rwt, router_b, idx_t, hidden.reshape(tok * top, width), og, capacity, lanes,
    )
    rows = trade(send_rows.reshape(lanes, capacity, send_rows.shape[1]), ("place", "row"))
    rows = rows.reshape(send_rows.shape)
    (combos,) = hold([combos.reshape((blocks,) + combos.shape[2:])], rows)
    mine = trade(combos, ("half", "place"))
    (rows,) = hold([rows], later(rows))
    here = stack([core_i])
    first = lane_grads(stack([1 - core_i]), rows, None, blocks, reps)
    summed = lane_grads(here, rows, swap(first), blocks, reps)
    (mine,) = hold([mine], summed)
    (summed,) = hold([summed], mine)
    arrived = trade(
        summed.reshape(2 * blocks, 2, row_share, width // reps), ("half", "place", "row")
    )

    other = swap(mine)
    me = stack([2 * place_i + row_i])
    (rows,) = hold([rows], later(summed))
    parts = run_lane(here, me, rows, mine, other, lanes)
    home = [parts[0]] + [
        lax.ppermute(parts[d], ("place", "row"), [(i, i ^ d) for i in range(lanes)])
        for d in range(1, lanes)
    ]
    arrived = arrived.reshape(2, 2 * lanes, row_share, width // reps)
    dots = coef_dots(stack([2 * row_i + core_i]), merge_map, source_w, arrived)
    source_w_grad = finish(merge_map, merge_coef, arrived, dots, scale)
    home = hold(home, source_w_grad)
    mixed, token_grad, part = combine(home, og, gates, pos, idx_t, rwt, xt)
    part = jnp.sum(trade(part, everyone), axis=0)
    hidden_grad = unplace(home, slot_pos).reshape(1, tok, top, width)
    news = jnp.concatenate([part, dots[:1]], axis=1)
    (news,) = hold([news], hidden_grad)
    news = trade(jnp.broadcast_to(news[None], (devices,) + news.shape), everyone)
    end = part.shape[1]
    return (
        mixed.reshape(1, tok, depth),
        hidden_grad,
        token_grad.T.reshape(1, tok, features),
        news[:, 0, :features].T * scale,
        news[:, 0, end - 1] * scale,
        jnp.sum(news[:, 0, end : end + sources], axis=0) * scale,
        source_w_grad,
    )


def solution(mesh):
    if mesh.shape["ctx"] == 8 and mesh.shape["rep"] == 4:
        mesh = jax.sharding.Mesh(
            mesh.devices.reshape(2, 4, 2, 2), ("half", "place", "row", "core")
        )
        ctx, rep, body = ("half", "place"), ("row", "core"), on_pairs
    else:
        ctx, rep, body = "ctx", "rep", on_device
    in_specs = (
        P(rep, ctx, None),
        P(),
        P(),
        P(rep, ctx, None, None),
        P(rep, ctx, None),
        P(),
        P(),
        P(None, ctx, None),
        P(rep, ctx, None),
    )
    out_specs = (
        P(rep, ctx, None),
        P(rep, ctx, None, None),
        P(rep, ctx, None),
        P(),
        P(),
        P(),
        P(None, ctx, rep),
    )
    return jax.shard_map(
        body, mesh=mesh, in_specs=in_specs, out_specs=out_specs, check_vma=False
    )
```

```python
import functools
import math

import jax
import jax.numpy as jnp
from jax import lax
from jax.experimental import pallas as pl
from jax.experimental.pallas import tpu as pltpu
from jax.sharding import PartitionSpec as P

MERGED = 16


def expert_rows(rows_hidden, rows_grad, rows_member, lane_weights):
    row_count = rows_hidden.shape[0]
    out_rows = jnp.zeros((row_count, lane_weights.shape[1]), jnp.float32)
    back_rows = jnp.zeros((row_count, lane_weights.shape[2]), jnp.float32)
    grad_list = []
    for member_now in range(lane_weights.shape[0]):
        weight = lane_weights[member_now]
        selected = (rows_member == member_now)[:, None]
        forward = lax.dot_general(
            rows_hidden, weight, (((1,), (1,)), ((), ())), preferred_element_type=jnp.float32
        )
        out_rows = jnp.where(selected, forward, out_rows)
        backward = jnp.dot(rows_grad, weight, preferred_element_type=jnp.float32)
        back_rows = jnp.where(selected, backward, back_rows)
        masked = jnp.where(selected, rows_grad, jnp.zeros_like(rows_grad))
        grad_list.append(
            lax.dot_general(
                masked, rows_hidden, (((0,), (0,)), ((), ())), preferred_element_type=jnp.float32
            )
        )
    return (out_rows, back_rows, jnp.stack(grad_list))


def on_device(
    tokens, router_w, router_b, hidden, teacher_idx, merge_map, merge_coef, source_w, out_grad
):
    ctx_count = lax.axis_size("ctx")
    rep_count = lax.axis_size("rep")
    tok_count = tokens.shape[1]
    feature_count = tokens.shape[2]
    top_count = teacher_idx.shape[2]
    hidden_width = hidden.shape[3]
    out_width = out_grad.shape[2]
    source_count = router_w.shape[1]
    row_share = source_w.shape[1]
    per_lane = max(1, MERGED // ctx_count)
    copies = max(1, ctx_count // MERGED)
    capacity = 5 * tok_count * top_count // (4 * ctx_count)
    slot_count = tok_count * top_count
    grad_scale = 1.0 / math.sqrt(tok_count * ctx_count * rep_count)
    flat_x = tokens.reshape(tok_count, feature_count)
    logits = jnp.dot(flat_x, router_w, preferred_element_type=jnp.float32) + router_b
    choice_ids = teacher_idx.reshape(tok_count, top_count)
    pick_table = choice_ids[:, :, None] == jnp.arange(source_count, dtype=jnp.int32)[None, None, :]
    pick_float = pick_table.astype(jnp.float32)
    chosen = jnp.sum(pick_float * logits[:, None, :], axis=2)
    raised = jnp.exp(chosen)
    gate_probs = raised / jnp.sum(raised, axis=1, keepdims=True)
    merged_id = jnp.sum(jnp.where(pick_table, merge_map[None, None, :], 0), axis=2)
    position = lax.axis_index("ctx") * tok_count + jnp.arange(tok_count, dtype=jnp.int32)
    lane_id = merged_id // per_lane * copies + (position % copies)[:, None]
    member_id = (merged_id % per_lane).reshape(-1)
    lane_flat = lane_id.reshape(-1)
    onehot = (lane_flat[:, None] == jnp.arange(ctx_count, dtype=jnp.int32)[None, :]).astype(
        jnp.int32
    )
    before = jnp.cumsum(onehot, axis=0) - onehot
    slot_rank = jnp.sum(before * onehot, axis=1)
    is_kept = slot_rank < capacity
    slot_index = jnp.where(is_kept, lane_flat * capacity + slot_rank, ctx_count * capacity)
    slot_source = (
        jnp.full((ctx_count * capacity + 1,), slot_count, jnp.int32)
        .at[slot_index]
        .set(jnp.arange(slot_count, dtype=jnp.int32))[: ctx_count * capacity]
    )
    slot_grad = (gate_probs[:, :, None] * out_grad.reshape(tok_count, 1, out_width)).astype(
        jnp.bfloat16
    )
    pad_hidden = jnp.concatenate(
        [hidden.reshape(slot_count, hidden_width), jnp.zeros((1, hidden_width), jnp.bfloat16)],
        axis=0,
    )
    pad_grad = jnp.concatenate(
        [slot_grad.reshape(slot_count, out_width), jnp.zeros((1, out_width), jnp.bfloat16)], axis=0
    )
    pad_member = jnp.concatenate([member_id, jnp.zeros((1,), jnp.int32)], axis=0)
    send_hidden = pad_hidden[slot_source].reshape(ctx_count, capacity, hidden_width)
    send_grad = pad_grad[slot_source].reshape(ctx_count, capacity, out_width)
    send_member = pad_member[slot_source].reshape(ctx_count, capacity)
    lane_group = lax.axis_index("ctx") // copies
    same_group = merge_map[:, None] == merge_map[None, :]
    earlier = jnp.arange(source_count)[:, None] > jnp.arange(source_count)[None, :]
    member_rank = jnp.sum((same_group & earlier).astype(jnp.int32), axis=1)
    source_order = (
        jnp.zeros((source_count,), jnp.int32)
        .at[2 * merge_map + member_rank]
        .set(jnp.arange(source_count, dtype=jnp.int32))
    )
    picked = source_w[source_order].reshape(
        MERGED // per_lane, 2 * per_lane, row_share, hidden_width
    )
    outgoing = jnp.repeat(picked, copies, axis=0)
    arrived = lax.all_to_all(outgoing, "ctx", split_axis=0, concat_axis=2, tiled=True)
    pair_rows = arrived.reshape(per_lane, 2, row_share * ctx_count, hidden_width)
    coef_table = merge_coef[source_order].reshape(MERGED // per_lane, per_lane, 2)
    pair_coef = lax.dynamic_index_in_dim(coef_table, lane_group, 0, keepdims=False)
    lane_weights = (
        pair_coef[:, 0, None, None] * pair_rows[:, 0].astype(jnp.float32)
        + pair_coef[:, 1, None, None] * pair_rows[:, 1].astype(jnp.float32)
    ).astype(jnp.bfloat16)
    recv_hidden, recv_grad, recv_member = (
        lax.all_to_all(send_hidden, "ctx", split_axis=0, concat_axis=0, tiled=True),
        lax.all_to_all(send_grad, "ctx", split_axis=0, concat_axis=0, tiled=True),
        lax.all_to_all(send_member, "ctx", split_axis=0, concat_axis=0, tiled=True),
    )
    out_rows, back_rows, lane_grads = expert_rows(
        recv_hidden.reshape(-1, hidden_width),
        recv_grad.reshape(-1, out_width),
        recv_member.reshape(-1),
        lane_weights,
    )
    home_out, home_back = (
        lax.all_to_all(
            out_rows.astype(jnp.bfloat16).reshape(ctx_count, capacity, out_width),
            "ctx",
            split_axis=0,
            concat_axis=0,
            tiled=True,
        ),
        lax.all_to_all(
            back_rows.astype(jnp.bfloat16).reshape(ctx_count, capacity, hidden_width),
            "ctx",
            split_axis=0,
            concat_axis=0,
            tiled=True,
        ),
    )
    slot_out = jnp.concatenate(
        [home_out.reshape(-1, out_width), jnp.zeros((1, out_width), jnp.bfloat16)], axis=0
    )[slot_index].reshape(tok_count, top_count, out_width)
    hidden_grad = jnp.concatenate(
        [home_back.reshape(-1, hidden_width), jnp.zeros((1, hidden_width), jnp.bfloat16)], axis=0
    )[slot_index].reshape(1, tok_count, top_count, hidden_width)
    mixed = (
        jnp.sum(gate_probs[:, :, None] * slot_out.astype(jnp.float32), axis=1)
        .astype(jnp.bfloat16)
        .reshape(1, tok_count, out_width)
    )
    score_grad = jnp.einsum(
        "td,tkd->tk",
        out_grad.reshape(tok_count, out_width),
        slot_out,
        preferred_element_type=jnp.float32,
    )
    chosen_grad = gate_probs * (
        score_grad - jnp.sum(gate_probs * score_grad, axis=1, keepdims=True)
    )
    logit_grad = jnp.sum(pick_float * chosen_grad[:, :, None], axis=1)
    logit_half = logit_grad.astype(jnp.bfloat16)
    token_grad = (
        lax.dot_general(
            logit_half, router_w, (((1,), (1,)), ((), ())), preferred_element_type=jnp.float32
        )
        .astype(jnp.bfloat16)
        .reshape(1, tok_count, feature_count)
    )
    part_router_w = lax.dot_general(
        flat_x, logit_half, (((0,), (0,)), ((), ())), preferred_element_type=jnp.float32
    )
    part_router_b = jnp.sum(logit_grad, axis=0)
    arrived_grads = lax.all_to_all(
        lane_grads.reshape(per_lane, ctx_count, row_share, hidden_width),
        "ctx",
        split_axis=1,
        concat_axis=0,
        tiled=True,
    )
    merged_grad = (
        arrived_grads.reshape(MERGED // per_lane, copies, per_lane, row_share, hidden_width)
        .sum(axis=1)
        .reshape(MERGED, row_share, hidden_width)
    )
    source_grad = merged_grad[merge_map]
    coef_part = jnp.einsum(
        "edf,edf->e", source_grad, source_w.astype(jnp.float32), precision=lax.Precision.HIGHEST
    )
    summed = lax.psum_scatter(
        source_grad * merge_coef[:, None, None], "rep", scatter_dimension=2, tiled=True
    )
    source_w_grad = summed * grad_scale
    router_sum, bias_sum, coef_sum = lax.psum(
        (part_router_w, part_router_b, coef_part), ("ctx", "rep")
    )
    return (
        mixed,
        hidden_grad,
        token_grad,
        router_sum * grad_scale,
        bias_sum * grad_scale,
        coef_sum * grad_scale,
        source_w_grad,
    )


BF = jnp.bfloat16
F32 = jnp.float32
I32 = jnp.int32
TILE = 256


def cost(us):
    return pl.CostEstimate(flops=us * 10**9, bytes_accessed=us * 10**6, transcendentals=0)


def any_spec():
    return pl.BlockSpec(memory_space=pl.ANY)


def smem_spec():
    return pl.BlockSpec(memory_space=pltpu.SMEM)


def vmem_spec():
    return pl.BlockSpec(memory_space=pltpu.VMEM)


def params(mib):
    return pltpu.CompilerParams(vmem_limit_bytes=mib * 1024 * 1024)


def dot(a, b, dims):
    return lax.dot_general(a, b, (dims, ((), ())), preferred_element_type=F32)


def merge_start(map_ref, place_ref, src_ref, places, order_ref, count_ref, held, sems):
    half = held.shape[2]
    expert_order(map_ref, order_ref, count_ref)
    at = pl.ds(pl.multiple_of(place_ref[1] * half, half), half)
    copies, experts = [], []
    for j in range(places):
        for m in range(2):
            combo = 4 * j + 2 * place_ref[0] + m
            for n in range(2):
                expert = order_ref[2 * combo + n]
                experts.append(expert)
                i = len(copies)
                copies.append(
                    pltpu.make_async_copy(src_ref.at[expert, :, at], held.at[i], sems.at[i])
                )
                copies[-1].start()
    return copies, experts


def merge_finish(copies, experts, coef_ref, held, out_ref):
    halves, places = out_ref.shape[:2]
    for j in range(places):
        for m in range(2):
            i = 4 * j + 2 * m
            copies[i].wait()
            copies[i + 1].wait()
            one, two = coef_ref[experts[i]], coef_ref[experts[i + 1]]
            merged = (one * held[i].astype(F32) + two * held[i + 1].astype(F32)).astype(BF)
            for h in range(halves):
                out_ref[h, j, m] = merged


def expert_order(map_ref, order_ref, count_ref):
    @pl.loop(0, count_ref.shape[0])
    def _(g):
        count_ref[g] = 0

    @pl.loop(0, order_ref.shape[0])
    def _(e):
        g = map_ref[e]
        n = count_ref[g]
        order_ref[2 * g + n] = e
        count_ref[g] = n + 1


def hbm_spec():
    return pl.BlockSpec(memory_space=pltpu.HBM)


def hold(arrays, *after):
    count = len(arrays)
    return pl.pallas_call(
        lambda *refs: None,
        in_specs=[hbm_spec()] * count + [any_spec()] * len(after),
        out_specs=[hbm_spec()] * count,
        out_shape=[jax.ShapeDtypeStruct(a.shape, a.dtype) for a in arrays],
        input_output_aliases={i: i for i in range(count)},
        name="hold",
    )(*arrays, *after)


def column(row):
    size = row.shape[1]
    same = lax.broadcasted_iota(I32, (size, size), 0) == lax.broadcasted_iota(I32, (size, size), 1)
    return jnp.sum(jnp.where(same, row, jnp.zeros_like(row)), axis=1, keepdims=True)


def to_row(col):
    size = col.shape[0]
    same = lax.broadcasted_iota(I32, (size, size), 0) == lax.broadcasted_iota(I32, (size, size), 1)
    return jnp.sum(jnp.where(same, col, jnp.zeros_like(col)), axis=0, keepdims=True)


def picks_of(idx_ref, k, sources):
    tok = idx_ref.shape[1]
    return lax.broadcasted_iota(I32, (sources, tok), 0) == idx_ref[k : k + 1, :]


def prepare_kernel(
    capacity, lanes,
    combo_ref, coef_ref, place_ref, src_ref,
    xt_ref, rwt_ref, rb_ref, idx_ref, map_ref, hid_ref, og_ref,
    merged_ref, send_ref, gate_ref, pos_ref, slot_ref,
    order_ref, count_ref, held, sems,
):
    copies, experts = merge_start(
        combo_ref, place_ref, src_ref, merged_ref.shape[1], order_ref, count_ref, held, sems
    )
    top, tok = idx_ref.shape
    sources = rwt_ref.shape[0]
    slots, width = hid_ref.shape
    places = lanes * capacity
    logits = jnp.dot(rwt_ref[...], xt_ref[...], preferred_element_type=F32) + column(rb_ref[...])
    raised, merged = [], []
    combos = column(map_ref[...])
    for k in range(top):
        pick = picks_of(idx_ref, k, sources)
        chosen = jnp.sum(jnp.where(pick, logits, 0.0), axis=0, keepdims=True)
        raised.append(jnp.exp(chosen))
        merged.append(jnp.sum(jnp.where(pick, combos, 0), axis=0, keepdims=True))
    total = raised[0]
    for k in range(1, top):
        total = total + raised[k]
    gates = [r / total for r in raised]
    lane = [jnp.right_shift(g, 1) for g in merged]
    member = [jnp.bitwise_and(g, 1) for g in merged]
    onehot = [(lax.broadcasted_iota(I32, (lanes, tok), 0) == l).astype(F32) for l in lane]
    all_hot = onehot[0]
    for k in range(1, top):
        all_hot = all_hot + onehot[k]
    earlier = (
        lax.broadcasted_iota(I32, (tok, tok), 0) < lax.broadcasted_iota(I32, (tok, tok), 1)
    ).astype(BF)
    before = jnp.dot(all_hot.astype(BF), earlier, preferred_element_type=F32)
    position, back = [], []
    for k in range(top):
        rank = jnp.sum(before * onehot[k], axis=0, keepdims=True).astype(I32)
        before = before + onehot[k]
        position.append(jnp.where(rank < capacity, lane[k] * capacity + rank, -1))
        partner = jnp.bitwise_xor(lane[k], place_ref[2])
        back.append(jnp.where(rank < capacity, partner * capacity + rank, -1))
    gate_ref[...] = jnp.zeros_like(gate_ref)
    pos_ref[...] = jnp.full_like(pos_ref, -1)
    for k in range(top):
        gate_ref[k : k + 1, :] = gates[k]
        pos_ref[k : k + 1, :] = back[k]
    spot = jnp.zeros((8, slots), F32)
    for k in range(top):
        spread = (
            lax.broadcasted_iota(I32, (tok, slots), 1)
            == lax.broadcasted_iota(I32, (tok, slots), 0) * top + k
        ).astype(BF)
        kept = position[k] >= 0
        parts = [
            jnp.where(kept, lane[k], 0),
            jnp.where(kept, position[k] - lane[k] * capacity, 0),
            jnp.where(kept, 1, 0),
            member[k],
        ]
        stacked = jnp.concatenate(
            [p.astype(F32) for p in parts] + [jnp.zeros((4, tok), F32)], axis=0
        ).astype(BF)
        spot = spot + jnp.dot(stacked, spread, preferred_element_type=F32)
    spot = spot.astype(I32)
    slot_pos = jnp.where(spot[2:3] > 0, spot[0:1] * capacity + spot[1:2], -1)
    partner = jnp.bitwise_xor(spot[0:1], place_ref[2])
    slot_back = jnp.where(spot[2:3] > 0, partner * capacity + spot[1:2], -1)
    slot_ref[...] = jnp.broadcast_to(slot_back, slot_ref.shape)
    take = lax.broadcasted_iota(I32, (places, slots), 0) == slot_pos
    placed = jnp.sum(jnp.where(take, spot[3:4].astype(F32), 0.0), axis=1, keepdims=True)
    depth = og_ref.shape[1]
    send_ref[:, depth + width :] = jnp.broadcast_to(placed, (places, 128)).astype(BF)
    take = take.astype(BF)
    for n in range(0, width, TILE):
        rows = jnp.dot(take, hid_ref[:, n : n + TILE], preferred_element_type=F32)
        send_ref[:, depth + n : depth + n + TILE] = rows.astype(BF)
    takes = [
        (lax.broadcasted_iota(I32, (places, tok), 0) == position[k]).astype(BF) for k in range(top)
    ]
    columns = [column(g) for g in gates]
    for n in range(0, depth, TILE):
        og = og_ref[:, n : n + TILE].astype(F32)
        rows = jnp.zeros((places, TILE), F32)
        for k in range(top):
            rows = rows + jnp.dot(takes[k], (columns[k] * og).astype(BF), preferred_element_type=F32)
        send_ref[:, n : n + TILE] = rows.astype(BF)
    merge_finish(copies, experts, coef_ref, held, merged_ref)


def prepare(
    place, merge_map, merge_coef, source_w, xt, rwt, router_b, idx_t, hid, og, capacity, lanes
):
    count, rows, whole = source_w.shape
    slots, width = hid.shape
    tok = idx_t.shape[1]
    half, places = whole // 2, lanes // 2
    return pl.pallas_call(
        functools.partial(prepare_kernel, capacity, lanes),
        in_specs=[smem_spec()] * 3 + [any_spec()] + [vmem_spec()] * 7,
        out_specs=[vmem_spec()] * 5,
        out_shape=[
            jax.ShapeDtypeStruct((2, places, 2, rows, half), BF),
            jax.ShapeDtypeStruct((lanes * capacity, og.shape[1] + width + 128), BF),
            jax.ShapeDtypeStruct((8, tok), F32),
            jax.ShapeDtypeStruct((8, tok), I32),
            jax.ShapeDtypeStruct((8, slots), I32),
        ],
        scratch_shapes=[
            pltpu.SMEM((count,), I32),
            pltpu.SMEM((count // 2,), I32),
            pltpu.VMEM((4 * places, rows, half), BF),
            pltpu.SemaphoreType.DMA((4 * places,)),
        ],
        compiler_params=params(56),
        cost_estimate=cost(10),
        name="prepare",
    )(
        merge_map, merge_coef, place, source_w,
        xt, rwt, router_b[None, :], idx_t, merge_map[None, :], hid, og,
    )


def gather_rows(refs, keep):
    each = refs[0].shape[0]
    for d, ref in enumerate(refs):
        keep[d * each : (d + 1) * each, :] = ref[...]


def load_weights(core_ref, mine, other, w_ref, sems):
    core = core_ref[0]
    blocks, _, rows, _ = mine.shape
    copies = []
    for c in range(blocks):
        at = pl.ds(c * rows, rows)
        for n, part in enumerate((mine, other)):
            to = core if n == 0 else 1 - core
            i = 2 * c + n
            copies.append(
                pltpu.make_async_copy(part.at[c], w_ref.at[to, :, at, :], sems.at[i])
            )
    for copy in copies:
        copy.start()
    for copy in copies:
        copy.wait()


def lane_kernel(
    core_ref, me_ref, grd_ref, hid_ref, flag_ref, mine, other, *refs
):
    outs, (keep, w_ref, sems) = refs[:-3], refs[-3:]
    load_weights(core_ref, mine, other, w_ref, sems)
    half, depth = w_ref.shape[3], w_ref.shape[2]
    first = flag_ref[:, :1].astype(F32) == 0.0
    for n in range(0, depth, TILE):
        at = slice(n, n + TILE)
        both = [
            dot(hid_ref[:, :half], w_ref[0, m, at, :], ((1,), (1,)))
            + dot(hid_ref[:, half:], w_ref[1, m, at, :], ((1,), (1,)))
            for m in range(2)
        ]
        keep[:, at] = jnp.where(first, both[0], both[1]).astype(BF)
    for h in range(2):
        for n in range(0, half, TILE):
            at = slice(n, n + TILE)
            both = [dot(grd_ref[...], w_ref[h, m, :, at], ((1,), (0,))) for m in range(2)]
            to = depth + h * half + n
            keep[:, to : to + TILE] = jnp.where(first, both[0], both[1]).astype(BF)
    each = outs[0].shape[0]
    for d, out_ref in enumerate(outs):
        at = pl.ds(pl.multiple_of(jnp.bitwise_xor(me_ref[0], d) * each, each), each)
        out_ref[...] = keep[at, :]


def run_lane(core, me, rows, mine, other, lanes):
    blocks, members, share, half = mine.shape
    depth = share * blocks
    count = rows.shape[0]
    wide = (rows.shape[1] - 128) // 2
    part = (count // lanes, 2 * wide)
    return pl.pallas_call(
        lane_kernel,
        grid=(1,),
        in_specs=[
            smem_spec(),
            smem_spec(),
            pl.BlockSpec((count, wide), lambda i: (0, 0)),
            pl.BlockSpec((count, wide), lambda i: (0, 1)),
            pl.BlockSpec((count, 128), lambda i: (0, 2 * wide // 128)),
            any_spec(),
            any_spec(),
        ],
        out_specs=[pl.BlockSpec(part, lambda i: (0, 0))] * lanes,
        out_shape=[jax.ShapeDtypeStruct(part, BF)] * lanes,
        scratch_shapes=[
            pltpu.VMEM((count, 2 * wide), BF),
            pltpu.VMEM((2, members, depth, half), BF),
            pltpu.SemaphoreType.DMA((2 * blocks,)),
        ],
        compiler_params=params(60),
        cost_estimate=cost(20),
        name="lane_products",
    )(core, me, rows, rows, rows, mine, other)


def lane_grad_kernel(has_other, _, grd_ref, hid_ref, flag_ref, *refs):
    out_ref = refs[-1]
    chosen = flag_ref[:, :1].astype(F32) == pl.program_id(1).astype(F32)
    hid = jnp.where(chosen, hid_ref[...], jnp.zeros_like(hid_ref))
    blocks, _, _, rows, cols = out_ref.shape
    each = 2 if blocks % 2 == 0 and 2 * rows % 128 == 0 else blocks
    for n in range(0, blocks, each):
        part = dot(grd_ref[:, n * rows : (n + each) * rows], hid, ((0,), (0,)))
        part = part.reshape(each, rows, cols)
        if has_other:
            part = part + refs[0][n : n + each, 0, 0].astype(F32)
        out_ref[n : n + each, 0, 0] = part.astype(BF)


def lane_grads(core, rows, other, blocks, reps):
    count = rows.shape[0]
    width = (rows.shape[1] - 128) // 2
    cols = width // reps
    shape = (blocks, 2, 2, width // blocks, cols)
    block = pl.BlockSpec((blocks, 1, 1, width // blocks, cols), lambda y, m, s: (0, y, m, 0, 0))
    extra = [] if other is None else [other]
    return pl.pallas_call(
        functools.partial(lane_grad_kernel, other is not None),
        grid_spec=pltpu.PrefetchScalarGridSpec(
            num_scalar_prefetch=1,
            grid=(2, 2),
            in_specs=[
                pl.BlockSpec((count, width), lambda y, m, s: (0, 0)),
                pl.BlockSpec((count, cols), lambda y, m, s: (0, reps + 2 * y + s[0])),
                pl.BlockSpec((count, 128), lambda y, m, s: (0, 2 * width // 128)),
            ]
            + [block] * len(extra),
            out_specs=block,
        ),
        out_shape=jax.ShapeDtypeStruct(shape, BF),
        compiler_params=params(56),
        cost_estimate=cost(8),
        name="lane_grads_add" if extra else "lane_grads_first",
    )(core, rows, rows, rows, *extra)


def combine_kernel(og_ref, gate_ref, pos_ref, idx_ref, rwt_ref, xt_ref, *refs):
    homes, (mixed_ref, tg_ref, part_ref, out_ref) = refs[:-4], refs[-4:]
    gather_rows(homes, out_ref)
    places, width = out_ref.shape
    top, tok = idx_ref.shape
    sources, features = rwt_ref.shape
    takes = [
        (lax.broadcasted_iota(I32, (places, tok), 0) == pos_ref[k : k + 1, :]).astype(BF)
        for k in range(top)
    ]
    gates = [gate_ref[k : k + 1, :] for k in range(top)]
    columns = [column(g) for g in gates]
    scores = [jnp.zeros((tok, 1), F32) for _ in range(top)]
    for n in range(0, width, TILE):
        og = og_ref[:, n : n + TILE].astype(F32)
        rows = out_ref[:, n : n + TILE]
        mixed = jnp.zeros((tok, TILE), F32)
        for k in range(top):
            slot_out = dot(takes[k], rows, ((0,), (0,)))
            mixed = mixed + columns[k] * slot_out
            scores[k] = scores[k] + jnp.sum(og * slot_out, axis=1, keepdims=True)
        mixed_ref[:, n : n + TILE] = mixed.astype(BF)
    scores = [to_row(s) for s in scores]
    middle = gates[0] * scores[0]
    for k in range(1, top):
        middle = middle + gates[k] * scores[k]
    logit_grad = jnp.zeros((sources, tok), F32)
    for k in range(top):
        chosen_grad = gates[k] * (scores[k] - middle)
        logit_grad = logit_grad + jnp.where(picks_of(idx_ref, k, sources), chosen_grad, 0.0)
    logit_half = logit_grad.astype(BF)
    tg_ref[...] = dot(rwt_ref[...], logit_half, ((0,), (0,))).astype(BF)
    part_ref[...] = jnp.zeros_like(part_ref)
    part_ref[:, 0, :features] = dot(logit_half, xt_ref[...], ((1,), (1,)))
    bias = jnp.sum(logit_grad, axis=1, keepdims=True)
    last = part_ref.shape[2] - 128
    part_ref[:, 0, last:] = jnp.broadcast_to(bias, (sources, 128))


def combine(homes, og, gates, pos, idx_t, rwt, xt):
    sources, features = rwt.shape
    tok, width = og.shape
    each = homes[0].shape[0]
    whole = lambda a: pl.BlockSpec(a.shape, lambda i: (0,) * len(a.shape))
    outs = [
        jax.ShapeDtypeStruct(og.shape, BF),
        jax.ShapeDtypeStruct((features, tok), BF),
        jax.ShapeDtypeStruct((sources, 1, (features + 127) // 128 * 128 + 128), F32),
    ]
    return pl.pallas_call(
        combine_kernel,
        grid=(1,),
        in_specs=[whole(a) for a in (og, gates, pos, idx_t, rwt, xt)]
        + [pl.BlockSpec((each, width), lambda i: (0, 0))] * len(homes),
        out_specs=[whole(a) for a in outs],
        out_shape=outs,
        scratch_shapes=[pltpu.VMEM((len(homes) * each, width), BF)],
        compiler_params=params(56),
        cost_estimate=cost(5),
        name="combine",
    )(og, gates, pos, idx_t, rwt, xt, *homes)


def unplace_kernel(slot_ref, *refs):
    homes, (out_ref, back_ref) = refs[:-2], refs[-2:]
    gather_rows(homes, back_ref)
    places, width = back_ref.shape
    slots = slot_ref.shape[1]
    take = (lax.broadcasted_iota(I32, (places, slots), 0) == slot_ref[0:1, :]).astype(BF)
    for n in range(0, width, TILE):
        out_ref[:, n : n + TILE] = dot(take, back_ref[:, n : n + TILE], ((0,), (0,))).astype(BF)


def unplace(homes, slot_pos):
    each, width = homes[0].shape[0], homes[0].shape[1] // 2
    slots = slot_pos.shape[1]
    return pl.pallas_call(
        unplace_kernel,
        grid=(1,),
        in_specs=[pl.BlockSpec(slot_pos.shape, lambda i: (0, 0))]
        + [pl.BlockSpec((each, width), lambda i: (0, 1))] * len(homes),
        out_specs=pl.BlockSpec((slots, width), lambda i: (0, 0)),
        out_shape=jax.ShapeDtypeStruct((slots, width), BF),
        scratch_shapes=[pltpu.VMEM((len(homes) * each, width), BF)],
        compiler_params=params(56),
        cost_estimate=cost(4),
        name="unplace",
    )(slot_pos, *homes)


def coef_kernel(rep_ref, map_ref, src_ref, got_ref, out_ref, order_ref, count_ref, held, weights, sems):
    count, rows, cols = weights.shape
    at = pl.ds(pl.multiple_of(rep_ref[0] * cols, cols), cols)
    copies = [
        pltpu.make_async_copy(src_ref.at[:, :, at], weights, sems.at[0]),
        pltpu.make_async_copy(got_ref, held, sems.at[1]),
    ]
    for copy in copies:
        copy.start()
    expert_order(map_ref, order_ref, count_ref)
    for copy in copies:
        copy.wait()
    lane = lax.broadcasted_iota(I32, (8, 128), 1)

    def one(g, total):
        merged = held[0, g].astype(F32) + held[1, g].astype(F32)
        for n in range(2):
            expert = order_ref[2 * g + n]
            product = merged * weights[expert].astype(F32)
            folded = jnp.sum(product.reshape(rows // 8, 8, cols), axis=0)
            small = folded[:, :128]
            for c in range(128, cols, 128):
                small = small + folded[:, c : c + 128]
            small = jnp.sum(jnp.sum(small, axis=0, keepdims=True), axis=1, keepdims=True)
            total = total + jnp.where(lane == expert, small, 0.0)
        return total

    out_ref[...] = lax.fori_loop(0, count // 2, one, jnp.zeros((8, 128), F32))


def finish_kernel(scale, map_ref, coef_ref, got_ref, out_ref, order_ref, count_ref, held, ready, sems, more):
    count = ready.shape[0]

    def load(g):
        return pltpu.make_async_copy(got_ref.at[:, g], held.at[:, g], sems.at[g])

    def send(i):
        return pltpu.make_async_copy(ready.at[i], out_ref.at[order_ref[i]], more.at[i])

    @pl.loop(0, count // 2)
    def _(g):
        load(g).start()

    expert_order(map_ref, order_ref, count_ref)

    @pl.loop(0, count // 2)
    def _(g):
        load(g).wait()
        merged = held[0, g].astype(F32) + held[1, g].astype(F32)
        for n in range(2):
            i = 2 * g + n
            ready[i] = merged * (coef_ref[order_ref[i]] * scale)
            send(i).start()

    @pl.loop(0, count)
    def _(i):
        send(i).wait()


def coef_dots(rep_index, merge_map, source_w, arrived):
    count = source_w.shape[0]
    _, _, rows, cols = arrived.shape
    return pl.pallas_call(
        coef_kernel,
        in_specs=[smem_spec(), smem_spec(), hbm_spec(), hbm_spec()],
        out_specs=vmem_spec(),
        out_shape=jax.ShapeDtypeStruct((8, 128), F32),
        scratch_shapes=[
            pltpu.SMEM((count,), I32),
            pltpu.SMEM((count // 2,), I32),
            pltpu.VMEM(arrived.shape, BF),
            pltpu.VMEM((count, rows, cols), BF),
            pltpu.SemaphoreType.DMA((2,)),
        ],
        compiler_params=params(56),
        cost_estimate=cost(0),
        name="coef_dots",
    )(rep_index, merge_map, source_w, arrived)


def finish(merge_map, merge_coef, arrived, after, scale):
    count = merge_map.shape[0]
    _, _, rows, cols = arrived.shape
    return pl.pallas_call(
        lambda a, b, c, _, *refs: finish_kernel(scale, a, b, c, *refs),
        in_specs=[smem_spec(), smem_spec(), hbm_spec(), any_spec()],
        out_specs=hbm_spec(),
        out_shape=jax.ShapeDtypeStruct((count, rows, cols), F32),
        scratch_shapes=[
            pltpu.SMEM((count,), I32),
            pltpu.SMEM((count // 2,), I32),
            pltpu.VMEM(arrived.shape, BF),
            pltpu.VMEM((count, rows, cols), F32),
            pltpu.SemaphoreType.DMA((count // 2,)),
            pltpu.SemaphoreType.DMA((count,)),
        ],
        compiler_params=params(56),
        cost_estimate=cost(0),
        name="finish",
    )(merge_map, merge_coef, arrived, after)


def swap(x):
    return lax.ppermute(x, "core", [(0, 1), (1, 0)])


def on_pairs(
    tokens, router_w, router_b, hidden, teacher_idx, merge_map, merge_coef, source_w, out_grad
):
    places = lax.axis_size("place")
    blocks = 2 * places
    reps = 4
    tok = tokens.shape[1]
    features = tokens.shape[2]
    top = teacher_idx.shape[2]
    width = hidden.shape[3]
    depth = out_grad.shape[2]
    sources = router_w.shape[1]
    row_share = source_w.shape[1]
    lanes = 2 * places
    capacity = 5 * tok * top // (4 * blocks)
    scale = 1.0 / math.sqrt(tok * blocks * reps)
    half_i, place_i = lax.axis_index("half"), lax.axis_index("place")
    row_i, core_i = lax.axis_index("row"), lax.axis_index("core")
    ctx_i = half_i * places + place_i
    everyone = ("half", "place", "row", "core")
    devices = blocks * reps

    def stack(numbers):
        return jnp.stack([jnp.asarray(n, I32) for n in numbers])

    def later(*x):
        return swap(hold([jnp.zeros((8, 128), F32)], *x)[0])

    def trade(x, axes):
        return lax.all_to_all(x, axes, split_axis=0, concat_axis=0, tiled=True)

    xt = tokens.reshape(tok, features).T
    rwt = router_w.T
    idx_t = teacher_idx.reshape(tok, top).T
    og = out_grad.reshape(tok, depth)
    combos, send_rows, gates, pos, slot_pos = prepare(
        stack([row_i, core_i, 2 * place_i + row_i]), merge_map, merge_coef, source_w,
        xt, rwt, router_b, idx_t, hidden.reshape(tok * top, width), og, capacity, lanes,
    )
    rows = trade(send_rows.reshape(lanes, capacity, send_rows.shape[1]), ("place", "row"))
    rows = rows.reshape(send_rows.shape)
    (combos,) = hold([combos.reshape((blocks,) + combos.shape[2:])], rows)
    mine = trade(combos, ("half", "place"))
    (rows,) = hold([rows], later(rows))
    here = stack([core_i])
    first = lane_grads(stack([1 - core_i]), rows, None, blocks, reps)
    summed = lane_grads(here, rows, swap(first), blocks, reps)
    (mine,) = hold([mine], summed)
    (summed,) = hold([summed], mine)
    arrived = trade(
        summed.reshape(2 * blocks, 2, row_share, width // reps), ("half", "place", "row")
    )

    other = swap(mine)
    me = stack([2 * place_i + row_i])
    (rows,) = hold([rows], later(summed))
    parts = run_lane(here, me, rows, mine, other, lanes)

    def give(d):
        return lax.ppermute(parts[d], ("place", "row"), [(i, i ^ d) for i in range(lanes)])

    order = [3] + list(range(4, lanes)) + [2, 1]
    home = [give(d) for d in order]
    arrived = arrived.reshape(2, 2 * lanes, row_share, width // reps)
    dots = coef_dots(stack([2 * row_i + core_i]), merge_map, source_w, arrived)
    source_w_grad = finish(merge_map, merge_coef, arrived, dots, scale)
    home = dict(zip(order, hold(home, source_w_grad)))
    home = [parts[0]] + [home[d] for d in range(1, lanes)]
    mixed, token_grad, part = combine(home, og, gates, pos, idx_t, rwt, xt)
    part = jnp.sum(trade(part, everyone), axis=0)
    hidden_grad = unplace(home, slot_pos).reshape(1, tok, top, width)
    news = jnp.concatenate([part, dots[:1]], axis=1)
    (news,) = hold([news], hidden_grad)
    news = trade(jnp.broadcast_to(news[None], (devices,) + news.shape), everyone)
    end = part.shape[1]
    return (
        mixed.reshape(1, tok, depth),
        hidden_grad,
        token_grad.T.reshape(1, tok, features),
        news[:, 0, :features].T * scale,
        news[:, 0, end - 1] * scale,
        jnp.sum(news[:, 0, end : end + sources], axis=0) * scale,
        source_w_grad,
    )


def solution(mesh):
    if mesh.shape["ctx"] == 8 and mesh.shape["rep"] == 4:
        mesh = jax.sharding.Mesh(
            mesh.devices.reshape(2, 4, 2, 2), ("half", "place", "row", "core")
        )
        ctx, rep, body = ("half", "place"), ("row", "core"), on_pairs
    else:
        ctx, rep, body = "ctx", "rep", on_device
    in_specs = (
        P(rep, ctx, None),
        P(),
        P(),
        P(rep, ctx, None, None),
        P(rep, ctx, None),
        P(),
        P(),
        P(None, ctx, None),
        P(rep, ctx, None),
    )
    out_specs = (
        P(rep, ctx, None),
        P(rep, ctx, None, None),
        P(rep, ctx, None),
        P(),
        P(),
        P(),
        P(None, ctx, rep),
    )
    return jax.shard_map(
        body, mesh=mesh, in_specs=in_specs, out_specs=out_specs, check_vma=False
    )
```
